32 devices in a mesh: dp: 16 (over z, y, x), mp: 2 (over core).
Axes of the slice: x: 2, y: 2, z: 4, core: 2. Of those that a mesh axis runs over, the one named last changes fastest.
Arguments:
- tokens: bfloat16 [2, 16, 512, 768], P(None, 'dp'), may hold values from -6 to 6
- pair_lengths: int32 [2, 16], P(None, 'dp'), may hold values from 128 to 512, as said below
- query_ids: int32 [2, 16], replicated, may hold values from 0 to 3, as said below
- distance_bucket: int32 [1023], replicated, may hold values from 0 to 31, as said below
- step_count: int32 [], replicated, may hold values from 1 to 20
- heads_in: float32 [768, 3, 768], P('dp', None, 'mp'), may hold values from -0.21650635 to 0.21650635
- heads_out: float32 [768, 768], P('dp', 'mp'), may hold values from -0.875 to 0.875
- hidden_in: float32 [768, 3072], P('dp', 'mp'), may hold values from -0.21875 to 0.21875
- hidden_out: float32 [768, 3072], P('dp', 'mp'), may hold values from -0.15625 to 0.15625
- gains: float32 [768, 3], P('dp'), may hold values from 0.3 to 2.5
- tied_rows: float32 [768, 2], P('dp'), may hold values from -6 to 6
- bias_table: float32 [32, 12], P(None, 'mp'), may hold values from -6 to 6
- first_heads_in: float32 [768, 3, 768], P('dp', None, 'mp'), may hold values from -5.722046e-06 to 5.722046e-06
- first_heads_out: float32 [768, 768], P('dp', 'mp'), may hold values from -5.722046e-06 to 5.722046e-06
- first_hidden_in: float32 [768, 3072], P('dp', 'mp'), may hold values from -5.722046e-06 to 5.722046e-06
- first_hidden_out: float32 [768, 3072], P('dp', 'mp'), may hold values from -5.722046e-06 to 5.722046e-06
- first_gains: float32 [768, 3], P('dp'), may hold values from -5.722046e-06 to 5.722046e-06
- first_tied: float32 [768, 2], P('dp'), may hold values from -5.722046e-06 to 5.722046e-06
- first_table: float32 [32, 12], P(None, 'mp'), may hold values from -5.722046e-06 to 5.722046e-06
- second_heads_in: float32 [768, 3, 768], P('dp', None, 'mp'), may hold values from 7.060041e-15 to 5.6480326e-14
- second_heads_out: float32 [768, 768], P('dp', 'mp'), may hold values from 7.060041e-15 to 5.6480326e-14
- second_hidden_in: float32 [768, 3072], P('dp', 'mp'), may hold values from 7.060041e-15 to 5.6480326e-14
- second_hidden_out: float32 [768, 3072], P('dp', 'mp'), may hold values from 7.060041e-15 to 5.6480326e-14
- second_gains: float32 [768, 3], P('dp'), may hold values from 7.060041e-15 to 5.6480326e-14
- second_tied: float32 [768, 2], P('dp'), may hold values from 7.060041e-15 to 5.6480326e-14
- second_table: float32 [32, 12], P(None, 'mp'), may hold values from 7.060041e-15 to 5.6480326e-14
Outputs:
- gradient_norm: float32 [], replicated
- token_gradient: float32 [2, 16, 512, 768], P(None, 'dp')
- next_heads_in: float32 [768, 3, 768], P('dp', None, 'mp')
- next_heads_out: float32 [768, 768], P('dp', 'mp')
- next_hidden_in: float32 [768, 3072], P('dp', 'mp')
- next_hidden_out: float32 [768, 3072], P('dp', 'mp')
- next_gains: float32 [768, 3], P('dp')
- next_tied: float32 [768, 2], P('dp')
- next_table: float32 [32, 12], P(None, 'mp')
- next_first_heads_in: float32 [768, 3, 768], P('dp', None, 'mp')
- next_first_heads_out: float32 [768, 768], P('dp', 'mp')
- next_first_hidden_in: float32 [768, 3072], P('dp', 'mp')
- next_first_hidden_out: float32 [768, 3072], P('dp', 'mp')
- next_first_gains: float32 [768, 3], P('dp')
- next_first_tied: float32 [768, 2], P('dp')
- next_first_table: float32 [32, 12], P(None, 'mp')
- next_second_heads_in: float32 [768, 3, 768], P('dp', None, 'mp')
- next_second_heads_out: float32 [768, 768], P('dp', 'mp')
- next_second_hidden_in: float32 [768, 3072], P('dp', 'mp')
- next_second_hidden_out: float32 [768, 3072], P('dp', 'mp')
- next_second_gains: float32 [768, 3], P('dp')
- next_second_tied: float32 [768, 2], P('dp')
- next_second_table: float32 [32, 12], P(None, 'mp')
The draws below stay inside these ranges and needn't reach their ends.
Inputs may be any that keep to these rules, and one draw needn't show every extreme that they name: `pair_lengths`: pair 0 of each micro-batch uses all 512 positions of its slot. `query_ids`: every id names at least one pair of each micro-batch. `distance_bucket`: entry r + 511 is the bucket of key minus query r: buckets 16 to 31 are for r > 0, 0 to 15 for r <= 0; a magnitude below 8 is its own bucket (plus 16 for r > 0); larger magnitudes take buckets 8 to 15 (plus 16) that never fall as the magnitude grows, and the largest magnitude takes 15 (plus 16).
All inputs are finite; a program needn't handle non-finite values.
Results may differ from the reference program's by a relative error of at most 0.014.
Values may be sent and summed in bfloat16 or wider, within the bound.
No kernel may reach another device: no remote copies, remote signals or barrier semaphores. Data moves between devices by JAX's collectives and lax.ppermute only.
A program may use at most 320 MiB of HBM per device.

```python
import math
import jax
import jax.numpy as jnp
from jax import lax

D = 768
H = 12
DH = 64
FF = 3072
BUCKETS = 32
SLOT = 512
MICRO = 2
LOSS_SCALE = 1024
PAIRS = 16
QUERIES = 4
PARAMS = 7082112


def draw_pair_lengths(key, part):
    drawn_len = jax.random.randint(key, (MICRO, PAIRS), SLOT // 4, SLOT + 1, dtype=jnp.int32)
    first_pair = jnp.arange(PAIRS, dtype=jnp.int32)[None, :] == 0
    return jnp.where(first_pair, SLOT, drawn_len).astype(jnp.int32)


def draw_query_ids(key, part):
    fill_key, order_key = jax.random.split(key)
    repeated = jax.random.randint(fill_key, (MICRO, PAIRS - QUERIES), 0, QUERIES, dtype=jnp.int32)
    each_query = jnp.broadcast_to(jnp.arange(QUERIES, dtype=jnp.int32)[None, :], (MICRO, QUERIES))
    joined = jnp.concatenate([each_query, repeated], axis=1)
    shuffle_order = jax.vmap(lambda sub_key: jax.random.permutation(sub_key, PAIRS))(jax.random.split(order_key, MICRO))
    return jnp.take_along_axis(joined, shuffle_order.astype(jnp.int32), axis=1).astype(jnp.int32)


def draw_distance_bucket(key, part):
    boundary_picks = jax.random.permutation(key, SLOT - 9)[:7].astype(jnp.int32) + 9
    boundaries = jnp.sort(boundary_picks)
    offsets = jnp.arange(2 * SLOT - 1, dtype=jnp.int32) - (SLOT - 1)
    magnitude = jnp.abs(offsets)
    distant = 8 + jnp.sum((magnitude[:, None] >= boundaries[None, :]).astype(jnp.int32), axis=1)
    bucket_ids = jnp.where(magnitude < 8, magnitude, distant)
    return (bucket_ids + jnp.where(offsets > 0, 16, 0)).astype(jnp.int32)


def draw_heads_in(key, part):
    raw = jnp.clip(jax.random.normal(key, (D, 3, D), dtype=jnp.float32), -6.0, 6.0) * D ** (-0.5)
    factor = jnp.where(jnp.arange(3)[None, :, None] == 0, DH ** (-0.5), 1.0)
    return (raw * factor).astype(jnp.float32)


def rising_gains(key, start, ratio):
    place = jnp.arange(D, dtype=jnp.float32) / (D - 1)
    base = start * ratio ** place
    jitter = jax.random.uniform(key, (D, 3), dtype=jnp.float32, minval=0.85, maxval=1.15)
    return (base[:, None] * jitter).astype(jnp.float32)


def draw_gains(key, part):
    key = jax.random.fold_in(key, 11)
    return rising_gains(key, 0.6, 3.0)


def shard_levels(own_key, dims, cuts, smallest, high):
    gain, own = 1.0, jax.random.fold_in(own_key, 6)
    for axis_at, parts in cuts:
        steps = jnp.exp(jax.random.uniform(jax.random.fold_in(own, axis_at), (parts,), jnp.float32, smallest / len(cuts), high / len(cuts)))
        gain = gain * jnp.repeat(steps, dims[axis_at] // parts).reshape([-1 if axis == axis_at else 1 for axis in range(len(dims))])
    return gain


def centred(own_key, shape, scale, bound, shards=(), kind=jnp.bfloat16):
    factor_of = shard_levels(own_key, shape, shards, -0.22, 0.18) if shards else 1.0
    values = jax.random.normal(own_key, shape, jnp.float32) * scale * factor_of
    return jnp.minimum(jnp.maximum(values, -bound), bound).astype(kind)


def setup_inputs(seed: int = 0) -> dict:
    streams_of = jax.random.split(jax.random.key(seed), 27)
    return {
        "tokens": centred(streams_of[0], (MICRO, PAIRS, SLOT, D), 1.0, 6.0, ((1, 16),)),
        "pair_lengths": draw_pair_lengths(jax.random.fold_in(streams_of[26], 71), 0),
        "query_ids": draw_query_ids(jax.random.fold_in(streams_of[26], 71), 0),
        "distance_bucket": draw_distance_bucket(jax.random.fold_in(streams_of[26], 71), 0),
        "step_count": jax.random.randint(streams_of[4], (), 1, 21).astype(jnp.int32),
        "heads_in": draw_heads_in(jax.random.fold_in(streams_of[26], 71), 0),
        "heads_out": centred(streams_of[6], (D, D), (D // 16) ** -0.5, 0.875, ((0, 16), (1, 2)), jnp.float32),
        "hidden_in": centred(streams_of[7], (D, FF), D ** -0.5, 0.21875, ((0, 16), (1, 2)), jnp.float32),
        "hidden_out": centred(streams_of[8], (D, FF), (FF // 2) ** -0.5, 0.15625, ((0, 16), (1, 2)), jnp.float32),
        "gains": draw_gains(jax.random.fold_in(streams_of[26], 71), 0),
        "tied_rows": centred(streams_of[10], (D, 2), 1.0, 6.0, ((0, 16),), jnp.float32),
        "bias_table": centred(streams_of[11], (BUCKETS, H), 1.0, 6.0, ((1, 2),), jnp.float32),
        "first_heads_in": centred(streams_of[12], (D, 3, D), (0.0011 * PARAMS ** -0.5), 5.7220458984375e-06, ((0, 16), (2, 2)), jnp.float32),
        "first_heads_out": centred(streams_of[13], (D, D), (0.0011 * PARAMS ** -0.5), 5.7220458984375e-06, ((0, 16), (1, 2)), jnp.float32),
        "first_hidden_in": centred(streams_of[14], (D, FF), (0.0011 * PARAMS ** -0.5), 5.7220458984375e-06, ((0, 16), (1, 2)), jnp.float32),
        "first_hidden_out": centred(streams_of[15], (D, FF), (0.0011 * PARAMS ** -0.5), 5.7220458984375e-06, ((0, 16), (1, 2)), jnp.float32),
        "first_gains": centred(streams_of[16], (D, 3), (0.0011 * PARAMS ** -0.5), 5.7220458984375e-06, ((0, 16),), jnp.float32),
        "first_tied": centred(streams_of[17], (D, 2), (0.0011 * PARAMS ** -0.5), 5.7220458984375e-06, ((0, 16),), jnp.float32),
        "first_table": centred(streams_of[18], (BUCKETS, H), (0.0011 * PARAMS ** -0.5), 5.7220458984375e-06, ((1, 2),), jnp.float32),
        "second_heads_in": jnp.clip(jnp.exp(math.log(5.64803263295062e-14) - 2.0794415 * jax.random.uniform(streams_of[19], (D, 3, D), jnp.float32) ** shard_levels(streams_of[19], (D, 3, D), ((0, 16), (2, 2)), -0.2, 0.2)), 7.060040791188275e-15, 5.64803263295062e-14),
        "second_heads_out": jnp.clip(jnp.exp(math.log(5.64803263295062e-14) - 2.0794415 * jax.random.uniform(streams_of[20], (D, D), jnp.float32) ** shard_levels(streams_of[20], (D, D), ((0, 16), (1, 2)), -0.2, 0.2)), 7.060040791188275e-15, 5.64803263295062e-14),
        "second_hidden_in": jnp.clip(jnp.exp(math.log(5.64803263295062e-14) - 2.0794415 * jax.random.uniform(streams_of[21], (D, FF), jnp.float32) ** shard_levels(streams_of[21], (D, FF), ((0, 16), (1, 2)), -0.2, 0.2)), 7.060040791188275e-15, 5.64803263295062e-14),
        "second_hidden_out": jnp.clip(jnp.exp(math.log(5.64803263295062e-14) - 2.0794415 * jax.random.uniform(streams_of[22], (D, FF), jnp.float32) ** shard_levels(streams_of[22], (D, FF), ((0, 16), (1, 2)), -0.2, 0.2)), 7.060040791188275e-15, 5.64803263295062e-14),
        "second_gains": jnp.clip(jnp.exp(math.log(5.64803263295062e-14) - 2.0794415 * jax.random.uniform(streams_of[23], (D, 3), jnp.float32) ** shard_levels(streams_of[23], (D, 3), ((0, 16),), -0.2, 0.2)), 7.060040791188275e-15, 5.64803263295062e-14),
        "second_tied": jnp.clip(jnp.exp(math.log(5.64803263295062e-14) - 2.0794415 * jax.random.uniform(streams_of[24], (D, 2), jnp.float32) ** shard_levels(streams_of[24], (D, 2), ((0, 16),), -0.2, 0.2)), 7.060040791188275e-15, 5.64803263295062e-14),
        "second_table": jnp.clip(jnp.exp(math.log(5.64803263295062e-14) - 2.0794415 * jax.random.uniform(streams_of[25], (BUCKETS, H), jnp.float32) ** shard_levels(streams_of[25], (BUCKETS, H), ((1, 2),), -0.2, 0.2)), 7.060040791188275e-15, 5.64803263295062e-14),
    }


norm_eps = 1e-06
clip_limit = 0.01
beta_first = 0.9
beta_second = 0.999
adam_eps = 1e-08
rate_matrix = 0.03
rate_vector = 0.25
decay_matrix = 0.1
masked_score = -1e+30
highest = lax.Precision.HIGHEST

@jax.custom_vjp
def low(v):
    return lax.optimization_barrier(v.astype(jnp.bfloat16)).astype(jnp.float32)

@jax.custom_vjp
def low_back(v):
    return v

def low_keep(v):
    return (low(v), None)

def low_pass(kept, grad):
    return (grad,)

def back_keep(v):
    return (v, None)

def back_low(kept, grad):
    return (low(grad),)
low.defvjp(low_keep, low_pass)
low_back.defvjp(back_keep, back_low)

def rms_scale(rows_in):
    return lax.rsqrt(lax.optimization_barrier(jnp.mean(rows_in * rows_in, axis=-1, keepdims=True)) + norm_eps)

def pair_block(params, rows_in, length_row, bias_full):
    heads_in, heads_out, hidden_in, hidden_out, gains, tied_rows, bias_table = params
    pair_count, slot_len, model_width = rows_in.shape
    head_dim = model_width // H
    normed_first = low(rows_in * rms_scale(rows_in) * gains[:, 0])
    projected = jnp.einsum('psd,dcf->cpsf', normed_first, heads_in, precision=highest)
    split_shape = (pair_count, slot_len, H, head_dim)
    queries = low(low_back(projected[0])).reshape(split_shape)
    key_rows = low(low_back(projected[1])).reshape(split_shape)
    value_rows = low(low_back(projected[2])).reshape(split_shape)
    scores = jnp.einsum('pqhe,pkhe->phqk', queries, key_rows, precision=highest) + bias_full[None]
    scores = low_back(scores)
    positions = jnp.arange(slot_len, dtype=jnp.int32)
    key_valid = positions[None, :] < length_row[:, None]
    scores = jnp.where(key_valid[:, None, None, :], scores, masked_score)
    row_max = lax.optimization_barrier(jnp.max(scores, axis=-1, keepdims=True))
    exp_terms = jnp.exp(scores - row_max)
    prob_low = low(exp_terms / lax.optimization_barrier(jnp.sum(exp_terms, axis=-1, keepdims=True)))
    attended = jnp.einsum('phqk,pkhe->pqhe', prob_low, value_rows, precision=highest).reshape(pair_count, slot_len, model_width)
    attended = low(low_back(attended))
    branch = low_back(jnp.einsum('psf,df->psd', attended, heads_out, precision=highest))
    middle = rows_in + branch
    normed_second = low(middle * rms_scale(middle) * gains[:, 1])
    hidden_pre = low_back(jnp.einsum('psd,df->psf', normed_second, hidden_in, precision=highest))
    activation = low(jax.nn.gelu(hidden_pre, approximate=True))
    block_out = middle + low_back(jnp.einsum('psf,df->psd', activation, hidden_out, precision=highest))
    tok_valid = key_valid.astype(jnp.float32)
    return lax.optimization_barrier(jnp.sum(block_out * tok_valid[..., None], axis=1)) / length_row.astype(jnp.float32)[:, None]

def listwise_loss(pooled, query_row, gain_final, tied_rows):
    final_rows = pooled * rms_scale(pooled) * gain_final
    logits = jnp.dot(final_rows, tied_rows, precision=highest) * pooled.shape[1] ** (-0.5)
    margin = logits[:, 0] - logits[:, 1]
    same_query = query_row[:, None] == query_row[None, :]
    pair_order = jnp.arange(query_row.shape[0])
    earlier = jnp.any(same_query & (pair_order[None, :] < pair_order[:, None]), axis=1)
    positive = jnp.where(earlier, 0.0, 1.0)
    row_max = lax.optimization_barrier(jnp.max(jnp.where(same_query, margin[None, :], masked_score), axis=1))
    group_total = lax.optimization_barrier(jnp.sum(jnp.where(same_query, jnp.exp(margin[None, :] - row_max[:, None]), 0.0), axis=1))
    log_chance = margin - row_max - jnp.log(group_total)
    return -jnp.sum(positive * log_chance)

def micro_loss(params_master, rows_in, length_row, query_row, bucket_full):
    params = tuple((low(piece) for piece in params_master))
    bias_full = jnp.moveaxis(params[6][bucket_full], 2, 0)
    pair_count = rows_in.shape[0]
    group_size = 4 if pair_count % 4 == 0 else 1
    rows_blocks = rows_in.reshape((pair_count // group_size, group_size) + rows_in.shape[1:])
    length_blocks = length_row.reshape(pair_count // group_size, group_size)
    block_fn = jax.checkpoint(lambda block_pair: pair_block(params, block_pair[0], block_pair[1], bias_full))
    pooled = lax.map(block_fn, (rows_blocks, length_blocks)).reshape(pair_count, -1)
    pooled = low(pooled)
    return listwise_loss(pooled, query_row, params[4][:, 2], params[5])

def adam_update(weight, first_old, second, clipped, rate, decay, step_count):
    next_first = beta_first * first_old + (1.0 - beta_first) * clipped
    next_second = beta_second * second + (1.0 - beta_second) * clipped * clipped
    step_float = step_count.astype(jnp.float32)
    first_hat = next_first / (1.0 - beta_first ** step_float)
    second_hat = next_second / (1.0 - beta_second ** step_float)
    next_weight = weight - rate * (first_hat / (jnp.sqrt(second_hat) + adam_eps) + decay * weight)
    return (next_weight, next_first, next_second)

def reference(tokens, pair_lengths, query_ids, distance_bucket, step_count, heads_in, heads_out, hidden_in, hidden_out, gains, tied_rows, bias_table, first_heads_in, first_heads_out, first_hidden_in, first_hidden_out, first_gains, first_tied, first_table, second_heads_in, second_heads_out, second_hidden_in, second_hidden_out, second_gains, second_tied, second_table):
    params = (heads_in, heads_out, hidden_in, hidden_out, gains, tied_rows, bias_table)
    firsts = (first_heads_in, first_heads_out, first_hidden_in, first_hidden_out, first_gains, first_tied, first_table)
    seconds = (second_heads_in, second_heads_out, second_hidden_in, second_hidden_out, second_gains, second_tied, second_table)
    slot_len = tokens.shape[2]
    positions = jnp.arange(slot_len, dtype=jnp.int32)
    bucket_full = distance_bucket[(positions[None, :] - positions[:, None] + slot_len - 1).astype(jnp.int32)]
    totals = tuple((jnp.zeros_like(piece) for piece in params))
    token_grads = []
    for micro_step in range(MICRO):
        rows_in = tokens[micro_step].astype(jnp.float32)
        length_row = pair_lengths[micro_step]
        query_row = query_ids[micro_step]
        loss_fn = lambda weights, rows_now: micro_loss(weights, rows_now, length_row, query_row, bucket_full)
        loss_value, pullback = jax.vjp(loss_fn, params, rows_in)
        grad_params, grad_rows = pullback(jnp.asarray(LOSS_SCALE, dtype=jnp.float32))
        totals = tuple((old + new for old, new in zip(totals, grad_params)))
        token_grads.append(grad_rows)
    grads = tuple((piece / LOSS_SCALE for piece in totals))
    gradient_norm = jnp.sqrt(sum((jnp.sum(piece * piece) for piece in grads)))
    clip_factor = jnp.minimum(1.0, clip_limit / (gradient_norm + 1e-06))
    step_rates = (rate_matrix,) * 4 + (rate_vector,) * 3
    decays = (decay_matrix,) * 4 + (0.0,) * 3
    results = [adam_update(params[index], firsts[index], seconds[index], grads[index] * clip_factor, step_rates[index], decays[index], step_count) for index in range(7)]
    token_gradient = jnp.stack(token_grads)
    return (gradient_norm, token_gradient, results[0][0], results[1][0], results[2][0], results[3][0], results[4][0], results[5][0], results[6][0], results[0][1], results[1][1], results[2][1], results[3][1], results[4][1], results[5][1], results[6][1], results[0][2], results[1][2], results[2][2], results[3][2], results[4][2], results[5][2], results[6][2])
```

```python
import jax
import jax.numpy as jnp
from jax import lax
from jax.experimental import pallas as pl
from jax.experimental.pallas import tpu as pltpu
from jax.sharding import PartitionSpec as P

BUCKETS = 32
LOSS_SCALE = 1024
LANES = 128

norm_eps = 1e-06
clip_limit = 0.01
beta_first = 0.9
beta_second = 0.999
adam_eps = 1e-08
rate_matrix = 0.03
rate_vector = 0.25
decay_matrix = 0.1
masked_score = -1e30
highest = lax.Precision.HIGHEST
low_type = jnp.bfloat16
full_type = jnp.float32
core_swap = [(0, 1), (1, 0)]


def rms_scale(rows_in):
    return lax.rsqrt(jnp.mean(rows_in * rows_in, axis=-1, keepdims=True) + norm_eps)


def norm_input_grad(d_normed, gain_row, rows_in, norm_scale):
    weighted = d_normed * gain_row
    return norm_scale * weighted - rows_in * norm_scale**3 * jnp.mean(
        weighted * rows_in, axis=-1, keepdims=True
    )


def swap(array, mask, size):
    return lax.ppermute(array, "dp", [(i, i ^ mask) for i in range(size)])


def stage_bits(size):
    if size == 16:
        return (4, 8, 2, 1)
    return tuple(1 << i for i in range(size.bit_length() - 1))


def block_masks(size):
    bits = stage_bits(size)
    return [sum(bit for i, bit in enumerate(bits) if k >> i & 1) for k in range(size)]


def gather_rows(part, size):
    if size != 16:
        for bit in stage_bits(size):
            part = jnp.concatenate([part, swap(part, bit, size)], axis=0)
        return part
    quarter = jnp.concatenate([part] + [swap(part, mask, size) for mask in (4, 8, 12)], axis=0)
    across_y = swap(quarter, 2, size)
    across_x = swap(quarter, 1, size)
    half = quarter.shape[0] // 2
    corner_low = swap(across_y[:half], 1, size)
    corner_high = swap(across_x[half:], 2, size)
    return jnp.concatenate([quarter, across_y, across_x, corner_low, corner_high], axis=0)


def gather_small(part, size):
    part = part[None]
    if size != 16:
        return gather_rows(part, size)
    quarter = jnp.concatenate([part] + [swap(part, mask, size) for mask in (4, 8, 12)], axis=0)
    return jnp.concatenate([quarter] + [swap(quarter, mask, size) for mask in (2, 1, 3)], axis=0)


def scatter_rows(grad, size):
    if size != 16:
        for bit in reversed(stage_bits(size)):
            half = grad.shape[0] // 2
            came = swap(grad[half:], bit, size)
            grad = (grad[:half].astype(full_type) + came.astype(full_type)).astype(low_type)
        return grad.astype(full_type)
    rows = grad.shape[0] // 4
    half = rows // 2
    keep, to_y, to_x, corner = (grad[i * rows : (i + 1) * rows] for i in range(4))
    came_low = swap(corner[:half], 1, size).astype(full_type)
    came_high = swap(corner[half:], 2, size).astype(full_type)
    blank = jnp.zeros((half, grad.shape[1]), full_type)
    to_y = to_y.astype(full_type) + jnp.concatenate([came_low, blank], axis=0)
    to_x = to_x.astype(full_type) + jnp.concatenate([blank, came_high], axis=0)
    from_y = swap(to_y.astype(low_type), 2, size).astype(full_type)
    from_x = swap(to_x.astype(low_type), 1, size).astype(full_type)
    keep = keep.astype(full_type) + from_y + from_x
    keep_low = keep.astype(low_type)
    own = rows // 4
    total = keep[:own]
    for i, mask in enumerate((4, 8, 12)):
        total = total + swap(keep_low[(i + 1) * own : (i + 2) * own], mask, size).astype(full_type)
    return total


def other_core(array):
    return lax.ppermute(array, "mp", core_swap)


def dot_nt(left, right):
    return lax.dot_general(left, right, (((1,), (1,)), ((), ())), preferred_element_type=full_type)


def dot_tn(left, right):
    return lax.dot_general(left, right, (((0,), (0,)), ((), ())), preferred_element_type=full_type)


def dot_nn(left, right):
    return lax.dot_general(left, right, (((1,), (0,)), ((), ())), preferred_element_type=full_type)


def head_lanes():
    lane = lax.broadcasted_iota(jnp.int32, (1, LANES), 1)
    return [lane < LANES // 2, lane >= LANES // 2]


def attention_kernel(len_ref, line_ref, q_ref, k_ref, v_ref, att_ref, prob_ref, tile_ref):
    micro, slot = q_ref.shape[0], q_ref.shape[1]
    blocks = slot // LANES
    lanes = head_lanes()
    for h in range(2):
        for d in range(2 * blocks - 1):
            piece = jnp.broadcast_to(
                line_ref[0, h : h + 1, d * LANES : (d + 2) * LANES], (LANES, 2 * LANES)
            )
            turned = pltpu.roll(piece, LANES + 1, 1, stride=1, stride_axis=0)
            tile_ref[h, d] = turned[:, :LANES]
    for m in range(micro):
        key_valid = lax.broadcasted_iota(jnp.int32, (1, slot), 1) < len_ref[m]
        keys, values = k_ref[m], v_ref[m]

        def block(i, carry):
            rows = pl.ds(pl.multiple_of(i * LANES, LANES), LANES)
            queries = q_ref[m, rows, :]
            outs = []
            for h in range(2):
                scores = dot_nt(queries * lanes[h].astype(low_type), keys)
                bias = jnp.concatenate(
                    [tile_ref[h, j - i + blocks - 1] for j in range(blocks)], axis=1
                )
                scores = jnp.where(key_valid, scores + bias, masked_score)
                terms = jnp.exp(scores - jnp.max(scores, axis=1, keepdims=True))
                probs = terms * (1.0 / jnp.sum(terms, axis=1, keepdims=True))
                prob_low = probs.astype(low_type)
                prob_ref[m, h, rows, :] = prob_low
                outs.append(dot_nn(prob_low, values))
            att_ref[m, rows, :] = jnp.where(lanes[0], outs[0], outs[1]).astype(low_type)
            return carry

        lax.fori_loop(0, blocks, block, 0)


def attention(lengths, lines, projected):
    micro, slot, width = projected.shape
    pairs = width // 3 // LANES
    spans = 2 * (slot // LANES) - 1
    column = lambda c: pl.BlockSpec((micro, slot, LANES), lambda i, c=c: (0, 0, c * pairs + i))
    return pl.pallas_call(
        attention_kernel,
        grid=(pairs,),
        in_specs=[
            pl.BlockSpec(memory_space=pltpu.SMEM),
            pl.BlockSpec((1, 2, lines.shape[2]), lambda i: (i, 0, 0)),
            column(0),
            column(1),
            column(2),
        ],
        out_specs=[
            pl.BlockSpec((micro, slot, LANES), lambda i: (0, 0, i)),
            pl.BlockSpec((micro, 2, slot, slot), lambda i: (0, i, 0, 0)),
        ],
        out_shape=[
            jax.ShapeDtypeStruct((micro, slot, pairs * LANES), low_type),
            jax.ShapeDtypeStruct((micro, 2 * pairs, slot, slot), low_type),
        ],
        scratch_shapes=[pltpu.VMEM((2, spans, LANES, LANES), full_type)],
        compiler_params=pltpu.CompilerParams(vmem_limit_bytes=48 * 1024 * 1024),
        name="attention_forward",
    )(lengths, lines, projected, projected, projected)


def attention_back_kernel(
    prob_ref, q_ref, k_ref, v_ref, d_ref, att_ref, out_ref, diag_ref, tile_ref, dk_ref, dv_ref
):
    micro, slot = q_ref.shape[0], q_ref.shape[1]
    blocks = slot // LANES
    spans = 2 * blocks - 1
    lanes = head_lanes()
    pair = pl.program_id(0)
    width = pl.num_programs(0) * LANES
    place = lambda c: pl.ds(pl.multiple_of(c * width + pair * LANES, LANES), LANES)
    tile_ref[...] = jnp.zeros_like(tile_ref)
    for m in range(micro):
        keys, values = k_ref[m], v_ref[m]
        dk_ref[...] = jnp.zeros_like(dk_ref)
        dv_ref[...] = jnp.zeros_like(dv_ref)

        def block(i, carry):
            rows = pl.ds(pl.multiple_of(i * LANES, LANES), LANES)
            queries, d_att = q_ref[m, rows, :], d_ref[m, rows, :]
            product = d_att.astype(full_type) * att_ref[m, rows, :].astype(full_type)
            d_queries = []
            for h in range(2):
                lane_low = lanes[h].astype(low_type)
                d_head = d_att * lane_low
                row_dot = jnp.sum(jnp.where(lanes[h], product, 0.0), axis=1, keepdims=True)
                d_prob = dot_nt(d_head, values)
                prob_low = prob_ref[m, h, rows, :]
                d_scores = prob_low.astype(full_type) * (d_prob - row_dot)
                d_low = d_scores.astype(low_type)
                for j in range(blocks):
                    tile_ref[h, j - i + blocks - 1] += d_scores[:, j * LANES : (j + 1) * LANES]
                d_queries.append(dot_nn(d_low, keys))
                dk_ref[...] += dot_tn(d_low, queries * lane_low)
                dv_ref[...] += dot_tn(prob_low, d_head)
            out_ref[m, rows, place(0)] = jnp.where(lanes[0], d_queries[0], d_queries[1]).astype(
                low_type
            )
            return carry

        lax.fori_loop(0, blocks, block, 0)
        out_ref[m, :, place(1)] = dk_ref[...].astype(low_type)
        out_ref[m, :, place(2)] = dv_ref[...].astype(low_type)
    flip = (
        lax.broadcasted_iota(jnp.int32, (LANES, LANES), 0)
        + lax.broadcasted_iota(jnp.int32, (LANES, LANES), 1)
        == LANES - 1
    )
    flip = jnp.where(flip, 1.0, 0.0).astype(low_type)
    for h in range(2):
        sums = []
        for d in range(spans):
            tile = tile_ref[h, d]
            high = tile.astype(low_type)
            rest = (tile - high.astype(full_type)).astype(low_type)
            flipped = dot_nn(flip, high) + dot_nn(flip, rest)
            wide = jnp.concatenate([flipped, jnp.zeros_like(flipped)], axis=1)
            turned = pltpu.roll(wide, 0, 1, stride=1, stride_axis=0)
            sums.append(jnp.sum(turned, axis=0, keepdims=True))
        sums.append(jnp.zeros_like(sums[0]))
        diag_ref[0, h] = jnp.concatenate(sums, axis=0)


def attention_back(probs, projected, d_attended, attended):
    micro, slot, width = projected.shape
    pairs = width // 3 // LANES
    spans = 2 * (slot // LANES) - 1
    column = lambda c: pl.BlockSpec((micro, slot, LANES), lambda i, c=c: (0, 0, c * pairs + i))
    return pl.pallas_call(
        attention_back_kernel,
        grid=(pairs,),
        in_specs=[
            pl.BlockSpec((micro, 2, slot, slot), lambda i: (0, i, 0, 0)),
            column(0),
            column(1),
            column(2),
            column(0),
            column(0),
        ],
        out_specs=[
            pl.BlockSpec((micro, slot, width), lambda i: (0, 0, 0)),
            pl.BlockSpec((1, 2, spans + 1, 2 * LANES), lambda i: (i, 0, 0, 0)),
        ],
        out_shape=[
            jax.ShapeDtypeStruct((micro, slot, width), low_type),
            jax.ShapeDtypeStruct((pairs, 2, spans + 1, 2 * LANES), full_type),
        ],
        scratch_shapes=[
            pltpu.VMEM((2, spans, LANES, LANES), full_type),
            pltpu.VMEM((slot, LANES), full_type),
            pltpu.VMEM((slot, LANES), full_type),
        ],
        compiler_params=pltpu.CompilerParams(vmem_limit_bytes=48 * 1024 * 1024),
        name="attention_backward",
    )(probs, projected, projected, projected, d_attended, attended)


def listwise_grad(pooled_f, query_row, pair_ids, gain_final, tied_full):
    norm_scale = rms_scale(pooled_f)
    final_rows = pooled_f * norm_scale * gain_final
    inv_width = pooled_f.shape[1] ** (-0.5)
    logits = jnp.dot(final_rows, tied_full, precision=highest) * inv_width
    margin = logits[:, 0] - logits[:, 1]
    same_query = query_row[:, None] == query_row[None, :]
    earlier = jnp.any(same_query & (pair_ids[None, :] < pair_ids[:, None]), axis=1)
    positive = jnp.where(earlier, 0.0, 1.0)
    row_max = jnp.max(jnp.where(same_query, margin[None, :], masked_score), axis=1)
    group_total = jnp.sum(
        jnp.where(same_query, jnp.exp(margin[None, :] - row_max[:, None]), 0.0), axis=1
    )
    chance = jnp.exp(margin - row_max) / group_total
    d_margin = LOSS_SCALE * (chance - positive)
    d_logits = jnp.stack([d_margin, -d_margin], axis=1) * inv_width
    d_final = jnp.dot(d_logits, tied_full.T, precision=highest)
    d_tied = jnp.dot(final_rows.T, d_logits, precision=highest)
    d_gain = jnp.sum(d_final * pooled_f * norm_scale, axis=0)
    d_pooled = norm_input_grad(d_final, gain_final, pooled_f, norm_scale)
    return (d_pooled, d_gain, d_tied)


def adam_update(weight, first_old, second, clipped, rate, decay, step_count):
    next_first = beta_first * first_old + (1.0 - beta_first) * clipped
    next_second = beta_second * second + (1.0 - beta_second) * clipped * clipped
    step_float = step_count.astype(jnp.float32)
    first_hat = next_first / (1.0 - beta_first**step_float)
    second_hat = next_second / (1.0 - beta_second**step_float)
    next_weight = weight - rate * (first_hat / (jnp.sqrt(second_hat) + adam_eps) + decay * weight)
    return (next_weight, next_first, next_second)


def body(
    tokens,
    pair_lengths,
    query_ids,
    distance_bucket,
    step_count,
    heads_in,
    heads_out,
    hidden_in,
    hidden_out,
    gains,
    tied_rows,
    bias_table,
    first_heads_in,
    first_heads_out,
    first_hidden_in,
    first_hidden_out,
    first_gains,
    first_tied,
    first_table,
    second_heads_in,
    second_heads_out,
    second_hidden_in,
    second_hidden_out,
    second_gains,
    second_tied,
    second_table,
):
    size = lax.axis_size("dp")
    me = lax.axis_index("dp")
    core = lax.axis_index("mp")
    micro, _, slot, width = tokens.shape
    count = micro * slot
    own, local_heads = heads_in.shape[0], bias_table.shape[1]
    head_width = heads_in.shape[2]
    in_width = 3 * head_width
    spans = 2 * (slot // LANES) - 1

    extra = jnp.concatenate(
        [gains, tied_rows, jnp.zeros((own, LANES - 5), full_type)], axis=1
    ).astype(low_type)
    packed_in = jnp.concatenate([heads_in.reshape(own, in_width).astype(low_type), extra], axis=1)
    full_in = gather_rows(packed_in, size)
    full_rest = gather_rows(
        jnp.concatenate([heads_out.astype(low_type), hidden_in.astype(low_type)], axis=1), size
    )
    full_down = gather_rows(hidden_out.astype(low_type), size)
    vectors = full_in[:, in_width:].astype(full_type).T
    gain_first, gain_second, gain_final = vectors[0], vectors[1], vectors[2]
    tied_full = vectors[3:5].T
    weight_in = full_in[:, :in_width]
    weight_out, weight_up = full_rest[:, :head_width], full_rest[:, head_width:]

    pair_ids = jnp.bitwise_xor(me, jnp.array(block_masks(size), jnp.int32))
    place = (pair_ids[:, None] * own + jnp.arange(own, dtype=jnp.int32)[None, :]).reshape(width)
    order = (jnp.arange(width, dtype=jnp.int32)[:, None] == place[None, :]).astype(low_type)

    lengths = pair_lengths.reshape(micro)
    length_f = lengths.astype(full_type)[:, None]
    token_valid = (jnp.arange(slot, dtype=jnp.int32)[None, :] < lengths[:, None]).astype(full_type)
    token_valid = token_valid.reshape(count, 1)
    bucket_line = jnp.concatenate([distance_bucket, jnp.zeros((1,), jnp.int32)])
    bucket_hot = (bucket_line[:, None] == jnp.arange(BUCKETS, dtype=jnp.int32)[None, :]).astype(
        full_type
    )
    bucket_hot = bucket_hot * (jnp.arange(2 * slot) < 2 * slot - 1).astype(full_type)[:, None]
    lines = jnp.dot(
        bias_table.astype(low_type).T, bucket_hot.astype(low_type).T, preferred_element_type=full_type
    ).reshape(local_heads // 2, 2, 2 * slot)

    rows_low = jnp.dot(tokens.reshape(count, width), order, preferred_element_type=full_type)
    rows_in = rows_low.astype(low_type).astype(full_type)
    first_scale = rms_scale(rows_in)
    normed_first = (rows_in * first_scale * gain_first).astype(low_type)
    projected = jnp.dot(normed_first, weight_in, preferred_element_type=full_type)
    projected = projected.astype(low_type).reshape(micro, slot, in_width)
    attended, probs = attention(lengths, lines, projected)
    attended_rows = attended.reshape(count, head_width)
    branch = dot_nt(attended_rows, weight_out)
    middle = rows_in + branch + other_core(branch.astype(low_type)).astype(full_type)
    second_scale = rms_scale(middle)
    normed_second = (middle * second_scale * gain_second).astype(low_type)
    hidden_pre = jnp.dot(normed_second, weight_up, preferred_element_type=full_type)
    gated, gate_back = jax.vjp(lambda v: jax.nn.gelu(v, approximate=True), hidden_pre)
    activation = gated.astype(low_type).astype(full_type)
    slope = (gate_back(jnp.ones_like(hidden_pre))[0] * token_valid).astype(low_type)
    act_sum = jnp.sum((activation * token_valid).reshape(micro, slot, -1), axis=1)
    middle_sum = jnp.sum((middle * token_valid).reshape(micro, slot, width), axis=1)
    act_high = act_sum.astype(low_type)
    act_rest = (act_sum - act_high.astype(full_type)).astype(low_type)
    down = dot_nt(jnp.concatenate([act_high, act_rest], axis=0), full_down)
    down = down[:micro] + down[micro:]
    pooled = ((middle_sum + down + other_core(down)) / length_f).astype(low_type)

    pooled_true = dot_nt(pooled, order).astype(low_type)
    pooled_all = gather_small(pooled_true, size).reshape(size * micro, width)
    pooled_all = jnp.dot(pooled_all, order, preferred_element_type=full_type)
    pooled_all = pooled_all.reshape(size, micro, width)
    length_col = jnp.broadcast_to(length_f, (micro, LANES))
    act_all = gather_small(jnp.concatenate([act_sum, length_col], axis=1), size)
    query_all = query_ids[:, pair_ids]
    d_pooled, d_gain, d_tied = jax.vmap(
        lambda p, q: listwise_grad(p, q, pair_ids, gain_final, tied_full), in_axes=(1, 0), out_axes=(1, 0, 0)
    )(pooled_all, query_all)
    d_line = d_pooled[0] / length_f
    d_line_low = d_line.astype(low_type)
    d_all_own = (d_pooled[:, :, :own] / act_all[:, :, -1:]).astype(low_type).astype(full_type)
    g_down = jnp.dot(
        d_all_own.reshape(size * micro, own).T,
        act_all[:, :, :-LANES].reshape(size * micro, -1),
        precision=highest,
    )
    d_act = jnp.dot(d_line_low, full_down, preferred_element_type=full_type)

    spread = lambda rows: jnp.broadcast_to(rows[:, None], (micro, slot) + rows.shape[1:]).reshape(
        count, -1
    )
    d_hidden = (slope.astype(full_type) * spread(d_act)).astype(low_type)
    d_normed_second = dot_nt(d_hidden, weight_up)
    d_normed_second_other = other_core(d_normed_second.astype(low_type)).astype(full_type)
    g_up = scatter_rows(dot_tn(normed_second, d_hidden).astype(low_type), size)
    g_gain_second = jnp.sum(d_normed_second * middle * second_scale, axis=0)
    d_middle = spread(d_line) * token_valid + norm_input_grad(
        d_normed_second + d_normed_second_other, gain_second, middle, second_scale
    )
    d_middle_low = d_middle.astype(low_type)
    d_attended = jnp.dot(d_middle_low, weight_out, preferred_element_type=full_type)
    d_attended = d_attended.astype(low_type).reshape(micro, slot, head_width)
    g_out = dot_tn(d_middle_low, attended_rows).astype(low_type)
    g_out = scatter_rows(g_out, size)
    d_project, diagonals = attention_back(probs, projected, d_attended, attended)
    d_project = d_project.reshape(count, in_width)
    d_normed_first = dot_nt(d_project, weight_in)
    g_gain_first = jnp.sum(d_normed_first * rows_in * first_scale, axis=0)

    hot_spans = jnp.concatenate(
        [bucket_hot[d * LANES : (d + 2) * LANES] for d in range(spans)], axis=0
    )
    diagonal_rows = diagonals[:, :, :spans, :].reshape(local_heads, spans * 2 * LANES)
    table_part = jnp.dot(hot_spans.T, diagonal_rows.T, precision=highest)
    entries = BUCKETS * local_heads
    per_block = -(-entries // size)
    table_flat = jnp.concatenate(
        [table_part.reshape(entries), jnp.zeros((per_block * size - entries,), full_type)]
    ).reshape(size, per_block)
    block_of = (pair_ids[:, None] == jnp.arange(size, dtype=jnp.int32)[None, :]).astype(full_type)
    table_blocks = jnp.dot(block_of, table_flat, precision=highest)
    table_cols = jnp.concatenate(
        [table_blocks, jnp.zeros((size, own * 8 - per_block), full_type)], axis=1
    ).reshape(width, 8)
    g_extra = jnp.concatenate(
        [
            table_cols,
            g_gain_first[:, None],
            g_gain_second[:, None],
            jnp.zeros((width, LANES - 10), full_type),
        ],
        axis=1,
    )
    g_in = jnp.concatenate(
        [dot_tn(normed_first, d_project).astype(low_type), g_extra.astype(low_type)], axis=1
    )
    g_in = scatter_rows(g_in, size)

    d_normed_first = d_normed_first + other_core(d_normed_first.astype(low_type)).astype(full_type)
    token_grad = d_middle + norm_input_grad(d_normed_first, gain_first, rows_in, first_scale)
    token_high = token_grad.astype(low_type)
    token_rest = (token_grad - token_high.astype(full_type)).astype(low_type)
    token_gradient = (dot_nt(token_high, order) + dot_nt(token_rest, order)).reshape(tokens.shape)

    g_extra = g_in[:, in_width:]
    table_own = g_extra[:, :8].reshape(1, own * 8)[:, :per_block] / LOSS_SCALE
    gain_pair = g_extra[:, 8:10]
    gain_pair = gain_pair + other_core(gain_pair)
    g_gains = jnp.concatenate([gain_pair, jnp.sum(d_gain, axis=0)[:own, None]], axis=1) / LOSS_SCALE
    g_tied = jnp.sum(d_tied, axis=0)[:own] / LOSS_SCALE
    g_in = g_in[:, :in_width].reshape(heads_in.shape) / LOSS_SCALE
    g_out, g_up, g_down = g_out / LOSS_SCALE, g_up / LOSS_SCALE, g_down / LOSS_SCALE
    squares = sum(jnp.sum(piece * piece) for piece in (g_in, g_out, g_up, g_down, table_own))
    squares = squares + (jnp.sum(g_gains * g_gains) + jnp.sum(g_tied * g_tied)) / lax.axis_size("mp")
    squares = squares + other_core(squares)
    line = jnp.concatenate(
        [squares.reshape(1, 1), table_own, jnp.zeros((1, LANES - 1 - per_block), full_type)], axis=1
    )
    line_all = gather_small(line, size).reshape(size, LANES)
    gradient_norm = jnp.sqrt(jnp.sum(line_all[:, 0]))
    table_all = jnp.dot(block_of.T, line_all[:, 1 : 1 + per_block], precision=highest)
    table_piece = table_all.reshape(-1)[:entries].reshape(BUCKETS, local_heads)
    clip_factor = jnp.minimum(1.0, clip_limit / (gradient_norm + 1e-06))
    weights = (heads_in, heads_out, hidden_in, hidden_out, gains, tied_rows, bias_table)
    firsts = (
        first_heads_in,
        first_heads_out,
        first_hidden_in,
        first_hidden_out,
        first_gains,
        first_tied,
        first_table,
    )
    seconds = (
        second_heads_in,
        second_heads_out,
        second_hidden_in,
        second_hidden_out,
        second_gains,
        second_tied,
        second_table,
    )
    grads = (g_in, g_out, g_up, g_down, g_gains, g_tied, table_piece)
    step_rates = (rate_matrix,) * 4 + (rate_vector,) * 3
    decays = (decay_matrix,) * 4 + (0.0,) * 3
    results = [
        adam_update(
            weights[index],
            firsts[index],
            seconds[index],
            grads[index] * clip_factor,
            step_rates[index],
            decays[index],
            step_count,
        )
        for index in range(7)
    ]
    return (
        gradient_norm,
        token_gradient,
        *(result[0] for result in results),
        *(result[1] for result in results),
        *(result[2] for result in results),
    )


def solution(mesh):
    in_specs = (
        P(None, "dp", None, None),
        P(None, "dp"),
        P(),
        P(),
        P(),
        P("dp", None, "mp"),
        P("dp", "mp"),
        P("dp", "mp"),
        P("dp", "mp"),
        P("dp", None),
        P("dp", None),
        P(None, "mp"),
        P("dp", None, "mp"),
        P("dp", "mp"),
        P("dp", "mp"),
        P("dp", "mp"),
        P("dp", None),
        P("dp", None),
        P(None, "mp"),
        P("dp", None, "mp"),
        P("dp", "mp"),
        P("dp", "mp"),
        P("dp", "mp"),
        P("dp", None),
        P("dp", None),
        P(None, "mp"),
    )
    out_specs = (
        P(),
        P(None, "dp", None, None),
        P("dp", None, "mp"),
        P("dp", "mp"),
        P("dp", "mp"),
        P("dp", "mp"),
        P("dp", None),
        P("dp", None),
        P(None, "mp"),
        P("dp", None, "mp"),
        P("dp", "mp"),
        P("dp", "mp"),
        P("dp", "mp"),
        P("dp", None),
        P("dp", None),
        P(None, "mp"),
        P("dp", None, "mp"),
        P("dp", "mp"),
        P("dp", "mp"),
        P("dp", "mp"),
        P("dp", None),
        P("dp", None),
        P(None, "mp"),
    )
    return jax.shard_map(body, mesh=mesh, in_specs=in_specs, out_specs=out_specs, check_vma=False)
```

```python
import functools

import jax
import jax.numpy as jnp
from jax import lax
from jax.experimental import pallas as pl
from jax.experimental.pallas import tpu as pltpu
from jax.sharding import PartitionSpec as P

BUCKETS = 32
LOSS_SCALE = 1024
LANES = 128
ROWS = 256

norm_eps = 1e-06
clip_limit = 0.01
beta_first = 0.9
beta_second = 0.999
adam_eps = 1e-08
rate_matrix = 0.03
rate_vector = 0.25
decay_matrix = 0.1
masked_score = -1e30
gelu_slope = 0.7978845608028654
gelu_cubic = 0.044715
low_type = jnp.bfloat16
full_type = jnp.float32
core_swap = [(0, 1), (1, 0)]


def rms_scale(rows_in):
    return lax.rsqrt(jnp.mean(rows_in * rows_in, axis=-1, keepdims=True) + norm_eps)


def norm_input_grad(d_normed, gain_row, rows_in, norm_scale):
    weighted = d_normed * gain_row
    return norm_scale * weighted - rows_in * norm_scale**3 * jnp.mean(
        weighted * rows_in, axis=-1, keepdims=True
    )


def dot_nt(left, right):
    return lax.dot_general(left, right, (((1,), (1,)), ((), ())), preferred_element_type=full_type)


def dot_tn(left, right):
    return lax.dot_general(left, right, (((0,), (0,)), ((), ())), preferred_element_type=full_type)


def dot_nn(left, right):
    return lax.dot_general(left, right, (((1,), (0,)), ((), ())), preferred_element_type=full_type)


def call(
    kernel, name, out_shape, cost=(0, 0), vmem=56, deps=(), passing=(), in_specs=None,
    out_specs=None, input_output_aliases=None, **options
):
    single = not isinstance(out_shape, (list, tuple))
    out_shapes = [out_shape] if single else list(out_shape)
    outputs, extra = len(out_shapes), len(deps) + len(passing)

    def apply(*operands):
        inputs = len(operands)
        specs = in_specs or [pl.BlockSpec(memory_space=pltpu.VMEM)] * inputs
        targets = out_specs or [pl.BlockSpec(memory_space=pltpu.VMEM)] * outputs
        targets = targets if isinstance(targets, (list, tuple)) else [targets]
        aliases = dict(input_output_aliases or {})
        for i in range(len(passing)):
            aliases[inputs + len(deps) + i] = outputs + i

        def run(*refs):
            own = inputs + extra
            kernel(*refs[:inputs], *refs[own : own + outputs], *refs[own + outputs + len(passing) :])

        results = pl.pallas_call(
            run,
            out_shape=[*out_shapes, *(shape_of(a.shape, a.dtype) for a in passing)],
            in_specs=[*specs, *[in_place()] * extra],
            out_specs=[*targets, *[in_place()] * len(passing)],
            input_output_aliases=aliases,
            compiler_params=pltpu.CompilerParams(vmem_limit_bytes=vmem * 1024 * 1024),
            cost_estimate=pl.CostEstimate(
                flops=int(cost[0] * 2e6), bytes_accessed=int(cost[1] * 1e3), transcendentals=0
            ),
            name=name,
            **options,
        )(*operands, *deps, *passing)
        return results[0] if single and not passing else results

    return apply


def in_place():
    return pl.BlockSpec(memory_space=pl.ANY)


def shape_of(shape, dtype):
    return jax.ShapeDtypeStruct(tuple(shape), dtype)


def whole(shape):
    return pl.BlockSpec(tuple(shape), lambda *_: (0,) * len(shape))


def on_scalars():
    return pl.BlockSpec(memory_space=pltpu.SMEM)


def row_blocks(shape, step=0):
    return pl.BlockSpec(tuple(shape), lambda i: (i,) + (0,) * (len(shape) - 1))


def column_blocks(shape, offset=0):
    return pl.BlockSpec(tuple(shape), lambda i: (0,) * (len(shape) - 1) + (i + offset,))


def fill_rows(target, pieces, columns=slice(None)):
    start = 0
    for piece in pieces:
        rows = piece.shape[0]
        target[start : start + rows, :] = piece[:, columns]
        start += rows


def spill_rows(value, pieces):
    start = 0
    for piece in pieces:
        rows = piece.shape[0]
        piece[...] = value[start : start + rows].astype(piece.dtype)
        start += rows


def swap(array, mask, size, label="exchange"):
    with jax.named_scope(f"{label}_across_{mask}"):
        return lax.ppermute(array, "dp", [(i, i ^ mask) for i in range(size)])


def other_core(array, label="other_core"):
    with jax.named_scope(label):
        return lax.ppermute(array, "mp", core_swap)


def stage_bits(size):
    if size == 16:
        return (4, 8, 2, 1)
    return tuple(1 << i for i in range(size.bit_length() - 1))


def block_masks(size):
    bits = stage_bits(size)
    return [sum(bit for i, bit in enumerate(bits) if k >> i & 1) for k in range(size)]


def piece_rows(size, width):
    if size != 16:
        return [width]
    return [width // 4] * 3 + [width // 8] * 2


def join_kernel(*refs):
    *part_refs, out_ref = refs
    start = 0
    for part in part_refs:
        rows = part.shape[0]
        out_ref[start : start + rows] = part[...]
        start += rows


def join(parts, **options):
    rows = sum(part.shape[0] for part in parts)
    return call(
        join_kernel, "join", shape_of((rows, *parts[0].shape[1:]), parts[0].dtype), **options
    )(*parts)


def step_kernel(parts, y_ref, x_ref, *refs):
    part_refs, (low_ref, high_ref, *line_refs) = refs[:parts], refs[parts:]
    low_ref[...] = y_ref[...]
    high_ref[...] = x_ref[...]
    if parts:
        join_kernel(*part_refs, *line_refs)


def gather_step(across_y, across_x, parts, **options):
    half = (across_y.shape[0] // 2, across_y.shape[1])
    shapes = [shape_of(half, across_y.dtype)] * 2
    if parts:
        shapes.append(shape_of((sum(p.shape[0] for p in parts), parts[0].shape[1]), parts[0].dtype))
    return call(
        functools.partial(step_kernel, len(parts)),
        "gather_step",
        shapes,
        grid=(1,),
        in_specs=[
            pl.BlockSpec(half, lambda i: (0, 0)),
            pl.BlockSpec(half, lambda i: (1, 0)),
            *(whole(part.shape) for part in parts),
        ],
        out_specs=[whole(shape.shape) for shape in shapes],
        **options,
    )(across_y, across_x, *parts)


def line_parts(part, size, label):
    return [part] + [swap(part, mask, size, label) for mask in (4, 8, 12)]


def side_parts(quarter, size, label):
    return [swap(quarter, mask, size, label) for mask in (2, 1)]


def corner_parts(low, high, size, label):
    return [swap(low, 1, size, label), swap(high, 2, size, label)]


def gather_doubling(part, size):
    for bit in stage_bits(size):
        part = jnp.concatenate([part, swap(part, bit, size)], axis=0)
    return part


def small_line(part, size, label):
    if size != 16:
        return part[None]
    return join(line_parts(part[None], size, label))


def small_plane(quarter, size, label):
    if size != 16:
        return [gather_doubling(quarter, size)]
    return [quarter] + [swap(quarter, mask, size, label) for mask in (2, 1, 3)]


def stacked(refs):
    return jnp.concatenate([ref[...] for ref in refs], axis=0)


def gather_small(part, size, label):
    return small_plane(small_line(part, size, label), size, label)


def plane_sum_kernel(y_ref, x_ref, low_ref, high_ref, y_out, x_out):
    half = low_ref.shape[0]
    y_out[:half] = (y_ref[:half].astype(full_type) + low_ref[...].astype(full_type)).astype(low_type)
    y_out[half:] = y_ref[half:]
    x_out[:half] = x_ref[:half]
    x_out[half:] = (x_ref[half:].astype(full_type) + high_ref[...].astype(full_type)).astype(low_type)


def line_sum_kernel(z_ref, y_ref, x_ref, own_ref, *out_refs):
    rows = own_ref.shape[0]
    for i in range(4):
        span = slice(i * rows, (i + 1) * rows)
        total = z_ref[span].astype(full_type) + y_ref[span].astype(full_type)
        total = total + x_ref[span].astype(full_type)
        target = own_ref if i == 0 else out_refs[i - 1]
        target[...] = total.astype(target.dtype)


class Scatter:
    def __init__(self, pieces, size, label):
        self.pieces, self.size, self.label = pieces, size, label
        if size == 16:
            *self.pieces, low, high = pieces
            self.came = [swap(low, 1, size, label), swap(high, 2, size, label)]

    def sides(self, deps=(), passing=()):
        if self.size != 16:
            return passing
        keep, to_y, to_x = self.pieces
        to_y, to_x, *passed = call(
            plane_sum_kernel,
            "plane_sum",
            [shape_of(to_y.shape, low_type)] * 2,
            deps=deps,
            passing=passing,
        )(to_y, to_x, *self.came)
        self.came = [swap(to_y, 2, self.size, self.label), swap(to_x, 1, self.size, self.label)]
        return passed

    def line(self, deps=(), passing=()):
        size, label = self.size, self.label
        if size != 16:
            grad = self.pieces[0]
            for bit in reversed(stage_bits(size)):
                half = grad.shape[0] // 2
                came = swap(grad[half:], bit, size, label)
                grad = (grad[:half].astype(full_type) + came.astype(full_type)).astype(low_type)
            return [grad.astype(full_type)], passing
        keep = self.pieces[0]
        part = (keep.shape[0] // 4, keep.shape[1])
        own, *others = call(
            line_sum_kernel,
            "line_sum",
            [shape_of(part, full_type)] + [shape_of(part, low_type)] * 3,
            deps=deps,
            passing=passing,
        )(keep, *self.came)
        came = [swap(other, mask, size, label) for other, mask in zip(others, (4, 8, 12))]
        return [own] + came, others[3:]


def pack_heads_kernel(in_ref, out_ref, gain_ref, tied_ref, a_ref):
    parts, rows, width = in_ref.shape
    for c in range(parts):
        a_ref[:, c * width : (c + 1) * width] = in_ref[c].astype(low_type)
    a_ref[:, parts * width : (parts + 1) * width] = out_ref[...].astype(low_type)
    gains, tied = gain_ref[...], tied_ref[...]
    vectors = few_rows([gains[i : i + 1] for i in range(3)] + [tied[i : i + 1] for i in range(2)], 16)
    pick = lax.broadcasted_iota(jnp.int32, (16, LANES), 0) == lax.broadcasted_iota(
        jnp.int32, (16, LANES), 1
    )
    extra = dot_tn(vectors.astype(low_type), jnp.where(pick, 1.0, 0.0).astype(low_type))
    a_ref[:, (parts + 1) * width :] = extra.astype(low_type)


def pack_hidden_kernel(up_ref, down_ref, b_ref, c_ref):
    b_ref[...] = up_ref[...].astype(low_type)
    c_ref[...] = down_ref[...].astype(low_type)


def order_kernel(x_ref, order_ref, out_ref):
    out_ref[...] = dot_nn(x_ref[...], order_ref[...]).astype(low_type)


def turn_kernel(x_ref, out_ref):
    out_ref[...] = x_ref[...].T


def head_lanes():
    lane = lax.broadcasted_iota(jnp.int32, (1, LANES), 1)
    return [lane < LANES // 2, lane >= LANES // 2]


def project_kernel(pieces, pairs, x_ref, *refs):
    weight_refs, (qkv_ref, normed_ref, vector_ref, w_ref) = refs[:pieces], refs[pieces:]
    parts = qkv_ref.shape[1]
    in_width = pairs * parts * LANES

    @pl.when(pl.program_id(0) == 0)
    def assemble():
        fill_rows(w_ref, weight_refs)
        pick = lax.broadcasted_iota(jnp.int32, (16, LANES), 0) == lax.broadcasted_iota(
            jnp.int32, (16, LANES), 1
        )
        vectors = dot_nt(jnp.where(pick, 1.0, 0.0).astype(low_type), w_ref[:, -LANES:])
        vector_ref[...] = vectors[:8]

    x = x_ref[...].astype(full_type)
    normed = (x * rms_scale(x) * vector_ref[0:1]).astype(low_type)
    normed_ref[...] = normed
    projected = dot_nn(normed, w_ref[:, :in_width]).astype(low_type)
    for c in range(parts):
        for p in range(pairs):
            start = (c * pairs + p) * LANES
            qkv_ref[p, c] = projected[:, start : start + LANES]


def project(rows_low, weights, pairs, deps):
    count, width = rows_low.shape
    parts = 3
    return call(
        functools.partial(project_kernel, len(weights), pairs),
        "projection",
        [
            shape_of((pairs, parts, count, LANES), low_type),
            shape_of((count, width), low_type),
            shape_of((8, width), full_type),
        ],
        deps=deps,
        grid=(count // ROWS,),
        in_specs=[row_blocks((ROWS, width)), *(whole(piece.shape) for piece in weights)],
        out_specs=[
            pl.BlockSpec((pairs, parts, ROWS, LANES), lambda i: (0, 0, i, 0)),
            row_blocks((ROWS, width)),
            whole((8, width)),
        ],
        scratch_shapes=[pltpu.VMEM((width, weights[0].shape[1]), low_type)],
    )(rows_low, *weights)


def attention_kernel(len_ref, line_ref, qkv_ref, *refs):
    att_ref, prob_ref, inv_ref, tile_ref = refs[-4:]
    micro, slot = prob_ref.shape[1], prob_ref.shape[3]
    blocks = slot // LANES
    lanes = head_lanes()
    for h in range(2):
        for d in range(2 * blocks - 1):
            piece = jnp.broadcast_to(
                line_ref[0, h : h + 1, d * LANES : (d + 2) * LANES], (LANES, 2 * LANES)
            )
            turned = pltpu.roll(piece, LANES + 1, 1, stride=1, stride_axis=0)
            tile_ref[h, d] = turned[:, :LANES]

    def micro_step(m, carry):
        start = pl.multiple_of(m * slot, slot)
        key_valid = lax.broadcasted_iota(jnp.int32, (1, slot), 1) < len_ref[m]
        keys = qkv_ref[0, 1, pl.ds(start, slot), :]
        values = qkv_ref[0, 2, pl.ds(start, slot), :]
        values = jnp.concatenate([values, jnp.ones_like(values)], axis=1)
        for r in range(slot // ROWS):
            rows = pl.ds(start + r * ROWS, ROWS)
            queries = qkv_ref[0, 0, rows, :]
            queries = jnp.concatenate(
                [queries * lanes[h].astype(low_type) for h in range(2)], axis=0
            )
            first = r * (ROWS // LANES)
            bias = jnp.concatenate(
                [
                    jnp.concatenate(
                        [tile_ref[h, j - first - i + blocks - 1] for j in range(blocks)], axis=1
                    )
                    for h in range(2)
                    for i in range(ROWS // LANES)
                ],
                axis=0,
            )
            scores = dot_nt(queries, keys)
            scores = jnp.where(key_valid, scores + bias, masked_score)
            terms = jnp.exp(scores - jnp.max(scores, axis=1, keepdims=True)).astype(low_type)
            for h in range(2):
                prob_ref[0, m, h, r * ROWS : (r + 1) * ROWS, :] = terms[h * ROWS : (h + 1) * ROWS]
            mixed = dot_nn(terms, values)
            inverse = 1.0 / mixed[:, LANES:]
            mixed = mixed[:, :LANES] * inverse
            att_ref[rows, :] = jnp.where(lanes[0], mixed[:ROWS], mixed[ROWS:]).astype(low_type)
            inv_ref[rows, :] = jnp.where(lanes[0], inverse[:ROWS], inverse[ROWS:])
        return carry

    lax.fori_loop(0, micro, micro_step, 0)


def attention(lengths, lines, qkv, pair, slot, before=(), deps=()):
    pairs, parts, count, _ = qkv.shape
    micro = count // slot
    spans = 2 * (slot // LANES) - 1
    column = pl.BlockSpec((count, LANES), lambda i: (0, pair))
    return call(
        attention_kernel,
        "attention_forward",
        [
            shape_of((count, pairs * LANES), low_type),
            shape_of((pairs, micro, 2, slot, slot), low_type),
            shape_of((count, pairs * LANES), full_type),
        ],
        deps=deps,
        grid=(1,),
        in_specs=[
            on_scalars(),
            pl.BlockSpec((1, 2, lines.shape[2]), lambda i: (pair, 0, 0)),
            pl.BlockSpec((1, parts, count, LANES), lambda i: (pair, 0, 0, 0)),
            *[in_place()] * len(before),
        ],
        out_specs=[
            column,
            pl.BlockSpec((1, micro, 2, slot, slot), lambda i: (pair, 0, 0, 0, 0)),
            column,
        ],
        input_output_aliases={3 + i: i for i in range(len(before))},
        scratch_shapes=[pltpu.VMEM((2, spans, LANES, LANES), full_type)],
    )(lengths, lines, qkv, *before)


def branch_kernel(att_ref, *refs):
    *weight_refs, out_ref, w_ref = refs

    @pl.when(pl.program_id(0) == 0)
    def assemble():
        fill_rows(w_ref, weight_refs)

    out_ref[...] = dot_nt(att_ref[...], w_ref[...]).astype(low_type)


def branch_rows(attended, weights, deps=()):
    count, head_width = attended.shape
    width = sum(piece.shape[0] for piece in weights)
    return call(
        branch_kernel,
        "branch",
        shape_of((count, width), low_type),
        deps=deps,
        grid=(count // (2 * ROWS),),
        in_specs=[
            row_blocks((2 * ROWS, head_width)),
            *(pl.BlockSpec((piece.shape[0], head_width), lambda i: (0, 3)) for piece in weights),
        ],
        out_specs=row_blocks((2 * ROWS, width)),
        scratch_shapes=[pltpu.VMEM((width, head_width), low_type)],
    )(attended, *weights)


def hidden_kernel(pieces, len_ref, x_ref, own_ref, came_ref, vector_ref, *refs):
    weight_refs, refs = refs[:pieces], refs[pieces:]
    normed_ref, slope_ref, act_ref, sum_ref, w_ref = refs
    m = pl.program_id(0)
    slot = x_ref.shape[0]

    @pl.when(m == 0)
    def assemble():
        fill_rows(w_ref, weight_refs)

    middle = middle_rows(x_ref, own_ref, came_ref)
    normed = (middle * rms_scale(middle) * vector_ref[1:2]).astype(low_type)
    valid = lax.broadcasted_iota(jnp.int32, (slot, 1), 0) < len_ref[m]
    normed_ref[...] = jnp.where(valid, normed, jnp.zeros_like(normed))
    counted = lax.broadcasted_iota(jnp.int32, (16, slot), 1) < len_ref[m]
    counted = jnp.where(counted, 1.0, 0.0).astype(low_type)
    sum_ref[0] = jnp.sum(jnp.where(valid, middle, 0.0), axis=0, keepdims=True)
    block = 3 * LANES
    for n in range(w_ref.shape[1] // block):
        columns = slice(n * block, (n + 1) * block)
        v = dot_nn(normed, w_ref[:, columns])
        square = v * v
        gate = jnp.tanh(v * (gelu_slope + (gelu_slope * gelu_cubic) * square))
        half = 0.5 + 0.5 * gate
        active = (v * half).astype(low_type)
        act_ref[0, :, columns] = dot_nn(counted, active)[0:1]
        inner = 0.5 * gelu_slope + (1.5 * gelu_slope * gelu_cubic) * square
        slope_ref[:, columns] = (half + v * (1.0 - gate * gate) * inner).astype(low_type)


def middle_rows(x_ref, own_ref, came_ref):
    branch = own_ref[...].astype(full_type) + came_ref[...].astype(full_type)
    return x_ref[...].astype(full_type) + branch


def hidden(lengths, rows_low, own, came, vectors, weights, slot):
    count, width = rows_low.shape
    micro = count // slot
    inner = weights[0].shape[1]
    return call(
        functools.partial(hidden_kernel, len(weights)),
        "hidden_forward",
        [
            shape_of((count, width), low_type),
            shape_of((count, inner), low_type),
            shape_of((micro, 1, inner), full_type),
            shape_of((micro, 1, width), full_type),
        ],
        cost=(1200, 20000),
        grid=(micro,),
        in_specs=[
            on_scalars(),
            *[row_blocks((slot, width))] * 3,
            whole(vectors.shape),
            *(whole(piece.shape) for piece in weights),
        ],
        out_specs=[
            row_blocks((slot, width)),
            row_blocks((slot, inner)),
            row_blocks((1, 1, inner)),
            row_blocks((1, 1, width)),
        ],
        scratch_shapes=[pltpu.VMEM((width, inner), low_type)],
    )(lengths, rows_low, own, came, vectors, *weights)


def few_rows(rows, count):
    place = lax.broadcasted_iota(jnp.int32, (count, rows[0].shape[1]), 0)
    total = jnp.zeros(place.shape, full_type)
    for i, row in enumerate(rows):
        total = jnp.where(place == i, row, total)
    return total


def pool_kernel(act_ref, *refs):
    *weight_refs, out_ref, w_ref = refs
    fill_rows(w_ref, weight_refs)
    sums = [act_ref[m] for m in range(act_ref.shape[0])]
    highs = [row.astype(low_type).astype(full_type) for row in sums]
    rests = [row - high for row, high in zip(sums, highs)]
    down = dot_nt(few_rows(highs + rests, 16).astype(low_type), w_ref[...])
    micro = len(sums)
    out_ref[...] = few_rows([down[m : m + 1] + down[micro + m : micro + m + 1] for m in range(micro)], 8)


def margin_kernel(len_ref, own_ref, other_ref, sum_ref, vector_ref, margin_ref, pooled_ref):
    margins, vectors_pooled = [], []
    for m in range(sum_ref.shape[0]):
        total = own_ref[m : m + 1] + other_ref[m : m + 1] + sum_ref[m]
        pooled = (total / len_ref[m].astype(full_type)).astype(low_type).astype(full_type)
        final = pooled * rms_scale(pooled) * vector_ref[2:3]
        logits = [
            jnp.sum(final * vector_ref[i : i + 1], axis=1, keepdims=True) * pooled.shape[1] ** (-0.5)
            for i in (3, 4)
        ]
        margins.append(jnp.broadcast_to(logits[0] - logits[1], (1, LANES)))
        vectors_pooled.append(pooled)
    margin_ref[...] = few_rows(margins, 8)
    pooled_ref[...] = few_rows(vectors_pooled, 8)


def rank_kernel(
    margin_pieces, down_pieces, up_pieces, len_ref, same_ref, positive_ref, pooled_ref,
    vector_ref, slope_ref, *refs
):
    margin_refs, refs = refs[:margin_pieces], refs[margin_pieces:]
    down_refs, refs = refs[:down_pieces], refs[down_pieces:]
    up_refs, refs = refs[:up_pieces], refs[up_pieces:]
    line_ref, act_ref, extra_ref, d_ref, down_ref, up_ref = refs
    m = pl.program_id(0)

    @pl.when(m == 0)
    def rank():
        fill_rows(down_ref, down_refs)
        fill_rows(up_ref, up_refs)
        margins, same = stacked(margin_refs), same_ref[...] > 0.5
        row_max = jnp.max(jnp.where(same, margins, masked_score), axis=0)
        total = jnp.sum(jnp.where(same, jnp.exp(margins - row_max[None]), 0.0), axis=0)
        chance = jnp.exp(margins[0] - row_max) / total
        d_margins = LOSS_SCALE * (chance - positive_ref[...])
        tied_gap = vector_ref[3:4] - vector_ref[4:5]
        gain = vector_ref[2:3]
        lines, d_gain, d_tied = [], 0.0, 0.0
        for i in range(2):
            pooled = pooled_ref[i : i + 1]
            scale = rms_scale(pooled)
            d_logit = d_margins[i : i + 1, 0:1] * pooled.shape[1] ** (-0.5)
            d_final = d_logit * tied_gap
            d_gain = d_gain + d_final * pooled * scale
            d_tied = d_tied + pooled * scale * gain * d_logit
            d_pooled = norm_input_grad(d_final, gain, pooled, scale)
            lines.append(d_pooled / len_ref[i].astype(full_type))
        line_ref[...] = few_rows(lines, 8)
        extra_ref[...] = few_rows([d_gain, d_tied], 8)
        d_act = dot_nn(few_rows(lines, 16).astype(low_type), down_ref[...])
        act_ref[...] = d_act[:8]

    d_row = jnp.where(m == 0, act_ref[0:1], act_ref[1:2])
    d_hidden = (slope_ref[...].astype(full_type) * d_row).astype(low_type)
    d_normed = dot_nt(d_hidden, up_ref[...])
    valid = lax.broadcasted_iota(jnp.int32, (d_normed.shape[0], 1), 0) < len_ref[m]
    d_ref[...] = jnp.where(valid, d_normed, 0.0).astype(low_type)


def rank_back(lengths, margins, same, positive, pooled, vectors, slope, down, up, slot):
    count, inner = slope.shape
    width = pooled.shape[1]
    return call(
        functools.partial(rank_kernel, len(margins), len(down), len(up)),
        "rank_backward",
        [
            shape_of((8, width), full_type),
            shape_of((8, inner), full_type),
            shape_of((8, width), full_type),
            shape_of((count, width), low_type),
        ],
        cost=(1200, 20000),
        grid=(count // slot,),
        in_specs=[
            on_scalars(),
            *(whole(array.shape) for array in (same, positive, pooled, vectors)),
            row_blocks((slot, inner)),
            *(whole(piece.shape) for piece in (*margins, *down, *up)),
        ],
        out_specs=[
            whole((8, width)),
            whole((8, inner)),
            whole((8, width)),
            row_blocks((slot, width)),
        ],
        scratch_shapes=[pltpu.VMEM((width, inner), low_type), pltpu.VMEM((width, inner), low_type)],
    )(lengths, same, positive, pooled, vectors, slope, *margins, *down, *up)


def up_grad_kernel(slot, normed_ref, slope_ref, act_ref, *refs):
    *out_refs, turned_ref = refs

    @pl.when(pl.program_id(0) == 0)
    def turn():
        turned_ref[...] = normed_ref[...].T

    total = 0.0
    for m in range(normed_ref.shape[0] // slot):
        rows = slice(m * slot, (m + 1) * slot)
        d_hidden = (slope_ref[rows].astype(full_type) * act_ref[m : m + 1]).astype(low_type)
        total = total + dot_nn(turned_ref[:, rows], d_hidden)
    spill_rows(total, out_refs)


def up_grad(normed, slope, d_act, rows, slot):
    count, width = normed.shape
    inner = slope.shape[1]
    block = 4 * LANES
    return call(
        functools.partial(up_grad_kernel, slot),
        "hidden_in_gradient",
        [shape_of((r, inner), low_type) for r in rows],
        cost=(1200, 15000),
        grid=(inner // block,),
        in_specs=[
            whole(normed.shape),
            column_blocks((count, block)),
            column_blocks((8, block)),
        ],
        out_specs=[column_blocks((r, block)) for r in rows],
        scratch_shapes=[pltpu.VMEM((width, count), low_type)],
    )(normed, slope, d_act)


def middle_kernel(
    pieces, len_ref, x_ref, branch_ref, other_ref, own_ref, came_ref, vector_ref, line_ref,
    att_ref, inv_ref, *refs
):
    weight_refs, refs = refs[:pieces], refs[pieces:]
    d_ref, d_att_ref, gain_ref, total_ref, w_ref = refs
    m = pl.program_id(0)

    @pl.when(m == 0)
    def assemble():
        fill_rows(w_ref, weight_refs)
        total_ref[...] = jnp.zeros_like(total_ref)
        gain_ref[...] = jnp.zeros_like(gain_ref)

    middle = middle_rows(x_ref, branch_ref, other_ref)
    own = own_ref[...].astype(full_type)
    scale = rms_scale(middle)
    gain_ref[...] += jnp.sum(own * middle * scale, axis=0, keepdims=True)
    valid = lax.broadcasted_iota(jnp.int32, (middle.shape[0], 1), 0) < len_ref[m]
    line = jnp.where(m == 0, line_ref[0:1], line_ref[1:2])
    d_middle = jnp.where(valid, line, 0.0) + norm_input_grad(
        own + came_ref[...].astype(full_type), vector_ref[1:2], middle, scale
    )
    d_ref[...] = d_middle
    d_low = d_middle.astype(low_type)
    d_att_ref[...] = (dot_nn(d_low, w_ref[...]) * inv_ref[...]).astype(low_type)
    total_ref[...] += dot_tn(d_low, att_ref[...])


def middle_back(
    lengths, rows_low, branch, other, own, came, vectors, lines, attended, inverse, weights, slot
):
    count, width = rows_low.shape
    head_width = attended.shape[1]
    return call(
        functools.partial(middle_kernel, len(weights)),
        "middle_backward",
        [
            shape_of((count, width), full_type),
            shape_of((count, head_width), low_type),
            shape_of((8, width), full_type),
            shape_of((width, head_width), full_type),
        ],
        cost=(600, 15000),
        grid=(count // slot,),
        in_specs=[
            on_scalars(),
            *[row_blocks((slot, width))] * 5,
            whole(vectors.shape),
            whole(lines.shape),
            row_blocks((slot, head_width)),
            row_blocks((slot, head_width)),
            *(
                pl.BlockSpec((piece.shape[0], head_width), lambda i: (0, 3)) for piece in weights
            ),
        ],
        out_specs=[
            row_blocks((slot, width)),
            row_blocks((slot, head_width)),
            whole((8, width)),
            whole((width, head_width)),
        ],
        scratch_shapes=[pltpu.VMEM((width, head_width), low_type)],
    )(
        lengths, rows_low, branch, other, own, came, vectors, lines, attended, inverse, *weights
    )


def attention_back_kernel(
    befores, steps, prob_ref, qkv_ref, d_ref, att_ref, turned_ref, hot_ref, grad_ref, *refs
):
    d_out_ref, table_ref, *out_refs, tile_ref, dk_ref, dv_ref = refs[befores:]
    step = pl.program_id(0)

    if steps > 1:

        @pl.when(step > 0)
        def projection():
            spill_rows(grad_ref[...], out_refs)

    @pl.when(step == 0)
    def heads():
        pair_back(
            prob_ref, qkv_ref, d_ref, att_ref, turned_ref, hot_ref, d_out_ref, table_ref, out_refs,
            tile_ref, dk_ref, dv_ref
        )


def pair_back(
    prob_ref, qkv_ref, d_ref, att_ref, turned_ref, hot_ref, d_out_ref, table_ref, out_refs,
    tile_ref, dk_ref, dv_ref
):
    micro, slot = prob_ref.shape[1], prob_ref.shape[3]
    blocks = slot // LANES
    spans = 2 * blocks - 1
    lanes = head_lanes()

    tile_ref[...] = jnp.zeros_like(tile_ref)

    def micro_step(m, carry):
        start = pl.multiple_of(m * slot, slot)
        everything = pl.ds(start, slot)
        keys, values = qkv_ref[0, 1, everything, :], qkv_ref[0, 2, everything, :]
        for r in range(slot // ROWS):
            rows = pl.ds(start + r * ROWS, ROWS)
            queries = qkv_ref[0, 0, rows, :]
            queries = jnp.concatenate(
                [queries * lanes[h].astype(low_type) for h in range(2)], axis=0
            )
            d_att = d_ref[rows, :]
            product = d_att.astype(full_type) * att_ref[rows, :].astype(full_type)
            row_dot = jnp.concatenate(
                [
                    jnp.sum(jnp.where(lanes[h], product, 0.0), axis=1, keepdims=True)
                    for h in range(2)
                ],
                axis=0,
            )
            d_att = jnp.concatenate([d_att * lanes[h].astype(low_type) for h in range(2)], axis=0)
            span = slice(r * ROWS, (r + 1) * ROWS)
            probs = jnp.concatenate([prob_ref[0, m, h, span, :] for h in range(2)], axis=0)
            d_scores = probs.astype(full_type) * (dot_nt(d_att, values) - row_dot)
            d_low = d_scores.astype(low_type)
            for h in range(2):
                for i in range(ROWS // LANES):
                    for j in range(blocks):
                        top = h * ROWS + i * LANES
                        tile_ref[h, j - r * (ROWS // LANES) - i + blocks - 1] += d_scores[
                            top : top + LANES, j * LANES : (j + 1) * LANES
                        ]
            d_queries = dot_nn(d_low, keys)
            d_out_ref[0, 0, rows, :] = jnp.where(
                lanes[0], d_queries[:ROWS], d_queries[ROWS:]
            ).astype(low_type)
            d_keys, d_values = dot_tn(d_low, queries), dot_tn(probs, d_att)
            dk_ref[...] = d_keys if r == 0 else dk_ref[...] + d_keys
            dv_ref[...] = d_values if r == 0 else dv_ref[...] + d_values
        d_out_ref[0, 1, everything, :] = dk_ref[...].astype(low_type)
        d_out_ref[0, 2, everything, :] = dv_ref[...].astype(low_type)
        return carry

    lax.fori_loop(0, micro, micro_step, 0)
    d_project = jnp.concatenate([d_out_ref[0, c] for c in range(3)], axis=1)
    spill_rows(dot_nn(turned_ref[...], d_project), out_refs)
    flip = (
        lax.broadcasted_iota(jnp.int32, (LANES, LANES), 0)
        + lax.broadcasted_iota(jnp.int32, (LANES, LANES), 1)
        == LANES - 1
    )
    flip = jnp.where(flip, 1.0, 0.0).astype(low_type)
    table = jnp.zeros((16, LANES), full_type)
    for d in range(spans):
        highs, rests = [], []
        for h in range(2):
            tile = tile_ref[h, d]
            high = tile.astype(low_type)
            rest = (tile - high.astype(full_type)).astype(low_type)
            flipped = dot_nn(flip, high) + dot_nn(flip, rest)
            wide = jnp.concatenate([flipped, jnp.zeros_like(flipped)], axis=1)
            turned = pltpu.roll(wide, 0, 1, stride=1, stride_axis=0)
            line = jnp.sum(turned, axis=0, keepdims=True)
            highs.append(line.astype(low_type).astype(full_type))
            rests.append(line - highs[-1])
        table = table + dot_nn(few_rows(highs + rests, 16).astype(low_type), hot_ref[d])
    table_ref[0] = few_rows([table[h : h + 1] + table[2 + h : 3 + h] for h in range(2)], 8)


def attention_back(
    probs, qkv, d_attended, attended, turned, hot, grad_out, rows, pair, slot, before=(), deps=()
):
    width, count = turned.shape
    micro = count // slot
    pairs = qkv.shape[0]
    spans = 2 * (slot // LANES) - 1
    steps = 2 if pair == pairs - 1 else 1
    lead = lambda shape: pl.BlockSpec(shape, lambda i: (pair,) + (0,) * (len(shape) - 1))
    column = pl.BlockSpec((count, LANES), lambda i: (0, pair))
    return call(
        functools.partial(attention_back_kernel, len(before), steps),
        "attention_backward",
        [
            shape_of((pairs, 3, count, LANES), low_type),
            shape_of((pairs, 8, LANES), full_type),
            *(shape_of((r, (pairs + 1) * 3 * LANES), low_type) for r in rows),
        ],
        deps=deps,
        grid=(steps,),
        in_specs=[
            lead((1, micro, 2, slot, slot)),
            lead((1, 3, count, LANES)),
            column,
            column,
            whole(turned.shape),
            whole(hot.shape),
            whole(grad_out.shape) if steps == 2 else in_place(),
            *[in_place()] * len(before),
        ],
        out_specs=[
            lead((1, 3, count, LANES)),
            lead((1, 8, LANES)),
            *(pl.BlockSpec((r, 3 * LANES), lambda i: (0, i + pair)) for r in rows),
        ],
        input_output_aliases={7 + i: i for i in range(len(before))},
        scratch_shapes=[
            pltpu.VMEM((2, spans, LANES, LANES), full_type),
            pltpu.VMEM((slot, LANES), full_type),
            pltpu.VMEM((slot, LANES), full_type),
        ],
    )(probs, qkv, d_attended, attended, turned, hot, grad_out, *before)


def normed_back_kernel(
    pieces, core_ref, x_ref, second_ref, rank_ref, line_ref, act_ref, table_ref, d_ref, *refs
):
    weight_refs, refs = refs[:pieces], refs[pieces:]
    own_ref, small_ref, w_ref, gain_ref = refs
    step, last = pl.program_id(0), pl.num_programs(0) - 1
    pairs, parts = d_ref.shape[0], d_ref.shape[1]
    width = x_ref.shape[1]

    @pl.when(step == 0)
    def assemble():
        fill_rows(w_ref, weight_refs, slice(0, w_ref.shape[1]))
        gain_ref[...] = jnp.zeros_like(gain_ref)

    blocks = [d_ref[p, c] for c in range(parts) for p in range(pairs)]
    d_normed = dot_nt(jnp.concatenate(blocks, axis=1), w_ref[...])
    own_ref[...] = d_normed.astype(low_type)
    x = x_ref[...].astype(full_type)
    gain_ref[...] += jnp.sum(d_normed * x * rms_scale(x), axis=0, keepdims=True)

    @pl.when(step == last)
    def small():
        micro = act_ref.shape[0]
        lines = [line_ref[m : m + 1].astype(low_type).astype(full_type) for m in range(micro)]
        for m in range(micro):
            act = act_ref[m]
            lines += [act[:, i * width : (i + 1) * width] for i in range(act.shape[1] // width)]
        share = jnp.where(core_ref[0] == 0, 1.0, 0.0)
        lines += [gain_ref[0:1], second_ref[0:1], rank_ref[0:1] * share, rank_ref[1:2] * share]
        lines.append(
            jnp.concatenate([table_ref[p, h : h + 1] for p in range(pairs) for h in range(2)], axis=1)
        )
        small_ref[...] = few_rows(lines, 16)


def normed_back(core, rows_low, second_gain, rank_gain, lines, act_sum, table, d_project, weights):
    count, width = rows_low.shape
    pairs, parts = d_project.shape[0], d_project.shape[1]
    in_width = pairs * parts * LANES
    return call(
        functools.partial(normed_back_kernel, len(weights)),
        "normed_backward",
        [shape_of((count, width), low_type), shape_of((16, width), full_type)],
        cost=(900, 15000),
        grid=(count // ROWS,),
        in_specs=[
            on_scalars(),
            row_blocks((ROWS, width)),
            *(whole(array.shape) for array in (second_gain, rank_gain, lines, act_sum, table)),
            pl.BlockSpec((pairs, parts, ROWS, LANES), lambda i: (0, 0, i, 0)),
            *(whole(piece.shape) for piece in weights),
        ],
        out_specs=[row_blocks((ROWS, width)), whole((16, width))],
        scratch_shapes=[pltpu.VMEM((width, in_width), low_type), pltpu.VMEM((8, width), full_type)],
    )(core, rows_low, second_gain, rank_gain, lines, act_sum, table, d_project, *weights)


def token_kernel(d_ref, own_ref, came_ref, x_ref, vector_ref, order_ref, out_ref):
    x = x_ref[...].astype(full_type)
    d_normed = own_ref[...].astype(full_type) + came_ref[...].astype(full_type)
    grad = d_ref[...] + norm_input_grad(d_normed, vector_ref[0:1], x, rms_scale(x))
    high = grad.astype(low_type)
    rest = (grad - high.astype(full_type)).astype(low_type)
    order = order_ref[...]
    out_ref[...] = dot_nt(high, order) + dot_nt(rest, order)


def token_back(d_middle, own, came, rows_low, vectors, order):
    count, width = rows_low.shape
    return call(
        token_kernel,
        "token_gradient",
        shape_of((count, width), full_type),
        cost=(1200, 15000),
        grid=(count // ROWS,),
        in_specs=[row_blocks((ROWS, width))] * 4 + [whole(vectors.shape), whole(order.shape)],
        out_specs=row_blocks((ROWS, width)),
    )(d_middle, own, came, rows_low, vectors, order)


def total_kernel(smalls, counts, micro, *refs):
    small_refs, refs = refs[:smalls], refs[smalls:]
    groups = []
    for count in counts:
        groups.append(refs[:count])
        refs = refs[count:]
    down_ref, line_ref, table_ref, *out_refs = refs
    size, width = sum(ref.shape[0] for ref in small_refs), small_refs[0].shape[2]
    row_of = lambda row: jnp.concatenate([ref[:, row, :] for ref in small_refs], axis=0)
    own = down_ref.shape[0]
    inverse = 1.0 / LOSS_SCALE
    add_up = lambda values: jnp.sum(values, axis=0, keepdims=True).sum(axis=1, keepdims=True)
    squares = 0.0
    for group, out_ref in zip(groups, out_refs):
        total = sum(ref[...].astype(full_type) for ref in group) * inverse
        out_ref[...] = total
        squares = squares + add_up(total * total)

    block = lax.broadcasted_iota(jnp.int32, (size, width), 1) // own
    mine = block == lax.broadcasted_iota(jnp.int32, (size, width), 0)
    fold = lax.broadcasted_iota(jnp.int32, (width, LANES), 0) % own == lax.broadcasted_iota(
        jnp.int32, (width, LANES), 1
    )
    fold = jnp.where(fold, 1.0, 0.0).astype(low_type)
    pick = lambda row: jnp.where(mine, row_of(row), 0.0)
    down = 0.0
    parts = down_ref.shape[1] // width
    for m in range(micro):
        lines = dot_nn(pick(m).astype(low_type), fold).astype(low_type)
        acts = [row_of(micro + m * parts + i) for i in range(parts)]
        acts = jnp.concatenate(acts, axis=1)
        high = acts.astype(low_type)
        rest = (acts - high.astype(full_type)).astype(low_type)
        down = down + dot_tn(lines, high) + dot_tn(lines, rest)
    down = down[:own] * inverse
    down_ref[...] = down
    squares = squares + add_up(down * down)

    first = micro + micro * parts
    vectors = [jnp.sum(pick(first + i), axis=0, keepdims=True) for i in range(4)]
    rest = few_rows(vectors, 16) * inverse
    extra = 0.0
    for _ in range(3):
        high = rest.astype(low_type)
        extra = extra + dot_nn(high, fold)
        rest = rest - high.astype(full_type)
    table = jnp.sum(row_of(first + 4), axis=0, keepdims=True) * inverse
    squares = squares + add_up(table * table) * (1.0 / size)
    heads = table_ref.shape[0]
    table_ref[...] = few_rows([table[:, h * LANES : (h + 1) * LANES] for h in range(heads)], heads)
    line_ref[:8] = extra[:8]
    line_ref[8:] = jnp.broadcast_to(squares, (8, LANES))


def totals(small_all, grads, heads, down_shape, micro):
    counts = tuple(len(group) for group in grads)
    flat = [array for group in grads for array in group]
    down, line, table, *sums = call(
        functools.partial(total_kernel, len(small_all), counts, micro),
        "gradient_totals",
        [
            shape_of(down_shape, full_type),
            shape_of((16, LANES), full_type),
            shape_of((heads, LANES), full_type),
            *(shape_of(group[0].shape, full_type) for group in grads),
        ],
        cost=(100, 10000),
    )(*small_all, *flat)
    return down, line, table, sums


def adam(weight, first_old, second, grad, factor, rate, decay, step_ref):
    clipped = grad * factor
    next_first = beta_first * first_old + (1.0 - beta_first) * clipped
    next_second = beta_second * second + (1.0 - beta_second) * clipped * clipped
    first_hat = next_first * step_ref[0]
    second_hat = next_second * step_ref[1]
    next_weight = weight - rate * (first_hat / (jnp.sqrt(second_hat) + adam_eps) + decay * weight)
    return next_weight, next_first, next_second


def square_kernel(own_ref, other_ref, out_ref, extra_ref):
    extra = own_ref[:8] + other_ref[:8]
    extra_ref[...] = extra
    place = lax.broadcasted_iota(jnp.int32, (8, LANES), 0)
    counted = jnp.where(place == 3, 2.0, 1.0) * extra * extra
    squares = jnp.sum(counted, axis=0, keepdims=True).sum(axis=1, keepdims=True)
    out_ref[...] = own_ref[8:] + other_ref[8:] + squares


def update_kernel(squares, groups, step_ref, table_ref, extra_ref, *refs):
    square_refs, refs = refs[:squares], refs[squares:]
    grad_refs, refs = refs[:groups], refs[groups:]
    state_refs, refs = refs[:21], refs[21:]
    norm_ref, *out_refs = refs
    squares = jnp.sum(stacked(square_refs), axis=0)[0:1, 0:1]
    norm = jnp.sqrt(squares)
    norm_ref[...] = jnp.broadcast_to(norm, norm_ref.shape)
    factor = jnp.minimum(1.0, clip_limit / (norm + 1e-06))
    weights, firsts, seconds = state_refs[:7], state_refs[7:14], state_refs[14:]
    next_weights, next_firsts, next_seconds = out_refs[:7], out_refs[7:14], out_refs[14:]

    def step(index, where, grad, rate, decay):
        results = adam(
            weights[index][where], firsts[index][where], seconds[index][where], grad, factor,
            rate, decay, step_ref,
        )
        for target, result in zip((next_weights, next_firsts, next_seconds), results):
            target[index][where] = result

    everything = (slice(None), slice(None))
    mixed_ref, up_ref, down_ref = grad_refs
    parts, rows, head_width = weights[0].shape
    pairs = head_width // LANES
    for p in range(pairs):
        for c in range(parts):
            start = (p * parts + c) * LANES
            where = (c, slice(None), slice(p * LANES, (p + 1) * LANES))
            step(0, where, mixed_ref[:, start : start + LANES], rate_matrix, decay_matrix)
    step(1, everything, mixed_ref[:, pairs * parts * LANES :], rate_matrix, decay_matrix)
    step(2, everything, up_ref[...], rate_matrix, decay_matrix)
    step(3, everything, down_ref[...], rate_matrix, decay_matrix)
    extra = extra_ref[...]
    step(4, everything, extra[0:3, :rows], rate_vector, 0.0)
    tied = extra[3:4, :rows]
    step(5, everything, jnp.concatenate([tied, -tied], axis=0), rate_vector, 0.0)
    step(6, everything, table_ref[:, :BUCKETS], rate_vector, 0.0)


def body(
    tokens,
    pair_lengths,
    query_ids,
    distance_bucket,
    step_count,
    heads_in,
    heads_out,
    hidden_in,
    hidden_out,
    gains,
    tied_rows,
    bias_table,
    first_heads_in,
    first_heads_out,
    first_hidden_in,
    first_hidden_out,
    first_gains,
    first_tied,
    first_table,
    second_heads_in,
    second_heads_out,
    second_hidden_in,
    second_hidden_out,
    second_gains,
    second_tied,
    second_table,
):
    size = lax.axis_size("dp")
    me = lax.axis_index("dp")
    core = lax.axis_index("mp")
    micro, _, slot, width = tokens.shape
    count = micro * slot
    own, local_heads = heads_in.shape[0], bias_table.shape[1]
    head_width = heads_in.shape[2]
    inner = hidden_in.shape[1]
    pairs = local_heads // 2
    spans = 2 * (slot // LANES) - 1
    turn_matrix = lambda array: jnp.transpose(array, (1, 0, 2))
    heads_in, first_heads_in, second_heads_in = (
        turn_matrix(array) for array in (heads_in, first_heads_in, second_heads_in)
    )
    gains, tied_rows, bias_table = gains.T, tied_rows.T, bias_table.T
    first_gains, first_tied, first_table = first_gains.T, first_tied.T, first_table.T
    second_gains, second_tied, second_table = second_gains.T, second_tied.T, second_table.T

    packed_heads = call(
        pack_heads_kernel, "pack_heads", shape_of((own, 4 * head_width + LANES), low_type)
    )(heads_in, heads_out, gains, tied_rows)
    packed_up, packed_down = call(
        pack_hidden_kernel, "pack_hidden", [shape_of((own, inner), low_type)] * 2
    )(hidden_in, hidden_out)
    pair_ids = jnp.bitwise_xor(me, jnp.array(block_masks(size), jnp.int32))
    place = (pair_ids[:, None] * own + jnp.arange(own, dtype=jnp.int32)[None, :]).reshape(width)
    order = (jnp.arange(width, dtype=jnp.int32)[:, None] == place[None, :]).astype(low_type)
    lengths = pair_lengths.reshape(micro)
    queries = query_ids[:, pair_ids]
    same_query = queries == queries[:, :1]
    earlier = jnp.any(same_query & (pair_ids < me)[None, :], axis=1)
    to_tile = lambda rows_m: jnp.broadcast_to(
        jnp.concatenate(
            [rows_m, jnp.zeros(rows_m.shape[:-1] + (8 - micro,), full_type)], axis=-1
        )[..., None],
        rows_m.shape[:-1] + (8, LANES),
    )
    same_tile = to_tile(same_query.astype(full_type).T)
    positive_tile = to_tile(jnp.where(earlier, 0.0, 1.0))

    bucket_line = jnp.concatenate([distance_bucket, jnp.full((1,), -1, jnp.int32)])
    bucket_hot = (
        bucket_line[:, None] == jnp.arange(LANES, dtype=jnp.int32)[None, :]
    ).astype(low_type)
    lines = dot_nt(bias_table.astype(low_type), bucket_hot[:, :BUCKETS])
    lines = lines.reshape(pairs, 2, 2 * slot)
    hot_spans = jnp.stack([bucket_hot[d * LANES : (d + 2) * LANES] for d in range(spans)])

    rows_low = call(
        order_kernel,
        "order_tokens",
        shape_of((count, width), low_type),
        cost=(600, 5000),
        grid=(count // ROWS,),
        in_specs=[row_blocks((ROWS, width)), whole((width, width))],
        out_specs=row_blocks((ROWS, width)),
    )(tokens.reshape(count, width), order)
    if size != 16:
        weight_heads, weight_up, weight_down = (
            [gather_doubling(part, size)] for part in (packed_heads, packed_up, packed_down)
        )
        qkv, normed_first, vectors = project(rows_low, weight_heads, pairs, ())
    else:
        heads_line, packed_up = join(line_parts(packed_heads, size, "heads"), passing=(packed_up,))
        heads_sides = side_parts(heads_line, size, "heads")
        low, high, up_line, packed_down = gather_step(
            *heads_sides, line_parts(packed_up, size, "up"), deps=(rows_low,), passing=(packed_down,)
        )
        heads_corner = corner_parts(low, high, size, "heads_corner")
        up_sides = side_parts(up_line, size, "up")
        low, high, down_line = gather_step(*up_sides, line_parts(packed_down, size, "down"))
        up_corner = corner_parts(low, high, size, "up_corner")
        down_sides = side_parts(down_line, size, "down")
        weight_heads = [heads_line, *heads_sides, *heads_corner]
        weight_up = [up_line, *up_sides, *up_corner]
        qkv, normed_first, vectors = project(rows_low, weight_heads, pairs, (down_line,))
    filled = ()
    for pair in range(pairs):
        filled = attention(lengths, lines, qkv, pair, slot, before=filled)
        if pair == 1 and size == 16:
            low, high = gather_step(*down_sides, [], deps=(filled[0], *up_corner))
            down_corner = corner_parts(low, high, size, "down_corner")
            weight_down = [down_line, *down_sides, *down_corner]
    turned_first = call(turn_kernel, "turn", shape_of((width, count), low_type))(normed_first)
    attended, probs, inverse = filled
    branch = branch_rows(attended, weight_heads)
    branch_came = other_core(branch, "branch_other_core")
    normed_second, slope, act_sum, middle_sum = hidden(
        lengths, rows_low, branch, branch_came, vectors, weight_up, slot
    )
    down = call(
        pool_kernel,
        "pool",
        shape_of((8, width), full_type),
        cost=(20, 5000),
        scratch_shapes=[pltpu.VMEM((width, inner), low_type)],
    )(act_sum, *weight_down)
    margin_tile, pooled = call(
        margin_kernel,
        "margin",
        [shape_of((8, LANES), full_type), shape_of((8, width), full_type)],
        in_specs=[on_scalars()] + [pl.BlockSpec(memory_space=pltpu.VMEM)] * 4,
    )(lengths, down, other_core(down, "pooled_part_other_core"), middle_sum, vectors)
    margins = gather_small(margin_tile, size, "margins")

    d_line, d_act, rank_extra, d_normed_second = rank_back(
        lengths, margins, same_tile, positive_tile, pooled, vectors, slope,
        weight_down, weight_up, slot,
    )
    d_normed_second_came = other_core(d_normed_second, "second_gradient_other_core")
    up_sum = Scatter(
        up_grad(normed_second, slope, d_act, piece_rows(size, width), slot), size, "up_gradient"
    )
    d_middle, d_attended, gain_second, g_out = middle_back(
        lengths, rows_low, branch, branch_came, d_normed_second, d_normed_second_came, vectors,
        d_line, attended, inverse, weight_heads, slot,
    )
    up_sum.sides(deps=(d_attended,))
    filled = ()
    for pair in range(pairs):
        filled = attention_back(
            probs, qkv, d_attended, attended, turned_first, hot_spans, g_out,
            piece_rows(size, width), pair, slot, before=filled,
            deps=up_parts if pair == pairs - 1 else (),
        )
        if pair == 0:
            up_parts, _ = up_sum.line(deps=(filled[1],))
    d_project, table_tile, *g_heads = filled
    heads_sum = Scatter(g_heads, size, "heads_gradient")
    d_normed_first, small = normed_back(
        core.reshape(1), rows_low, gain_second, rank_extra, d_line, act_sum, table_tile, d_project,
        weight_heads,
    )
    small, d_normed_first = heads_sum.sides(passing=(small, d_normed_first))
    small = small_line(small, size, "small_sums")
    token_gradient = token_back(
        d_middle, d_normed_first, other_core(d_normed_first, "first_gradient_other_core"), rows_low, vectors, order
    )

    head_parts, (small,) = heads_sum.line(deps=(token_gradient,), passing=(small,))
    small_all = small_plane(small, size, "small_sums")

    g_down, line, table, grad_sums = totals(
        small_all, [head_parts, up_parts], local_heads, (own, inner), micro
    )
    square_tile, extra = call(
        square_kernel,
        "squares",
        [shape_of((8, LANES), full_type), shape_of((8, LANES), full_type)],
    )(line, other_core(line, "totals_other_core"))
    squares_all = gather_small(square_tile, size, "squares")
    step_float = step_count.astype(full_type)
    corrections = jnp.stack(
        [1.0 / (1.0 - beta_first**step_float), 1.0 / (1.0 - beta_second**step_float)]
    )
    grads = [*grad_sums, g_down]
    weights = (heads_in, heads_out, hidden_in, hidden_out, gains, tied_rows, bias_table)
    firsts = (
        first_heads_in,
        first_heads_out,
        first_hidden_in,
        first_hidden_out,
        first_gains,
        first_tied,
        first_table,
    )
    seconds = (
        second_heads_in,
        second_heads_out,
        second_hidden_in,
        second_hidden_out,
        second_gains,
        second_tied,
        second_table,
    )
    states = (*weights, *firsts, *seconds)
    norm, *results = call(
        functools.partial(update_kernel, len(squares_all), len(grads)),
        "update",
        [shape_of((8, LANES), full_type)] + [shape_of(s.shape, full_type) for s in states],
        in_specs=[on_scalars()]
        + [pl.BlockSpec(memory_space=pltpu.VMEM)] * (2 + len(squares_all) + len(grads) + len(states)),
        cost=(0, 6000),
    )(corrections, table, extra, *squares_all, *grads, *states)
    for index in (0, 7, 14):
        results[index] = turn_matrix(results[index])
        for other in (4, 5, 6):
            results[index + other] = results[index + other].T
    return (norm[0, 0], token_gradient.reshape(tokens.shape), *results)


def solution(mesh):
    in_specs = (
        P(None, "dp", None, None),
        P(None, "dp"),
        P(),
        P(),
        P(),
        P("dp", None, "mp"),
        P("dp", "mp"),
        P("dp", "mp"),
        P("dp", "mp"),
        P("dp", None),
        P("dp", None),
        P(None, "mp"),
        P("dp", None, "mp"),
        P("dp", "mp"),
        P("dp", "mp"),
        P("dp", "mp"),
        P("dp", None),
        P("dp", None),
        P(None, "mp"),
        P("dp", None, "mp"),
        P("dp", "mp"),
        P("dp", "mp"),
        P("dp", "mp"),
        P("dp", None),
        P("dp", None),
        P(None, "mp"),
    )
    out_specs = (
        P(),
        P(None, "dp", None, None),
        P("dp", None, "mp"),
        P("dp", "mp"),
        P("dp", "mp"),
        P("dp", "mp"),
        P("dp", None),
        P("dp", None),
        P(None, "mp"),
        P("dp", None, "mp"),
        P("dp", "mp"),
        P("dp", "mp"),
        P("dp", "mp"),
        P("dp", None),
        P("dp", None),
        P(None, "mp"),
        P("dp", None, "mp"),
        P("dp", "mp"),
        P("dp", "mp"),
        P("dp", "mp"),
        P("dp", None),
        P("dp", None),
        P(None, "mp"),
    )
    return jax.shard_map(body, mesh=mesh, in_specs=in_specs, out_specs=out_specs, check_vma=False)
```

```python
import functools

import jax
import jax.numpy as jnp
from jax import lax
from jax.experimental import pallas as pl
from jax.experimental.pallas import tpu as pltpu
from jax.sharding import PartitionSpec as P

BUCKETS = 32
LOSS_SCALE = 1024
LANES = 128
ROWS = 256

norm_eps = 1e-06
clip_limit = 0.01
beta_first = 0.9
beta_second = 0.999
adam_eps = 1e-08
rate_matrix = 0.03
rate_vector = 0.25
decay_matrix = 0.1
masked_score = -1e30
gelu_slope = 0.7978845608028654
gelu_cubic = 0.044715
low_type = jnp.bfloat16
full_type = jnp.float32
core_swap = [(0, 1), (1, 0)]


def rms_scale(rows_in):
    return lax.rsqrt(jnp.mean(rows_in * rows_in, axis=-1, keepdims=True) + norm_eps)


def norm_input_grad(d_normed, gain_row, rows_in, norm_scale):
    weighted = d_normed * gain_row
    return norm_scale * weighted - rows_in * norm_scale**3 * jnp.mean(
        weighted * rows_in, axis=-1, keepdims=True
    )


def dot_nt(left, right):
    return lax.dot_general(left, right, (((1,), (1,)), ((), ())), preferred_element_type=full_type)


def dot_tn(left, right):
    return lax.dot_general(left, right, (((0,), (0,)), ((), ())), preferred_element_type=full_type)


def dot_nn(left, right):
    return lax.dot_general(left, right, (((1,), (0,)), ((), ())), preferred_element_type=full_type)


def call(
    kernel, name, out_shape, cost=(0, 0), vmem=16, deps=(), passing=(), in_specs=None,
    out_specs=None, input_output_aliases=None, **options
):
    single = not isinstance(out_shape, (list, tuple))
    out_shapes = [out_shape] if single else list(out_shape)
    outputs, extra = len(out_shapes), len(deps) + len(passing)

    def apply(*operands):
        inputs = len(operands)
        if not in_specs:
            options["grid"] = (1,)
        specs = in_specs or [whole(operand.shape) for operand in operands]
        targets = out_specs or [whole(shape.shape) for shape in out_shapes]
        targets = targets if isinstance(targets, (list, tuple)) else [targets]
        aliases = dict(input_output_aliases or {})
        for i in range(len(passing)):
            aliases[inputs + len(deps) + i] = outputs + i

        def run(*refs):
            own = inputs + extra
            kernel(*refs[:inputs], *refs[own : own + outputs], *refs[own + outputs + len(passing) :])

        results = pl.pallas_call(
            run,
            out_shape=[*out_shapes, *(shape_of(a.shape, a.dtype) for a in passing)],
            in_specs=[*specs, *[in_place()] * extra],
            out_specs=[*targets, *[in_place()] * len(passing)],
            input_output_aliases=aliases,
            compiler_params=pltpu.CompilerParams(vmem_limit_bytes=vmem * 1024 * 1024),
            cost_estimate=pl.CostEstimate(
                flops=int(cost[0] * 2e6), bytes_accessed=int(cost[1] * 1e3), transcendentals=0
            ),
            name=name,
            **options,
        )(*operands, *deps, *passing)
        return results[0] if single and not passing else results

    return apply


def in_place():
    return pl.BlockSpec(memory_space=pl.ANY)


def shape_of(shape, dtype):
    return jax.ShapeDtypeStruct(tuple(shape), dtype)


def whole(shape):
    return pl.BlockSpec(tuple(shape), lambda *_: (0,) * len(shape))


def on_scalars():
    return pl.BlockSpec(memory_space=pltpu.SMEM)


def row_blocks(shape, step=0):
    return pl.BlockSpec(tuple(shape), lambda i: (i,) + (0,) * (len(shape) - 1))


def column_blocks(shape, offset=0):
    return pl.BlockSpec(tuple(shape), lambda i: (0,) * (len(shape) - 1) + (i + offset,))


def fill_rows(target, pieces, columns=slice(None)):
    start = 0
    for piece in pieces:
        rows = piece.shape[0]
        target[start : start + rows, :] = piece[:, columns]
        start += rows


def spill_rows(value, pieces):
    start = 0
    for piece in pieces:
        rows = piece.shape[0]
        piece[...] = value[start : start + rows].astype(piece.dtype)
        start += rows


def swap(array, mask, size, label="exchange"):
    with jax.named_scope(f"{label}_across_{mask}"):
        return lax.ppermute(array, "dp", [(i, i ^ mask) for i in range(size)])


def other_core(array, label="other_core"):
    with jax.named_scope(label):
        return lax.ppermute(array, "mp", core_swap)


def stage_bits(size):
    if size == 16:
        return (4, 8, 2, 1)
    return tuple(1 << i for i in range(size.bit_length() - 1))


def block_masks(size):
    bits = stage_bits(size)
    return [sum(bit for i, bit in enumerate(bits) if k >> i & 1) for k in range(size)]


def piece_rows(size, width):
    if size != 16:
        return [width]
    return [width // 4] * 3 + [width // 8] * 2


def join_kernel(*refs):
    *part_refs, out_ref = refs
    start = 0
    for part in part_refs:
        rows = part.shape[0]
        out_ref[start : start + rows] = part[...]
        start += rows


def join(parts, **options):
    rows = sum(part.shape[0] for part in parts)
    return call(
        join_kernel, "join", shape_of((rows, *parts[0].shape[1:]), parts[0].dtype), **options
    )(*parts)


def step_kernel(parts, y_ref, x_ref, *refs):
    part_refs, (low_ref, high_ref, *line_refs) = refs[:parts], refs[parts:]
    low_ref[...] = y_ref[...]
    high_ref[...] = x_ref[...]
    if parts:
        join_kernel(*part_refs, *line_refs)


def gather_step(across_y, across_x, parts, **options):
    half = (across_y.shape[0] // 2, across_y.shape[1])
    shapes = [shape_of(half, across_y.dtype)] * 2
    if parts:
        shapes.append(shape_of((sum(p.shape[0] for p in parts), parts[0].shape[1]), parts[0].dtype))
    return call(
        functools.partial(step_kernel, len(parts)),
        "gather_step",
        shapes,
        grid=(1,),
        in_specs=[
            pl.BlockSpec(half, lambda i: (0, 0)),
            pl.BlockSpec(half, lambda i: (1, 0)),
            *(whole(part.shape) for part in parts),
        ],
        out_specs=[whole(shape.shape) for shape in shapes],
        **options,
    )(across_y, across_x, *parts)


def line_parts(part, size, label):
    return [part] + [swap(part, mask, size, label) for mask in (4, 8, 12)]


def side_parts(quarter, size, label):
    return [swap(quarter, mask, size, label) for mask in (2, 1)]


def corner_parts(low, high, size, label):
    return [swap(low, 1, size, label), swap(high, 2, size, label)]


def gather_doubling(part, size):
    for bit in stage_bits(size):
        part = jnp.concatenate([part, swap(part, bit, size)], axis=0)
    return part


def small_line(part, size, label):
    if size != 16:
        return part[None]
    return join(line_parts(part[None], size, label))


def small_plane(quarter, size, label):
    if size != 16:
        return [gather_doubling(quarter, size)]
    return [quarter] + [swap(quarter, mask, size, label) for mask in (2, 1, 3)]


def stacked(refs):
    return jnp.concatenate([ref[...] for ref in refs], axis=0)


def gather_small(part, size, label):
    return small_plane(small_line(part, size, label), size, label)


def plane_sum_kernel(y_ref, x_ref, low_ref, high_ref, y_out, x_out):
    half = low_ref.shape[0]
    y_out[:half] = (y_ref[:half].astype(full_type) + low_ref[...].astype(full_type)).astype(low_type)
    y_out[half:] = y_ref[half:]
    x_out[:half] = x_ref[:half]
    x_out[half:] = (x_ref[half:].astype(full_type) + high_ref[...].astype(full_type)).astype(low_type)


def line_sum_kernel(z_ref, y_ref, x_ref, own_ref, *out_refs):
    rows = own_ref.shape[0]
    for i in range(4):
        span = slice(i * rows, (i + 1) * rows)
        total = z_ref[span].astype(full_type) + y_ref[span].astype(full_type)
        total = total + x_ref[span].astype(full_type)
        target = own_ref if i == 0 else out_refs[i - 1]
        target[...] = total.astype(target.dtype)


class Scatter:
    def __init__(self, pieces, size, label):
        self.pieces, self.size, self.label, self.sources = pieces, size, label, ()
        if size == 16:
            *self.pieces, low, high = pieces
            self.came = [swap(low, 1, size, label), swap(high, 2, size, label)]

    def sides(self, deps=(), passing=()):
        if self.size != 16:
            return passing
        keep, to_y, to_x = self.pieces
        to_y, to_x, *passed = call(
            plane_sum_kernel,
            "plane_sum",
            [shape_of(to_y.shape, low_type)] * 2,
            deps=deps,
            passing=passing,
        )(to_y, to_x, *self.came)
        self.sources = (to_y, to_x)
        self.came = [swap(to_y, 2, self.size, self.label), swap(to_x, 1, self.size, self.label)]
        return passed

    def line(self, deps=(), passing=()):
        size, label = self.size, self.label
        if size != 16:
            grad = self.pieces[0]
            for bit in reversed(stage_bits(size)):
                half = grad.shape[0] // 2
                came = swap(grad[half:], bit, size, label)
                grad = (grad[:half].astype(full_type) + came.astype(full_type)).astype(low_type)
            return [grad.astype(full_type)], passing
        keep = self.pieces[0]
        part = (keep.shape[0] // 4, keep.shape[1])
        own, *others = call(
            line_sum_kernel,
            "line_sum",
            [shape_of(part, full_type)] + [shape_of(part, low_type)] * 3,
            deps=deps,
            passing=passing,
        )(keep, *self.came)
        came = [swap(other, mask, size, label) for other, mask in zip(others, (4, 8, 12))]
        return [own] + came, others[3:]


def pack_heads_kernel(in_ref, out_ref, gain_ref, tied_ref, a_ref):
    parts, rows, width = in_ref.shape
    for c in range(parts):
        a_ref[:, c * width : (c + 1) * width] = in_ref[c].astype(low_type)
    a_ref[:, parts * width : (parts + 1) * width] = out_ref[...].astype(low_type)
    gains, tied = gain_ref[...], tied_ref[...]
    vectors = few_rows([gains[i : i + 1] for i in range(3)] + [tied[i : i + 1] for i in range(2)], 16)
    pick = lax.broadcasted_iota(jnp.int32, (16, LANES), 0) == lax.broadcasted_iota(
        jnp.int32, (16, LANES), 1
    )
    extra = dot_tn(vectors.astype(low_type), jnp.where(pick, 1.0, 0.0).astype(low_type))
    a_ref[:, (parts + 1) * width :] = extra.astype(low_type)


def pack_hidden_kernel(up_ref, down_ref, b_ref, c_ref):
    b_ref[...] = up_ref[...].astype(low_type)
    c_ref[...] = down_ref[...].astype(low_type)


def order_kernel(x_ref, order_ref, out_ref):
    out_ref[...] = dot_nn(x_ref[...], order_ref[...]).astype(low_type)


def turn_kernel(x_ref, out_ref):
    out_ref[...] = x_ref[...].T


def head_lanes():
    lane = lax.broadcasted_iota(jnp.int32, (1, LANES), 1)
    return [lane < LANES // 2, lane >= LANES // 2]


def project_kernel(pieces, pairs, x_ref, *refs):
    weight_refs, (qkv_ref, normed_ref, vector_ref, w_ref) = refs[:pieces], refs[pieces:]
    parts = qkv_ref.shape[1]
    in_width = pairs * parts * LANES

    @pl.when(pl.program_id(0) == 0)
    def assemble():
        fill_rows(w_ref, weight_refs)
        pick = lax.broadcasted_iota(jnp.int32, (16, LANES), 0) == lax.broadcasted_iota(
            jnp.int32, (16, LANES), 1
        )
        vectors = dot_nt(jnp.where(pick, 1.0, 0.0).astype(low_type), w_ref[:, -LANES:])
        vector_ref[...] = vectors[:8]

    x = x_ref[...].astype(full_type)
    normed = (x * rms_scale(x) * vector_ref[0:1]).astype(low_type)
    normed_ref[...] = normed
    projected = dot_nn(normed, w_ref[:, :in_width]).astype(low_type)
    for c in range(parts):
        for p in range(pairs):
            start = (c * pairs + p) * LANES
            qkv_ref[p, c] = projected[:, start : start + LANES]


def project(rows_low, weights, pairs, deps):
    count, width = rows_low.shape
    parts = 3
    return call(
        functools.partial(project_kernel, len(weights), pairs),
        "projection",
        [
            shape_of((pairs, parts, count, LANES), low_type),
            shape_of((count, width), low_type),
            shape_of((8, width), full_type),
        ],
        deps=deps,
        grid=(count // ROWS,),
        in_specs=[row_blocks((ROWS, width)), *(whole(piece.shape) for piece in weights)],
        out_specs=[
            pl.BlockSpec((pairs, parts, ROWS, LANES), lambda i: (0, 0, i, 0)),
            row_blocks((ROWS, width)),
            whole((8, width)),
        ],
        scratch_shapes=[pltpu.VMEM((width, weights[0].shape[1]), low_type)],
    )(rows_low, *weights)


def attention_kernel(len_ref, line_ref, qkv_ref, *refs):
    att_ref, prob_ref, inv_ref, tile_ref = refs[-4:]
    micro, slot = prob_ref.shape[1], prob_ref.shape[3]
    blocks = slot // LANES
    lanes = head_lanes()
    for h in range(2):
        for d in range(2 * blocks - 1):
            piece = jnp.broadcast_to(
                line_ref[0, h : h + 1, d * LANES : (d + 2) * LANES], (LANES, 2 * LANES)
            )
            turned = pltpu.roll(piece, LANES + 1, 1, stride=1, stride_axis=0)
            tile_ref[h, d] = turned[:, :LANES]

    def micro_step(m, carry):
        start = pl.multiple_of(m * slot, slot)
        key_valid = lax.broadcasted_iota(jnp.int32, (1, slot), 1) < len_ref[m]
        keys = qkv_ref[0, 1, pl.ds(start, slot), :]
        values = qkv_ref[0, 2, pl.ds(start, slot), :]
        values = jnp.concatenate([values, jnp.ones_like(values)], axis=1)
        for r in range(slot // ROWS):
            rows = pl.ds(start + r * ROWS, ROWS)
            queries = qkv_ref[0, 0, rows, :]
            queries = jnp.concatenate(
                [queries * lanes[h].astype(low_type) for h in range(2)], axis=0
            )
            first = r * (ROWS // LANES)
            bias = jnp.concatenate(
                [
                    jnp.concatenate(
                        [tile_ref[h, j - first - i + blocks - 1] for j in range(blocks)], axis=1
                    )
                    for h in range(2)
                    for i in range(ROWS // LANES)
                ],
                axis=0,
            )
            scores = dot_nt(queries, keys)
            scores = jnp.where(key_valid, scores + bias, masked_score)
            terms = jnp.exp(scores - jnp.max(scores, axis=1, keepdims=True)).astype(low_type)
            for h in range(2):
                prob_ref[0, m, h, r * ROWS : (r + 1) * ROWS, :] = terms[h * ROWS : (h + 1) * ROWS]
            mixed = dot_nn(terms, values)
            inverse = 1.0 / mixed[:, LANES:]
            mixed = mixed[:, :LANES] * inverse
            att_ref[rows, :] = jnp.where(lanes[0], mixed[:ROWS], mixed[ROWS:]).astype(low_type)
            inv_ref[rows, :] = jnp.where(lanes[0], inverse[:ROWS], inverse[ROWS:])
        return carry

    lax.fori_loop(0, micro, micro_step, 0)


def attention(lengths, lines, qkv, pair, slot, before=(), deps=()):
    pairs, parts, count, _ = qkv.shape
    micro = count // slot
    spans = 2 * (slot // LANES) - 1
    column = pl.BlockSpec((count, LANES), lambda i: (0, pair))
    return call(
        attention_kernel,
        "attention_forward",
        [
            shape_of((count, pairs * LANES), low_type),
            shape_of((pairs, micro, 2, slot, slot), low_type),
            shape_of((count, pairs * LANES), full_type),
        ],
        deps=deps,
        grid=(1,),
        in_specs=[
            on_scalars(),
            pl.BlockSpec((1, 2, lines.shape[2]), lambda i: (pair, 0, 0)),
            pl.BlockSpec((1, parts, count, LANES), lambda i: (pair, 0, 0, 0)),
            *[in_place()] * len(before),
        ],
        out_specs=[
            column,
            pl.BlockSpec((1, micro, 2, slot, slot), lambda i: (pair, 0, 0, 0, 0)),
            column,
        ],
        input_output_aliases={3 + i: i for i in range(len(before))},
        scratch_shapes=[pltpu.VMEM((2, spans, LANES, LANES), full_type)],
    )(lengths, lines, qkv, *before)


def branch_kernel(att_ref, *refs):
    *weight_refs, out_ref, w_ref = refs

    @pl.when(pl.program_id(0) == 0)
    def assemble():
        fill_rows(w_ref, weight_refs)

    out_ref[...] = dot_nt(att_ref[...], w_ref[...]).astype(low_type)


def branch_rows(attended, weights, deps=()):
    count, head_width = attended.shape
    width = sum(piece.shape[0] for piece in weights)
    return call(
        branch_kernel,
        "branch",
        shape_of((count, width), low_type),
        deps=deps,
        grid=(count // (2 * ROWS),),
        in_specs=[
            row_blocks((2 * ROWS, head_width)),
            *(pl.BlockSpec((piece.shape[0], head_width), lambda i: (0, 3)) for piece in weights),
        ],
        out_specs=row_blocks((2 * ROWS, width)),
        scratch_shapes=[pltpu.VMEM((width, head_width), low_type)],
    )(attended, *weights)


def hidden_kernel(pieces, len_ref, x_ref, own_ref, came_ref, vector_ref, *refs):
    weight_refs, refs = refs[:pieces], refs[pieces:]
    normed_ref, slope_ref, act_ref, sum_ref, w_ref = refs
    m = pl.program_id(0)
    slot = x_ref.shape[0]

    @pl.when(m == 0)
    def assemble():
        fill_rows(w_ref, weight_refs)

    middle = middle_rows(x_ref, own_ref, came_ref)
    normed = (middle * rms_scale(middle) * vector_ref[1:2]).astype(low_type)
    valid = lax.broadcasted_iota(jnp.int32, (slot, 1), 0) < len_ref[m]
    normed_ref[...] = jnp.where(valid, normed, jnp.zeros_like(normed))
    counted = lax.broadcasted_iota(jnp.int32, (16, slot), 1) < len_ref[m]
    counted = jnp.where(counted, 1.0, 0.0).astype(low_type)
    sum_ref[0] = jnp.sum(jnp.where(valid, middle, 0.0), axis=0, keepdims=True)
    block = 3 * LANES

    def columns_step(n, carry):
        columns = pl.ds(pl.multiple_of(n * block, block), block)
        v = dot_nn(normed, w_ref[:, columns])
        square = v * v
        gate = jnp.tanh(v * (gelu_slope + (gelu_slope * gelu_cubic) * square))
        half = 0.5 + 0.5 * gate
        active = (v * half).astype(low_type)
        act_ref[0, :, columns] = dot_nn(counted, active)[0:1]
        inner = 0.5 * gelu_slope + (1.5 * gelu_slope * gelu_cubic) * square
        slope_ref[:, columns] = (half + v * (1.0 - gate * gate) * inner).astype(low_type)
        return carry

    lax.fori_loop(0, w_ref.shape[1] // block, columns_step, 0)


def middle_rows(x_ref, own_ref, came_ref):
    branch = own_ref[...].astype(full_type) + came_ref[...].astype(full_type)
    return x_ref[...].astype(full_type) + branch


def hidden(lengths, rows_low, own, came, vectors, weights, slot):
    count, width = rows_low.shape
    micro = count // slot
    inner = weights[0].shape[1]
    return call(
        functools.partial(hidden_kernel, len(weights)),
        "hidden_forward",
        [
            shape_of((count, width), low_type),
            shape_of((count, inner), low_type),
            shape_of((micro, 1, inner), full_type),
            shape_of((micro, 1, width), full_type),
        ],
        cost=(1200, 20000),
        grid=(micro,),
        in_specs=[
            on_scalars(),
            *[row_blocks((slot, width))] * 3,
            whole(vectors.shape),
            *(whole(piece.shape) for piece in weights),
        ],
        out_specs=[
            row_blocks((slot, width)),
            row_blocks((slot, inner)),
            row_blocks((1, 1, inner)),
            row_blocks((1, 1, width)),
        ],
        scratch_shapes=[pltpu.VMEM((width, inner), low_type)],
    )(lengths, rows_low, own, came, vectors, *weights)


def few_rows(rows, count):
    place = lax.broadcasted_iota(jnp.int32, (count, rows[0].shape[1]), 0)
    total = jnp.zeros(place.shape, full_type)
    for i, row in enumerate(rows):
        total = jnp.where(place == i, row, total)
    return total


def pool_kernel(act_ref, *refs):
    *weight_refs, out_ref, w_ref = refs
    fill_rows(w_ref, weight_refs)
    sums = [act_ref[m] for m in range(act_ref.shape[0])]
    highs = [row.astype(low_type).astype(full_type) for row in sums]
    rests = [row - high for row, high in zip(sums, highs)]
    down = dot_nt(few_rows(highs + rests, 16).astype(low_type), w_ref[...])
    micro = len(sums)
    out_ref[...] = few_rows([down[m : m + 1] + down[micro + m : micro + m + 1] for m in range(micro)], 8)


def margin_kernel(len_ref, own_ref, other_ref, sum_ref, vector_ref, margin_ref, pooled_ref):
    margins, vectors_pooled = [], []
    for m in range(sum_ref.shape[0]):
        total = own_ref[m : m + 1] + other_ref[m : m + 1] + sum_ref[m]
        pooled = (total / len_ref[m].astype(full_type)).astype(low_type).astype(full_type)
        final = pooled * rms_scale(pooled) * vector_ref[2:3]
        logits = [
            jnp.sum(final * vector_ref[i : i + 1], axis=1, keepdims=True) * pooled.shape[1] ** (-0.5)
            for i in (3, 4)
        ]
        margins.append(jnp.broadcast_to(logits[0] - logits[1], (1, LANES)))
        vectors_pooled.append(pooled)
    margin_ref[...] = few_rows(margins, 8)
    pooled_ref[...] = few_rows(vectors_pooled, 8)


def rank_kernel(
    margin_pieces, down_pieces, up_pieces, len_ref, same_ref, positive_ref, pooled_ref,
    vector_ref, sum_ref, slope_ref, *refs
):
    margin_refs, refs = refs[:margin_pieces], refs[margin_pieces:]
    down_refs, refs = refs[:down_pieces], refs[down_pieces:]
    up_refs, refs = refs[:up_pieces], refs[up_pieces:]
    line_ref, act_ref, small_ref, d_ref, down_ref, up_ref = refs
    m = pl.program_id(0)

    @pl.when(m == 0)
    def rank():
        fill_rows(down_ref, down_refs)
        fill_rows(up_ref, up_refs)
        margins, same = stacked(margin_refs), same_ref[...] > 0.5
        row_max = jnp.max(jnp.where(same, margins, masked_score), axis=0)
        total = jnp.sum(jnp.where(same, jnp.exp(margins - row_max[None]), 0.0), axis=0)
        chance = jnp.exp(margins[0] - row_max) / total
        d_margins = LOSS_SCALE * (chance - positive_ref[...])
        tied_gap = vector_ref[3:4] - vector_ref[4:5]
        gain = vector_ref[2:3]
        lines, tied = [], 0.0
        for i in range(2):
            pooled = pooled_ref[i : i + 1]
            scale = rms_scale(pooled)
            d_logit = d_margins[i : i + 1, 0:1] * pooled.shape[1] ** (-0.5)
            d_final = d_logit * tied_gap
            tied = tied + pooled * scale * d_logit
            d_pooled = norm_input_grad(d_final, gain, pooled, scale)
            lines.append(d_pooled / len_ref[i].astype(full_type))
        line_ref[...] = few_rows(lines, 8)
        width, parts = tied.shape[1], sum_ref.shape[2] // tied.shape[1]
        rows = [line.astype(low_type).astype(full_type) for line in lines]
        for i in range(2):
            sums = sum_ref[i]
            rows += [sums[:, part * width : (part + 1) * width] for part in range(parts)]
        small_ref[...] = few_rows([*rows, tied], 8)
        d_act = dot_nn(few_rows(lines, 16).astype(low_type), down_ref[...])
        act_ref[...] = d_act[:8]

    d_row = jnp.where(m == 0, act_ref[0:1], act_ref[1:2])
    d_hidden = (slope_ref[...].astype(full_type) * d_row).astype(low_type)
    d_normed = dot_nt(d_hidden, up_ref[...])
    valid = lax.broadcasted_iota(jnp.int32, (d_normed.shape[0], 1), 0) < len_ref[m]
    d_ref[...] = jnp.where(valid, d_normed, 0.0).astype(low_type)


def rank_back(lengths, margins, same, positive, pooled, vectors, act_sum, slope, down, up, slot, deps):
    count, inner = slope.shape
    width = pooled.shape[1]
    return call(
        functools.partial(rank_kernel, len(margins), len(down), len(up)),
        "rank_backward",
        [
            shape_of((8, width), full_type),
            shape_of((8, inner), full_type),
            shape_of((8, width), full_type),
            shape_of((count, width), low_type),
        ],
        cost=(1200, 20000),
        deps=deps,
        grid=(count // slot,),
        in_specs=[
            on_scalars(),
            *(whole(array.shape) for array in (same, positive, pooled, vectors, act_sum)),
            row_blocks((slot, inner)),
            *(whole(piece.shape) for piece in (*margins, *down, *up)),
        ],
        out_specs=[
            whole((8, width)),
            whole((8, inner)),
            whole((8, width)),
            row_blocks((slot, width)),
        ],
        scratch_shapes=[pltpu.VMEM((width, inner), low_type), pltpu.VMEM((width, inner), low_type)],
    )(lengths, same, positive, pooled, vectors, act_sum, slope, *margins, *down, *up)


def up_grad_kernel(slot, normed_ref, slope_ref, act_ref, *refs):
    *out_refs, turned_ref = refs

    @pl.when(pl.program_id(0) == 0)
    def turn():
        turned_ref[...] = normed_ref[...].T

    total = 0.0
    for m in range(normed_ref.shape[0] // slot):
        rows = slice(m * slot, (m + 1) * slot)
        d_hidden = (slope_ref[rows].astype(full_type) * act_ref[m : m + 1]).astype(low_type)
        total = total + dot_nn(turned_ref[:, rows], d_hidden)
    spill_rows(total, out_refs)


def up_grad(normed, slope, d_act, rows, slot):
    count, width = normed.shape
    inner = slope.shape[1]
    block = 4 * LANES
    return call(
        functools.partial(up_grad_kernel, slot),
        "hidden_in_gradient",
        [shape_of((r, inner), low_type) for r in rows],
        cost=(1200, 15000),
        grid=(inner // block,),
        in_specs=[
            whole(normed.shape),
            column_blocks((count, block)),
            column_blocks((8, block)),
        ],
        out_specs=[column_blocks((r, block)) for r in rows],
        scratch_shapes=[pltpu.VMEM((width, count), low_type)],
    )(normed, slope, d_act)


def middle_kernel(
    pieces, len_ref, x_ref, branch_ref, other_ref, own_ref, came_ref, vector_ref, line_ref,
    att_ref, inv_ref, *refs
):
    weight_refs, refs = refs[:pieces], refs[pieces:]
    d_ref, d_att_ref, total_ref, w_ref = refs
    m = pl.program_id(0)

    @pl.when(m == 0)
    def assemble():
        fill_rows(w_ref, weight_refs)
        total_ref[...] = jnp.zeros_like(total_ref)

    middle = middle_rows(x_ref, branch_ref, other_ref)
    own = own_ref[...].astype(full_type)
    scale = rms_scale(middle)
    valid = lax.broadcasted_iota(jnp.int32, (middle.shape[0], 1), 0) < len_ref[m]
    line = jnp.where(m == 0, line_ref[0:1], line_ref[1:2])
    d_middle = jnp.where(valid, line, 0.0) + norm_input_grad(
        own + came_ref[...].astype(full_type), vector_ref[1:2], middle, scale
    )
    d_ref[...] = d_middle
    d_low = d_middle.astype(low_type)
    d_att_ref[...] = (dot_nn(d_low, w_ref[...]) * inv_ref[...]).astype(low_type)
    total_ref[...] += dot_tn(d_low, att_ref[...])


def middle_back(
    lengths, rows_low, branch, other, own, came, vectors, lines, attended, inverse, weights, slot
):
    count, width = rows_low.shape
    head_width = attended.shape[1]
    return call(
        functools.partial(middle_kernel, len(weights)),
        "middle_backward",
        [
            shape_of((count, width), full_type),
            shape_of((count, head_width), low_type),
            shape_of((width, head_width), full_type),
        ],
        cost=(600, 15000),
        grid=(count // slot,),
        in_specs=[
            on_scalars(),
            *[row_blocks((slot, width))] * 5,
            whole(vectors.shape),
            whole(lines.shape),
            row_blocks((slot, head_width)),
            row_blocks((slot, head_width)),
            *(
                pl.BlockSpec((piece.shape[0], head_width), lambda i: (0, 3)) for piece in weights
            ),
        ],
        out_specs=[
            row_blocks((slot, width)),
            row_blocks((slot, head_width)),
            whole((width, head_width)),
        ],
        scratch_shapes=[pltpu.VMEM((width, head_width), low_type)],
    )(
        lengths, rows_low, branch, other, own, came, vectors, lines, attended, inverse, *weights
    )


def attention_back_kernel(
    befores, grads, tables, own, prob_ref, qkv_ref, d_ref, att_ref, turned_ref, hot_ref, *refs
):
    table_refs, refs = refs[:tables], refs[tables:]
    grad_refs, refs = refs[:grads], refs[grads:]
    d_out_ref, table_ref, *out_refs, tile_ref, dk_ref, dv_ref = refs[befores:]
    step = pl.program_id(0)

    if grads:

        @pl.when(step > 0)
        def projection():
            spill_rows(grad_refs[0][...], out_refs)

    @pl.when(step == 0)
    def heads():
        pair_back(
            prob_ref, qkv_ref, d_ref, att_ref, turned_ref, hot_ref, d_out_ref, table_ref, out_refs,
            tile_ref, dk_ref, dv_ref
        )
        if tables:
            lines = [ref[0, h : h + 1] for ref in (*table_refs, table_ref) for h in range(2)]
            width = turned_ref.shape[0]
            place = lax.broadcasted_iota(jnp.int32, (width, 16), 0) % own
            pick = place == lax.broadcasted_iota(jnp.int32, (width, 16), 1)
            pick = jnp.where(pick, 1.0, 0.0).astype(low_type)
            spread = dot_nn(pick, few_rows(lines, 16).astype(low_type))
            spill_rows(spread, [ref.at[:, 3 * LANES :] for ref in out_refs])


def pair_back(
    prob_ref, qkv_ref, d_ref, att_ref, turned_ref, hot_ref, d_out_ref, table_ref, out_refs,
    tile_ref, dk_ref, dv_ref
):
    micro, slot = prob_ref.shape[1], prob_ref.shape[3]
    blocks = slot // LANES
    spans = 2 * blocks - 1
    lanes = head_lanes()

    tile_ref[...] = jnp.zeros_like(tile_ref)

    def micro_step(m, carry):
        start = pl.multiple_of(m * slot, slot)
        everything = pl.ds(start, slot)
        keys, values = qkv_ref[0, 1, everything, :], qkv_ref[0, 2, everything, :]
        for r in range(slot // ROWS):
            rows = pl.ds(start + r * ROWS, ROWS)
            queries = qkv_ref[0, 0, rows, :]
            queries = jnp.concatenate(
                [queries * lanes[h].astype(low_type) for h in range(2)], axis=0
            )
            d_att = d_ref[rows, :]
            product = d_att.astype(full_type) * att_ref[rows, :].astype(full_type)
            row_dot = jnp.concatenate(
                [
                    jnp.sum(jnp.where(lanes[h], product, 0.0), axis=1, keepdims=True)
                    for h in range(2)
                ],
                axis=0,
            )
            d_att = jnp.concatenate([d_att * lanes[h].astype(low_type) for h in range(2)], axis=0)
            span = slice(r * ROWS, (r + 1) * ROWS)
            probs = jnp.concatenate([prob_ref[0, m, h, span, :] for h in range(2)], axis=0)
            d_scores = probs.astype(full_type) * (dot_nt(d_att, values) - row_dot)
            d_low = d_scores.astype(low_type)
            for h in range(2):
                for i in range(ROWS // LANES):
                    for j in range(blocks):
                        top = h * ROWS + i * LANES
                        tile_ref[h, j - r * (ROWS // LANES) - i + blocks - 1] += d_scores[
                            top : top + LANES, j * LANES : (j + 1) * LANES
                        ]
            d_queries = dot_nn(d_low, keys)
            d_out_ref[0, 0, rows, :] = jnp.where(
                lanes[0], d_queries[:ROWS], d_queries[ROWS:]
            ).astype(low_type)
            d_keys, d_values = dot_tn(d_low, queries), dot_tn(probs, d_att)
            dk_ref[...] = d_keys if r == 0 else dk_ref[...] + d_keys
            dv_ref[...] = d_values if r == 0 else dv_ref[...] + d_values
        d_out_ref[0, 1, everything, :] = dk_ref[...].astype(low_type)
        d_out_ref[0, 2, everything, :] = dv_ref[...].astype(low_type)
        return carry

    lax.fori_loop(0, micro, micro_step, 0)
    d_project = jnp.concatenate([d_out_ref[0, c] for c in range(3)], axis=1)
    spill_rows(dot_nn(turned_ref[...], d_project), [ref.at[:, : 3 * LANES] for ref in out_refs])
    flip = (
        lax.broadcasted_iota(jnp.int32, (LANES, LANES), 0)
        + lax.broadcasted_iota(jnp.int32, (LANES, LANES), 1)
        == LANES - 1
    )
    flip = jnp.where(flip, 1.0, 0.0).astype(low_type)
    table = jnp.zeros((16, LANES), full_type)
    for d in range(spans):
        highs, rests = [], []
        for h in range(2):
            tile = tile_ref[h, d]
            high = tile.astype(low_type)
            rest = (tile - high.astype(full_type)).astype(low_type)
            flipped = dot_nn(flip, high) + dot_nn(flip, rest)
            wide = jnp.concatenate([flipped, jnp.zeros_like(flipped)], axis=1)
            turned = pltpu.roll(wide, 0, 1, stride=1, stride_axis=0)
            line = jnp.sum(turned, axis=0, keepdims=True)
            highs.append(line.astype(low_type).astype(full_type))
            rests.append(line - highs[-1])
        table = table + dot_nn(few_rows(highs + rests, 16).astype(low_type), hot_ref[d])
    table_ref[0] = few_rows([table[h : h + 1] + table[2 + h : 3 + h] for h in range(2)], 8)


def attention_back(
    probs, qkv, d_attended, attended, turned, hot, rows, pair, slot, own,
    grad_out=None, tables=(), before=(), deps=()
):
    width, count = turned.shape
    micro = count // slot
    pairs = qkv.shape[0]
    spans = 2 * (slot // LANES) - 1
    lead = lambda shape: pl.BlockSpec(shape, lambda i: (pair,) + (0,) * (len(shape) - 1))
    column = pl.BlockSpec((count, LANES), lambda i: (0, pair))
    if tables:
        steps, extra, extra_specs = 1, tables, [whole(table.shape) for table in tables]
        gradients = [shape_of((r, 4 * LANES), low_type) for r in rows]
        gradient_specs = [whole((r, 4 * LANES)) for r in rows]
    else:
        steps = 1 if grad_out is None else 2
        extra = () if grad_out is None else (grad_out,)
        extra_specs = [whole(array.shape) for array in extra]
        gradients = [shape_of((r, pairs * 3 * LANES), low_type) for r in rows]
        gradient_specs = [pl.BlockSpec((r, 3 * LANES), lambda i: (0, i + pair)) for r in rows]
    first = 6 + len(extra)
    return call(
        functools.partial(
            attention_back_kernel, len(before), 0 if grad_out is None else 1, len(tables), own
        ),
        "attention_backward",
        [
            shape_of((pairs, 3, count, LANES), low_type),
            shape_of((1, 8, LANES), full_type),
            *gradients,
        ],
        deps=deps,
        grid=(steps,),
        in_specs=[
            lead((1, micro, 2, slot, slot)),
            lead((1, 3, count, LANES)),
            column,
            column,
            whole(turned.shape),
            whole(hot.shape),
            *extra_specs,
            *[in_place()] * len(before),
        ],
        out_specs=[lead((1, 3, count, LANES)), whole((1, 8, LANES)), *gradient_specs],
        input_output_aliases={first + i: i if i == 0 else i + 1 for i in range(len(before))},
        scratch_shapes=[
            pltpu.VMEM((2, spans, LANES, LANES), full_type),
            pltpu.VMEM((slot, LANES), full_type),
            pltpu.VMEM((slot, LANES), full_type),
        ],
    )(probs, qkv, d_attended, attended, turned, hot, *extra, *before)


def normed_back_kernel(d_ref, *refs):
    *weight_refs, out_ref, w_ref = refs
    pairs, parts = d_ref.shape[0], d_ref.shape[1]

    @pl.when(pl.program_id(0) == 0)
    def assemble():
        fill_rows(w_ref, weight_refs, slice(0, w_ref.shape[1]))

    blocks = [d_ref[p, c] for c in range(parts) for p in range(pairs)]
    d_normed = dot_nt(jnp.concatenate(blocks, axis=1), w_ref[...])
    out_ref[...] = d_normed.astype(low_type)


def normed_back(d_project, weights, deps):
    pairs, parts, count, _ = d_project.shape
    width = sum(piece.shape[0] for piece in weights)
    return call(
        normed_back_kernel,
        "normed_backward",
        shape_of((count, width), low_type),
        cost=(900, 15000),
        deps=deps,
        grid=(count // ROWS,),
        in_specs=[
            pl.BlockSpec((pairs, parts, ROWS, LANES), lambda i: (0, 0, i, 0)),
            *(whole(piece.shape) for piece in weights),
        ],
        out_specs=row_blocks((ROWS, width)),
        scratch_shapes=[pltpu.VMEM((width, pairs * parts * LANES), low_type)],
    )(d_project, *weights)


def token_kernel(d_ref, own_ref, came_ref, x_ref, vector_ref, order_ref, out_ref):
    x = x_ref[...].astype(full_type)
    d_normed = own_ref[...].astype(full_type) + came_ref[...].astype(full_type)
    grad = d_ref[...] + norm_input_grad(d_normed, vector_ref[0:1], x, rms_scale(x))
    high = grad.astype(low_type)
    rest = (grad - high.astype(full_type)).astype(low_type)
    order = order_ref[...]
    out_ref[...] = dot_nt(high, order) + dot_nt(rest, order)


def token_back(d_middle, own, came, rows_low, vectors, order, deps):
    count, width = rows_low.shape
    return call(
        token_kernel,
        "token_gradient",
        shape_of((count, width), full_type),
        cost=(1200, 15000),
        deps=deps,
        grid=(count // ROWS,),
        in_specs=[row_blocks((ROWS, width))] * 4 + [whole(vectors.shape), whole(order.shape)],
        out_specs=row_blocks((ROWS, width)),
    )(d_middle, own, came, rows_low, vectors, order)


def total_kernel(smalls, counts, micro, pairs, *refs):
    small_refs, refs = refs[:smalls], refs[smalls:]
    groups = []
    for count in counts:
        groups.append(refs[:count])
        refs = refs[count:]
    in_ref, up_ref, gain_ref, tied_ref, down_ref, line_ref, *out_refs = refs
    size, width = sum(ref.shape[0] for ref in small_refs), small_refs[0].shape[2]
    row_of = lambda row: jnp.concatenate([ref[:, row, :] for ref in small_refs], axis=0)
    own = down_ref.shape[0]
    inverse = 1.0 / LOSS_SCALE
    add_up = lambda values: jnp.sum(values, axis=0, keepdims=True).sum(axis=1, keepdims=True)
    squares, sums = 0.0, []
    for group, out_ref in zip(groups, out_refs):
        total = sum(ref[...].astype(full_type) for ref in group) * inverse
        total, rest = total[:, : out_ref.shape[1]], total[:, out_ref.shape[1] :]
        out_ref[...] = total
        sums.append((total, rest))
        squares = squares + add_up(total * total)
    table = sums[1][1]

    block = lax.broadcasted_iota(jnp.int32, (size, width), 1) // own
    mine = block == lax.broadcasted_iota(jnp.int32, (size, width), 0)
    fold = lax.broadcasted_iota(jnp.int32, (width, LANES), 0) % own == lax.broadcasted_iota(
        jnp.int32, (width, LANES), 1
    )
    fold = jnp.where(fold, 1.0, 0.0).astype(low_type)
    pick = lambda row: jnp.where(mine, row_of(row), 0.0)
    down = 0.0
    parts = down_ref.shape[1] // width
    for m in range(micro):
        lines = dot_nn(pick(m).astype(low_type), fold).astype(low_type)
        acts = [row_of(micro + m * parts + i) for i in range(parts)]
        acts = jnp.concatenate(acts, axis=1)
        high = acts.astype(low_type)
        rest = (acts - high.astype(full_type)).astype(low_type)
        down = down + dot_tn(lines, high) + dot_tn(lines, rest)
    down = down[:own] * inverse
    down_ref[...] = down
    squares = squares + add_up(down * down)

    rest = jnp.sum(pick(micro + micro * parts), axis=0, keepdims=True) * inverse
    rest = jnp.broadcast_to(rest, (16, width))
    ranked = 0.0
    for _ in range(3):
        high = rest.astype(low_type)
        ranked = ranked + dot_nn(high, fold)
        rest = rest - high.astype(full_type)
    ranked = ranked[0:1, :own]
    rounded = lambda ref, i: ref[i : i + 1].astype(low_type).astype(full_type)
    tied_gap = rounded(tied_ref, 0) - rounded(tied_ref, 1)

    def through(products):
        ones = jnp.ones((16, products.shape[1]), low_type)
        high = products.astype(low_type)
        rest = (products - high.astype(full_type)).astype(low_type)
        return (dot_nt(ones, high) + dot_nt(ones, rest))[0:1]

    weighed = lambda ref, total: ref.astype(low_type).astype(full_type) * total
    first = 0.0
    for p in range(pairs):
        source = sums[0][0] if p < pairs - 1 else sums[1][0]
        offset = p * 3 * LANES if p < pairs - 1 else 0
        for c in range(3):
            columns = slice(offset + c * LANES, offset + (c + 1) * LANES)
            first = first + weighed(in_ref[c, :, p * LANES : (p + 1) * LANES], source[:, columns])
    rows = [
        through(first) / rounded(gain_ref, 0),
        through(weighed(up_ref[...], sums[2][0])) / rounded(gain_ref, 1),
        tied_gap * ranked,
        rounded(gain_ref, 2) * ranked,
    ]
    place = lax.broadcasted_iota(jnp.int32, (8, own), 0)
    extra = jnp.zeros((8, own), full_type)
    for i, row in enumerate(rows):
        extra = jnp.where(place == i, row, extra)
    line_ref[...] = jnp.zeros_like(line_ref)
    line_ref[:8, :own] = extra
    line_ref[8:16] = jnp.broadcast_to(squares, (8, LANES))
    line_ref[16 : 16 + 2 * pairs] = table[: 2 * pairs]


def totals(small_all, grads, heads_in, hidden_in, gains, tied_rows, widths, micro, deps):
    counts = tuple(len(group) for group in grads)
    flat = [array for group in grads for array in group]
    own, inner = hidden_in.shape
    down, line, *sums = call(
        functools.partial(
            total_kernel, len(small_all), counts, micro, heads_in.shape[2] // LANES
        ),
        "gradient_totals",
        [
            shape_of((own, inner), full_type),
            shape_of((24, LANES), full_type),
            *(shape_of((own, width), full_type) for width in widths),
        ],
        cost=(100, 10000),
        deps=deps,
    )(*small_all, *flat, heads_in, hidden_in, gains, tied_rows)
    return down, line, sums


def adam(weight, first_old, second, grad, factor, rate, decay, step_ref):
    clipped = grad * factor
    next_first = beta_first * first_old + (1.0 - beta_first) * clipped
    next_second = beta_second * second + (1.0 - beta_second) * clipped * clipped
    first_hat = next_first * step_ref[0]
    second_hat = next_second * step_ref[1]
    next_weight = weight - rate * (first_hat / (jnp.sqrt(second_hat) + adam_eps) + decay * weight)
    return next_weight, next_first, next_second


def square_kernel(heads, own_ref, other_ref, out_ref, extra_ref):
    place = lax.broadcasted_iota(jnp.int32, (8, LANES), 0)
    extra = own_ref[:8] + jnp.where(place < 2, other_ref[:8], 0.0)
    extra_ref[...] = extra
    counted = jnp.where(place == 3, 2.0, 1.0) * extra * extra
    add_up = lambda values: jnp.sum(values, axis=0, keepdims=True).sum(axis=1, keepdims=True)
    squares = own_ref[8:16] + other_ref[8:16] + add_up(counted)
    out_ref[:8] = squares
    tables = own_ref[16:24] * own_ref[16:24] + other_ref[16:24] * other_ref[16:24]
    out_ref[8:16] = own_ref[16:24]
    out_ref[16:24] = jnp.broadcast_to(add_up(tables), (8, LANES))


def update_kernel(squares, groups, pick_ref, step_ref, extra_ref, *refs):
    square_refs, refs = refs[:squares], refs[squares:]
    grad_refs, refs = refs[:groups], refs[groups:]
    state_refs, refs = refs[:21], refs[21:]
    norm_ref, *out_refs = refs
    tiles = stacked(square_refs)
    device = lax.broadcasted_iota(jnp.int32, (tiles.shape[0], 1, 1), 0)
    tables = jnp.sum(jnp.where(device == pick_ref[0], tiles[:, 8:24], 0.0), axis=0)
    norm = jnp.sqrt(jnp.sum(tiles[:, 0:8], axis=0)[0:1, 0:1] + tables[8:9, 0:1])
    norm_ref[...] = norm
    factor = jnp.minimum(1.0, clip_limit / (norm + 1e-06))
    weights, firsts, seconds = state_refs[:7], state_refs[7:14], state_refs[14:]
    next_weights, next_firsts, next_seconds = out_refs[:7], out_refs[7:14], out_refs[14:]

    def step(index, where, grad, rate, decay):
        results = adam(
            weights[index][where], firsts[index][where], seconds[index][where], grad, factor,
            rate, decay, step_ref,
        )
        for target, result in zip((next_weights, next_firsts, next_seconds), results):
            target[index][where] = result

    everything = (slice(None), slice(None))
    early_ref, late_ref, up_ref, down_ref = grad_refs
    part = pl.program_id(0)
    pairs = weights[0].shape[2] // LANES
    for p in range(pairs):
        source, offset = (early_ref, p * 3) if p < pairs - 1 else (late_ref, 0)
        columns = pl.ds(pl.multiple_of((offset + part) * LANES, LANES), LANES)
        where = (0, slice(None), slice(p * LANES, (p + 1) * LANES))
        step(0, where, source[:, columns], rate_matrix, decay_matrix)
    columns = pl.ds(pl.multiple_of(((pairs - 1) * 3 + part) * LANES, LANES), LANES)
    step(1, everything, early_ref[:, columns], rate_matrix, decay_matrix)
    step(2, everything, up_ref[...], rate_matrix, decay_matrix)
    step(3, everything, down_ref[...], rate_matrix, decay_matrix)

    @pl.when(part == 0)
    def small():
        rows = weights[4].shape[1]
        extra = extra_ref[...]
        step(4, everything, extra[0:3, :rows], rate_vector, 0.0)
        tied = extra[3:4, :rows]
        step(5, everything, jnp.concatenate([tied, -tied], axis=0), rate_vector, 0.0)
        step(6, everything, tables[: 2 * pairs, :BUCKETS], rate_vector, 0.0)


def update(pick, corrections, extra, squares, grads, states):
    parts = states[0].shape[0]
    thirds = lambda array: column_blocks((array.shape[0], array.shape[1] // parts))
    state_specs = []
    for _ in range(3):
        one = states[len(state_specs) : len(state_specs) + 7]
        state_specs += [pl.BlockSpec((1, *one[0].shape[1:]), lambda i: (i, 0, 0))]
        state_specs += [thirds(array) for array in one[1:4]]
        state_specs += [whole(array.shape) for array in one[4:]]
    return call(
        functools.partial(update_kernel, len(squares), len(grads)),
        "update",
        [shape_of((1, 1), full_type)] + [shape_of(s.shape, full_type) for s in states],
        cost=(0, 6000),
        grid=(parts,),
        in_specs=[
            on_scalars(),
            on_scalars(),
            whole(extra.shape),
            *(whole(array.shape) for array in squares),
            *(whole(array.shape) for array in grads[:2]),
            *(thirds(array) for array in grads[2:]),
            *state_specs,
        ],
        out_specs=[whole((1, 1)), *state_specs],
    )(pick, corrections, extra, *squares, *grads, *states)


def body(
    tokens,
    pair_lengths,
    query_ids,
    distance_bucket,
    step_count,
    heads_in,
    heads_out,
    hidden_in,
    hidden_out,
    gains,
    tied_rows,
    bias_table,
    first_heads_in,
    first_heads_out,
    first_hidden_in,
    first_hidden_out,
    first_gains,
    first_tied,
    first_table,
    second_heads_in,
    second_heads_out,
    second_hidden_in,
    second_hidden_out,
    second_gains,
    second_tied,
    second_table,
):
    size = lax.axis_size("dp")
    me = lax.axis_index("dp")
    core = lax.axis_index("mp")
    micro, _, slot, width = tokens.shape
    count = micro * slot
    own, local_heads = heads_in.shape[0], bias_table.shape[1]
    head_width = heads_in.shape[2]
    inner = hidden_in.shape[1]
    pairs = local_heads // 2
    spans = 2 * (slot // LANES) - 1
    turn_matrix = lambda array: jnp.transpose(array, (1, 0, 2))
    heads_in, first_heads_in, second_heads_in = (
        turn_matrix(array) for array in (heads_in, first_heads_in, second_heads_in)
    )
    gains, tied_rows, bias_table = gains.T, tied_rows.T, bias_table.T
    first_gains, first_tied, first_table = first_gains.T, first_tied.T, first_table.T
    second_gains, second_tied, second_table = second_gains.T, second_tied.T, second_table.T

    packed_heads = call(
        pack_heads_kernel, "pack_heads", shape_of((own, 4 * head_width + LANES), low_type)
    )(heads_in, heads_out, gains, tied_rows)
    packed_up, packed_down = call(
        pack_hidden_kernel, "pack_hidden", [shape_of((own, inner), low_type)] * 2
    )(hidden_in, hidden_out)
    pair_ids = jnp.bitwise_xor(me, jnp.array(block_masks(size), jnp.int32))
    place = (pair_ids[:, None] * own + jnp.arange(own, dtype=jnp.int32)[None, :]).reshape(width)
    order = (jnp.arange(width, dtype=jnp.int32)[:, None] == place[None, :]).astype(low_type)
    lengths = pair_lengths.reshape(micro)
    queries = query_ids[:, pair_ids]
    same_query = queries == queries[:, :1]
    earlier = jnp.any(same_query & (pair_ids < me)[None, :], axis=1)
    to_tile = lambda rows_m: jnp.broadcast_to(
        jnp.concatenate(
            [rows_m, jnp.zeros(rows_m.shape[:-1] + (8 - micro,), full_type)], axis=-1
        )[..., None],
        rows_m.shape[:-1] + (8, LANES),
    )
    same_tile = to_tile(same_query.astype(full_type).T)
    positive_tile = to_tile(jnp.where(earlier, 0.0, 1.0))

    bucket_line = jnp.concatenate([distance_bucket, jnp.full((1,), -1, jnp.int32)])
    bucket_hot = (
        bucket_line[:, None] == jnp.arange(LANES, dtype=jnp.int32)[None, :]
    ).astype(low_type)
    lines = dot_nt(bias_table.astype(low_type), bucket_hot[:, :BUCKETS])
    lines = lines.reshape(pairs, 2, 2 * slot)
    hot_spans = jnp.stack([bucket_hot[d * LANES : (d + 2) * LANES] for d in range(spans)])

    rows_low = call(
        order_kernel,
        "order_tokens",
        shape_of((count, width), low_type),
        cost=(600, 5000),
        grid=(count // ROWS,),
        in_specs=[row_blocks((ROWS, width)), whole((width, width))],
        out_specs=row_blocks((ROWS, width)),
    )(tokens.reshape(count, width), order)
    if size != 16:
        weight_heads, weight_up, weight_down = (
            [gather_doubling(part, size)] for part in (packed_heads, packed_up, packed_down)
        )
        qkv, normed_first, vectors = project(rows_low, weight_heads, pairs, ())
    else:
        heads_line, packed_up = join(line_parts(packed_heads, size, "heads"), passing=(packed_up,))
        heads_sides = side_parts(heads_line, size, "heads")
        up_line_parts = line_parts(packed_up, size, "up")
        low, high = gather_step(*heads_sides, [], deps=(rows_low, *up_line_parts[1:]))
        heads_corner = corner_parts(low, high, size, "heads_corner")
        up_line, packed_down = join(up_line_parts, deps=heads_corner, passing=(packed_down,))
        up_sides = side_parts(up_line, size, "up")
        down_parts = line_parts(packed_down, size, "down")
        weight_heads = [heads_line, *heads_sides, *heads_corner]
        qkv, normed_first, vectors = project(
            rows_low, weight_heads, pairs, (same_tile, positive_tile)
        )
    filled = ()
    for pair in range(pairs):
        filled = attention(lengths, lines, qkv, pair, slot, before=filled)
        if pair == 0 and size == 16:
            low, high, down_line = gather_step(*up_sides, down_parts, deps=(filled[0],))
            up_corner = corner_parts(low, high, size, "up_corner")
            down_sides = side_parts(down_line, size, "down")
            weight_up = [up_line, *up_sides, *up_corner]
    turned_first = call(turn_kernel, "turn", shape_of((width, count), low_type))(normed_first)
    attended, probs, inverse = filled
    branch = branch_rows(
        attended, weight_heads, (*down_sides, *up_corner, turned_first) if size == 16 else ()
    )
    if size == 16:
        low, high = gather_step(*down_sides, [], deps=(branch,))
        down_corner = corner_parts(low, high, size, "down_corner")
        weight_down = [down_line, *down_sides, *down_corner]
    branch_came = other_core(branch, "branch_other_core")
    normed_second, slope, act_sum, middle_sum = hidden(
        lengths, rows_low, branch, branch_came, vectors, weight_up, slot
    )
    down = call(
        pool_kernel,
        "pool",
        shape_of((8, width), full_type),
        cost=(20, 5000),
        scratch_shapes=[pltpu.VMEM((width, inner), low_type)],
    )(act_sum, *weight_down)
    margin_tile, pooled = call(
        margin_kernel,
        "margin",
        [shape_of((8, LANES), full_type), shape_of((8, width), full_type)],
        grid=(1,),
        in_specs=[on_scalars(), *[whole(down.shape)] * 2, whole(middle_sum.shape), whole(vectors.shape)],
    )(lengths, down, other_core(down, "pooled_part_other_core"), middle_sum, vectors)
    margins = gather_small(margin_tile, size, "margins")

    d_line, d_act, small, d_normed_second = rank_back(
        lengths, margins, same_tile, positive_tile, pooled, vectors, act_sum,
        slope, weight_down, weight_up, slot, (turned_first,),
    )
    d_normed_second_came = other_core(d_normed_second, "second_gradient_other_core")
    up_sum = Scatter(
        up_grad(normed_second, slope, d_act, piece_rows(size, width), slot), size, "up_gradient"
    )
    d_middle, d_attended, g_out = middle_back(
        lengths, rows_low, branch, branch_came, d_normed_second, d_normed_second_came, vectors,
        d_line, attended, inverse, weight_heads, slot,
    )
    up_sum.sides(deps=(d_attended,))
    filled, tables = (), []
    for pair in range(pairs - 1):
        d_project, table, *g_early = attention_back(
            probs, qkv, d_attended, attended, turned_first, hot_spans, piece_rows(size, width),
            pair, slot, own, grad_out=g_out if pair == pairs - 2 else None, before=filled,
        )
        filled = (d_project, *g_early)
        tables.append(table)
    up_parts, _ = up_sum.line(deps=(d_project,))
    early_sum = Scatter(g_early, size, "early_gradient")
    d_project, table, *g_late = attention_back(
        probs, qkv, d_attended, attended, turned_first, hot_spans, piece_rows(size, width),
        pairs - 1, slot, own, tables=tuple(tables), before=(d_project,), deps=(up_parts[0],),
    )
    late_sum = Scatter(g_late, size, "late_gradient")
    early_sum.sides(deps=(table,))
    d_normed_first = normed_back(d_project, weight_heads, (*early_sum.sources, *up_parts[1:]))
    d_normed_first, small = late_sum.sides(passing=(d_normed_first, small))
    small = small_line(small, size, "small_sums")
    early_parts, _ = early_sum.line(deps=late_sum.sources)
    token_gradient = token_back(
        d_middle, d_normed_first, other_core(d_normed_first, "first_gradient_other_core"), rows_low,
        vectors, order, (early_parts[0],),
    )
    late_parts, (small,) = late_sum.line(deps=(token_gradient,), passing=(small,))
    small_all = small_plane(small, size, "small_sums")

    g_down, line, grad_sums = totals(
        small_all, [early_parts, late_parts, up_parts], heads_in, hidden_in, gains, tied_rows,
        (head_width * 3, 3 * LANES, inner), micro, (),
    )
    square_tile, extra = call(
        functools.partial(square_kernel, local_heads),
        "squares",
        [shape_of((24, LANES), full_type), shape_of((8, LANES), full_type)],
    )(line, other_core(line, "totals_other_core"))
    squares_all = gather_small(square_tile, size, "squares")
    step_float = step_count.astype(full_type)
    corrections = jnp.stack(
        [1.0 / (1.0 - beta_first**step_float), 1.0 / (1.0 - beta_second**step_float)]
    )
    grads = [*grad_sums, g_down]
    weights = (heads_in, heads_out, hidden_in, hidden_out, gains, tied_rows, bias_table)
    firsts = (
        first_heads_in,
        first_heads_out,
        first_hidden_in,
        first_hidden_out,
        first_gains,
        first_tied,
        first_table,
    )
    seconds = (
        second_heads_in,
        second_heads_out,
        second_hidden_in,
        second_hidden_out,
        second_gains,
        second_tied,
        second_table,
    )
    states = (*weights, *firsts, *seconds)
    first_place = jnp.sum(jnp.where(pair_ids == 0, jnp.arange(size, dtype=jnp.int32), 0)).reshape(1)
    norm, *results = update(first_place, corrections, extra, squares_all, grads, states)
    for index in (0, 7, 14):
        results[index] = turn_matrix(results[index])
        for other in (4, 5, 6):
            results[index + other] = results[index + other].T
    return (norm.reshape(()), token_gradient.reshape(tokens.shape), *results)


def solution(mesh):
    in_specs = (
        P(None, "dp", None, None),
        P(None, "dp"),
        P(),
        P(),
        P(),
        P("dp", None, "mp"),
        P("dp", "mp"),
        P("dp", "mp"),
        P("dp", "mp"),
        P("dp", None),
        P("dp", None),
        P(None, "mp"),
        P("dp", None, "mp"),
        P("dp", "mp"),
        P("dp", "mp"),
        P("dp", "mp"),
        P("dp", None),
        P("dp", None),
        P(None, "mp"),
        P("dp", None, "mp"),
        P("dp", "mp"),
        P("dp", "mp"),
        P("dp", "mp"),
        P("dp", None),
        P("dp", None),
        P(None, "mp"),
    )
    out_specs = (
        P(),
        P(None, "dp", None, None),
        P("dp", None, "mp"),
        P("dp", "mp"),
        P("dp", "mp"),
        P("dp", "mp"),
        P("dp", None),
        P("dp", None),
        P(None, "mp"),
        P("dp", None, "mp"),
        P("dp", "mp"),
        P("dp", "mp"),
        P("dp", "mp"),
        P("dp", None),
        P("dp", None),
        P(None, "mp"),
        P("dp", None, "mp"),
        P("dp", "mp"),
        P("dp", "mp"),
        P("dp", "mp"),
        P("dp", None),
        P("dp", None),
        P(None, "mp"),
    )
    return jax.shard_map(body, mesh=mesh, in_specs=in_specs, out_specs=out_specs, check_vma=False)
```

```python
import functools

import jax
import jax.numpy as jnp
from jax import lax
from jax.experimental import pallas as pl
from jax.experimental.pallas import tpu as pltpu
from jax.sharding import PartitionSpec as P

BUCKETS = 32
LOSS_SCALE = 1024
LANES = 128
ROWS = 256

norm_eps = 1e-06
clip_limit = 0.01
beta_first = 0.9
beta_second = 0.999
adam_eps = 1e-08
rate_matrix = 0.03
rate_vector = 0.25
decay_matrix = 0.1
masked_score = -1e30
gelu_slope = 0.7978845608028654
gelu_cubic = 0.044715
low_type = jnp.bfloat16
full_type = jnp.float32
core_swap = [(0, 1), (1, 0)]


def rms_scale(rows_in):
    return lax.rsqrt(jnp.mean(rows_in * rows_in, axis=-1, keepdims=True) + norm_eps)


def norm_input_grad(d_normed, gain_row, rows_in, norm_scale):
    weighted = d_normed * gain_row
    return norm_scale * weighted - rows_in * norm_scale**3 * jnp.mean(
        weighted * rows_in, axis=-1, keepdims=True
    )


def dot_nt(left, right):
    return lax.dot_general(left, right, (((1,), (1,)), ((), ())), preferred_element_type=full_type)


def dot_tn(left, right):
    return lax.dot_general(left, right, (((0,), (0,)), ((), ())), preferred_element_type=full_type)


def dot_nn(left, right):
    return lax.dot_general(left, right, (((1,), (0,)), ((), ())), preferred_element_type=full_type)


def call(
    kernel, name, out_shape, cost=(0, 0), vmem=16, deps=(), passing=(), in_specs=None,
    out_specs=None, input_output_aliases=None, **options
):
    single = not isinstance(out_shape, (list, tuple))
    out_shapes = [out_shape] if single else list(out_shape)
    outputs, extra = len(out_shapes), len(deps) + len(passing)

    def apply(*operands):
        inputs = len(operands)
        if in_specs is None:
            options["grid"] = (1,)
        specs = [whole(operand.shape) for operand in operands] if in_specs is None else in_specs
        targets = out_specs or [whole(shape.shape) for shape in out_shapes]
        targets = targets if isinstance(targets, (list, tuple)) else [targets]
        aliases = dict(input_output_aliases or {})
        for i in range(len(passing)):
            aliases[inputs + len(deps) + i] = outputs + i

        def run(*refs):
            own = inputs + extra
            kernel(*refs[:inputs], *refs[own : own + outputs], *refs[own + outputs + len(passing) :])

        results = pl.pallas_call(
            run,
            out_shape=[*out_shapes, *(shape_of(a.shape, a.dtype) for a in passing)],
            in_specs=[*specs, *[in_place()] * extra],
            out_specs=[*targets, *[in_place()] * len(passing)],
            input_output_aliases=aliases,
            compiler_params=pltpu.CompilerParams(vmem_limit_bytes=vmem * 1024 * 1024),
            cost_estimate=pl.CostEstimate(
                flops=int(cost[0] * 2e6), bytes_accessed=int(cost[1] * 1e3), transcendentals=0
            ),
            name=name,
            **options,
        )(*operands, *deps, *passing)
        return results[0] if single and not passing else results

    return apply


def in_place():
    return pl.BlockSpec(memory_space=pl.ANY)


def shape_of(shape, dtype):
    return jax.ShapeDtypeStruct(tuple(shape), dtype)


def whole(shape):
    return pl.BlockSpec(tuple(shape), lambda *_: (0,) * len(shape))


def on_scalars():
    return pl.BlockSpec(memory_space=pltpu.SMEM)


def row_blocks(shape, step=0):
    return pl.BlockSpec(tuple(shape), lambda i: (i,) + (0,) * (len(shape) - 1))


def column_blocks(shape, offset=0):
    return pl.BlockSpec(tuple(shape), lambda i: (0,) * (len(shape) - 1) + (i + offset,))


def fill_rows(target, pieces, columns=slice(None)):
    start = 0
    for piece in pieces:
        rows = piece.shape[0]
        target[start : start + rows, :] = piece[:, columns]
        start += rows


def spill_rows(value, pieces):
    start = 0
    for piece in pieces:
        rows = piece.shape[0]
        piece[...] = value[start : start + rows].astype(piece.dtype)
        start += rows


def swap(array, mask, size, label="exchange"):
    with jax.named_scope(f"{label}_across_{mask}"):
        return lax.ppermute(array, "dp", [(i, i ^ mask) for i in range(size)])


def tie(arrays, deps):
    return call(lambda: None, "tie", [], deps=deps, passing=arrays, in_specs=[], grid=(1,))()


def other_core(array, label="other_core"):
    with jax.named_scope(label):
        return lax.ppermute(array, "mp", core_swap)


def stage_bits(size):
    if size == 16:
        return (8, 4, 2, 1)
    return tuple(1 << i for i in range(size.bit_length() - 1))


def block_masks(size):
    bits = stage_bits(size)
    return [sum(bit for i, bit in enumerate(bits) if k >> i & 1) for k in range(size)]


def piece_rows(size, width):
    if size != 16:
        return [width]
    return [width // 4] * 3 + [width // 8] * 2


def join_kernel(*refs):
    *part_refs, out_ref = refs
    start = 0
    for part in part_refs:
        rows = part.shape[0]
        out_ref[start : start + rows] = part[...]
        start += rows


def join(parts, **options):
    rows = sum(part.shape[0] for part in parts)
    return call(
        join_kernel, "join", shape_of((rows, *parts[0].shape[1:]), parts[0].dtype), **options
    )(*parts)


def step_kernel(groups, y_ref, x_ref, *refs):
    part_refs, (low_ref, high_ref, *joined_refs) = refs[: sum(groups)], refs[sum(groups) :]
    low_ref[...] = y_ref[...]
    high_ref[...] = x_ref[...]
    for group, joined_ref in zip(groups, joined_refs):
        join_kernel(*part_refs[:group], joined_ref)
        part_refs = part_refs[group:]


def gather_step(across_y, across_x, *groups, **options):
    half = (across_y.shape[0] // 2, across_y.shape[1])
    shapes = [shape_of(half, across_y.dtype)] * 2
    for parts in groups:
        shapes.append(shape_of((sum(p.shape[0] for p in parts), parts[0].shape[1]), parts[0].dtype))
    flat = [part for parts in groups for part in parts]
    return call(
        functools.partial(step_kernel, tuple(len(parts) for parts in groups)),
        "gather_step",
        shapes,
        grid=(1,),
        in_specs=[
            pl.BlockSpec(half, lambda i: (0, 0)),
            pl.BlockSpec(half, lambda i: (1, 0)),
            *(whole(part.shape) for part in flat),
        ],
        out_specs=[whole(shape.shape) for shape in shapes],
        **options,
    )(across_y, across_x, *flat)


def line_parts(part, size, label):
    return [part] + [swap(part, mask, size, label) for mask in (8, 4, 12)]


def side_parts(quarter, size, label):
    return [swap(quarter, mask, size, label) for mask in (2, 1)]


def corner_parts(low, high, size, label):
    return [swap(low, 1, size, label), swap(high, 2, size, label)]


def gather_doubling(part, size):
    for bit in stage_bits(size):
        part = jnp.concatenate([part, swap(part, bit, size)], axis=0)
    return part


def small_line(part, size, label):
    if size != 16:
        return part[None]
    return join(line_parts(part[None], size, label))


def small_plane(quarter, size, label):
    if size != 16:
        return [gather_doubling(quarter, size)]
    return [quarter] + [swap(quarter, mask, size, label) for mask in (2, 1, 3)]


def stacked(refs):
    return jnp.concatenate([ref[...] for ref in refs], axis=0)


def stacked_row(refs, row):
    return jnp.concatenate([ref[:, row, :] for ref in refs], axis=0)


def gather_small(part, size, label):
    return small_plane(small_line(part, size, label), size, label)


def plane_sum_kernel(y_ref, x_ref, low_ref, high_ref, y_out, x_out):
    half = low_ref.shape[0]
    y_out[:half] = (y_ref[:half].astype(full_type) + low_ref[...].astype(full_type)).astype(low_type)
    y_out[half:] = y_ref[half:]
    x_out[:half] = x_ref[:half]
    x_out[half:] = (x_ref[half:].astype(full_type) + high_ref[...].astype(full_type)).astype(low_type)


def line_sum_kernel(*refs):
    count = sum(ref.shape[0] == refs[0].shape[0] for ref in refs)
    add_refs, out_refs = refs[:count], refs[count:]
    rows = out_refs[0].shape[0]
    for i, out_ref in enumerate(out_refs):
        span = slice(i * rows, (i + 1) * rows)
        total = add_refs[0][span].astype(full_type)
        for ref in add_refs[1:]:
            total = total + ref[span].astype(full_type)
        out_ref[...] = total.astype(out_ref.dtype)


class Scatter:
    def __init__(self, pieces, size, label):
        self.pieces, self.size, self.label = pieces, size, label
        self.sources, self.came = (), ()
        if size == 16:
            *self.pieces, low, high = pieces
            self.came = [swap(low, 1, size, label), swap(high, 2, size, label)]

    def sides(self, deps=(), passing=()):
        if self.size != 16:
            return passing
        keep, to_y, to_x = self.pieces
        to_y, to_x, *passed = call(
            plane_sum_kernel,
            "plane_sum",
            [shape_of(to_y.shape, low_type)] * 2,
            deps=deps,
            passing=passing,
        )(to_y, to_x, *self.came)
        self.sources = (to_y, to_x)
        self.came = [swap(to_y, 2, self.size, self.label), swap(to_x, 1, self.size, self.label)]
        return passed

    def near(self, deps=()):
        if self.size != 16:
            return
        keep = self.pieces[0]
        half = (keep.shape[0] // 2, keep.shape[1])
        kept, sent = call(
            line_sum_kernel,
            "line_sum",
            [shape_of(half, full_type), shape_of(half, low_type)],
            deps=deps,
        )(keep, *self.came)
        self.sources, self.came, self.pieces = (sent,), [swap(sent, 4, self.size, self.label)], [kept]

    def far(self, deps=()):
        if self.size != 16:
            return self.line(deps)[0]
        kept = self.pieces[0]
        half = (kept.shape[0] // 2, kept.shape[1])
        own, sent = call(
            line_sum_kernel,
            "line_sum",
            [shape_of(half, full_type), shape_of(half, low_type)],
            deps=deps,
        )(kept, *self.came)
        self.sources = (sent,)
        return [own, swap(sent, 8, self.size, self.label)]

    def line(self, deps=(), passing=()):
        size, label = self.size, self.label
        if size != 16:
            grad = self.pieces[0]
            for bit in reversed(stage_bits(size)):
                half = grad.shape[0] // 2
                came = swap(grad[half:], bit, size, label)
                grad = (grad[:half].astype(full_type) + came.astype(full_type)).astype(low_type)
            return [grad.astype(full_type)], passing
        keep = self.pieces[0]
        part = (keep.shape[0] // 4, keep.shape[1])
        own, *others = call(
            line_sum_kernel,
            "line_sum",
            [shape_of(part, full_type)] + [shape_of(part, low_type)] * 3,
            deps=deps,
            passing=passing,
        )(keep, *self.came)
        came = [swap(other, mask, size, label) for other, mask in zip(others, (8, 4, 12))]
        return [own] + came, others[3:]


def pack_heads_kernel(in_ref, out_ref, gain_ref, tied_ref, a_ref):
    parts, rows, width = in_ref.shape
    for c in range(parts):
        a_ref[:, c * width : (c + 1) * width] = in_ref[c].astype(low_type)
    a_ref[:, parts * width : (parts + 1) * width] = out_ref[...].astype(low_type)
    gains, tied = gain_ref[...], tied_ref[...]
    vectors = few_rows([gains[i : i + 1] for i in range(3)] + [tied[i : i + 1] for i in range(2)], 16)
    pick = lax.broadcasted_iota(jnp.int32, (16, LANES), 0) == lax.broadcasted_iota(
        jnp.int32, (16, LANES), 1
    )
    extra = dot_tn(vectors.astype(low_type), jnp.where(pick, 1.0, 0.0).astype(low_type))
    a_ref[:, (parts + 1) * width :] = extra.astype(low_type)


def pack_hidden_kernel(up_ref, down_ref, b_ref, c_ref):
    b_ref[...] = up_ref[...].astype(low_type)
    c_ref[...] = down_ref[...].astype(low_type)


def order_kernel(x_ref, order_ref, out_ref):
    out_ref[...] = dot_nn(x_ref[...], order_ref[...]).astype(low_type)


def turn_kernel(x_ref, out_ref):
    out_ref[...] = x_ref[...].T


def head_lanes():
    lane = lax.broadcasted_iota(jnp.int32, (1, LANES), 1)
    return [lane < LANES // 2, lane >= LANES // 2]


def project_kernel(pieces, pairs, x_ref, *refs):
    weight_refs, (qkv_ref, normed_ref, vector_ref, w_ref) = refs[:pieces], refs[pieces:]
    parts = qkv_ref.shape[1]
    in_width = pairs * parts * LANES

    @pl.when(pl.program_id(0) == 0)
    def assemble():
        fill_rows(w_ref, weight_refs)
        pick = lax.broadcasted_iota(jnp.int32, (16, LANES), 0) == lax.broadcasted_iota(
            jnp.int32, (16, LANES), 1
        )
        vectors = dot_nt(jnp.where(pick, 1.0, 0.0).astype(low_type), w_ref[:, -LANES:])
        vector_ref[...] = vectors[:8]

    x = x_ref[...].astype(full_type)
    normed = (x * rms_scale(x) * vector_ref[0:1]).astype(low_type)
    normed_ref[...] = normed
    projected = dot_nn(normed, w_ref[:, :in_width]).astype(low_type)
    for c in range(parts):
        for p in range(pairs):
            start = (c * pairs + p) * LANES
            qkv_ref[p, c] = projected[:, start : start + LANES]


def project(rows_low, weights, pairs, deps):
    count, width = rows_low.shape
    parts = 3
    return call(
        functools.partial(project_kernel, len(weights), pairs),
        "projection",
        [
            shape_of((pairs, parts, count, LANES), low_type),
            shape_of((count, width), low_type),
            shape_of((8, width), full_type),
        ],
        deps=deps,
        grid=(count // ROWS,),
        in_specs=[row_blocks((ROWS, width)), *(whole(piece.shape) for piece in weights)],
        out_specs=[
            pl.BlockSpec((pairs, parts, ROWS, LANES), lambda i: (0, 0, i, 0)),
            row_blocks((ROWS, width)),
            whole((8, width)),
        ],
        scratch_shapes=[pltpu.VMEM((width, weights[0].shape[1]), low_type)],
    )(rows_low, *weights)


def attention_kernel(len_ref, line_ref, qkv_ref, *refs):
    att_ref, prob_ref, inv_ref, tile_ref = refs[-4:]
    micro, slot = prob_ref.shape[1], prob_ref.shape[3]
    blocks = slot // LANES
    lanes = head_lanes()
    for h in range(2):
        for d in range(2 * blocks - 1):
            piece = jnp.broadcast_to(
                line_ref[0, h : h + 1, d * LANES : (d + 2) * LANES], (LANES, 2 * LANES)
            )
            turned = pltpu.roll(piece, LANES + 1, 1, stride=1, stride_axis=0)
            tile_ref[h, d] = turned[:, :LANES]

    def micro_step(m, carry):
        start = pl.multiple_of(m * slot, slot)
        key_valid = lax.broadcasted_iota(jnp.int32, (1, slot), 1) < len_ref[m]
        keys = qkv_ref[0, 1, pl.ds(start, slot), :]
        values = qkv_ref[0, 2, pl.ds(start, slot), :]
        values = jnp.concatenate([values, jnp.ones_like(values)], axis=1)
        for r in range(slot // ROWS):
            rows = pl.ds(start + r * ROWS, ROWS)
            queries = qkv_ref[0, 0, rows, :]
            queries = jnp.concatenate(
                [queries * lanes[h].astype(low_type) for h in range(2)], axis=0
            )
            first = r * (ROWS // LANES)
            bias = jnp.concatenate(
                [
                    jnp.concatenate(
                        [tile_ref[h, j - first - i + blocks - 1] for j in range(blocks)], axis=1
                    )
                    for h in range(2)
                    for i in range(ROWS // LANES)
                ],
                axis=0,
            )
            scores = dot_nt(queries, keys)
            scores = jnp.where(key_valid, scores + bias, masked_score)
            terms = jnp.exp(scores - jnp.max(scores, axis=1, keepdims=True)).astype(low_type)
            for h in range(2):
                prob_ref[0, m, h, r * ROWS : (r + 1) * ROWS, :] = terms[h * ROWS : (h + 1) * ROWS]
            mixed = dot_nn(terms, values)
            inverse = 1.0 / mixed[:, LANES:]
            mixed = mixed[:, :LANES] * inverse
            att_ref[rows, :] = jnp.where(lanes[0], mixed[:ROWS], mixed[ROWS:]).astype(low_type)
            inv_ref[rows, :] = jnp.where(lanes[0], inverse[:ROWS], inverse[ROWS:])
        return carry

    lax.fori_loop(0, micro, micro_step, 0)


def attention(lengths, lines, qkv, pair, slot, before=(), deps=()):
    pairs, parts, count, _ = qkv.shape
    micro = count // slot
    spans = 2 * (slot // LANES) - 1
    column = pl.BlockSpec((count, LANES), lambda i: (0, pair))
    return call(
        attention_kernel,
        "attention_forward",
        [
            shape_of((count, pairs * LANES), low_type),
            shape_of((pairs, micro, 2, slot, slot), low_type),
            shape_of((count, pairs * LANES), full_type),
        ],
        deps=deps,
        grid=(1,),
        in_specs=[
            on_scalars(),
            pl.BlockSpec((1, 2, lines.shape[2]), lambda i: (pair, 0, 0)),
            pl.BlockSpec((1, parts, count, LANES), lambda i: (pair, 0, 0, 0)),
            *[in_place()] * len(before),
        ],
        out_specs=[
            column,
            pl.BlockSpec((1, micro, 2, slot, slot), lambda i: (pair, 0, 0, 0, 0)),
            column,
        ],
        input_output_aliases={3 + i: i for i in range(len(before))},
        scratch_shapes=[pltpu.VMEM((2, spans, LANES, LANES), full_type)],
    )(lengths, lines, qkv, *before)


def branch_kernel(att_ref, *refs):
    *weight_refs, out_ref, w_ref = refs

    @pl.when(pl.program_id(0) == 0)
    def assemble():
        fill_rows(w_ref, weight_refs)

    out_ref[...] = dot_nt(att_ref[...], w_ref[...]).astype(low_type)


def branch_rows(attended, weights, deps=()):
    count, head_width = attended.shape
    width = sum(piece.shape[0] for piece in weights)
    return call(
        branch_kernel,
        "branch",
        shape_of((count, width), low_type),
        deps=deps,
        grid=(count // (2 * ROWS),),
        in_specs=[
            row_blocks((2 * ROWS, head_width)),
            *(pl.BlockSpec((piece.shape[0], head_width), lambda i: (0, 3)) for piece in weights),
        ],
        out_specs=row_blocks((2 * ROWS, width)),
        scratch_shapes=[pltpu.VMEM((width, head_width), low_type)],
    )(attended, *weights)


def hidden_kernel(pieces, len_ref, x_ref, own_ref, came_ref, vector_ref, *refs):
    weight_refs, refs = refs[:pieces], refs[pieces:]
    normed_ref, slope_ref, act_ref, sum_ref, w_ref = refs
    m = pl.program_id(0)
    slot = x_ref.shape[0]

    @pl.when(m == 0)
    def assemble():
        fill_rows(w_ref, weight_refs)

    middle = middle_rows(x_ref, own_ref, came_ref)
    normed = (middle * rms_scale(middle) * vector_ref[1:2]).astype(low_type)
    valid = lax.broadcasted_iota(jnp.int32, (slot, 1), 0) < len_ref[m]
    normed_ref[...] = jnp.where(valid, normed, jnp.zeros_like(normed))
    counted = lax.broadcasted_iota(jnp.int32, (16, slot), 1) < len_ref[m]
    counted = jnp.where(counted, 1.0, 0.0).astype(low_type)
    sum_ref[0] = jnp.sum(jnp.where(valid, middle, 0.0), axis=0, keepdims=True)
    block = 3 * LANES

    def columns_step(n, carry):
        columns = pl.ds(pl.multiple_of(n * block, block), block)
        v = dot_nn(normed, w_ref[:, columns])
        square = v * v
        gate = jnp.tanh(v * (gelu_slope + (gelu_slope * gelu_cubic) * square))
        half = 0.5 + 0.5 * gate
        active = (v * half).astype(low_type)
        act_ref[0, :, columns] = dot_nn(counted, active)[0:1]
        inner = 0.5 * gelu_slope + (1.5 * gelu_slope * gelu_cubic) * square
        slope_ref[:, columns] = (half + v * (1.0 - gate * gate) * inner).astype(low_type)
        return carry

    lax.fori_loop(0, w_ref.shape[1] // block, columns_step, 0)


def middle_rows(x_ref, own_ref, came_ref):
    branch = own_ref[...].astype(full_type) + came_ref[...].astype(full_type)
    return x_ref[...].astype(full_type) + branch


def hidden(lengths, rows_low, own, came, vectors, weights, slot):
    count, width = rows_low.shape
    micro = count // slot
    inner = weights[0].shape[1]
    return call(
        functools.partial(hidden_kernel, len(weights)),
        "hidden_forward",
        [
            shape_of((count, width), low_type),
            shape_of((count, inner), low_type),
            shape_of((micro, 1, inner), full_type),
            shape_of((micro, 1, width), full_type),
        ],
        cost=(1200, 20000),
        grid=(micro,),
        in_specs=[
            on_scalars(),
            *[row_blocks((slot, width))] * 3,
            whole(vectors.shape),
            *(whole(piece.shape) for piece in weights),
        ],
        out_specs=[
            row_blocks((slot, width)),
            row_blocks((slot, inner)),
            row_blocks((1, 1, inner)),
            row_blocks((1, 1, width)),
        ],
        scratch_shapes=[pltpu.VMEM((width, inner), low_type)],
    )(lengths, rows_low, own, came, vectors, *weights)


def few_rows(rows, count):
    place = lax.broadcasted_iota(jnp.int32, (count, rows[0].shape[1]), 0)
    total = jnp.zeros(place.shape, full_type)
    for i, row in enumerate(rows):
        total = jnp.where(place == i, row, total)
    return total


def pool_kernel(act_ref, *refs):
    *weight_refs, out_ref, w_ref = refs
    fill_rows(w_ref, weight_refs)
    sums = [act_ref[m] for m in range(act_ref.shape[0])]
    highs = [row.astype(low_type).astype(full_type) for row in sums]
    rests = [row - high for row, high in zip(sums, highs)]
    down = dot_nt(few_rows(highs + rests, 16).astype(low_type), w_ref[...])
    micro = len(sums)
    out_ref[...] = few_rows([down[m : m + 1] + down[micro + m : micro + m + 1] for m in range(micro)], 8)


def margin_kernel(len_ref, own_ref, other_ref, sum_ref, act_ref, vector_ref, send_ref):
    margins, rows = [], []
    for m in range(sum_ref.shape[0]):
        length = len_ref[m].astype(full_type)
        total = own_ref[m : m + 1] + other_ref[m : m + 1] + sum_ref[m]
        pooled = (total / length).astype(low_type).astype(full_type)
        final = pooled * rms_scale(pooled) * vector_ref[2:3]
        logits = [
            jnp.sum(final * vector_ref[i : i + 1], axis=1, keepdims=True) * pooled.shape[1] ** (-0.5)
            for i in (3, 4)
        ]
        lane = lax.broadcasted_iota(jnp.int32, pooled.shape, 1)
        margins.append(jnp.where(lane < LANES, logits[0] - logits[1], length))
        rows.append(pooled)
    width = rows[0].shape[1]
    for m in range(sum_ref.shape[0]):
        sums = act_ref[m]
        rows += [sums[:, i * width : (i + 1) * width] for i in range(sums.shape[1] // width)]
    send_ref[...] = few_rows(rows + margins, 8)


def ranking(margins, same, positive):
    place = lax.broadcasted_iota(jnp.int32, margins.shape, 0)
    lane = lax.broadcasted_iota(jnp.int32, margins.shape, 1)
    others = jnp.sum(jnp.where(place == lane, margins, 0.0), axis=0, keepdims=True)
    row_max = jnp.max(jnp.where(same, others, masked_score), axis=1, keepdims=True)
    terms = jnp.where(same, jnp.exp(jnp.where(same, others - row_max, 0.0)), 0.0)
    chance = jnp.exp(margins - row_max) / jnp.sum(terms, axis=1, keepdims=True)
    return LOSS_SCALE * (chance - positive)


def pooled_grad(pooled, d_margin, vector_ref):
    scale = rms_scale(pooled)
    d_logit = d_margin * pooled.shape[1] ** (-0.5)
    d_final = d_logit * (vector_ref[3:4] - vector_ref[4:5])
    return norm_input_grad(d_final, vector_ref[2:3], pooled, scale)


def rank_kernel(
    small_pieces, down_pieces, up_pieces, len_ref, same_ref, positive_ref, vector_ref, slope_ref,
    *refs
):
    small_refs, refs = refs[:small_pieces], refs[small_pieces:]
    down_refs, refs = refs[:down_pieces], refs[down_pieces:]
    up_refs, refs = refs[:up_pieces], refs[up_pieces:]
    line_ref, act_ref, rank_ref, d_ref, down_ref, up_ref = refs
    m = pl.program_id(0)

    @pl.when(m == 0)
    def rank():
        fill_rows(down_ref, down_refs)
        fill_rows(up_ref, up_refs)
        lines = []
        for i in range(2):
            margins = stacked_row(small_refs, 6 + i)[:, :LANES]
            d_margins = ranking(margins, same_ref[i] > 0.5, positive_ref[i])
            rank_ref[i] = d_margins
            pooled = small_refs[0][0, i : i + 1, :]
            d_pooled = pooled_grad(pooled, d_margins[0:1, 0:1], vector_ref)
            lines.append(d_pooled / len_ref[i].astype(full_type))
        line_ref[...] = few_rows(lines, 8)
        d_act = dot_nn(few_rows(lines, 16).astype(low_type), down_ref[...])
        act_ref[...] = d_act[:8]

    d_row = jnp.where(m == 0, act_ref[0:1], act_ref[1:2])
    d_hidden = (slope_ref[...].astype(full_type) * d_row).astype(low_type)
    d_normed = dot_nt(d_hidden, up_ref[...])
    valid = lax.broadcasted_iota(jnp.int32, (d_normed.shape[0], 1), 0) < len_ref[m]
    d_ref[...] = jnp.where(valid, d_normed, 0.0).astype(low_type)


def rank_back(lengths, same, positive, vectors, slope, small_all, down, up, slot, deps):
    count, inner = slope.shape
    width = vectors.shape[1]
    return call(
        functools.partial(rank_kernel, len(small_all), len(down), len(up)),
        "rank_backward",
        [
            shape_of((8, width), full_type),
            shape_of((8, inner), full_type),
            shape_of(positive.shape, full_type),
            shape_of((count, width), low_type),
        ],
        cost=(1200, 20000),
        deps=deps,
        grid=(count // slot,),
        in_specs=[
            on_scalars(),
            *(whole(array.shape) for array in (same, positive, vectors)),
            row_blocks((slot, inner)),
            *(whole(piece.shape) for piece in (*small_all, *down, *up)),
        ],
        out_specs=[
            whole((8, width)),
            whole((8, inner)),
            whole(positive.shape),
            row_blocks((slot, width)),
        ],
        scratch_shapes=[pltpu.VMEM((width, inner), low_type), pltpu.VMEM((width, inner), low_type)],
    )(lengths, same, positive, vectors, slope, *small_all, *down, *up)


def up_grad_kernel(slot, normed_ref, slope_ref, act_ref, *refs):
    *out_refs, turned_ref = refs

    @pl.when(pl.program_id(0) == 0)
    def turn():
        turned_ref[...] = normed_ref[...].T

    total = 0.0
    for m in range(normed_ref.shape[0] // slot):
        rows = slice(m * slot, (m + 1) * slot)
        d_hidden = (slope_ref[rows].astype(full_type) * act_ref[m : m + 1]).astype(low_type)
        total = total + dot_nn(turned_ref[:, rows], d_hidden)
    spill_rows(total, out_refs)


def up_grad(normed, slope, d_act, rows, slot):
    count, width = normed.shape
    inner = slope.shape[1]
    block = 4 * LANES
    return call(
        functools.partial(up_grad_kernel, slot),
        "hidden_in_gradient",
        [shape_of((r, inner), low_type) for r in rows],
        cost=(1200, 15000),
        grid=(inner // block,),
        in_specs=[
            whole(normed.shape),
            column_blocks((count, block)),
            column_blocks((8, block)),
        ],
        out_specs=[column_blocks((r, block)) for r in rows],
        scratch_shapes=[pltpu.VMEM((width, count), low_type)],
    )(normed, slope, d_act)


def middle_kernel(
    pieces, len_ref, x_ref, branch_ref, other_ref, own_ref, came_ref, vector_ref, line_ref,
    att_ref, inv_ref, *refs
):
    weight_refs, refs = refs[:pieces], refs[pieces:]
    d_ref, d_att_ref, total_ref, w_ref = refs
    m = pl.program_id(0)

    @pl.when(m == 0)
    def assemble():
        fill_rows(w_ref, weight_refs)
        total_ref[...] = jnp.zeros_like(total_ref)

    middle = middle_rows(x_ref, branch_ref, other_ref)
    own = own_ref[...].astype(full_type)
    scale = rms_scale(middle)
    valid = lax.broadcasted_iota(jnp.int32, (middle.shape[0], 1), 0) < len_ref[m]
    line = jnp.where(m == 0, line_ref[0:1], line_ref[1:2])
    d_middle = jnp.where(valid, line, 0.0) + norm_input_grad(
        own + came_ref[...].astype(full_type), vector_ref[1:2], middle, scale
    )
    d_ref[...] = d_middle
    d_low = d_middle.astype(low_type)
    d_att_ref[...] = (dot_nn(d_low, w_ref[...]) * inv_ref[...]).astype(low_type)
    total_ref[...] += dot_tn(d_low, att_ref[...])


def middle_back(
    lengths, rows_low, branch, other, own, came, vectors, lines, attended, inverse, weights, slot
):
    count, width = rows_low.shape
    head_width = attended.shape[1]
    return call(
        functools.partial(middle_kernel, len(weights)),
        "middle_backward",
        [
            shape_of((count, width), full_type),
            shape_of((count, head_width), low_type),
            shape_of((width, head_width), full_type),
        ],
        cost=(600, 15000),
        grid=(count // slot,),
        in_specs=[
            on_scalars(),
            *[row_blocks((slot, width))] * 5,
            whole(vectors.shape),
            whole(lines.shape),
            row_blocks((slot, head_width)),
            row_blocks((slot, head_width)),
            *(
                pl.BlockSpec((piece.shape[0], head_width), lambda i: (0, 3)) for piece in weights
            ),
        ],
        out_specs=[
            row_blocks((slot, width)),
            row_blocks((slot, head_width)),
            whole((width, head_width)),
        ],
        scratch_shapes=[pltpu.VMEM((width, head_width), low_type)],
    )(
        lengths, rows_low, branch, other, own, came, vectors, lines, attended, inverse, *weights
    )


def attention_back_kernel(
    befores, grads, tables, own, prob_ref, qkv_ref, d_ref, att_ref, turned_ref, hot_ref, *refs
):
    table_refs, refs = refs[:tables], refs[tables:]
    grad_refs, refs = refs[:grads], refs[grads:]
    d_out_ref, table_ref, *out_refs, tile_ref, dk_ref, dv_ref = refs[befores:]
    step = pl.program_id(0)

    if grads:

        @pl.when(step > 0)
        def projection():
            spill_rows(grad_refs[0][...], out_refs)

    @pl.when(step == 0)
    def heads():
        pair_back(
            prob_ref, qkv_ref, d_ref, att_ref, turned_ref, hot_ref, d_out_ref, table_ref, out_refs,
            tile_ref, dk_ref, dv_ref
        )
        if tables:
            lines = [ref[0, h : h + 1] for ref in (*table_refs, table_ref) for h in range(2)]
            width = turned_ref.shape[0]
            place = lax.broadcasted_iota(jnp.int32, (width, 16), 0) % own
            pick = place == lax.broadcasted_iota(jnp.int32, (width, 16), 1)
            pick = jnp.where(pick, 1.0, 0.0).astype(low_type)
            spread = dot_nn(pick, few_rows(lines, 16).astype(low_type))
            spill_rows(spread, [ref.at[:, 3 * LANES :] for ref in out_refs])


def pair_back(
    prob_ref, qkv_ref, d_ref, att_ref, turned_ref, hot_ref, d_out_ref, table_ref, out_refs,
    tile_ref, dk_ref, dv_ref
):
    micro, slot = prob_ref.shape[1], prob_ref.shape[3]
    blocks = slot // LANES
    spans = 2 * blocks - 1
    lanes = head_lanes()

    tile_ref[...] = jnp.zeros_like(tile_ref)

    def micro_step(m, carry):
        start = pl.multiple_of(m * slot, slot)
        everything = pl.ds(start, slot)
        keys, values = qkv_ref[0, 1, everything, :], qkv_ref[0, 2, everything, :]
        for r in range(slot // ROWS):
            rows = pl.ds(start + r * ROWS, ROWS)
            queries = qkv_ref[0, 0, rows, :]
            queries = jnp.concatenate(
                [queries * lanes[h].astype(low_type) for h in range(2)], axis=0
            )
            d_att = d_ref[rows, :]
            product = d_att.astype(full_type) * att_ref[rows, :].astype(full_type)
            row_dot = jnp.concatenate(
                [
                    jnp.sum(jnp.where(lanes[h], product, 0.0), axis=1, keepdims=True)
                    for h in range(2)
                ],
                axis=0,
            )
            d_att = jnp.concatenate([d_att * lanes[h].astype(low_type) for h in range(2)], axis=0)
            span = slice(r * ROWS, (r + 1) * ROWS)
            probs = jnp.concatenate([prob_ref[0, m, h, span, :] for h in range(2)], axis=0)
            d_scores = probs.astype(full_type) * (dot_nt(d_att, values) - row_dot)
            d_low = d_scores.astype(low_type)
            for h in range(2):
                for i in range(ROWS // LANES):
                    for j in range(blocks):
                        top = h * ROWS + i * LANES
                        tile_ref[h, j - r * (ROWS // LANES) - i + blocks - 1] += d_scores[
                            top : top + LANES, j * LANES : (j + 1) * LANES
                        ]
            d_queries = dot_nn(d_low, keys)
            d_out_ref[0, 0, rows, :] = jnp.where(
                lanes[0], d_queries[:ROWS], d_queries[ROWS:]
            ).astype(low_type)
            d_keys, d_values = dot_tn(d_low, queries), dot_tn(probs, d_att)
            dk_ref[...] = d_keys if r == 0 else dk_ref[...] + d_keys
            dv_ref[...] = d_values if r == 0 else dv_ref[...] + d_values
        d_out_ref[0, 1, everything, :] = dk_ref[...].astype(low_type)
        d_out_ref[0, 2, everything, :] = dv_ref[...].astype(low_type)
        return carry

    lax.fori_loop(0, micro, micro_step, 0)
    d_project = jnp.concatenate([d_out_ref[0, c] for c in range(3)], axis=1)
    spill_rows(dot_nn(turned_ref[...], d_project), [ref.at[:, : 3 * LANES] for ref in out_refs])
    flip = (
        lax.broadcasted_iota(jnp.int32, (LANES, LANES), 0)
        + lax.broadcasted_iota(jnp.int32, (LANES, LANES), 1)
        == LANES - 1
    )
    flip = jnp.where(flip, 1.0, 0.0).astype(low_type)
    table = jnp.zeros((16, LANES), full_type)
    for d in range(spans):
        highs, rests = [], []
        for h in range(2):
            tile = tile_ref[h, d]
            high = tile.astype(low_type)
            rest = (tile - high.astype(full_type)).astype(low_type)
            flipped = dot_nn(flip, high) + dot_nn(flip, rest)
            wide = jnp.concatenate([flipped, jnp.zeros_like(flipped)], axis=1)
            turned = pltpu.roll(wide, 0, 1, stride=1, stride_axis=0)
            line = jnp.sum(turned, axis=0, keepdims=True)
            highs.append(line.astype(low_type).astype(full_type))
            rests.append(line - highs[-1])
        table = table + dot_nn(few_rows(highs + rests, 16).astype(low_type), hot_ref[d])
    table_ref[0] = few_rows([table[h : h + 1] + table[2 + h : 3 + h] for h in range(2)], 8)


def attention_back(
    probs, qkv, d_attended, attended, turned, hot, rows, pair, slot, own,
    grad_out=None, tables=(), before=(), deps=()
):
    width, count = turned.shape
    micro = count // slot
    pairs = qkv.shape[0]
    spans = 2 * (slot // LANES) - 1
    lead = lambda shape: pl.BlockSpec(shape, lambda i: (pair,) + (0,) * (len(shape) - 1))
    column = pl.BlockSpec((count, LANES), lambda i: (0, pair))
    if tables:
        steps, extra, extra_specs = 1, tables, [whole(table.shape) for table in tables]
        gradients = [shape_of((r, 4 * LANES), low_type) for r in rows]
        gradient_specs = [whole((r, 4 * LANES)) for r in rows]
    else:
        steps = 1 if grad_out is None else 2
        extra = () if grad_out is None else (grad_out,)
        extra_specs = [whole(array.shape) for array in extra]
        gradients = [shape_of((r, pairs * 3 * LANES), low_type) for r in rows]
        gradient_specs = [pl.BlockSpec((r, 3 * LANES), lambda i: (0, i + pair)) for r in rows]
    first = 6 + len(extra)
    return call(
        functools.partial(
            attention_back_kernel, len(before), 0 if grad_out is None else 1, len(tables), own
        ),
        "attention_backward",
        [
            shape_of((pairs, 3, count, LANES), low_type),
            shape_of((1, 8, LANES), full_type),
            *gradients,
        ],
        deps=deps,
        grid=(steps,),
        in_specs=[
            lead((1, micro, 2, slot, slot)),
            lead((1, 3, count, LANES)),
            column,
            column,
            whole(turned.shape),
            whole(hot.shape),
            *extra_specs,
            *[in_place()] * len(before),
        ],
        out_specs=[lead((1, 3, count, LANES)), whole((1, 8, LANES)), *gradient_specs],
        input_output_aliases={first + i: i if i == 0 else i + 1 for i in range(len(before))},
        scratch_shapes=[
            pltpu.VMEM((2, spans, LANES, LANES), full_type),
            pltpu.VMEM((slot, LANES), full_type),
            pltpu.VMEM((slot, LANES), full_type),
        ],
    )(probs, qkv, d_attended, attended, turned, hot, *extra, *before)


def normed_back_kernel(d_ref, *refs):
    *weight_refs, out_ref, w_ref = refs
    pairs, parts = d_ref.shape[0], d_ref.shape[1]

    @pl.when(pl.program_id(0) == 0)
    def assemble():
        fill_rows(w_ref, weight_refs, slice(0, w_ref.shape[1]))

    blocks = [d_ref[p, c] for c in range(parts) for p in range(pairs)]
    d_normed = dot_nt(jnp.concatenate(blocks, axis=1), w_ref[...])
    out_ref[...] = d_normed.astype(low_type)


def normed_back(d_project, weights, deps):
    pairs, parts, count, _ = d_project.shape
    width = sum(piece.shape[0] for piece in weights)
    return call(
        normed_back_kernel,
        "normed_backward",
        shape_of((count, width), low_type),
        cost=(900, 15000),
        deps=deps,
        grid=(count // ROWS,),
        in_specs=[
            pl.BlockSpec((pairs, parts, ROWS, LANES), lambda i: (0, 0, i, 0)),
            *(whole(piece.shape) for piece in weights),
        ],
        out_specs=row_blocks((ROWS, width)),
        scratch_shapes=[pltpu.VMEM((width, pairs * parts * LANES), low_type)],
    )(d_project, *weights)


def token_kernel(d_ref, own_ref, came_ref, x_ref, vector_ref, order_ref, out_ref, done_ref):
    x = x_ref[...].astype(full_type)
    d_normed = own_ref[...].astype(full_type) + came_ref[...].astype(full_type)
    grad = d_ref[...] + norm_input_grad(d_normed, vector_ref[0:1], x, rms_scale(x))
    high = grad.astype(low_type)
    rest = (grad - high.astype(full_type)).astype(low_type)
    order = order_ref[...]
    out_ref[...] = dot_nt(high, order) + dot_nt(rest, order)
    done_ref[...] = jnp.zeros_like(done_ref)


def token_back(d_middle, own, came, rows_low, vectors, order, deps):
    count, width = rows_low.shape
    return call(
        token_kernel,
        "token_gradient",
        [shape_of((count, width), full_type), shape_of((8, LANES), full_type)],
        cost=(1200, 15000),
        deps=deps,
        grid=(count // ROWS,),
        in_specs=[row_blocks((ROWS, width))] * 4 + [whole(vectors.shape), whole(order.shape)],
        out_specs=[row_blocks((ROWS, width)), whole((8, LANES))],
    )(d_middle, own, came, rows_low, vectors, order)


def total_kernel(smalls, counts, micro, pairs, *refs):
    small_refs, refs = refs[:smalls], refs[smalls:]
    groups = []
    for count in counts:
        groups.append(refs[:count])
        refs = refs[count:]
    rank_ref, vector_ref, in_ref, up_ref, gain_ref, tied_ref, down_ref, line_ref, *out_refs = refs
    size, width = sum(ref.shape[0] for ref in small_refs), small_refs[0].shape[2]
    row_of = lambda row: stacked_row(small_refs, row)
    own = down_ref.shape[0]
    inverse = 1.0 / LOSS_SCALE
    add_up = lambda values: jnp.sum(values, axis=0, keepdims=True).sum(axis=1, keepdims=True)
    squares, sums = 0.0, []
    for group, out_ref in zip(groups, out_refs):
        total = sum(ref[...].astype(full_type) for ref in group) * inverse
        total, rest = total[:, : out_ref.shape[1]], total[:, out_ref.shape[1] :]
        out_ref[...] = total
        sums.append((total, rest))
        squares = squares + add_up(total * total)
    table = sums[1][1]

    block = lax.broadcasted_iota(jnp.int32, (size, width), 1) // own
    mine = block == lax.broadcasted_iota(jnp.int32, (size, width), 0)
    fold = lax.broadcasted_iota(jnp.int32, (width, LANES), 0) % own == lax.broadcasted_iota(
        jnp.int32, (width, LANES), 1
    )
    fold = jnp.where(fold, 1.0, 0.0).astype(low_type)
    down, ranked = 0.0, 0.0
    lane = lax.broadcasted_iota(jnp.int32, (1, LANES), 1)
    own_factor = (vector_ref[3:4, :LANES] - vector_ref[4:5, :LANES]) * vector_ref[2:3, :LANES]
    own_factor = jnp.where(lane < own, own_factor, 0.0)
    parts = down_ref.shape[1] // width
    for m in range(micro):
        pooled = row_of(m)
        scale = rms_scale(pooled)
        lengths = row_of(micro + micro * parts + m)
        margins, lengths = lengths[:, 0:1], lengths[:, LANES : LANES + 1]
        d_logit = rank_ref[m][:, 0:1] * width ** (-0.5)
        mean = d_logit * margins * (width**0.5 / width) / scale
        mine_low = dot_nn(jnp.where(mine, pooled, 0.0).astype(low_type), fold)
        ranked = ranked + jnp.sum(mine_low * scale * d_logit, axis=0, keepdims=True)
        d_pooled = scale * d_logit * own_factor - mine_low * scale**3 * mean
        lines = (d_pooled / lengths).astype(low_type)
        acts = [row_of(micro + m * parts + i) for i in range(parts)]
        acts = jnp.concatenate(acts, axis=1)
        high = acts.astype(low_type)
        rest = (acts - high.astype(full_type)).astype(low_type)
        down = down + dot_tn(lines, high) + dot_tn(lines, rest)
    down = down[:own] * inverse
    down_ref[...] = down
    squares = squares + add_up(down * down)

    ranked = ranked[:, :own] * inverse
    rounded = lambda ref, i: ref[i : i + 1].astype(low_type).astype(full_type)
    tied_gap = rounded(tied_ref, 0) - rounded(tied_ref, 1)

    def through(products):
        ones = jnp.ones((16, products.shape[1]), low_type)
        high = products.astype(low_type)
        rest = (products - high.astype(full_type)).astype(low_type)
        return (dot_nt(ones, high) + dot_nt(ones, rest))[0:1]

    weighed = lambda ref, total: ref.astype(low_type).astype(full_type) * total
    first = 0.0
    for p in range(pairs):
        source = sums[0][0] if p < pairs - 1 else sums[1][0]
        offset = p * 3 * LANES if p < pairs - 1 else 0
        for c in range(3):
            columns = slice(offset + c * LANES, offset + (c + 1) * LANES)
            first = first + weighed(in_ref[c, :, p * LANES : (p + 1) * LANES], source[:, columns])
    rows = [
        through(first) / rounded(gain_ref, 0),
        through(weighed(up_ref[...], sums[2][0])) / rounded(gain_ref, 1),
        tied_gap * ranked,
        rounded(gain_ref, 2) * ranked,
    ]
    place = lax.broadcasted_iota(jnp.int32, (8, own), 0)
    extra = jnp.zeros((8, own), full_type)
    for i, row in enumerate(rows):
        extra = jnp.where(place == i, row, extra)
    line_ref[...] = jnp.zeros_like(line_ref)
    line_ref[:8, :own] = extra
    line_ref[8:16] = jnp.broadcast_to(squares, (8, LANES))
    line_ref[16 : 16 + 2 * pairs] = table[: 2 * pairs]


def totals(
    small_all, ranks, vectors, grads, heads_in, hidden_in, gains, tied_rows, widths, micro, deps
):
    counts = tuple(len(group) for group in grads)
    flat = [array for group in grads for array in group]
    own, inner = hidden_in.shape
    down, line, *sums = call(
        functools.partial(
            total_kernel, len(small_all), counts, micro, heads_in.shape[2] // LANES
        ),
        "gradient_totals",
        [
            shape_of((own, inner), full_type),
            shape_of((24, LANES), full_type),
            *(shape_of((own, width), full_type) for width in widths),
        ],
        cost=(100, 10000),
        deps=deps,
    )(*small_all, *flat, ranks, vectors, heads_in, hidden_in, gains, tied_rows)
    return down, line, sums


def adam(weight, first_old, second, grad, factor, rate, decay, step_ref):
    clipped = grad * factor
    next_first = beta_first * first_old + (1.0 - beta_first) * clipped
    next_second = beta_second * second + (1.0 - beta_second) * clipped * clipped
    first_hat = next_first * step_ref[0]
    second_hat = next_second * step_ref[1]
    next_weight = weight - rate * (first_hat / (jnp.sqrt(second_hat) + adam_eps) + decay * weight)
    return next_weight, next_first, next_second


def square_kernel(heads, own_ref, other_ref, out_ref, extra_ref):
    place = lax.broadcasted_iota(jnp.int32, (8, LANES), 0)
    extra = own_ref[:8] + jnp.where(place < 2, other_ref[:8], 0.0)
    extra_ref[...] = extra
    counted = jnp.where(place == 3, 2.0, 1.0) * extra * extra
    add_up = lambda values: jnp.sum(values, axis=0, keepdims=True).sum(axis=1, keepdims=True)
    squares = own_ref[8:16] + other_ref[8:16] + add_up(counted)
    out_ref[:8] = squares
    tables = own_ref[16:24] * own_ref[16:24] + other_ref[16:24] * other_ref[16:24]
    out_ref[8:16] = own_ref[16:24]
    out_ref[16:24] = jnp.broadcast_to(add_up(tables), (8, LANES))


def update_kernel(squares, groups, pick_ref, step_ref, extra_ref, *refs):
    square_refs, refs = refs[:squares], refs[squares:]
    grad_refs, refs = refs[:groups], refs[groups:]
    state_refs, refs = refs[:21], refs[21:]
    norm_ref, *out_refs = refs
    tiles = stacked(square_refs)
    device = lax.broadcasted_iota(jnp.int32, (tiles.shape[0], 1, 1), 0)
    tables = jnp.sum(jnp.where(device == pick_ref[0], tiles[:, 8:24], 0.0), axis=0)
    norm = jnp.sqrt(jnp.sum(tiles[:, 0:8], axis=0)[0:1, 0:1] + tables[8:9, 0:1])
    norm_ref[...] = norm
    factor = jnp.minimum(1.0, clip_limit / (norm + 1e-06))
    weights, firsts, seconds = state_refs[:7], state_refs[7:14], state_refs[14:]
    next_weights, next_firsts, next_seconds = out_refs[:7], out_refs[7:14], out_refs[14:]

    def step(index, where, grad, rate, decay):
        results = adam(
            weights[index][where], firsts[index][where], seconds[index][where], grad, factor,
            rate, decay, step_ref,
        )
        for target, result in zip((next_weights, next_firsts, next_seconds), results):
            target[index][where] = result

    everything = (slice(None), slice(None))
    early_ref, late_ref, up_ref, down_ref = grad_refs
    pairs = weights[0].shape[2] // LANES
    for p in range(pairs):
        source, offset = (early_ref, p * 3) if p < pairs - 1 else (late_ref, 0)
        for c in range(3):
            columns = slice((offset + c) * LANES, (offset + c + 1) * LANES)
            where = (c, slice(None), slice(p * LANES, (p + 1) * LANES))
            step(0, where, source[:, columns], rate_matrix, decay_matrix)
    step(1, everything, early_ref[:, (pairs - 1) * 3 * LANES :], rate_matrix, decay_matrix)
    step(2, everything, up_ref[...], rate_matrix, decay_matrix)
    step(3, everything, down_ref[...], rate_matrix, decay_matrix)
    rows = weights[4].shape[1]
    extra = extra_ref[...]
    step(4, everything, extra[0:3, :rows], rate_vector, 0.0)
    tied = extra[3:4, :rows]
    step(5, everything, jnp.concatenate([tied, -tied], axis=0), rate_vector, 0.0)
    step(6, everything, tables[: 2 * pairs, :BUCKETS], rate_vector, 0.0)


def update(pick, corrections, extra, squares, grads, states):
    return call(
        functools.partial(update_kernel, len(squares), len(grads)),
        "update",
        [shape_of((1, 1), full_type)] + [shape_of(s.shape, full_type) for s in states],
        cost=(0, 6000),
        vmem=56,
        grid=(1,),
        in_specs=[
            on_scalars(),
            on_scalars(),
            *(whole(array.shape) for array in (extra, *squares, *grads, *states)),
        ],
    )(pick, corrections, extra, *squares, *grads, *states)


def body(
    tokens,
    pair_lengths,
    query_ids,
    distance_bucket,
    step_count,
    heads_in,
    heads_out,
    hidden_in,
    hidden_out,
    gains,
    tied_rows,
    bias_table,
    first_heads_in,
    first_heads_out,
    first_hidden_in,
    first_hidden_out,
    first_gains,
    first_tied,
    first_table,
    second_heads_in,
    second_heads_out,
    second_hidden_in,
    second_hidden_out,
    second_gains,
    second_tied,
    second_table,
):
    size = lax.axis_size("dp")
    me = lax.axis_index("dp")
    core = lax.axis_index("mp")
    micro, _, slot, width = tokens.shape
    count = micro * slot
    own, local_heads = heads_in.shape[0], bias_table.shape[1]
    head_width = heads_in.shape[2]
    inner = hidden_in.shape[1]
    pairs = local_heads // 2
    spans = 2 * (slot // LANES) - 1
    turn_matrix = lambda array: jnp.transpose(array, (1, 0, 2))
    heads_in, first_heads_in, second_heads_in = (
        turn_matrix(array) for array in (heads_in, first_heads_in, second_heads_in)
    )
    gains, tied_rows, bias_table = gains.T, tied_rows.T, bias_table.T
    first_gains, first_tied, first_table = first_gains.T, first_tied.T, first_table.T
    second_gains, second_tied, second_table = second_gains.T, second_tied.T, second_table.T

    packed_heads = call(
        pack_heads_kernel, "pack_heads", shape_of((own, 4 * head_width + LANES), low_type), vmem=56
    )(heads_in, heads_out, gains, tied_rows)
    packed_up, packed_down = call(
        pack_hidden_kernel, "pack_hidden", [shape_of((own, inner), low_type)] * 2
    )(hidden_in, hidden_out)
    pair_ids = jnp.bitwise_xor(me, jnp.array(block_masks(size), jnp.int32))
    place = (pair_ids[:, None] * own + jnp.arange(own, dtype=jnp.int32)[None, :]).reshape(width)
    order = (jnp.arange(width, dtype=jnp.int32)[:, None] == place[None, :]).astype(low_type)
    lengths = pair_lengths.reshape(micro)
    queries = query_ids[:, pair_ids]
    same_query = queries[:, :, None] == queries[:, None, :]
    padded = jnp.pad(queries, ((0, 0), (0, LANES - size)), constant_values=-1)
    same_tile = (queries[:, :, None] == padded[:, None, :]).astype(full_type)
    earlier = same_query & (pair_ids[None, :] < pair_ids[:, None])[None]
    positive_tile = jnp.where(jnp.any(earlier, axis=2), 0.0, 1.0)[:, :, None]
    positive_tile = jnp.broadcast_to(positive_tile, (micro, size, LANES))

    bucket_line = jnp.concatenate([distance_bucket, jnp.full((1,), -1, jnp.int32)])
    bucket_hot = (
        bucket_line[:, None] == jnp.arange(LANES, dtype=jnp.int32)[None, :]
    ).astype(low_type)
    lines = dot_nt(bias_table.astype(low_type), bucket_hot[:, :BUCKETS])
    lines = lines.reshape(pairs, 2, 2 * slot)
    hot_spans = jnp.stack([bucket_hot[d * LANES : (d + 2) * LANES] for d in range(spans)])

    step_float = step_count.astype(full_type)
    corrections = jnp.stack(
        [1.0 / (1.0 - beta_first**step_float), 1.0 / (1.0 - beta_second**step_float)]
    )
    first_place = jnp.sum(jnp.where(pair_ids == 0, jnp.arange(size, dtype=jnp.int32), 0)).reshape(1)

    rows_low = call(
        order_kernel,
        "order_tokens",
        shape_of((count, width), low_type),
        cost=(600, 5000),
        grid=(count // ROWS,),
        in_specs=[row_blocks((ROWS, width)), whole((width, width))],
        out_specs=row_blocks((ROWS, width)),
    )(tokens.reshape(count, width), order)
    if size != 16:
        weight_heads, weight_up, weight_down = (
            [gather_doubling(part, size)] for part in (packed_heads, packed_up, packed_down)
        )
        qkv, normed_first, vectors = project(rows_low, weight_heads, pairs, (same_tile, positive_tile, corrections))
    else:
        heads_line, packed_up, packed_down = join(
            line_parts(packed_heads, size, "heads"), passing=(packed_up, packed_down)
        )
        heads_sides = side_parts(heads_line, size, "heads")
        up_pair = join([packed_up, swap(packed_up, 8, size, "up")], deps=(rows_low,))
        up_near = swap(up_pair, 4, size, "up")
        low, high, packed_down = gather_step(*heads_sides, deps=(up_pair,), passing=(packed_down,))
        down_far = swap(packed_down, 8, size, "down")
        heads_corner = corner_parts(low, high, size, "heads_corner")
        up_line = join([up_pair, up_near], deps=(low,))
        down_pair = join([packed_down, down_far], deps=(up_line,))
        down_near = swap(down_pair, 4, size, "down")
        up_sides = side_parts(up_line, size, "up")
        weight_heads = [heads_line, *heads_sides, *heads_corner]
        qkv, normed_first, vectors = project(
            rows_low, weight_heads, pairs, (same_tile, positive_tile, down_pair, corrections, first_place)
        )
    filled = ()
    for pair in range(pairs):
        filled = attention(lengths, lines, qkv, pair, slot, before=filled)
        if pair == 0 and size == 16:
            down_line = join([down_pair, down_near], deps=(filled[0],))
            down_sides = side_parts(down_line, size, "down")
        if pair == 1 and size == 16:
            low, high = gather_step(*up_sides, deps=(filled[0],))
            up_corner = corner_parts(low, high, size, "up_corner")
            weight_up = [up_line, *up_sides, *up_corner]
    turned_first = call(turn_kernel, "turn", shape_of((width, count), low_type))(normed_first)
    attended, probs, inverse = filled
    branch = branch_rows(
        attended, weight_heads, (*down_sides, turned_first) if size == 16 else ()
    )
    if size == 16:
        low, high = gather_step(*down_sides, deps=(branch,))
        down_corner = corner_parts(low, high, size, "down_corner")
        weight_down = [down_line, *down_sides, *down_corner]
    branch_came = other_core(branch, "branch_other_core")
    normed_second, slope, act_sum, middle_sum = hidden(
        lengths, rows_low, branch, branch_came, vectors, weight_up, slot
    )
    down = call(
        pool_kernel,
        "pool",
        shape_of((8, width), full_type),
        cost=(20, 5000),
        scratch_shapes=[pltpu.VMEM((width, inner), low_type)],
    )(act_sum, *weight_down)
    small = call(
        margin_kernel,
        "margin",
        shape_of((8, width), full_type),
        grid=(1,),
        in_specs=[
            on_scalars(),
            *(whole(array.shape) for array in (down, down, middle_sum, act_sum, vectors)),
        ],
        out_specs=whole((8, width)),
    )(lengths, down, other_core(down, "pooled_part_other_core"), middle_sum, act_sum, vectors)
    small_all = gather_small(small, size, "small_sums")

    d_line, d_act, ranks, d_normed_second = rank_back(
        lengths, same_tile, positive_tile, vectors, slope, small_all, weight_down, weight_up, slot,
        (turned_first,),
    )
    d_normed_second_came = other_core(d_normed_second, "second_gradient_other_core")
    up_sum = Scatter(
        up_grad(normed_second, slope, d_act, piece_rows(size, width), slot), size, "up_gradient"
    )
    d_middle, d_attended, g_out = middle_back(
        lengths, rows_low, branch, branch_came, d_normed_second, d_normed_second_came, vectors,
        d_line, attended, inverse, weight_heads, slot,
    )
    up_sum.sides(deps=(d_attended,))
    filled, tables = (), []
    for pair in range(pairs - 1):
        d_project, table, *g_early = attention_back(
            probs, qkv, d_attended, attended, turned_first, hot_spans, piece_rows(size, width),
            pair, slot, own, grad_out=g_out if pair == pairs - 2 else None, before=filled,
        )
        filled = (d_project, *g_early)
        tables.append(table)
    up_sum.near(deps=(d_project,))
    early_sum = Scatter(g_early, size, "early_gradient")
    d_project, table, *g_late = attention_back(
        probs, qkv, d_attended, attended, turned_first, hot_spans, piece_rows(size, width),
        pairs - 1, slot, own, tables=tuple(tables), before=(d_project,), deps=up_sum.sources,
    )
    late_sum = Scatter(g_late, size, "late_gradient")
    early_sum.sides(deps=(table,))
    up_parts = up_sum.far(deps=(table, *early_sum.sources))
    d_normed_first = normed_back(d_project, weight_heads, (up_parts[0],))
    (d_normed_first,) = late_sum.sides(deps=(*early_sum.came, *up_parts[1:]), passing=(d_normed_first,))
    early_sum.near(deps=late_sum.sources)
    token_gradient, token_done = token_back(
        d_middle, d_normed_first, other_core(d_normed_first, "first_gradient_other_core"), rows_low,
        vectors, order, early_sum.sources,
    )
    early_parts = early_sum.far(deps=(token_done,))
    late_parts, _ = late_sum.line(deps=(early_parts[0],))

    g_down, line, grad_sums = totals(
        small_all, ranks, vectors, [early_parts, late_parts, up_parts], heads_in, hidden_in, gains, tied_rows,
        (head_width * 3, 3 * LANES, inner), micro, (),
    )
    square_tile, extra = call(
        functools.partial(square_kernel, local_heads),
        "squares",
        [shape_of((24, LANES), full_type), shape_of((8, LANES), full_type)],
    )(line, other_core(line, "totals_other_core"))
    squares_all = gather_small(square_tile, size, "squares")
    grads = [*grad_sums, g_down]
    weights = (heads_in, heads_out, hidden_in, hidden_out, gains, tied_rows, bias_table)
    firsts = (
        first_heads_in,
        first_heads_out,
        first_hidden_in,
        first_hidden_out,
        first_gains,
        first_tied,
        first_table,
    )
    seconds = (
        second_heads_in,
        second_heads_out,
        second_hidden_in,
        second_hidden_out,
        second_gains,
        second_tied,
        second_table,
    )
    states = (*weights, *firsts, *seconds)
    norm, *results = update(first_place, corrections, extra, squares_all, grads, states)
    for index in (0, 7, 14):
        results[index] = turn_matrix(results[index])
        for other in (4, 5, 6):
            results[index + other] = results[index + other].T
    return (norm.reshape(()), token_gradient.reshape(tokens.shape), *results)


def solution(mesh):
    in_specs = (
        P(None, "dp", None, None),
        P(None, "dp"),
        P(),
        P(),
        P(),
        P("dp", None, "mp"),
        P("dp", "mp"),
        P("dp", "mp"),
        P("dp", "mp"),
        P("dp", None),
        P("dp", None),
        P(None, "mp"),
        P("dp", None, "mp"),
        P("dp", "mp"),
        P("dp", "mp"),
        P("dp", "mp"),
        P("dp", None),
        P("dp", None),
        P(None, "mp"),
        P("dp", None, "mp"),
        P("dp", "mp"),
        P("dp", "mp"),
        P("dp", "mp"),
        P("dp", None),
        P("dp", None),
        P(None, "mp"),
    )
    out_specs = (
        P(),
        P(None, "dp", None, None),
        P("dp", None, "mp"),
        P("dp", "mp"),
        P("dp", "mp"),
        P("dp", "mp"),
        P("dp", None),
        P("dp", None),
        P(None, "mp"),
        P("dp", None, "mp"),
        P("dp", "mp"),
        P("dp", "mp"),
        P("dp", "mp"),
        P("dp", None),
        P("dp", None),
        P(None, "mp"),
        P("dp", None, "mp"),
        P("dp", "mp"),
        P("dp", "mp"),
        P("dp", "mp"),
        P("dp", None),
        P("dp", None),
        P(None, "mp"),
    )
    return jax.shard_map(body, mesh=mesh, in_specs=in_specs, out_specs=out_specs, check_vma=False)
```

```python
import functools

import jax
import jax.numpy as jnp
from jax import lax
from jax.experimental import pallas as pl
from jax.experimental.pallas import tpu as pltpu
from jax.sharding import PartitionSpec as P

BUCKETS = 32
LOSS_SCALE = 1024
LANES = 128
ROWS = 256
SPAN = 512

norm_eps = 1e-06
clip_limit = 0.01
beta_first = 0.9
beta_second = 0.999
adam_eps = 1e-08
rate_matrix = 0.03
rate_vector = 0.25
decay_matrix = 0.1
masked_score = -1e30
gelu_slope = 0.7978845608028654
gelu_cubic = 0.044715
low_type = jnp.bfloat16
full_type = jnp.float32
core_swap = [(0, 1), (1, 0)]


def rms_scale(rows_in):
    return lax.rsqrt(jnp.mean(rows_in * rows_in, axis=-1, keepdims=True) + norm_eps)


def norm_input_grad(d_normed, gain_row, rows_in, norm_scale):
    weighted = d_normed * gain_row
    return norm_scale * weighted - rows_in * norm_scale**3 * jnp.mean(
        weighted * rows_in, axis=-1, keepdims=True
    )


def dot_nt(left, right):
    return lax.dot_general(left, right, (((1,), (1,)), ((), ())), preferred_element_type=full_type)


def dot_tn(left, right):
    return lax.dot_general(left, right, (((0,), (0,)), ((), ())), preferred_element_type=full_type)


def dot_nn(left, right):
    return lax.dot_general(left, right, (((1,), (0,)), ((), ())), preferred_element_type=full_type)


def call(
    kernel, name, out_shape, cost=(0, 0), vmem=16, deps=(), passing=(), in_specs=None,
    out_specs=None, input_output_aliases=None, **options
):
    single = not isinstance(out_shape, (list, tuple))
    out_shapes = [out_shape] if single else list(out_shape)
    outputs, extra = len(out_shapes), len(deps) + len(passing)

    def apply(*operands):
        inputs = len(operands)
        if in_specs is None:
            options["grid"] = (1,)
        specs = [whole(operand.shape) for operand in operands] if in_specs is None else in_specs
        targets = out_specs or [whole(shape.shape) for shape in out_shapes]
        targets = targets if isinstance(targets, (list, tuple)) else [targets]
        aliases = dict(input_output_aliases or {})
        for i in range(len(passing)):
            aliases[inputs + len(deps) + i] = outputs + i

        def run(*refs):
            own = inputs + extra
            kernel(*refs[:inputs], *refs[own : own + outputs], *refs[own + outputs + len(passing) :])

        results = pl.pallas_call(
            run,
            out_shape=[*out_shapes, *(shape_of(a.shape, a.dtype) for a in passing)],
            in_specs=[*specs, *[in_place()] * extra],
            out_specs=[*targets, *[in_place()] * len(passing)],
            input_output_aliases=aliases,
            compiler_params=pltpu.CompilerParams(vmem_limit_bytes=vmem * 1024 * 1024),
            cost_estimate=pl.CostEstimate(
                flops=int(cost[0] * 2e6), bytes_accessed=int(cost[1] * 1e3), transcendentals=0
            ),
            name=name,
            **options,
        )(*operands, *deps, *passing)
        return results[0] if single and not passing else results

    return apply


def in_place():
    return pl.BlockSpec(memory_space=pl.ANY)


def shape_of(shape, dtype):
    return jax.ShapeDtypeStruct(tuple(shape), dtype)


def whole(shape):
    return pl.BlockSpec(tuple(shape), lambda *_: (0,) * len(shape))


def on_scalars():
    return pl.BlockSpec(memory_space=pltpu.SMEM)


def row_blocks(shape, step=0):
    return pl.BlockSpec(tuple(shape), lambda i: (i,) + (0,) * (len(shape) - 1))


def column_blocks(shape, offset=0):
    return pl.BlockSpec(tuple(shape), lambda i: (0,) * (len(shape) - 1) + (i + offset,))


def fill_rows(target, pieces, columns=slice(None)):
    start = 0
    for piece in pieces:
        rows = piece.shape[0]
        target[start : start + rows, :] = piece[:, columns]
        start += rows


def spill_rows(value, pieces, first=0):
    start = 0
    for piece in pieces:
        rows = piece.shape[0]
        low, high = max(start, first), min(start + rows, first + value.shape[0])
        if low < high:
            piece[low - start : high - start] = value[low - first : high - first].astype(piece.dtype)
        start += rows


def swap(array, mask, size, label="exchange"):
    with jax.named_scope(f"{label}_across_{mask}"):
        return lax.ppermute(array, "dp", [(i, i ^ mask) for i in range(size)])


def tie(arrays, deps):
    return call(lambda: None, "tie", [], deps=deps, passing=arrays, in_specs=[], grid=(1,))()


def other_core(array, label="other_core"):
    with jax.named_scope(label):
        return lax.ppermute(array, "mp", core_swap)


def stage_bits(size):
    if size == 16:
        return (8, 4, 2, 1)
    return tuple(1 << i for i in range(size.bit_length() - 1))


def block_masks(size):
    bits = stage_bits(size)
    return [sum(bit for i, bit in enumerate(bits) if k >> i & 1) for k in range(size)]


def piece_rows(size, width):
    if size != 16:
        return [width]
    return [width // 4] * 3 + [width // 8] * 2


def join_kernel(*refs):
    *part_refs, out_ref = refs
    start = 0
    for part in part_refs:
        rows = part.shape[0]
        out_ref[start : start + rows] = part[...]
        start += rows


def join(parts, **options):
    rows = sum(part.shape[0] for part in parts)
    return call(
        join_kernel, "join", shape_of((rows, *parts[0].shape[1:]), parts[0].dtype), **options
    )(*parts)


def step_kernel(groups, y_ref, x_ref, *refs):
    part_refs, (low_ref, high_ref, *joined_refs) = refs[: sum(groups)], refs[sum(groups) :]
    low_ref[...] = y_ref[...]
    high_ref[...] = x_ref[...]
    for group, joined_ref in zip(groups, joined_refs):
        join_kernel(*part_refs[:group], joined_ref)
        part_refs = part_refs[group:]


def gather_step(across_y, across_x, *groups, **options):
    half = (across_y.shape[0] // 2, across_y.shape[1])
    shapes = [shape_of(half, across_y.dtype)] * 2
    for parts in groups:
        shapes.append(shape_of((sum(p.shape[0] for p in parts), parts[0].shape[1]), parts[0].dtype))
    flat = [part for parts in groups for part in parts]
    return call(
        functools.partial(step_kernel, tuple(len(parts) for parts in groups)),
        "gather_step",
        shapes,
        grid=(1,),
        in_specs=[
            pl.BlockSpec(half, lambda i: (0, 0)),
            pl.BlockSpec(half, lambda i: (1, 0)),
            *(whole(part.shape) for part in flat),
        ],
        out_specs=[whole(shape.shape) for shape in shapes],
        **options,
    )(across_y, across_x, *flat)


def line_parts(part, size, label):
    return [part] + [swap(part, mask, size, label) for mask in (8, 4, 12)]


def side_parts(quarter, size, label):
    return [swap(quarter, mask, size, label) for mask in (2, 1)]


def corner_parts(low, high, size, label):
    return [swap(low, 1, size, label), swap(high, 2, size, label)]


def gather_doubling(part, size):
    for bit in stage_bits(size):
        part = jnp.concatenate([part, swap(part, bit, size)], axis=0)
    return part


def small_line(part, size, label):
    if size != 16:
        return part[None]
    return join(line_parts(part[None], size, label))


def small_plane(quarter, size, label):
    if size != 16:
        return [gather_doubling(quarter, size)]
    return [quarter] + [swap(quarter, mask, size, label) for mask in (2, 1, 3)]


def stacked(refs):
    return jnp.concatenate([ref[...] for ref in refs], axis=0)


def stacked_row(refs, row):
    return jnp.concatenate([ref[:, row, :] for ref in refs], axis=0)


def gather_small(part, size, label):
    return small_plane(small_line(part, size, label), size, label)


def plane_sum_kernel(*refs):
    count = len(refs) // 6
    for i in range(count):
        y_ref, x_ref, low_ref, high_ref = refs[4 * i : 4 * i + 4]
        y_out, x_out = refs[4 * count + 2 * i : 4 * count + 2 * i + 2]
        half = low_ref.shape[0]
        y_out[:half] = (y_ref[:half].astype(full_type) + low_ref[...].astype(full_type)).astype(
            low_type
        )
        y_out[half:] = y_ref[half:]
        x_out[:half] = x_ref[:half]
        x_out[half:] = (x_ref[half:].astype(full_type) + high_ref[...].astype(full_type)).astype(
            low_type
        )


def line_sum_kernel(*refs):
    count = sum(ref.shape[0] == refs[0].shape[0] for ref in refs)
    add_refs, out_refs = refs[:count], refs[count:]
    rows = out_refs[0].shape[0]
    for i, out_ref in enumerate(out_refs):
        span = slice(i * rows, (i + 1) * rows)
        total = add_refs[0][span].astype(full_type)
        for ref in add_refs[1:]:
            total = total + ref[span].astype(full_type)
        out_ref[...] = total.astype(out_ref.dtype)


class Scatter:
    def __init__(self, pieces, size, label):
        self.pieces, self.size, self.label = pieces, size, label
        self.sources, self.came = (), ()
        if size == 16:
            *self.pieces, low, high = pieces
            self.came = [swap(low, 1, size, label), swap(high, 2, size, label)]

    def near(self, deps=(), passing=()):
        if self.size != 16:
            return passing
        keep = self.pieces[0]
        half = (keep.shape[0] // 2, keep.shape[1])
        kept, sent, *passed = call(
            line_sum_kernel,
            "line_sum",
            [shape_of(half, full_type), shape_of(half, low_type)],
            deps=deps,
            passing=passing,
        )(keep, *self.came)
        self.sources, self.came, self.pieces = (sent,), [swap(sent, 4, self.size, self.label)], [kept]
        return passed

    def far(self, deps=()):
        if self.size != 16:
            return self.line(deps)[0]
        kept = self.pieces[0]
        half = (kept.shape[0] // 2, kept.shape[1])
        own, sent = call(
            line_sum_kernel,
            "line_sum",
            [shape_of(half, full_type), shape_of(half, low_type)],
            deps=deps,
        )(kept, *self.came)
        self.sources = (sent,)
        return [own, swap(sent, 8, self.size, self.label)]

    def line(self, deps=(), passing=()):
        size, label = self.size, self.label
        if size != 16:
            grad = self.pieces[0]
            for bit in reversed(stage_bits(size)):
                half = grad.shape[0] // 2
                came = swap(grad[half:], bit, size, label)
                grad = (grad[:half].astype(full_type) + came.astype(full_type)).astype(low_type)
            return [grad.astype(full_type)], passing
        keep = self.pieces[0]
        part = (keep.shape[0] // 4, keep.shape[1])
        own, *others = call(
            line_sum_kernel,
            "line_sum",
            [shape_of(part, full_type)] + [shape_of(part, low_type)] * 3,
            deps=deps,
            passing=passing,
        )(keep, *self.came)
        came = [swap(other, mask, size, label) for other, mask in zip(others, (8, 4, 12))]
        return [own] + came, others[3:]


def scatter_sides(scatters, deps=()):
    if scatters[0].size != 16:
        return ()
    sides = [part for scatter in scatters for part in scatter.pieces[1:]]
    operands = [part for s in scatters for part in (*s.pieces[1:], *s.came)]
    sums = call(
        plane_sum_kernel, "plane_sum", [shape_of(part.shape, low_type) for part in sides], deps=deps
    )(*operands)
    for i, scatter in enumerate(scatters):
        to_y, to_x = sums[2 * i : 2 * i + 2]
        scatter.came = [
            swap(to_y, 2, scatter.size, scatter.label), swap(to_x, 1, scatter.size, scatter.label)
        ]
    return tuple(sums)


def pack_heads_kernel(in_ref, out_ref, gain_ref, tied_ref, a_ref):
    parts, rows, width = in_ref.shape
    for c in range(parts):
        a_ref[:, c * width : (c + 1) * width] = in_ref[c].astype(low_type)
    a_ref[:, parts * width : (parts + 1) * width] = out_ref[...].astype(low_type)
    gains, tied = gain_ref[...], tied_ref[...]
    vectors = few_rows([gains[i : i + 1] for i in range(3)] + [tied[i : i + 1] for i in range(2)], 16)
    pick = lax.broadcasted_iota(jnp.int32, (16, LANES), 0) == lax.broadcasted_iota(
        jnp.int32, (16, LANES), 1
    )
    extra = dot_tn(vectors.astype(low_type), jnp.where(pick, 1.0, 0.0).astype(low_type))
    a_ref[:, (parts + 1) * width :] = extra.astype(low_type)


def pack_hidden_kernel(up_ref, down_ref, b_ref, c_ref):
    b_ref[...] = up_ref[...].astype(low_type)
    c_ref[...] = down_ref[...].astype(low_type)


def order_kernel(x_ref, order_ref, out_ref):
    out_ref[...] = dot_nn(x_ref[...], order_ref[...]).astype(low_type)


def turn_kernel(x_ref, out_ref):
    out_ref[...] = x_ref[...].T


def head_lanes():
    lane = lax.broadcasted_iota(jnp.int32, (1, LANES), 1)
    return [lane < LANES // 2, lane >= LANES // 2]


def project_kernel(pieces, pairs, x_ref, *refs):
    weight_refs, (qkv_ref, normed_ref, vector_ref, w_ref) = refs[:pieces], refs[pieces:]
    parts = qkv_ref.shape[1]
    in_width = pairs * parts * LANES

    @pl.when(pl.program_id(0) == 0)
    def assemble():
        fill_rows(w_ref, weight_refs)
        pick = lax.broadcasted_iota(jnp.int32, (16, LANES), 0) == lax.broadcasted_iota(
            jnp.int32, (16, LANES), 1
        )
        vectors = dot_nt(jnp.where(pick, 1.0, 0.0).astype(low_type), w_ref[:, -LANES:])
        vector_ref[...] = vectors[:8]

    x = x_ref[...].astype(full_type)
    normed = (x * rms_scale(x) * vector_ref[0:1]).astype(low_type)
    normed_ref[...] = normed
    projected = dot_nn(normed, w_ref[:, :in_width]).astype(low_type)
    for c in range(parts):
        for p in range(pairs):
            start = (c * pairs + p) * LANES
            qkv_ref[p, c] = projected[:, start : start + LANES]


def project(rows_low, weights, pairs, deps):
    count, width = rows_low.shape
    parts = 3
    return call(
        functools.partial(project_kernel, len(weights), pairs),
        "projection",
        [
            shape_of((pairs, parts, count, LANES), low_type),
            shape_of((count, width), low_type),
            shape_of((8, width), full_type),
        ],
        deps=deps,
        grid=(count // ROWS,),
        in_specs=[row_blocks((ROWS, width)), *(whole(piece.shape) for piece in weights)],
        out_specs=[
            pl.BlockSpec((pairs, parts, ROWS, LANES), lambda i: (0, 0, i, 0)),
            row_blocks((ROWS, width)),
            whole((8, width)),
        ],
        scratch_shapes=[pltpu.VMEM((width, weights[0].shape[1]), low_type)],
    )(rows_low, *weights)


def attention_kernel(len_ref, line_ref, qkv_ref, *refs):
    att_ref, prob_ref, inv_ref, tile_ref = refs[-4:]
    micro, slot = prob_ref.shape[1], prob_ref.shape[3]
    blocks = slot // LANES
    lanes = head_lanes()
    for h in range(2):
        for d in range(2 * blocks - 1):
            piece = jnp.broadcast_to(
                line_ref[0, h : h + 1, d * LANES : (d + 2) * LANES], (LANES, 2 * LANES)
            )
            turned = pltpu.roll(piece, LANES + 1, 1, stride=1, stride_axis=0)
            tile_ref[h, d] = turned[:, :LANES]

    def micro_step(m, carry):
        start = pl.multiple_of(m * slot, slot)
        key_valid = lax.broadcasted_iota(jnp.int32, (1, slot), 1) < len_ref[m]
        keys = qkv_ref[0, 1, pl.ds(start, slot), :]
        values = qkv_ref[0, 2, pl.ds(start, slot), :]
        values = jnp.concatenate([values, jnp.ones_like(values)], axis=1)
        for r in range(slot // ROWS):
            rows = pl.ds(start + r * ROWS, ROWS)
            queries = qkv_ref[0, 0, rows, :]
            queries = jnp.concatenate(
                [queries * lanes[h].astype(low_type) for h in range(2)], axis=0
            )
            first = r * (ROWS // LANES)
            bias = jnp.concatenate(
                [
                    jnp.concatenate(
                        [tile_ref[h, j - first - i + blocks - 1] for j in range(blocks)], axis=1
                    )
                    for h in range(2)
                    for i in range(ROWS // LANES)
                ],
                axis=0,
            )
            scores = dot_nt(queries, keys)
            scores = jnp.where(key_valid, scores + bias, masked_score)
            terms = jnp.exp(scores - jnp.max(scores, axis=1, keepdims=True)).astype(low_type)
            for h in range(2):
                prob_ref[0, m, h, r * ROWS : (r + 1) * ROWS, :] = terms[h * ROWS : (h + 1) * ROWS]
            mixed = dot_nn(terms, values)
            inverse = 1.0 / mixed[:, LANES:]
            mixed = mixed[:, :LANES] * inverse
            att_ref[rows, :] = jnp.where(lanes[0], mixed[:ROWS], mixed[ROWS:]).astype(low_type)
            inv_ref[rows, :] = jnp.where(lanes[0], inverse[:ROWS], inverse[ROWS:])
        return carry

    lax.fori_loop(0, micro, micro_step, 0)


def attention(lengths, lines, qkv, pair, slot, before=(), deps=()):
    pairs, parts, count, _ = qkv.shape
    micro = count // slot
    spans = 2 * (slot // LANES) - 1
    column = pl.BlockSpec((count, LANES), lambda i: (0, pair))
    return call(
        attention_kernel,
        "attention_forward",
        [
            shape_of((count, pairs * LANES), low_type),
            shape_of((pairs, micro, 2, slot, slot), low_type),
            shape_of((count, pairs * LANES), full_type),
        ],
        deps=deps,
        grid=(1,),
        in_specs=[
            on_scalars(),
            pl.BlockSpec((1, 2, lines.shape[2]), lambda i: (pair, 0, 0)),
            pl.BlockSpec((1, parts, count, LANES), lambda i: (pair, 0, 0, 0)),
            *[in_place()] * len(before),
        ],
        out_specs=[
            column,
            pl.BlockSpec((1, micro, 2, slot, slot), lambda i: (pair, 0, 0, 0, 0)),
            column,
        ],
        input_output_aliases={3 + i: i for i in range(len(before))},
        scratch_shapes=[pltpu.VMEM((2, spans, LANES, LANES), full_type)],
    )(lengths, lines, qkv, *before)


def branch_kernel(att_ref, *refs):
    *weight_refs, out_ref, w_ref = refs

    @pl.when(pl.program_id(0) == 0)
    def assemble():
        fill_rows(w_ref, weight_refs)

    out_ref[...] = dot_nt(att_ref[...], w_ref[...]).astype(low_type)


def branch_rows(attended, weights, deps=()):
    count, head_width = attended.shape
    width = sum(piece.shape[0] for piece in weights)
    return call(
        branch_kernel,
        "branch",
        shape_of((count, width), low_type),
        deps=deps,
        grid=(count // (2 * ROWS),),
        in_specs=[
            row_blocks((2 * ROWS, head_width)),
            *(pl.BlockSpec((piece.shape[0], head_width), lambda i: (0, 3)) for piece in weights),
        ],
        out_specs=row_blocks((2 * ROWS, width)),
        scratch_shapes=[pltpu.VMEM((width, head_width), low_type)],
    )(attended, *weights)


def hidden_kernel(pieces, len_ref, x_ref, own_ref, came_ref, vector_ref, *refs):
    weight_refs, refs = refs[:pieces], refs[pieces:]
    normed_ref, slope_ref, act_ref, sum_ref, w_ref = refs
    m = pl.program_id(0)
    slot = x_ref.shape[0]

    @pl.when(m == 0)
    def assemble():
        fill_rows(w_ref, weight_refs)

    middle = middle_rows(x_ref, own_ref, came_ref)
    normed = (middle * rms_scale(middle) * vector_ref[1:2]).astype(low_type)
    valid = lax.broadcasted_iota(jnp.int32, (slot, 1), 0) < len_ref[m]
    normed_ref[...] = jnp.where(valid, normed, jnp.zeros_like(normed))
    counted = lax.broadcasted_iota(jnp.int32, (16, slot), 1) < len_ref[m]
    counted = jnp.where(counted, 1.0, 0.0).astype(low_type)
    sum_ref[0] = jnp.sum(jnp.where(valid, middle, 0.0), axis=0, keepdims=True)
    v = dot_nn(normed, w_ref[...])
    square = v * v
    gate = jnp.tanh(v * (gelu_slope + (gelu_slope * gelu_cubic) * square))
    half = 0.5 + 0.5 * gate
    active = (v * half).astype(low_type)
    act_ref[0] = dot_nn(counted, active)[0:1]
    inner = 0.5 * gelu_slope + (1.5 * gelu_slope * gelu_cubic) * square
    slope_ref[...] = (half + v * (1.0 - gate * gate) * inner).astype(low_type)


def middle_rows(x_ref, own_ref, came_ref):
    branch = own_ref[...].astype(full_type) + came_ref[...].astype(full_type)
    return x_ref[...].astype(full_type) + branch


def hidden(lengths, rows_low, own, came, vectors, weights, slot):
    count, width = rows_low.shape
    micro = count // slot
    inner = weights[0].shape[1]
    return call(
        functools.partial(hidden_kernel, len(weights)),
        "hidden_forward",
        [
            shape_of((count, width), low_type),
            shape_of((count, inner), low_type),
            shape_of((micro, 1, inner), full_type),
            shape_of((micro, 1, width), full_type),
            shape_of((width, inner), low_type),
        ],
        cost=(1200, 20000),
        grid=(micro,),
        in_specs=[
            on_scalars(),
            *[row_blocks((slot, width))] * 3,
            whole(vectors.shape),
            *(whole(piece.shape) for piece in weights),
        ],
        out_specs=[
            row_blocks((slot, width)),
            row_blocks((slot, inner)),
            row_blocks((1, 1, inner)),
            row_blocks((1, 1, width)),
            whole((width, inner)),
        ],
    )(lengths, rows_low, own, came, vectors, *weights)


def few_rows(rows, count):
    place = lax.broadcasted_iota(jnp.int32, (count, rows[0].shape[1]), 0)
    total = jnp.zeros(place.shape, full_type)
    for i, row in enumerate(rows):
        total = jnp.where(place == i, row, total)
    return total


def pool_kernel(act_ref, *refs):
    *weight_refs, out_ref, w_ref = refs
    fill_rows(w_ref, weight_refs)
    sums = [act_ref[m] for m in range(act_ref.shape[0])]
    highs = [row.astype(low_type).astype(full_type) for row in sums]
    rests = [row - high for row, high in zip(sums, highs)]
    down = dot_nt(few_rows(highs + rests, 16).astype(low_type), w_ref[...])
    micro = len(sums)
    out_ref[...] = few_rows([down[m : m + 1] + down[micro + m : micro + m + 1] for m in range(micro)], 8)


def margin_kernel(len_ref, own_ref, other_ref, sum_ref, act_ref, vector_ref, send_ref):
    margins, rows = [], []
    for m in range(sum_ref.shape[0]):
        length = len_ref[m].astype(full_type)
        total = own_ref[m : m + 1] + other_ref[m : m + 1] + sum_ref[m]
        pooled = (total / length).astype(low_type).astype(full_type)
        final = pooled * rms_scale(pooled) * vector_ref[2:3]
        logits = [
            jnp.sum(final * vector_ref[i : i + 1], axis=1, keepdims=True) * pooled.shape[1] ** (-0.5)
            for i in (3, 4)
        ]
        lane = lax.broadcasted_iota(jnp.int32, pooled.shape, 1)
        margins.append(jnp.where(lane < LANES, logits[0] - logits[1], length))
        rows.append(pooled)
    width = rows[0].shape[1]
    for m in range(sum_ref.shape[0]):
        sums = act_ref[m]
        rows += [sums[:, i * width : (i + 1) * width] for i in range(sums.shape[1] // width)]
    send_ref[...] = few_rows(rows + margins, 8)


def ranking(margins, same, positive):
    place = lax.broadcasted_iota(jnp.int32, margins.shape, 0)
    lane = lax.broadcasted_iota(jnp.int32, margins.shape, 1)
    others = jnp.sum(jnp.where(place == lane, margins, 0.0), axis=0, keepdims=True)
    row_max = jnp.max(jnp.where(same, others, masked_score), axis=1, keepdims=True)
    terms = jnp.where(same, jnp.exp(jnp.where(same, others - row_max, 0.0)), 0.0)
    chance = jnp.exp(margins - row_max) / jnp.sum(terms, axis=1, keepdims=True)
    return LOSS_SCALE * (chance - positive)


def pooled_grad(pooled, d_margin, vector_ref):
    scale = rms_scale(pooled)
    d_logit = d_margin * pooled.shape[1] ** (-0.5)
    d_final = d_logit * (vector_ref[3:4] - vector_ref[4:5])
    return norm_input_grad(d_final, vector_ref[2:3], pooled, scale)


def rank_kernel(
    small_pieces, len_ref, same_ref, positive_ref, vector_ref, slope_ref, down_ref, up_ref, *refs
):
    small_refs, refs = refs[:small_pieces], refs[small_pieces:]
    line_ref, act_ref, rank_ref, hidden_ref, d_ref = refs
    m = pl.program_id(0)

    @pl.when(m == 0)
    def rank():
        lines = []
        for i in range(2):
            margins = stacked_row(small_refs, 6 + i)[:, :LANES]
            d_margins = ranking(margins, same_ref[i] > 0.5, positive_ref[i])
            rank_ref[i] = d_margins
            pooled = small_refs[0][0, i : i + 1, :]
            d_pooled = pooled_grad(pooled, d_margins[0:1, 0:1], vector_ref)
            lines.append(d_pooled / len_ref[i].astype(full_type))
        line_ref[...] = few_rows(lines, 8)
        d_act = dot_nn(few_rows(lines, 16).astype(low_type), down_ref[...])
        act_ref[...] = d_act[:8]

    d_row = jnp.where(m == 0, act_ref[0:1], act_ref[1:2])
    d_hidden = (slope_ref[...].astype(full_type) * d_row).astype(low_type)
    hidden_ref[...] = d_hidden
    d_normed = dot_nt(d_hidden, up_ref[...])
    valid = lax.broadcasted_iota(jnp.int32, (d_normed.shape[0], 1), 0) < len_ref[m]
    d_ref[...] = jnp.where(valid, d_normed, 0.0).astype(low_type)


def rank_back(lengths, same, positive, vectors, slope, small_all, down, up, slot, deps):
    count, inner = slope.shape
    width = vectors.shape[1]
    return call(
        functools.partial(rank_kernel, len(small_all)),
        "rank_backward",
        [
            shape_of((8, width), full_type),
            shape_of((8, inner), full_type),
            shape_of(positive.shape, full_type),
            shape_of((count, inner), low_type),
            shape_of((count, width), low_type),
        ],
        cost=(1200, 20000),
        deps=deps,
        grid=(count // slot,),
        in_specs=[
            on_scalars(),
            *(whole(array.shape) for array in (same, positive, vectors)),
            row_blocks((slot, inner)),
            *(whole(array.shape) for array in (down, up, *small_all)),
        ],
        out_specs=[
            whole((8, width)),
            whole((8, inner)),
            whole(positive.shape),
            row_blocks((slot, inner)),
            row_blocks((slot, width)),
        ],
    )(lengths, same, positive, vectors, slope, down, up, *small_all)


def up_grad_kernel(normed_ref, d_ref, *out_refs):
    for n in range(normed_ref.shape[1] // ROWS):
        columns = slice(n * ROWS, (n + 1) * ROWS)
        spill_rows(dot_tn(normed_ref[:, columns], d_ref[...]), out_refs, n * ROWS)


def up_grad(normed, d_hidden, rows):
    return call(
        up_grad_kernel,
        "hidden_in_gradient",
        [shape_of((r, d_hidden.shape[1]), low_type) for r in rows],
        cost=(1200, 15000),
    )(normed, d_hidden)


def middle_kernel(
    pieces, len_ref, x_ref, branch_ref, other_ref, own_ref, came_ref, vector_ref, line_ref,
    att_ref, inv_ref, *refs
):
    weight_refs, refs = refs[:pieces], refs[pieces:]
    d_ref, d_att_ref, total_ref, w_ref = refs
    m = pl.program_id(0)

    @pl.when(m == 0)
    def assemble():
        fill_rows(w_ref, weight_refs)
        total_ref[...] = jnp.zeros_like(total_ref)

    middle = middle_rows(x_ref, branch_ref, other_ref)
    own = own_ref[...].astype(full_type)
    scale = rms_scale(middle)
    valid = lax.broadcasted_iota(jnp.int32, (middle.shape[0], 1), 0) < len_ref[m]
    line = jnp.where(m == 0, line_ref[0:1], line_ref[1:2])
    d_middle = jnp.where(valid, line, 0.0) + norm_input_grad(
        own + came_ref[...].astype(full_type), vector_ref[1:2], middle, scale
    )
    d_ref[...] = d_middle
    d_low = d_middle.astype(low_type)
    d_att_ref[...] = (dot_nn(d_low, w_ref[...]) * inv_ref[...]).astype(low_type)
    total_ref[...] += dot_tn(d_low, att_ref[...])


def middle_back(
    lengths, rows_low, branch, other, own, came, vectors, lines, attended, inverse, weights, slot
):
    count, width = rows_low.shape
    head_width = attended.shape[1]
    return call(
        functools.partial(middle_kernel, len(weights)),
        "middle_backward",
        [
            shape_of((count, width), full_type),
            shape_of((count, head_width), low_type),
            shape_of((width, head_width), full_type),
        ],
        cost=(600, 15000),
        grid=(count // slot,),
        in_specs=[
            on_scalars(),
            *[row_blocks((slot, width))] * 5,
            whole(vectors.shape),
            whole(lines.shape),
            row_blocks((slot, head_width)),
            row_blocks((slot, head_width)),
            *(
                pl.BlockSpec((piece.shape[0], head_width), lambda i: (0, 3)) for piece in weights
            ),
        ],
        out_specs=[
            row_blocks((slot, width)),
            row_blocks((slot, head_width)),
            whole((width, head_width)),
        ],
        scratch_shapes=[pltpu.VMEM((width, head_width), low_type)],
    )(
        lengths, rows_low, branch, other, own, came, vectors, lines, attended, inverse, *weights
    )


def attention_back_kernel(
    befores, grads, tables, own, prob_ref, qkv_ref, d_ref, att_ref, turned_ref, hot_ref, *refs
):
    table_refs, refs = refs[:tables], refs[tables:]
    grad_refs, refs = refs[:grads], refs[grads:]
    d_out_ref, table_ref, *out_refs, tile_ref, dk_ref, dv_ref = refs[befores:]
    step = pl.program_id(0)

    if grads:

        @pl.when(step > 0)
        def projection():
            spill_rows(grad_refs[0][...], out_refs)

    @pl.when(step == 0)
    def heads():
        pair_back(
            prob_ref, qkv_ref, d_ref, att_ref, turned_ref, hot_ref, d_out_ref, table_ref, out_refs,
            tile_ref, dk_ref, dv_ref
        )
        if tables:
            lines = [ref[0, h : h + 1] for ref in (*table_refs, table_ref) for h in range(2)]
            width = turned_ref.shape[0]
            place = lax.broadcasted_iota(jnp.int32, (width, 16), 0) % own
            pick = place == lax.broadcasted_iota(jnp.int32, (width, 16), 1)
            pick = jnp.where(pick, 1.0, 0.0).astype(low_type)
            spread = dot_nn(pick, few_rows(lines, 16).astype(low_type))
            spill_rows(spread, [ref.at[:, 3 * LANES :] for ref in out_refs])


def pair_back(
    prob_ref, qkv_ref, d_ref, att_ref, turned_ref, hot_ref, d_out_ref, table_ref, out_refs,
    tile_ref, dk_ref, dv_ref
):
    micro, slot = prob_ref.shape[1], prob_ref.shape[3]
    blocks = slot // LANES
    spans = 2 * blocks - 1
    lanes = head_lanes()

    tile_ref[...] = jnp.zeros_like(tile_ref)

    def micro_step(m, carry):
        start = pl.multiple_of(m * slot, slot)
        everything = pl.ds(start, slot)
        keys, values = qkv_ref[0, 1, everything, :], qkv_ref[0, 2, everything, :]
        for r in range(slot // SPAN):
            rows = pl.ds(start + r * SPAN, SPAN)
            queries = qkv_ref[0, 0, rows, :]
            queries = jnp.concatenate(
                [queries * lanes[h].astype(low_type) for h in range(2)], axis=0
            )
            d_att = d_ref[rows, :]
            product = d_att.astype(full_type) * att_ref[rows, :].astype(full_type)
            row_dot = jnp.concatenate(
                [
                    jnp.sum(jnp.where(lanes[h], product, 0.0), axis=1, keepdims=True)
                    for h in range(2)
                ],
                axis=0,
            )
            d_att = jnp.concatenate([d_att * lanes[h].astype(low_type) for h in range(2)], axis=0)
            span = slice(r * SPAN, (r + 1) * SPAN)
            probs = jnp.concatenate([prob_ref[0, m, h, span, :] for h in range(2)], axis=0)
            d_scores = probs.astype(full_type) * (dot_nt(d_att, values) - row_dot)
            d_low = d_scores.astype(low_type)
            for h in range(2):
                for i in range(SPAN // LANES):
                    for j in range(blocks):
                        top = h * SPAN + i * LANES
                        tile_ref[h, j - r * (SPAN // LANES) - i + blocks - 1] += d_scores[
                            top : top + LANES, j * LANES : (j + 1) * LANES
                        ]
            d_queries = dot_nn(d_low, keys)
            d_out_ref[0, 0, rows, :] = jnp.where(
                lanes[0], d_queries[:SPAN], d_queries[SPAN:]
            ).astype(low_type)
            d_keys, d_values = dot_tn(d_low, queries), dot_tn(probs, d_att)
            dk_ref[...] = d_keys if r == 0 else dk_ref[...] + d_keys
            dv_ref[...] = d_values if r == 0 else dv_ref[...] + d_values
        d_out_ref[0, 1, everything, :] = dk_ref[...].astype(low_type)
        d_out_ref[0, 2, everything, :] = dv_ref[...].astype(low_type)
        return carry

    lax.fori_loop(0, micro, micro_step, 0, unroll=True)
    d_project = jnp.concatenate([d_out_ref[0, c] for c in range(3)], axis=1)
    spill_rows(dot_nn(turned_ref[...], d_project), [ref.at[:, : 3 * LANES] for ref in out_refs])
    flip = (
        lax.broadcasted_iota(jnp.int32, (LANES, LANES), 0)
        + lax.broadcasted_iota(jnp.int32, (LANES, LANES), 1)
        == LANES - 1
    )
    flip = jnp.where(flip, 1.0, 0.0).astype(low_type)
    tiles = tile_ref[...].reshape(2 * spans * LANES, LANES)
    high = tiles.astype(low_type)
    rest = (tiles - high.astype(full_type)).astype(low_type)
    flipped = dot_nn(high, flip) + dot_nn(rest, flip)
    zeros = jnp.zeros((LANES, LANES), full_type)
    lines = []
    for h in range(2):
        sums = []
        for d in range(spans):
            top = (h * spans + d) * LANES
            wide = jnp.concatenate([flipped[top : top + LANES], zeros], axis=1)
            turned = pltpu.roll(wide, 0, 1, stride=1, stride_axis=0)
            sums.append(jnp.sum(turned, axis=0, keepdims=True))
        lines.append(jnp.concatenate(sums, axis=1))
    highs = [line.astype(low_type).astype(full_type) for line in lines]
    rests = [line - high for line, high in zip(lines, highs)]
    table = dot_nn(few_rows(highs + rests, 16).astype(low_type), hot_ref[...])
    table_ref[0] = few_rows([table[h : h + 1] + table[2 + h : 3 + h] for h in range(2)], 8)


def attention_back(
    probs, qkv, d_attended, attended, turned, hot, rows, pair, slot, own,
    grad_out=None, tables=(), before=(), deps=()
):
    width, count = turned.shape
    micro = count // slot
    pairs = qkv.shape[0]
    spans = 2 * (slot // LANES) - 1
    lead = lambda shape: pl.BlockSpec(shape, lambda i: (pair,) + (0,) * (len(shape) - 1))
    column = pl.BlockSpec((count, LANES), lambda i: (0, pair))
    if tables:
        steps, extra, extra_specs = 1, tables, [whole(table.shape) for table in tables]
        gradients = [shape_of((r, 4 * LANES), low_type) for r in rows]
        gradient_specs = [whole((r, 4 * LANES)) for r in rows]
    else:
        steps = 1 if grad_out is None else 2
        extra = () if grad_out is None else (grad_out,)
        extra_specs = [whole(array.shape) for array in extra]
        gradients = [shape_of((r, pairs * 3 * LANES), low_type) for r in rows]
        gradient_specs = [pl.BlockSpec((r, 3 * LANES), lambda i: (0, i + pair)) for r in rows]
    first = 6 + len(extra)
    return call(
        functools.partial(
            attention_back_kernel, len(before), 0 if grad_out is None else 1, len(tables), own
        ),
        "attention_backward",
        [
            shape_of((pairs, 3, count, LANES), low_type),
            shape_of((1, 8, LANES), full_type),
            *gradients,
        ],
        deps=deps,
        grid=(steps,),
        in_specs=[
            lead((1, micro, 2, slot, slot)),
            lead((1, 3, count, LANES)),
            column,
            column,
            whole(turned.shape),
            whole(hot.shape),
            *extra_specs,
            *[in_place()] * len(before),
        ],
        out_specs=[lead((1, 3, count, LANES)), whole((1, 8, LANES)), *gradient_specs],
        input_output_aliases={first + i: i if i == 0 else i + 1 for i in range(len(before))},
        scratch_shapes=[
            pltpu.VMEM((2, spans, LANES, LANES), full_type),
            pltpu.VMEM((slot, LANES), full_type),
            pltpu.VMEM((slot, LANES), full_type),
        ],
    )(probs, qkv, d_attended, attended, turned, hot, *extra, *before)


def normed_back_kernel(d_ref, *refs):
    *weight_refs, out_ref, w_ref = refs
    pairs, parts = d_ref.shape[0], d_ref.shape[1]

    @pl.when(pl.program_id(0) == 0)
    def assemble():
        fill_rows(w_ref, weight_refs, slice(0, w_ref.shape[1]))

    blocks = [d_ref[p, c] for c in range(parts) for p in range(pairs)]
    d_normed = dot_nt(jnp.concatenate(blocks, axis=1), w_ref[...])
    out_ref[...] = d_normed.astype(low_type)


def normed_back(d_project, weights, deps):
    pairs, parts, count, _ = d_project.shape
    width = sum(piece.shape[0] for piece in weights)
    return call(
        normed_back_kernel,
        "normed_backward",
        shape_of((count, width), low_type),
        cost=(900, 15000),
        deps=deps,
        grid=(count // ROWS,),
        in_specs=[
            pl.BlockSpec((pairs, parts, ROWS, LANES), lambda i: (0, 0, i, 0)),
            *(whole(piece.shape) for piece in weights),
        ],
        out_specs=row_blocks((ROWS, width)),
        scratch_shapes=[pltpu.VMEM((width, pairs * parts * LANES), low_type)],
    )(d_project, *weights)


def token_kernel(d_ref, own_ref, came_ref, x_ref, vector_ref, order_ref, out_ref, done_ref):
    x = x_ref[...].astype(full_type)
    d_normed = own_ref[...].astype(full_type) + came_ref[...].astype(full_type)
    grad = d_ref[...] + norm_input_grad(d_normed, vector_ref[0:1], x, rms_scale(x))
    high = grad.astype(low_type)
    rest = (grad - high.astype(full_type)).astype(low_type)
    order = order_ref[...]
    out_ref[...] = dot_nt(high, order) + dot_nt(rest, order)
    done_ref[...] = jnp.zeros_like(done_ref)


def token_back(d_middle, own, came, rows_low, vectors, order, deps):
    count, width = rows_low.shape
    return call(
        token_kernel,
        "token_gradient",
        [shape_of((count, width), full_type), shape_of((8, LANES), full_type)],
        cost=(1200, 15000),
        deps=deps,
        grid=(count // ROWS,),
        in_specs=[row_blocks((ROWS, width))] * 4 + [whole(vectors.shape), whole(order.shape)],
        out_specs=[row_blocks((ROWS, width)), whole((8, LANES))],
    )(d_middle, own, came, rows_low, vectors, order)


def total_kernel(smalls, counts, micro, pairs, *refs):
    small_refs, refs = refs[:smalls], refs[smalls:]
    groups = []
    for count in counts:
        groups.append(refs[:count])
        refs = refs[count:]
    rank_ref, vector_ref, in_ref, up_ref, gain_ref, tied_ref, down_ref, line_ref, *out_refs = refs
    size, width = sum(ref.shape[0] for ref in small_refs), small_refs[0].shape[2]
    row_of = lambda row: stacked_row(small_refs, row)
    own = down_ref.shape[0]
    inverse = 1.0 / LOSS_SCALE
    add_up = lambda values: jnp.sum(values, axis=0, keepdims=True).sum(axis=1, keepdims=True)
    squares, sums = 0.0, []
    for group, out_ref in zip(groups, out_refs):
        total = sum(ref[...].astype(full_type) for ref in group) * inverse
        total, rest = total[:, : out_ref.shape[1]], total[:, out_ref.shape[1] :]
        out_ref[...] = total
        sums.append((total, rest))
        squares = squares + add_up(total * total)
    table = sums[1][1]

    block = lax.broadcasted_iota(jnp.int32, (size, width), 1) // own
    mine = block == lax.broadcasted_iota(jnp.int32, (size, width), 0)
    fold = lax.broadcasted_iota(jnp.int32, (width, LANES), 0) % own == lax.broadcasted_iota(
        jnp.int32, (width, LANES), 1
    )
    fold = jnp.where(fold, 1.0, 0.0).astype(low_type)
    down, ranked = 0.0, 0.0
    lane = lax.broadcasted_iota(jnp.int32, (1, LANES), 1)
    own_factor = (vector_ref[3:4, :LANES] - vector_ref[4:5, :LANES]) * vector_ref[2:3, :LANES]
    own_factor = jnp.where(lane < own, own_factor, 0.0)
    parts = down_ref.shape[1] // width
    for m in range(micro):
        pooled = row_of(m)
        scale = rms_scale(pooled)
        lengths = row_of(micro + micro * parts + m)
        margins, lengths = lengths[:, 0:1], lengths[:, LANES : LANES + 1]
        d_logit = rank_ref[m][:, 0:1] * width ** (-0.5)
        mean = d_logit * margins * (width**0.5 / width) / scale
        mine_low = dot_nn(jnp.where(mine, pooled, 0.0).astype(low_type), fold)
        ranked = ranked + jnp.sum(mine_low * scale * d_logit, axis=0, keepdims=True)
        d_pooled = scale * d_logit * own_factor - mine_low * scale**3 * mean
        lines = (d_pooled / lengths).astype(low_type)
        acts = [row_of(micro + m * parts + i) for i in range(parts)]
        acts = jnp.concatenate(acts, axis=1)
        high = acts.astype(low_type)
        rest = (acts - high.astype(full_type)).astype(low_type)
        down = down + dot_tn(lines, high) + dot_tn(lines, rest)
    down = down[:own] * inverse
    down_ref[...] = down
    squares = squares + add_up(down * down)

    ranked = ranked[:, :own] * inverse
    rounded = lambda ref, i: ref[i : i + 1].astype(low_type).astype(full_type)
    tied_gap = rounded(tied_ref, 0) - rounded(tied_ref, 1)

    def through(products):
        ones = jnp.ones((16, products.shape[1]), low_type)
        high = products.astype(low_type)
        rest = (products - high.astype(full_type)).astype(low_type)
        return (dot_nt(ones, high) + dot_nt(ones, rest))[0:1]

    weighed = lambda ref, total: ref.astype(low_type).astype(full_type) * total
    first = 0.0
    for p in range(pairs):
        source = sums[0][0] if p < pairs - 1 else sums[1][0]
        offset = p * 3 * LANES if p < pairs - 1 else 0
        for c in range(3):
            columns = slice(offset + c * LANES, offset + (c + 1) * LANES)
            first = first + weighed(in_ref[c, :, p * LANES : (p + 1) * LANES], source[:, columns])
    rows = [
        through(first) / rounded(gain_ref, 0),
        through(weighed(up_ref[...], sums[2][0])) / rounded(gain_ref, 1),
        tied_gap * ranked,
        rounded(gain_ref, 2) * ranked,
    ]
    place = lax.broadcasted_iota(jnp.int32, (8, own), 0)
    extra = jnp.zeros((8, own), full_type)
    for i, row in enumerate(rows):
        extra = jnp.where(place == i, row, extra)
    line_ref[...] = jnp.zeros_like(line_ref)
    line_ref[:8, :own] = extra
    line_ref[8:16] = jnp.broadcast_to(squares, (8, LANES))
    line_ref[16 : 16 + 2 * pairs] = table[: 2 * pairs]


def totals(
    small_all, ranks, vectors, grads, heads_in, hidden_in, gains, tied_rows, widths, micro, deps
):
    counts = tuple(len(group) for group in grads)
    flat = [array for group in grads for array in group]
    own, inner = hidden_in.shape
    down, line, *sums = call(
        functools.partial(
            total_kernel, len(small_all), counts, micro, heads_in.shape[2] // LANES
        ),
        "gradient_totals",
        [
            shape_of((own, inner), full_type),
            shape_of((24, LANES), full_type),
            *(shape_of((own, width), full_type) for width in widths),
        ],
        cost=(100, 10000),
        deps=deps,
    )(*small_all, *flat, ranks, vectors, heads_in, hidden_in, gains, tied_rows)
    return down, line, sums


def stage_kernel(*refs):
    count = len(refs) // 2
    for ref, target in zip(refs[:count], refs[count:]):
        target[...] = ref[...]


def adam(weight, first_old, second, grad, factor, rate, decay, step_ref):
    clipped = grad * factor
    next_first = beta_first * first_old + (1.0 - beta_first) * clipped
    next_second = beta_second * second + (1.0 - beta_second) * clipped * clipped
    first_hat = next_first * step_ref[0]
    second_hat = next_second * step_ref[1]
    next_weight = weight - rate * (first_hat / (jnp.sqrt(second_hat) + adam_eps) + decay * weight)
    return next_weight, next_first, next_second


def square_kernel(heads, own_ref, other_ref, out_ref, extra_ref):
    place = lax.broadcasted_iota(jnp.int32, (8, LANES), 0)
    extra = own_ref[:8] + jnp.where(place < 2, other_ref[:8], 0.0)
    extra_ref[...] = extra
    counted = jnp.where(place == 3, 2.0, 1.0) * extra * extra
    add_up = lambda values: jnp.sum(values, axis=0, keepdims=True).sum(axis=1, keepdims=True)
    squares = own_ref[8:16] + other_ref[8:16] + add_up(counted)
    out_ref[:8] = squares
    tables = own_ref[16:24] * own_ref[16:24] + other_ref[16:24] * other_ref[16:24]
    out_ref[8:16] = own_ref[16:24]
    out_ref[16:24] = jnp.broadcast_to(add_up(tables), (8, LANES))


def update_kernel(squares, groups, pick_ref, step_ref, extra_ref, *refs):
    square_refs, refs = refs[:squares], refs[squares:]
    grad_refs, refs = refs[:groups], refs[groups:]
    state_refs, refs = refs[:21], refs[21:]
    norm_ref, *out_refs = refs
    tiles = stacked(square_refs)
    device = lax.broadcasted_iota(jnp.int32, (tiles.shape[0], 1, 1), 0)
    tables = jnp.sum(jnp.where(device == pick_ref[0], tiles[:, 8:24], 0.0), axis=0)
    norm = jnp.sqrt(jnp.sum(tiles[:, 0:8], axis=0)[0:1, 0:1] + tables[8:9, 0:1])
    norm_ref[...] = norm
    factor = jnp.minimum(1.0, clip_limit / (norm + 1e-06))
    weights, firsts, seconds = state_refs[:7], state_refs[7:14], state_refs[14:]
    next_weights, next_firsts, next_seconds = out_refs[:7], out_refs[7:14], out_refs[14:]

    def step(index, where, grad, rate, decay):
        results = adam(
            weights[index][where], firsts[index][where], seconds[index][where], grad, factor,
            rate, decay, step_ref,
        )
        for target, result in zip((next_weights, next_firsts, next_seconds), results):
            target[index][where] = result

    everything = (slice(None), slice(None))
    early_ref, late_ref, up_ref, down_ref = grad_refs
    pairs = weights[0].shape[2] // LANES
    for p in range(pairs):
        source, offset = (early_ref, p * 3) if p < pairs - 1 else (late_ref, 0)
        for c in range(3):
            columns = slice((offset + c) * LANES, (offset + c + 1) * LANES)
            where = (c, slice(None), slice(p * LANES, (p + 1) * LANES))
            step(0, where, source[:, columns], rate_matrix, decay_matrix)
    step(1, everything, early_ref[:, (pairs - 1) * 3 * LANES :], rate_matrix, decay_matrix)
    step(2, everything, up_ref[...], rate_matrix, decay_matrix)
    step(3, everything, down_ref[...], rate_matrix, decay_matrix)
    rows = weights[4].shape[1]
    extra = extra_ref[...]
    step(4, everything, extra[0:3, :rows], rate_vector, 0.0)
    tied = extra[3:4, :rows]
    step(5, everything, jnp.concatenate([tied, -tied], axis=0), rate_vector, 0.0)
    step(6, everything, tables[: 2 * pairs, :BUCKETS], rate_vector, 0.0)


def update(pick, corrections, extra, squares, grads, states):
    return call(
        functools.partial(update_kernel, len(squares), len(grads)),
        "update",
        [shape_of((1, 1), full_type)] + [shape_of(s.shape, full_type) for s in states],
        cost=(0, 6000),
        grid=(1,),
        in_specs=[
            on_scalars(),
            on_scalars(),
            *(whole(array.shape) for array in (extra, *squares, *grads, *states)),
        ],
    )(pick, corrections, extra, *squares, *grads, *states)


def body(
    tokens,
    pair_lengths,
    query_ids,
    distance_bucket,
    step_count,
    heads_in,
    heads_out,
    hidden_in,
    hidden_out,
    gains,
    tied_rows,
    bias_table,
    first_heads_in,
    first_heads_out,
    first_hidden_in,
    first_hidden_out,
    first_gains,
    first_tied,
    first_table,
    second_heads_in,
    second_heads_out,
    second_hidden_in,
    second_hidden_out,
    second_gains,
    second_tied,
    second_table,
):
    size = lax.axis_size("dp")
    me = lax.axis_index("dp")
    core = lax.axis_index("mp")
    micro, _, slot, width = tokens.shape
    count = micro * slot
    own, local_heads = heads_in.shape[0], bias_table.shape[1]
    head_width = heads_in.shape[2]
    inner = hidden_in.shape[1]
    pairs = local_heads // 2
    spans = 2 * (slot // LANES) - 1
    turn_matrix = lambda array: jnp.transpose(array, (1, 0, 2))
    heads_in, first_heads_in, second_heads_in = (
        turn_matrix(array) for array in (heads_in, first_heads_in, second_heads_in)
    )
    gains, tied_rows, bias_table = gains.T, tied_rows.T, bias_table.T
    first_gains, first_tied, first_table = first_gains.T, first_tied.T, first_table.T
    second_gains, second_tied, second_table = second_gains.T, second_tied.T, second_table.T

    packed_heads = call(
        pack_heads_kernel, "pack_heads", shape_of((own, 4 * head_width + LANES), low_type), vmem=56
    )(heads_in, heads_out, gains, tied_rows)
    packed_up, packed_down = call(
        pack_hidden_kernel, "pack_hidden", [shape_of((own, inner), low_type)] * 2
    )(hidden_in, hidden_out)
    weights = (heads_in, heads_out, hidden_in, hidden_out, gains, tied_rows, bias_table)
    firsts = (
        first_heads_in,
        first_heads_out,
        first_hidden_in,
        first_hidden_out,
        first_gains,
        first_tied,
        first_table,
    )
    seconds = (
        second_heads_in,
        second_heads_out,
        second_hidden_in,
        second_hidden_out,
        second_gains,
        second_tied,
        second_table,
    )
    states = [*weights, *firsts, *seconds]
    large = [index for index, state in enumerate(states) if index % 7 < 4]
    staged = call(
        stage_kernel, "stage", [shape_of(states[i].shape, full_type) for i in large], vmem=56
    )(*(states[i] for i in large))
    for i, array in zip(large, staged):
        states[i] = array

    pair_ids = jnp.bitwise_xor(me, jnp.array(block_masks(size), jnp.int32))
    place = (pair_ids[:, None] * own + jnp.arange(own, dtype=jnp.int32)[None, :]).reshape(width)
    order = (jnp.arange(width, dtype=jnp.int32)[:, None] == place[None, :]).astype(low_type)
    lengths = pair_lengths.reshape(micro)
    queries = query_ids[:, pair_ids]
    same_query = queries[:, :, None] == queries[:, None, :]
    padded = jnp.pad(queries, ((0, 0), (0, LANES - size)), constant_values=-1)
    same_tile = (queries[:, :, None] == padded[:, None, :]).astype(full_type)
    earlier = same_query & (pair_ids[None, :] < pair_ids[:, None])[None]
    positive_tile = jnp.where(jnp.any(earlier, axis=2), 0.0, 1.0)[:, :, None]
    positive_tile = jnp.broadcast_to(positive_tile, (micro, size, LANES))

    bucket_line = jnp.concatenate([distance_bucket, jnp.full((1,), -1, jnp.int32)])
    bucket_hot = (
        bucket_line[:, None] == jnp.arange(LANES, dtype=jnp.int32)[None, :]
    ).astype(low_type)
    lines = dot_nt(bias_table.astype(low_type), bucket_hot[:, :BUCKETS])
    lines = lines.reshape(pairs, 2, 2 * slot)
    places = jnp.arange(spans * 2 * LANES, dtype=jnp.int32)
    places = places // (2 * LANES) * LANES + 2 * LANES - 2 - places % (2 * LANES)
    hot_spans = dot_nn(
        (places[:, None] == jnp.arange(2 * slot, dtype=jnp.int32)[None, :]).astype(low_type),
        bucket_hot,
    ).astype(low_type)

    step_float = step_count.astype(full_type)
    corrections = jnp.stack(
        [1.0 / (1.0 - beta_first**step_float), 1.0 / (1.0 - beta_second**step_float)]
    )
    first_place = jnp.sum(jnp.where(pair_ids == 0, jnp.arange(size, dtype=jnp.int32), 0)).reshape(1)

    rows_low = call(
        order_kernel,
        "order_tokens",
        shape_of((count, width), low_type),
        cost=(600, 5000),
        grid=(count // ROWS,),
        in_specs=[row_blocks((ROWS, width)), whole((width, width))],
        out_specs=row_blocks((ROWS, width)),
    )(tokens.reshape(count, width), order)
    if size != 16:
        weight_heads, weight_up, weight_down = (
            [gather_doubling(part, size)] for part in (packed_heads, packed_up, packed_down)
        )
        qkv, normed_first, vectors = project(rows_low, weight_heads, pairs, (same_tile, positive_tile, corrections, hot_spans))
    else:
        heads_line, packed_up, packed_down = join(
            line_parts(packed_heads, size, "heads"), passing=(packed_up, packed_down)
        )
        heads_sides = side_parts(heads_line, size, "heads")
        up_pair = join([packed_up, swap(packed_up, 8, size, "up")], deps=(rows_low,))
        up_near = swap(up_pair, 4, size, "up")
        low, high, packed_down = gather_step(*heads_sides, deps=(up_pair,), passing=(packed_down,))
        down_far = swap(packed_down, 8, size, "down")
        heads_corner = corner_parts(low, high, size, "heads_corner")
        up_line = join([up_pair, up_near], deps=(low,))
        down_pair = join([packed_down, down_far], deps=(up_line,))
        down_near = swap(down_pair, 4, size, "down")
        up_sides = side_parts(up_line, size, "up")
        weight_heads = [heads_line, *heads_sides, *heads_corner]
        qkv, normed_first, vectors = project(
            rows_low,
            weight_heads,
            pairs,
            (same_tile, positive_tile, down_pair, corrections, first_place, hot_spans, staged[0]),
        )
    filled = ()
    for pair in range(pairs):
        filled = attention(lengths, lines, qkv, pair, slot, before=filled)
        if pair == 0 and size == 16:
            down_line = join([down_pair, down_near], deps=(filled[0],))
            down_sides = side_parts(down_line, size, "down")
        if pair == 1 and size == 16:
            low, high = gather_step(*up_sides, deps=(filled[0],))
            up_corner = corner_parts(low, high, size, "up_corner")
            weight_up = [up_line, *up_sides, *up_corner]
    turned_first = call(turn_kernel, "turn", shape_of((width, count), low_type))(normed_first)
    attended, probs, inverse = filled
    branch = branch_rows(
        attended, weight_heads, (*down_sides, turned_first) if size == 16 else ()
    )
    if size == 16:
        low, high = gather_step(*down_sides, deps=(branch,))
        down_corner = corner_parts(low, high, size, "down_corner")
        weight_down = [down_line, *down_sides, *down_corner]
    branch_came = other_core(branch, "branch_other_core")
    normed_second, slope, act_sum, middle_sum, full_up = hidden(
        lengths, rows_low, branch, branch_came, vectors, weight_up, slot
    )
    down, full_down = call(
        pool_kernel,
        "pool",
        [shape_of((8, width), full_type), shape_of((width, inner), low_type)],
        cost=(20, 5000),
    )(act_sum, *weight_down)
    small = call(
        margin_kernel,
        "margin",
        shape_of((8, width), full_type),
        grid=(1,),
        in_specs=[
            on_scalars(),
            *(whole(array.shape) for array in (down, down, middle_sum, act_sum, vectors)),
        ],
        out_specs=whole((8, width)),
    )(lengths, down, other_core(down, "pooled_part_other_core"), middle_sum, act_sum, vectors)
    small_all = gather_small(small, size, "small_sums")

    d_line, _, ranks, d_hidden, d_normed_second = rank_back(
        lengths, same_tile, positive_tile, vectors, slope, small_all, full_down, full_up, slot,
        (turned_first,),
    )
    d_normed_second_came = other_core(d_normed_second, "second_gradient_other_core")
    up_sum = Scatter(
        up_grad(normed_second, d_hidden, piece_rows(size, width)), size, "up_gradient"
    )
    d_middle, d_attended, g_out = middle_back(
        lengths, rows_low, branch, branch_came, d_normed_second, d_normed_second_came, vectors,
        d_line, attended, inverse, weight_heads, slot,
    )
    scatter_sides([up_sum], deps=(d_attended,))
    filled, tables = (), []
    for pair in range(pairs - 1):
        d_project, table, *g_early = attention_back(
            probs, qkv, d_attended, attended, turned_first, hot_spans, piece_rows(size, width),
            pair, slot, own, grad_out=g_out if pair == pairs - 2 else None, before=filled,
        )
        filled = (d_project, *g_early)
        tables.append(table)
    early_sum = Scatter(g_early, size, "early_gradient")
    d_project, table, *g_late = attention_back(
        probs, qkv, d_attended, attended, turned_first, hot_spans, piece_rows(size, width),
        pairs - 1, slot, own, tables=tuple(tables), before=(d_project,),
    )
    late_sum = Scatter(g_late, size, "late_gradient")
    up_sum.near(deps=(table,))
    sides = scatter_sides([early_sum, late_sum], deps=tuple(up_sum.came))
    d_normed_first = normed_back(d_project, weight_heads, sides)
    up_parts = up_sum.far(deps=sides)
    (d_normed_first,) = early_sum.near(deps=tuple(up_parts), passing=(d_normed_first,))
    token_gradient, token_done = token_back(
        d_middle, d_normed_first, other_core(d_normed_first, "first_gradient_other_core"), rows_low,
        vectors, order, early_sum.sources,
    )
    early_parts = early_sum.far(deps=(token_done,))
    late_parts, _ = late_sum.line(deps=(early_parts[0],))

    g_down, line, grad_sums = totals(
        small_all, ranks, vectors, [early_parts, late_parts, up_parts], heads_in, hidden_in, gains, tied_rows,
        (head_width * 3, 3 * LANES, inner), micro, (),
    )
    square_tile, extra = call(
        functools.partial(square_kernel, local_heads),
        "squares",
        [shape_of((24, LANES), full_type), shape_of((8, LANES), full_type)],
    )(line, other_core(line, "totals_other_core"))
    squares_all = gather_small(square_tile, size, "squares")
    grads = [*grad_sums, g_down]
    norm, *results = update(first_place, corrections, extra, squares_all, grads, states)
    for index in (0, 7, 14):
        results[index] = turn_matrix(results[index])
        for other in (4, 5, 6):
            results[index + other] = results[index + other].T
    return (norm.reshape(()), token_gradient.reshape(tokens.shape), *results)


def solution(mesh):
    in_specs = (
        P(None, "dp", None, None),
        P(None, "dp"),
        P(),
        P(),
        P(),
        P("dp", None, "mp"),
        P("dp", "mp"),
        P("dp", "mp"),
        P("dp", "mp"),
        P("dp", None),
        P("dp", None),
        P(None, "mp"),
        P("dp", None, "mp"),
        P("dp", "mp"),
        P("dp", "mp"),
        P("dp", "mp"),
        P("dp", None),
        P("dp", None),
        P(None, "mp"),
        P("dp", None, "mp"),
        P("dp", "mp"),
        P("dp", "mp"),
        P("dp", "mp"),
        P("dp", None),
        P("dp", None),
        P(None, "mp"),
    )
    out_specs = (
        P(),
        P(None, "dp", None, None),
        P("dp", None, "mp"),
        P("dp", "mp"),
        P("dp", "mp"),
        P("dp", "mp"),
        P("dp", None),
        P("dp", None),
        P(None, "mp"),
        P("dp", None, "mp"),
        P("dp", "mp"),
        P("dp", "mp"),
        P("dp", "mp"),
        P("dp", None),
        P("dp", None),
        P(None, "mp"),
        P("dp", None, "mp"),
        P("dp", "mp"),
        P("dp", "mp"),
        P("dp", "mp"),
        P("dp", None),
        P("dp", None),
        P(None, "mp"),
    )
    return jax.shard_map(body, mesh=mesh, in_specs=in_specs, out_specs=out_specs, check_vma=False)
```

```python
import functools

import jax
import jax.numpy as jnp
from jax import lax
from jax.experimental import pallas as pl
from jax.experimental.pallas import tpu as pltpu
from jax.sharding import PartitionSpec as P

BUCKETS = 32
LOSS_SCALE = 1024
LANES = 128
ROWS = 256
SPAN = 512

norm_eps = 1e-06
clip_limit = 0.01
beta_first = 0.9
beta_second = 0.999
adam_eps = 1e-08
rate_matrix = 0.03
rate_vector = 0.25
decay_matrix = 0.1
masked_score = -1e30
gelu_slope = 0.7978845608028654
gelu_cubic = 0.044715
low_type = jnp.bfloat16
full_type = jnp.float32
core_swap = [(0, 1), (1, 0)]


def rms_scale(rows_in):
    return lax.rsqrt(jnp.mean(rows_in * rows_in, axis=-1, keepdims=True) + norm_eps)


def norm_input_grad(d_normed, gain_row, rows_in, norm_scale):
    weighted = d_normed * gain_row
    return norm_scale * weighted - rows_in * norm_scale**3 * jnp.mean(
        weighted * rows_in, axis=-1, keepdims=True
    )


def dot_nt(left, right):
    return lax.dot_general(left, right, (((1,), (1,)), ((), ())), preferred_element_type=full_type)


def dot_tn(left, right):
    return lax.dot_general(left, right, (((0,), (0,)), ((), ())), preferred_element_type=full_type)


def dot_nn(left, right):
    return lax.dot_general(left, right, (((1,), (0,)), ((), ())), preferred_element_type=full_type)


def call(
    kernel, name, out_shape, cost=(0, 0), vmem=16, deps=(), passing=(), in_specs=None,
    out_specs=None, input_output_aliases=None, **options
):
    single = not isinstance(out_shape, (list, tuple))
    out_shapes = [out_shape] if single else list(out_shape)
    outputs, extra = len(out_shapes), len(deps) + len(passing)

    def apply(*operands):
        inputs = len(operands)
        if in_specs is None:
            options["grid"] = (1,)
        specs = [whole(operand.shape) for operand in operands] if in_specs is None else in_specs
        targets = out_specs or [whole(shape.shape) for shape in out_shapes]
        targets = targets if isinstance(targets, (list, tuple)) else [targets]
        aliases = dict(input_output_aliases or {})
        for i in range(len(passing)):
            aliases[inputs + len(deps) + i] = outputs + i

        def run(*refs):
            own = inputs + extra
            kernel(*refs[:inputs], *refs[own : own + outputs], *refs[own + outputs + len(passing) :])

        results = pl.pallas_call(
            run,
            out_shape=[*out_shapes, *(shape_of(a.shape, a.dtype) for a in passing)],
            in_specs=[*specs, *[in_place()] * extra],
            out_specs=[*targets, *[in_place()] * len(passing)],
            input_output_aliases=aliases,
            compiler_params=pltpu.CompilerParams(vmem_limit_bytes=vmem * 1024 * 1024),
            cost_estimate=pl.CostEstimate(
                flops=int(cost[0] * 2e6), bytes_accessed=int(cost[1] * 1e3), transcendentals=0
            ),
            name=name,
            **options,
        )(*operands, *deps, *passing)
        return results[0] if single and not passing else results

    return apply


def in_place():
    return pl.BlockSpec(memory_space=pl.ANY)


def shape_of(shape, dtype):
    return jax.ShapeDtypeStruct(tuple(shape), dtype)


def whole(shape):
    return pl.BlockSpec(tuple(shape), lambda *_: (0,) * len(shape))


def on_scalars():
    return pl.BlockSpec(memory_space=pltpu.SMEM)


def row_blocks(shape, step=0):
    return pl.BlockSpec(tuple(shape), lambda i: (i,) + (0,) * (len(shape) - 1))


def column_blocks(shape, offset=0):
    return pl.BlockSpec(tuple(shape), lambda i: (0,) * (len(shape) - 1) + (i + offset,))


def fill_rows(target, pieces, columns=slice(None)):
    start = 0
    for piece in pieces:
        rows = piece.shape[0]
        target[start : start + rows, :] = piece[:, columns]
        start += rows


def spill_rows(value, pieces, first=0):
    start = 0
    for piece in pieces:
        rows = piece.shape[0]
        low, high = max(start, first), min(start + rows, first + value.shape[0])
        if low < high:
            piece[low - start : high - start] = value[low - first : high - first].astype(piece.dtype)
        start += rows


def swap(array, mask, size, label="exchange"):
    with jax.named_scope(f"{label}_across_{mask}"):
        return lax.ppermute(array, "dp", [(i, i ^ mask) for i in range(size)])


def tie(arrays, deps):
    return call(lambda: None, "tie", [], deps=deps, passing=arrays, in_specs=[], grid=(1,))()


def other_core(array, label="other_core"):
    with jax.named_scope(label):
        return lax.ppermute(array, "mp", core_swap)


def stage_bits(size):
    if size == 16:
        return (8, 4, 2, 1)
    return tuple(1 << i for i in range(size.bit_length() - 1))


def device_of(place, me, size):
    mask = jnp.zeros_like(place)
    for i, bit in enumerate(stage_bits(size)):
        mask = mask + jnp.bitwise_and(place >> i, 1) * bit
    return jnp.bitwise_xor(mask, me)


def piece_rows(size, width):
    if size != 16:
        return [width]
    return [width // 4] * 3 + [width // 8] * 2


def join_kernel(*refs):
    *part_refs, out_ref = refs
    start = 0
    for part in part_refs:
        rows = part.shape[0]
        out_ref[start : start + rows] = part[...]
        start += rows


def join(parts, **options):
    rows = sum(part.shape[0] for part in parts)
    return call(
        join_kernel, "join", shape_of((rows, *parts[0].shape[1:]), parts[0].dtype), **options
    )(*parts)


def step_kernel(groups, y_ref, x_ref, *refs):
    part_refs, (low_ref, high_ref, *joined_refs) = refs[: sum(groups)], refs[sum(groups) :]
    low_ref[...] = y_ref[...]
    high_ref[...] = x_ref[...]
    for group, joined_ref in zip(groups, joined_refs):
        join_kernel(*part_refs[:group], joined_ref)
        part_refs = part_refs[group:]


def gather_step(across_y, across_x, *groups, **options):
    half = (across_y.shape[0] // 2, across_y.shape[1])
    shapes = [shape_of(half, across_y.dtype)] * 2
    for parts in groups:
        shapes.append(shape_of((sum(p.shape[0] for p in parts), parts[0].shape[1]), parts[0].dtype))
    flat = [part for parts in groups for part in parts]
    return call(
        functools.partial(step_kernel, tuple(len(parts) for parts in groups)),
        "gather_step",
        shapes,
        grid=(1,),
        in_specs=[
            pl.BlockSpec(half, lambda i: (0, 0)),
            pl.BlockSpec(half, lambda i: (1, 0)),
            *(whole(part.shape) for part in flat),
        ],
        out_specs=[whole(shape.shape) for shape in shapes],
        **options,
    )(across_y, across_x, *flat)


def line_parts(part, size, label):
    return [part] + [swap(part, mask, size, label) for mask in (8, 4, 12)]


def side_parts(quarter, size, label):
    return [swap(quarter, mask, size, label) for mask in (2, 1)]


def corner_parts(low, high, size, label):
    return [swap(low, 1, size, label), swap(high, 2, size, label)]


def gather_doubling(part, size):
    for bit in stage_bits(size):
        part = jnp.concatenate([part, swap(part, bit, size)], axis=0)
    return part


def small_line(part, size, label):
    if size != 16:
        return part[None]
    return join(line_parts(part[None], size, label))


def small_plane(quarter, size, label):
    if size != 16:
        return [gather_doubling(quarter, size)]
    return [quarter] + [swap(quarter, mask, size, label) for mask in (2, 1, 3)]


def stacked(refs):
    return jnp.concatenate([ref[...] for ref in refs], axis=0)


def stacked_row(refs, row):
    return jnp.concatenate([ref[:, row, :] for ref in refs], axis=0)


def gather_small(part, size, label):
    return small_plane(small_line(part, size, label), size, label)


def plane_sum_kernel(*refs):
    count = len(refs) // 6
    for i in range(count):
        y_ref, x_ref, low_ref, high_ref = refs[4 * i : 4 * i + 4]
        y_out, x_out = refs[4 * count + 2 * i : 4 * count + 2 * i + 2]
        half = low_ref.shape[0]
        y_out[:half] = (y_ref[:half].astype(full_type) + low_ref[...].astype(full_type)).astype(
            low_type
        )
        y_out[half:] = y_ref[half:]
        x_out[:half] = x_ref[:half]
        x_out[half:] = (x_ref[half:].astype(full_type) + high_ref[...].astype(full_type)).astype(
            low_type
        )


def line_sum_kernel(*refs):
    count = sum(ref.shape[0] == refs[0].shape[0] for ref in refs)
    add_refs, out_refs = refs[:count], refs[count:]
    rows = out_refs[0].shape[0]
    for i, out_ref in enumerate(out_refs):
        span = slice(i * rows, (i + 1) * rows)
        total = add_refs[0][span].astype(full_type)
        for ref in add_refs[1:]:
            total = total + ref[span].astype(full_type)
        out_ref[...] = total.astype(out_ref.dtype)


class Scatter:
    def __init__(self, pieces, size, label):
        self.pieces, self.size, self.label = pieces, size, label
        self.sources, self.came = (), ()
        if size == 16:
            *self.pieces, low, high = pieces
            self.came = [swap(low, 1, size, label), swap(high, 2, size, label)]

    def near(self, deps=(), passing=()):
        if self.size != 16:
            return passing
        keep = self.pieces[0]
        half = (keep.shape[0] // 2, keep.shape[1])
        kept, sent, *passed = call(
            line_sum_kernel,
            "line_sum",
            [shape_of(half, full_type), shape_of(half, low_type)],
            deps=deps,
            passing=passing,
        )(keep, *self.came)
        self.sources, self.came, self.pieces = (sent,), [swap(sent, 4, self.size, self.label)], [kept]
        return passed

    def far(self, deps=()):
        if self.size != 16:
            return self.line(deps)[0]
        kept = self.pieces[0]
        half = (kept.shape[0] // 2, kept.shape[1])
        own, sent = call(
            line_sum_kernel,
            "line_sum",
            [shape_of(half, full_type), shape_of(half, low_type)],
            deps=deps,
        )(kept, *self.came)
        self.sources = (sent,)
        return [own, swap(sent, 8, self.size, self.label)]

    def line(self, deps=(), passing=()):
        size, label = self.size, self.label
        if size != 16:
            grad = self.pieces[0]
            for bit in reversed(stage_bits(size)):
                half = grad.shape[0] // 2
                came = swap(grad[half:], bit, size, label)
                grad = (grad[:half].astype(full_type) + came.astype(full_type)).astype(low_type)
            return [grad.astype(full_type)], passing
        keep = self.pieces[0]
        part = (keep.shape[0] // 4, keep.shape[1])
        own, *others = call(
            line_sum_kernel,
            "line_sum",
            [shape_of(part, full_type)] + [shape_of(part, low_type)] * 3,
            deps=deps,
            passing=passing,
        )(keep, *self.came)
        came = [swap(other, mask, size, label) for other, mask in zip(others, (8, 4, 12))]
        return [own] + came, others[3:]


def scatter_sides(scatters, deps=()):
    if scatters[0].size != 16:
        return ()
    sides = [part for scatter in scatters for part in scatter.pieces[1:]]
    operands = [part for s in scatters for part in (*s.pieces[1:], *s.came)]
    sums = call(
        plane_sum_kernel, "plane_sum", [shape_of(part.shape, low_type) for part in sides], deps=deps
    )(*operands)
    for i, scatter in enumerate(scatters):
        to_y, to_x = sums[2 * i : 2 * i + 2]
        scatter.came = [
            swap(to_y, 2, scatter.size, scatter.label), swap(to_x, 1, scatter.size, scatter.label)
        ]
    return tuple(sums)


def pack_heads_kernel(in_ref, out_ref, gain_ref, tied_ref, a_ref):
    parts, rows, width = in_ref.shape
    for c in range(parts):
        a_ref[:, c * width : (c + 1) * width] = in_ref[c].astype(low_type)
    a_ref[:, parts * width : (parts + 1) * width] = out_ref[...].astype(low_type)
    gains, tied = gain_ref[...], tied_ref[...]
    vectors = few_rows([gains[i : i + 1] for i in range(3)] + [tied[i : i + 1] for i in range(2)], 16)
    pick = lax.broadcasted_iota(jnp.int32, (16, LANES), 0) == lax.broadcasted_iota(
        jnp.int32, (16, LANES), 1
    )
    extra = dot_tn(vectors.astype(low_type), jnp.where(pick, 1.0, 0.0).astype(low_type))
    a_ref[:, (parts + 1) * width :] = extra.astype(low_type)


def pack_hidden_kernel(up_ref, down_ref, b_ref, c_ref):
    b_ref[...] = up_ref[...].astype(low_type)
    c_ref[...] = down_ref[...].astype(low_type)


def prepare_kernel(
    size, me_ref, line_ref, table_ref, query_ref, order_ref, bias_ref, hot_ref, same_ref, positive_ref
):
    me = me_ref[0]
    lane = lambda shape: lax.broadcasted_iota(jnp.int32, shape, 1)
    row = lambda shape: lax.broadcasted_iota(jnp.int32, shape, 0)
    low = lambda hit: jnp.where(hit, 1.0, 0.0).astype(low_type)
    width = order_ref.shape[0]
    own = width // size
    feature = lane((1, width))
    place = device_of(feature // own, me, size) * own + feature % own
    for start in range(0, width, LANES):
        order_ref[start : start + LANES] = low(row((LANES, width)) + start == place)
    length = line_ref.shape[1]
    hot = low(row((LANES, length)) == line_ref[...])
    lines = dot_nn(table_ref[...].astype(low_type), hot[:BUCKETS])
    for head in range(table_ref.shape[0]):
        bias_ref[head // 2, head % 2 : head % 2 + 1] = lines[head : head + 1]
    step = 2 * LANES
    for start in range(0, hot_ref.shape[0], step):
        wanted = start // 2 + step - 2 - row((step, length))
        hot_ref[start : start + step] = dot_nt(low(wanted == lane((step, length))), hot).astype(
            low_type
        )
    shape = (size, LANES)
    pair = device_of(row(shape), me, size)
    other = device_of(lane(shape), me, size)
    for m in range(query_ref.shape[0]):
        queries = query_ref[m : m + 1]
        if size < LANES:
            blank = jnp.zeros((1, LANES - size), jnp.int32)
            queries = jnp.concatenate([queries, blank], axis=1)
        picked = jnp.where(lane(shape) == pair, queries, 0).astype(full_type)
        mine = jnp.sum(picked, axis=1, keepdims=True)
        theirs = jnp.sum(jnp.where(lane(shape) == row(shape), mine, 0.0), axis=0, keepdims=True)
        same = jnp.where((mine == theirs) & (lane(shape) < size), 1.0, 0.0)
        same_ref[m] = same
        earlier = jnp.max(jnp.where(other < pair, same, 0.0), axis=1, keepdims=True)
        positive_ref[m] = jnp.broadcast_to(1.0 - earlier, shape)


def order_kernel(x_ref, order_ref, out_ref):
    out_ref[...] = dot_nn(x_ref[...], order_ref[...]).astype(low_type)


def turn_kernel(x_ref, out_ref):
    out_ref[...] = x_ref[...].T


def head_lanes():
    lane = lax.broadcasted_iota(jnp.int32, (1, LANES), 1)
    return [lane < LANES // 2, lane >= LANES // 2]


def project_kernel(pieces, pairs, x_ref, *refs):
    weight_refs, (qkv_ref, normed_ref, vector_ref, w_ref) = refs[:pieces], refs[pieces:]
    parts = qkv_ref.shape[1]
    in_width = pairs * parts * LANES

    @pl.when(pl.program_id(0) == 0)
    def assemble():
        fill_rows(w_ref, weight_refs)
        pick = lax.broadcasted_iota(jnp.int32, (16, LANES), 0) == lax.broadcasted_iota(
            jnp.int32, (16, LANES), 1
        )
        vectors = dot_nt(jnp.where(pick, 1.0, 0.0).astype(low_type), w_ref[:, -LANES:])
        vector_ref[...] = vectors[:8]

    x = x_ref[...].astype(full_type)
    normed = (x * rms_scale(x) * vector_ref[0:1]).astype(low_type)
    normed_ref[...] = normed
    projected = dot_nn(normed, w_ref[:, :in_width]).astype(low_type)
    for c in range(parts):
        for p in range(pairs):
            start = (c * pairs + p) * LANES
            qkv_ref[p, c] = projected[:, start : start + LANES]


def project(rows_low, weights, pairs, deps):
    count, width = rows_low.shape
    parts = 3
    return call(
        functools.partial(project_kernel, len(weights), pairs),
        "projection",
        [
            shape_of((pairs, parts, count, LANES), low_type),
            shape_of((count, width), low_type),
            shape_of((8, width), full_type),
        ],
        deps=deps,
        grid=(count // ROWS,),
        in_specs=[row_blocks((ROWS, width)), *(whole(piece.shape) for piece in weights)],
        out_specs=[
            pl.BlockSpec((pairs, parts, ROWS, LANES), lambda i: (0, 0, i, 0)),
            row_blocks((ROWS, width)),
            whole((8, width)),
        ],
        scratch_shapes=[pltpu.VMEM((width, weights[0].shape[1]), low_type)],
    )(rows_low, *weights)


def attention_kernel(len_ref, line_ref, qkv_ref, *refs):
    att_ref, prob_ref, inv_ref, tile_ref = refs[-4:]
    micro, slot = prob_ref.shape[1], prob_ref.shape[3]
    blocks = slot // LANES
    lanes = head_lanes()
    for h in range(2):
        for d in range(2 * blocks - 1):
            piece = jnp.broadcast_to(
                line_ref[0, h : h + 1, d * LANES : (d + 2) * LANES], (LANES, 2 * LANES)
            )
            turned = pltpu.roll(piece, LANES + 1, 1, stride=1, stride_axis=0)
            tile_ref[h, d] = turned[:, :LANES]

    def micro_step(m, carry):
        start = pl.multiple_of(m * slot, slot)
        key_valid = lax.broadcasted_iota(jnp.int32, (1, slot), 1) < len_ref[m]
        keys = qkv_ref[0, 1, pl.ds(start, slot), :]
        values = qkv_ref[0, 2, pl.ds(start, slot), :]
        values = jnp.concatenate([values, jnp.ones_like(values)], axis=1)
        for r in range(slot // ROWS):
            rows = pl.ds(start + r * ROWS, ROWS)
            queries = qkv_ref[0, 0, rows, :]
            queries = jnp.concatenate(
                [queries * lanes[h].astype(low_type) for h in range(2)], axis=0
            )
            first = r * (ROWS // LANES)
            bias = jnp.concatenate(
                [
                    jnp.concatenate(
                        [tile_ref[h, j - first - i + blocks - 1] for j in range(blocks)], axis=1
                    )
                    for h in range(2)
                    for i in range(ROWS // LANES)
                ],
                axis=0,
            )
            scores = dot_nt(queries, keys)
            scores = jnp.where(key_valid, scores + bias, masked_score)
            terms = jnp.exp(scores - jnp.max(scores, axis=1, keepdims=True)).astype(low_type)
            for h in range(2):
                prob_ref[0, m, h, r * ROWS : (r + 1) * ROWS, :] = terms[h * ROWS : (h + 1) * ROWS]
            mixed = dot_nn(terms, values)
            inverse = 1.0 / mixed[:, LANES:]
            mixed = mixed[:, :LANES] * inverse
            att_ref[rows, :] = jnp.where(lanes[0], mixed[:ROWS], mixed[ROWS:]).astype(low_type)
            inv_ref[rows, :] = jnp.where(lanes[0], inverse[:ROWS], inverse[ROWS:])
        return carry

    lax.fori_loop(0, micro, micro_step, 0)


def attention(lengths, lines, qkv, first, number, slot, before=(), deps=()):
    pairs, parts, count, _ = qkv.shape
    micro = count // slot
    spans = 2 * (slot // LANES) - 1
    column = pl.BlockSpec((count, LANES), lambda i: (0, i + first))
    return call(
        attention_kernel,
        "attention_forward",
        [
            shape_of((count, pairs * LANES), low_type),
            shape_of((pairs, micro, 2, slot, slot), low_type),
            shape_of((count, pairs * LANES), full_type),
        ],
        deps=deps,
        grid=(number,),
        in_specs=[
            on_scalars(),
            pl.BlockSpec((1, 2, lines.shape[2]), lambda i: (i + first, 0, 0)),
            pl.BlockSpec((1, parts, count, LANES), lambda i: (i + first, 0, 0, 0)),
            *[in_place()] * len(before),
        ],
        out_specs=[
            column,
            pl.BlockSpec((1, micro, 2, slot, slot), lambda i: (i + first, 0, 0, 0, 0)),
            column,
        ],
        input_output_aliases={3 + i: i for i in range(len(before))},
        scratch_shapes=[pltpu.VMEM((2, spans, LANES, LANES), full_type)],
    )(lengths, lines, qkv, *before)


def branch_kernel(att_ref, *refs):
    *weight_refs, out_ref, w_ref = refs

    @pl.when(pl.program_id(0) == 0)
    def assemble():
        fill_rows(w_ref, weight_refs)

    out_ref[...] = dot_nt(att_ref[...], w_ref[...]).astype(low_type)


def branch_rows(attended, weights, deps=()):
    count, head_width = attended.shape
    width = sum(piece.shape[0] for piece in weights)
    return call(
        branch_kernel,
        "branch",
        shape_of((count, width), low_type),
        deps=deps,
        grid=(count // (2 * ROWS),),
        in_specs=[
            row_blocks((2 * ROWS, head_width)),
            *(pl.BlockSpec((piece.shape[0], head_width), lambda i: (0, 3)) for piece in weights),
        ],
        out_specs=row_blocks((2 * ROWS, width)),
        scratch_shapes=[pltpu.VMEM((width, head_width), low_type)],
    )(attended, *weights)


def hidden_kernel(pieces, len_ref, x_ref, own_ref, came_ref, vector_ref, *refs):
    weight_refs, refs = refs[:pieces], refs[pieces:]
    normed_ref, slope_ref, act_ref, sum_ref, w_ref, rows_ref = refs
    m = pl.program_id(0)
    slot = x_ref.shape[0]

    @pl.when(m == 0)
    def assemble():
        fill_rows(w_ref, weight_refs)

    middle = middle_rows(x_ref, own_ref, came_ref)
    normed = (middle * rms_scale(middle) * vector_ref[1:2]).astype(low_type)
    valid = lax.broadcasted_iota(jnp.int32, (slot, 1), 0) < len_ref[m]
    normed_ref[...] = jnp.where(valid, normed, jnp.zeros_like(normed))
    rows_ref[...] = normed
    sum_ref[0] = jnp.sum(jnp.where(valid, middle, 0.0), axis=0, keepdims=True)
    act_ref[...] = jnp.zeros_like(act_ref)

    def rows_step(i, carry):
        rows = pl.ds(pl.multiple_of(i * ROWS, ROWS), ROWS)
        v = dot_nn(rows_ref[rows, :], w_ref[...])
        square = v * v
        gate = jnp.tanh(v * (gelu_slope + (gelu_slope * gelu_cubic) * square))
        half = 0.5 + 0.5 * gate
        active = (v * half).astype(low_type)
        counted = lax.broadcasted_iota(jnp.int32, (16, ROWS), 1) + i * ROWS < len_ref[m]
        counted = jnp.where(counted, 1.0, 0.0).astype(low_type)
        act_ref[0] += dot_nn(counted, active)[0:1]
        inner = 0.5 * gelu_slope + (1.5 * gelu_slope * gelu_cubic) * square
        slope_ref[rows, :] = (half + v * (1.0 - gate * gate) * inner).astype(low_type)
        return carry

    lax.fori_loop(0, slot // ROWS, rows_step, 0)


def middle_rows(x_ref, own_ref, came_ref):
    branch = own_ref[...].astype(full_type) + came_ref[...].astype(full_type)
    return x_ref[...].astype(full_type) + branch


def hidden(lengths, rows_low, own, came, vectors, weights, slot):
    count, width = rows_low.shape
    micro = count // slot
    inner = weights[0].shape[1]
    return call(
        functools.partial(hidden_kernel, len(weights)),
        "hidden_forward",
        [
            shape_of((count, width), low_type),
            shape_of((count, inner), low_type),
            shape_of((micro, 1, inner), full_type),
            shape_of((micro, 1, width), full_type),
            shape_of((width, inner), low_type),
        ],
        cost=(1200, 20000),
        grid=(micro,),
        in_specs=[
            on_scalars(),
            *[row_blocks((slot, width))] * 3,
            whole(vectors.shape),
            *(whole(piece.shape) for piece in weights),
        ],
        out_specs=[
            row_blocks((slot, width)),
            row_blocks((slot, inner)),
            row_blocks((1, 1, inner)),
            row_blocks((1, 1, width)),
            whole((width, inner)),
        ],
        scratch_shapes=[pltpu.VMEM((slot, width), low_type)],
    )(lengths, rows_low, own, came, vectors, *weights)


def few_rows(rows, count):
    place = lax.broadcasted_iota(jnp.int32, (count, rows[0].shape[1]), 0)
    total = jnp.zeros(place.shape, full_type)
    for i, row in enumerate(rows):
        total = jnp.where(place == i, row, total)
    return total


def pool_kernel(act_ref, *refs):
    *weight_refs, out_ref, w_ref = refs
    fill_rows(w_ref, weight_refs)
    sums = [act_ref[m] for m in range(act_ref.shape[0])]
    highs = [row.astype(low_type).astype(full_type) for row in sums]
    rests = [row - high for row, high in zip(sums, highs)]
    down = dot_nt(few_rows(highs + rests, 16).astype(low_type), w_ref[...])
    micro = len(sums)
    out_ref[...] = few_rows([down[m : m + 1] + down[micro + m : micro + m + 1] for m in range(micro)], 8)


def margin_kernel(len_ref, own_ref, other_ref, sum_ref, act_ref, vector_ref, send_ref):
    margins, rows = [], []
    for m in range(sum_ref.shape[0]):
        length = len_ref[m].astype(full_type)
        total = own_ref[m : m + 1] + other_ref[m : m + 1] + sum_ref[m]
        pooled = (total / length).astype(low_type).astype(full_type)
        final = pooled * rms_scale(pooled) * vector_ref[2:3]
        logits = [
            jnp.sum(final * vector_ref[i : i + 1], axis=1, keepdims=True) * pooled.shape[1] ** (-0.5)
            for i in (3, 4)
        ]
        lane = lax.broadcasted_iota(jnp.int32, pooled.shape, 1)
        margins.append(jnp.where(lane < LANES, logits[0] - logits[1], length))
        rows.append(pooled)
    width = rows[0].shape[1]
    for m in range(sum_ref.shape[0]):
        sums = act_ref[m]
        rows += [sums[:, i * width : (i + 1) * width] for i in range(sums.shape[1] // width)]
    send_ref[...] = few_rows(rows + margins, 8)


def ranking(margins, same, positive):
    place = lax.broadcasted_iota(jnp.int32, margins.shape, 0)
    lane = lax.broadcasted_iota(jnp.int32, margins.shape, 1)
    others = jnp.sum(jnp.where(place == lane, margins, 0.0), axis=0, keepdims=True)
    row_max = jnp.max(jnp.where(same, others, masked_score), axis=1, keepdims=True)
    terms = jnp.where(same, jnp.exp(jnp.where(same, others - row_max, 0.0)), 0.0)
    chance = jnp.exp(margins - row_max) / jnp.sum(terms, axis=1, keepdims=True)
    return LOSS_SCALE * (chance - positive)


def pooled_grad(pooled, d_margin, vector_ref):
    scale = rms_scale(pooled)
    d_logit = d_margin * pooled.shape[1] ** (-0.5)
    d_final = d_logit * (vector_ref[3:4] - vector_ref[4:5])
    return norm_input_grad(d_final, vector_ref[2:3], pooled, scale)


def rank_kernel(
    small_pieces, len_ref, same_ref, positive_ref, vector_ref, slope_ref, down_ref, up_ref, *refs
):
    small_refs, refs = refs[:small_pieces], refs[small_pieces:]
    line_ref, act_ref, rank_ref, hidden_ref, d_ref = refs
    m = pl.program_id(0)

    @pl.when(m == 0)
    def rank():
        lines = []
        for i in range(2):
            margins = stacked_row(small_refs, 6 + i)[:, :LANES]
            d_margins = ranking(margins, same_ref[i] > 0.5, positive_ref[i])
            rank_ref[i] = d_margins
            pooled = small_refs[0][0, i : i + 1, :]
            d_pooled = pooled_grad(pooled, d_margins[0:1, 0:1], vector_ref)
            lines.append(d_pooled / len_ref[i].astype(full_type))
        line_ref[...] = few_rows(lines, 8)
        d_act = dot_nn(few_rows(lines, 16).astype(low_type), down_ref[...])
        act_ref[...] = d_act[:8]

    d_row = jnp.where(m == 0, act_ref[0:1], act_ref[1:2])
    d_hidden = (slope_ref[...].astype(full_type) * d_row).astype(low_type)
    hidden_ref[...] = d_hidden
    d_normed = dot_nt(d_hidden, up_ref[...])
    valid = lax.broadcasted_iota(jnp.int32, (d_normed.shape[0], 1), 0) < len_ref[m]
    d_ref[...] = jnp.where(valid, d_normed, 0.0).astype(low_type)


def rank_back(lengths, same, positive, vectors, slope, small_all, down, up, slot, deps):
    count, inner = slope.shape
    width = vectors.shape[1]
    return call(
        functools.partial(rank_kernel, len(small_all)),
        "rank_backward",
        [
            shape_of((8, width), full_type),
            shape_of((8, inner), full_type),
            shape_of(positive.shape, full_type),
            shape_of((count, inner), low_type),
            shape_of((count, width), low_type),
        ],
        cost=(1200, 20000),
        deps=deps,
        grid=(count // slot,),
        in_specs=[
            on_scalars(),
            *(whole(array.shape) for array in (same, positive, vectors)),
            row_blocks((slot, inner)),
            *(whole(array.shape) for array in (down, up, *small_all)),
        ],
        out_specs=[
            whole((8, width)),
            whole((8, inner)),
            whole(positive.shape),
            row_blocks((slot, inner)),
            row_blocks((slot, width)),
        ],
    )(lengths, same, positive, vectors, slope, down, up, *small_all)


def up_grad_kernel(normed_ref, d_ref, *out_refs):
    for n in range(normed_ref.shape[1] // ROWS):
        columns = slice(n * ROWS, (n + 1) * ROWS)
        spill_rows(dot_tn(normed_ref[:, columns], d_ref[...]), out_refs, n * ROWS)


def up_grad(normed, d_hidden, rows):
    return call(
        up_grad_kernel,
        "hidden_in_gradient",
        [shape_of((r, d_hidden.shape[1]), low_type) for r in rows],
        cost=(1200, 15000),
    )(normed, d_hidden)


def middle_kernel(
    pieces, len_ref, x_ref, branch_ref, other_ref, own_ref, came_ref, vector_ref, line_ref,
    att_ref, inv_ref, *refs
):
    weight_refs, refs = refs[:pieces], refs[pieces:]
    d_ref, d_att_ref, total_ref, w_ref = refs
    m = pl.program_id(0)

    @pl.when(m == 0)
    def assemble():
        fill_rows(w_ref, weight_refs)
        total_ref[...] = jnp.zeros_like(total_ref)

    middle = middle_rows(x_ref, branch_ref, other_ref)
    own = own_ref[...].astype(full_type)
    scale = rms_scale(middle)
    valid = lax.broadcasted_iota(jnp.int32, (middle.shape[0], 1), 0) < len_ref[m]
    line = jnp.where(m == 0, line_ref[0:1], line_ref[1:2])
    d_middle = jnp.where(valid, line, 0.0) + norm_input_grad(
        own + came_ref[...].astype(full_type), vector_ref[1:2], middle, scale
    )
    d_ref[...] = d_middle
    d_low = d_middle.astype(low_type)
    d_att_ref[...] = (dot_nn(d_low, w_ref[...]) * inv_ref[...]).astype(low_type)
    total_ref[...] += dot_tn(d_low, att_ref[...])


def middle_back(
    lengths, rows_low, branch, other, own, came, vectors, lines, attended, inverse, weights, slot
):
    count, width = rows_low.shape
    head_width = attended.shape[1]
    return call(
        functools.partial(middle_kernel, len(weights)),
        "middle_backward",
        [
            shape_of((count, width), full_type),
            shape_of((count, head_width), low_type),
            shape_of((width, head_width), full_type),
        ],
        cost=(600, 15000),
        grid=(count // slot,),
        in_specs=[
            on_scalars(),
            *[row_blocks((slot, width))] * 5,
            whole(vectors.shape),
            whole(lines.shape),
            row_blocks((slot, head_width)),
            row_blocks((slot, head_width)),
            *(
                pl.BlockSpec((piece.shape[0], head_width), lambda i: (0, 3)) for piece in weights
            ),
        ],
        out_specs=[
            row_blocks((slot, width)),
            row_blocks((slot, head_width)),
            whole((width, head_width)),
        ],
        scratch_shapes=[pltpu.VMEM((width, head_width), low_type)],
    )(
        lengths, rows_low, branch, other, own, came, vectors, lines, attended, inverse, *weights
    )


def attention_back_kernel(
    befores, grads, tables, own, prob_ref, qkv_ref, d_ref, att_ref, turned_ref, hot_ref, *refs
):
    table_refs, refs = refs[:tables], refs[tables:]
    grad_refs, refs = refs[:grads], refs[grads:]
    d_out_ref, table_ref, *out_refs, tile_ref, dk_ref, dv_ref = refs[befores:]
    step, last = pl.program_id(0), pl.num_programs(0) - 1
    steps = last - 1 if grads else last

    if grads:

        @pl.when(step == last)
        def projection():
            spill_rows(grad_refs[0][...], out_refs)

    @pl.when(step <= steps)
    def heads():
        pair_back(
            prob_ref, qkv_ref, d_ref, att_ref, turned_ref, hot_ref, d_out_ref, table_ref, out_refs,
            tile_ref, dk_ref, dv_ref
        )
        if tables:
            lines = [
                ref[p, h : h + 1]
                for ref in (*table_refs, table_ref)
                for p in range(ref.shape[0])
                for h in range(2)
            ]
            width = turned_ref.shape[0]
            place = lax.broadcasted_iota(jnp.int32, (width, 16), 0) % own
            pick = place == lax.broadcasted_iota(jnp.int32, (width, 16), 1)
            pick = jnp.where(pick, 1.0, 0.0).astype(low_type)
            spread = dot_nn(pick, few_rows(lines, 16).astype(low_type))
            spill_rows(spread, [ref.at[:, 3 * LANES :] for ref in out_refs])


def pair_back(
    prob_ref, qkv_ref, d_ref, att_ref, turned_ref, hot_ref, d_out_ref, table_ref, out_refs,
    tile_ref, dk_ref, dv_ref
):
    micro, slot = prob_ref.shape[1], prob_ref.shape[3]
    blocks = slot // LANES
    spans = 2 * blocks - 1
    lanes = head_lanes()

    tile_ref[...] = jnp.zeros_like(tile_ref)

    def micro_step(m, carry):
        start = pl.multiple_of(m * slot, slot)
        everything = pl.ds(start, slot)
        keys, values = qkv_ref[0, 1, everything, :], qkv_ref[0, 2, everything, :]
        for r in range(slot // SPAN):
            rows = pl.ds(start + r * SPAN, SPAN)
            queries = qkv_ref[0, 0, rows, :]
            queries = jnp.concatenate(
                [queries * lanes[h].astype(low_type) for h in range(2)], axis=0
            )
            d_att = d_ref[rows, :]
            product = d_att.astype(full_type) * att_ref[rows, :].astype(full_type)
            row_dot = jnp.concatenate(
                [
                    jnp.sum(jnp.where(lanes[h], product, 0.0), axis=1, keepdims=True)
                    for h in range(2)
                ],
                axis=0,
            )
            d_att = jnp.concatenate([d_att * lanes[h].astype(low_type) for h in range(2)], axis=0)
            span = slice(r * SPAN, (r + 1) * SPAN)
            probs = jnp.concatenate([prob_ref[0, m, h, span, :] for h in range(2)], axis=0)
            d_scores = probs.astype(full_type) * (dot_nt(d_att, values) - row_dot)
            d_low = d_scores.astype(low_type)
            for h in range(2):
                for i in range(SPAN // LANES):
                    for j in range(blocks):
                        top = h * SPAN + i * LANES
                        tile_ref[h, j - r * (SPAN // LANES) - i + blocks - 1] += d_scores[
                            top : top + LANES, j * LANES : (j + 1) * LANES
                        ]
            d_queries = dot_nn(d_low, keys)
            d_out_ref[0, 0, rows, :] = jnp.where(
                lanes[0], d_queries[:SPAN], d_queries[SPAN:]
            ).astype(low_type)
            d_keys, d_values = dot_tn(d_low, queries), dot_tn(probs, d_att)
            dk_ref[...] = d_keys if r == 0 else dk_ref[...] + d_keys
            dv_ref[...] = d_values if r == 0 else dv_ref[...] + d_values
        d_out_ref[0, 1, everything, :] = dk_ref[...].astype(low_type)
        d_out_ref[0, 2, everything, :] = dv_ref[...].astype(low_type)
        return carry

    lax.fori_loop(0, micro, micro_step, 0, unroll=True)
    d_project = jnp.concatenate([d_out_ref[0, c] for c in range(3)], axis=1)
    spill_rows(dot_nn(turned_ref[...], d_project), [ref.at[:, : 3 * LANES] for ref in out_refs])
    flip = (
        lax.broadcasted_iota(jnp.int32, (LANES, LANES), 0)
        + lax.broadcasted_iota(jnp.int32, (LANES, LANES), 1)
        == LANES - 1
    )
    flip = jnp.where(flip, 1.0, 0.0).astype(low_type)
    tiles = tile_ref[...].reshape(2 * spans * LANES, LANES)
    high = tiles.astype(low_type)
    rest = (tiles - high.astype(full_type)).astype(low_type)
    flipped = dot_nn(high, flip) + dot_nn(rest, flip)
    zeros = jnp.zeros((LANES, LANES), full_type)
    lines = []
    for h in range(2):
        sums = []
        for d in range(spans):
            top = (h * spans + d) * LANES
            wide = jnp.concatenate([flipped[top : top + LANES], zeros], axis=1)
            turned = pltpu.roll(wide, 0, 1, stride=1, stride_axis=0)
            sums.append(jnp.sum(turned, axis=0, keepdims=True))
        lines.append(jnp.concatenate(sums, axis=1))
    highs = [line.astype(low_type).astype(full_type) for line in lines]
    rests = [line - high for line, high in zip(lines, highs)]
    table = dot_nn(few_rows(highs + rests, 16).astype(low_type), hot_ref[...])
    table_ref[0] = few_rows([table[h : h + 1] + table[2 + h : 3 + h] for h in range(2)], 8)


def attention_back(
    probs, qkv, d_attended, attended, turned, hot, rows, first, number, slot, own,
    grad_out=None, tables=(), before=(), deps=()
):
    width, count = turned.shape
    micro = count // slot
    pairs = qkv.shape[0]
    spans = 2 * (slot // LANES) - 1
    at = lambda i: jnp.minimum(i, number - 1)
    lead = lambda shape: pl.BlockSpec(shape, lambda i: (at(i) + first,) + (0,) * (len(shape) - 1))
    column = pl.BlockSpec((count, LANES), lambda i: (0, at(i) + first))
    if tables:
        steps, extra, extra_specs = number, tables, [whole(table.shape) for table in tables]
        gradients = [shape_of((r, 4 * LANES), low_type) for r in rows]
        gradient_specs = [whole((r, 4 * LANES)) for r in rows]
    else:
        steps = number + (grad_out is not None)
        extra = () if grad_out is None else (grad_out,)
        extra_specs = [whole(array.shape) for array in extra]
        gradients = [shape_of((r, pairs * 3 * LANES), low_type) for r in rows]
        gradient_specs = [pl.BlockSpec((r, 3 * LANES), lambda i: (0, i + first)) for r in rows]
    position = 6 + len(extra)
    return call(
        functools.partial(
            attention_back_kernel, len(before), 0 if grad_out is None else 1, len(tables), own
        ),
        "attention_backward",
        [
            shape_of((pairs, 3, count, LANES), low_type),
            shape_of((number, 8, LANES), full_type),
            *gradients,
        ],
        deps=deps,
        grid=(steps,),
        in_specs=[
            lead((1, micro, 2, slot, slot)),
            lead((1, 3, count, LANES)),
            column,
            column,
            whole(turned.shape),
            whole(hot.shape),
            *extra_specs,
            *[in_place()] * len(before),
        ],
        out_specs=[lead((1, 3, count, LANES)), pl.BlockSpec((1, 8, LANES), lambda i: (at(i), 0, 0)), *gradient_specs],
        input_output_aliases={position + i: i if i == 0 else i + 1 for i in range(len(before))},
        scratch_shapes=[
            pltpu.VMEM((2, spans, LANES, LANES), full_type),
            pltpu.VMEM((slot, LANES), full_type),
            pltpu.VMEM((slot, LANES), full_type),
        ],
    )(probs, qkv, d_attended, attended, turned, hot, *extra, *before)


def normed_back_kernel(d_ref, *refs):
    *weight_refs, out_ref, w_ref = refs
    pairs, parts = d_ref.shape[0], d_ref.shape[1]

    @pl.when(pl.program_id(0) == 0)
    def assemble():
        fill_rows(w_ref, weight_refs, slice(0, w_ref.shape[1]))

    blocks = [d_ref[p, c] for c in range(parts) for p in range(pairs)]
    d_normed = dot_nt(jnp.concatenate(blocks, axis=1), w_ref[...])
    out_ref[...] = d_normed.astype(low_type)


def normed_back(d_project, weights, deps):
    pairs, parts, count, _ = d_project.shape
    width = sum(piece.shape[0] for piece in weights)
    return call(
        normed_back_kernel,
        "normed_backward",
        shape_of((count, width), low_type),
        cost=(900, 15000),
        deps=deps,
        grid=(count // ROWS,),
        in_specs=[
            pl.BlockSpec((pairs, parts, ROWS, LANES), lambda i: (0, 0, i, 0)),
            *(whole(piece.shape) for piece in weights),
        ],
        out_specs=row_blocks((ROWS, width)),
        scratch_shapes=[pltpu.VMEM((width, pairs * parts * LANES), low_type)],
    )(d_project, *weights)


def token_kernel(d_ref, own_ref, came_ref, x_ref, vector_ref, order_ref, out_ref, done_ref):
    x = x_ref[...].astype(full_type)
    d_normed = own_ref[...].astype(full_type) + came_ref[...].astype(full_type)
    grad = d_ref[...] + norm_input_grad(d_normed, vector_ref[0:1], x, rms_scale(x))
    high = grad.astype(low_type)
    rest = (grad - high.astype(full_type)).astype(low_type)
    order = order_ref[...]
    out_ref[...] = dot_nt(high, order) + dot_nt(rest, order)
    done_ref[...] = jnp.zeros_like(done_ref)


def token_back(d_middle, own, came, rows_low, vectors, order, deps):
    count, width = rows_low.shape
    return call(
        token_kernel,
        "token_gradient",
        [shape_of((count, width), full_type), shape_of((8, LANES), full_type)],
        cost=(1200, 15000),
        deps=deps,
        grid=(count // ROWS,),
        in_specs=[row_blocks((ROWS, width))] * 4 + [whole(vectors.shape), whole(order.shape)],
        out_specs=[row_blocks((ROWS, width)), whole((8, LANES))],
    )(d_middle, own, came, rows_low, vectors, order)


def total_kernel(smalls, counts, micro, pairs, *refs):
    small_refs, refs = refs[:smalls], refs[smalls:]
    groups = []
    for count in counts:
        groups.append(refs[:count])
        refs = refs[count:]
    rank_ref, vector_ref, in_ref, up_ref, gain_ref, tied_ref, down_ref, line_ref, *out_refs = refs
    size, width = sum(ref.shape[0] for ref in small_refs), small_refs[0].shape[2]
    row_of = lambda row: stacked_row(small_refs, row)
    own = down_ref.shape[0]
    inverse = 1.0 / LOSS_SCALE
    add_up = lambda values: jnp.sum(values, axis=0, keepdims=True).sum(axis=1, keepdims=True)
    squares, sums = 0.0, []
    for group, out_ref in zip(groups, out_refs):
        total = sum(ref[...].astype(full_type) for ref in group) * inverse
        total, rest = total[:, : out_ref.shape[1]], total[:, out_ref.shape[1] :]
        out_ref[...] = total
        sums.append((total, rest))
        squares = squares + add_up(total * total)
    table = sums[1][1]

    block = lax.broadcasted_iota(jnp.int32, (size, width), 1) // own
    mine = block == lax.broadcasted_iota(jnp.int32, (size, width), 0)
    fold = lax.broadcasted_iota(jnp.int32, (width, LANES), 0) % own == lax.broadcasted_iota(
        jnp.int32, (width, LANES), 1
    )
    fold = jnp.where(fold, 1.0, 0.0).astype(low_type)
    down, ranked = 0.0, 0.0
    lane = lax.broadcasted_iota(jnp.int32, (1, LANES), 1)
    own_factor = (vector_ref[3:4, :LANES] - vector_ref[4:5, :LANES]) * vector_ref[2:3, :LANES]
    own_factor = jnp.where(lane < own, own_factor, 0.0)
    parts = down_ref.shape[1] // width
    for m in range(micro):
        pooled = row_of(m)
        scale = rms_scale(pooled)
        lengths = row_of(micro + micro * parts + m)
        margins, lengths = lengths[:, 0:1], lengths[:, LANES : LANES + 1]
        d_logit = rank_ref[m][:, 0:1] * width ** (-0.5)
        mean = d_logit * margins * (width**0.5 / width) / scale
        mine_low = dot_nn(jnp.where(mine, pooled, 0.0).astype(low_type), fold)
        ranked = ranked + jnp.sum(mine_low * scale * d_logit, axis=0, keepdims=True)
        d_pooled = scale * d_logit * own_factor - mine_low * scale**3 * mean
        lines = (d_pooled / lengths).astype(low_type)
        acts = [row_of(micro + m * parts + i) for i in range(parts)]
        acts = jnp.concatenate(acts, axis=1)
        high = acts.astype(low_type)
        rest = (acts - high.astype(full_type)).astype(low_type)
        down = down + dot_tn(lines, high) + dot_tn(lines, rest)
    down = down[:own] * inverse
    down_ref[...] = down
    squares = squares + add_up(down * down)

    ranked = ranked[:, :own] * inverse
    rounded = lambda ref, i: ref[i : i + 1].astype(low_type).astype(full_type)
    tied_gap = rounded(tied_ref, 0) - rounded(tied_ref, 1)

    def through(products):
        ones = jnp.ones((16, products.shape[1]), low_type)
        high = products.astype(low_type)
        rest = (products - high.astype(full_type)).astype(low_type)
        return (dot_nt(ones, high) + dot_nt(ones, rest))[0:1]

    weighed = lambda ref, total: ref.astype(low_type).astype(full_type) * total
    first = 0.0
    for p in range(pairs):
        source = sums[0][0] if p < pairs - 1 else sums[1][0]
        offset = p * 3 * LANES if p < pairs - 1 else 0
        for c in range(3):
            columns = slice(offset + c * LANES, offset + (c + 1) * LANES)
            first = first + weighed(in_ref[c, :, p * LANES : (p + 1) * LANES], source[:, columns])
    rows = [
        through(first) / rounded(gain_ref, 0),
        through(weighed(up_ref[...], sums[2][0])) / rounded(gain_ref, 1),
        tied_gap * ranked,
        rounded(gain_ref, 2) * ranked,
    ]
    place = lax.broadcasted_iota(jnp.int32, (8, own), 0)
    extra = jnp.zeros((8, own), full_type)
    for i, row in enumerate(rows):
        extra = jnp.where(place == i, row, extra)
    line_ref[...] = jnp.zeros_like(line_ref)
    line_ref[:8, :own] = extra
    line_ref[8:16] = jnp.broadcast_to(squares, (8, LANES))
    line_ref[16 : 16 + 2 * pairs] = table[: 2 * pairs]


def totals(
    small_all, ranks, vectors, grads, heads_in, hidden_in, gains, tied_rows, widths, micro, deps
):
    counts = tuple(len(group) for group in grads)
    flat = [array for group in grads for array in group]
    own, inner = hidden_in.shape
    down, line, *sums = call(
        functools.partial(
            total_kernel, len(small_all), counts, micro, heads_in.shape[2] // LANES
        ),
        "gradient_totals",
        [
            shape_of((own, inner), full_type),
            shape_of((24, LANES), full_type),
            *(shape_of((own, width), full_type) for width in widths),
        ],
        cost=(100, 10000),
        deps=deps,
    )(*small_all, *flat, ranks, vectors, heads_in, hidden_in, gains, tied_rows)
    return down, line, sums


def stage_kernel(*refs):
    count = len(refs) // 2
    for ref, target in zip(refs[:count], refs[count:]):
        target[...] = ref[...]


def adam(weight, first_old, second, grad, factor, rate, decay, step_ref):
    clipped = grad * factor
    next_first = beta_first * first_old + (1.0 - beta_first) * clipped
    next_second = beta_second * second + (1.0 - beta_second) * clipped * clipped
    first_hat = next_first * step_ref[0]
    second_hat = next_second * step_ref[1]
    next_weight = weight - rate * (first_hat / (jnp.sqrt(second_hat) + adam_eps) + decay * weight)
    return next_weight, next_first, next_second


def square_kernel(heads, own_ref, other_ref, out_ref, extra_ref):
    place = lax.broadcasted_iota(jnp.int32, (8, LANES), 0)
    extra = own_ref[:8] + jnp.where(place < 2, other_ref[:8], 0.0)
    extra_ref[...] = extra
    counted = jnp.where(place == 3, 2.0, 1.0) * extra * extra
    add_up = lambda values: jnp.sum(values, axis=0, keepdims=True).sum(axis=1, keepdims=True)
    squares = own_ref[8:16] + other_ref[8:16] + add_up(counted)
    out_ref[:8] = squares
    tables = own_ref[16:24] * own_ref[16:24] + other_ref[16:24] * other_ref[16:24]
    out_ref[8:16] = own_ref[16:24]
    out_ref[16:24] = jnp.broadcast_to(add_up(tables), (8, LANES))


def update_kernel(size, squares, groups, me_ref, step_ref, extra_ref, *refs):
    square_refs, refs = refs[:squares], refs[squares:]
    grad_refs, refs = refs[:groups], refs[groups:]
    state_refs, refs = refs[:21], refs[21:]
    norm_ref, *out_refs = refs
    tiles = stacked(square_refs)
    place = lax.broadcasted_iota(jnp.int32, (tiles.shape[0], 1, 1), 0)
    first = device_of(place, me_ref[0], size) == 0
    tables = jnp.sum(jnp.where(first, tiles[:, 8:24], 0.0), axis=0)
    norm = jnp.sqrt(jnp.sum(tiles[:, 0:8], axis=0)[0:1, 0:1] + tables[8:9, 0:1])
    norm_ref[...] = norm
    factor = jnp.minimum(1.0, clip_limit / (norm + 1e-06))
    weights, firsts, seconds = state_refs[:7], state_refs[7:14], state_refs[14:]
    next_weights, next_firsts, next_seconds = out_refs[:7], out_refs[7:14], out_refs[14:]

    def step(index, where, grad, rate, decay):
        results = adam(
            weights[index][where], firsts[index][where], seconds[index][where], grad, factor,
            rate, decay, step_ref,
        )
        for target, result in zip((next_weights, next_firsts, next_seconds), results):
            target[index][where] = result

    everything = (slice(None), slice(None))
    early_ref, late_ref, up_ref, down_ref = grad_refs
    pairs = weights[0].shape[2] // LANES
    for p in range(pairs):
        source, offset = (early_ref, p * 3) if p < pairs - 1 else (late_ref, 0)
        for c in range(3):
            columns = slice((offset + c) * LANES, (offset + c + 1) * LANES)
            where = (c, slice(None), slice(p * LANES, (p + 1) * LANES))
            step(0, where, source[:, columns], rate_matrix, decay_matrix)
    step(1, everything, early_ref[:, (pairs - 1) * 3 * LANES :], rate_matrix, decay_matrix)
    step(2, everything, up_ref[...], rate_matrix, decay_matrix)
    step(3, everything, down_ref[...], rate_matrix, decay_matrix)
    rows = weights[4].shape[1]
    extra = extra_ref[...]
    step(4, everything, extra[0:3, :rows], rate_vector, 0.0)
    tied = extra[3:4, :rows]
    step(5, everything, jnp.concatenate([tied, -tied], axis=0), rate_vector, 0.0)
    step(6, everything, tables[: 2 * pairs, :BUCKETS], rate_vector, 0.0)


def update(size, pick, corrections, extra, squares, grads, states):
    return call(
        functools.partial(update_kernel, size, len(squares), len(grads)),
        "update",
        [shape_of((1, 1), full_type)] + [shape_of(s.shape, full_type) for s in states],
        cost=(0, 6000),
        grid=(1,),
        in_specs=[
            on_scalars(),
            on_scalars(),
            *(whole(array.shape) for array in (extra, *squares, *grads, *states)),
        ],
    )(pick, corrections, extra, *squares, *grads, *states)


def body(
    tokens,
    pair_lengths,
    query_ids,
    distance_bucket,
    step_count,
    heads_in,
    heads_out,
    hidden_in,
    hidden_out,
    gains,
    tied_rows,
    bias_table,
    first_heads_in,
    first_heads_out,
    first_hidden_in,
    first_hidden_out,
    first_gains,
    first_tied,
    first_table,
    second_heads_in,
    second_heads_out,
    second_hidden_in,
    second_hidden_out,
    second_gains,
    second_tied,
    second_table,
):
    size = lax.axis_size("dp")
    me = lax.axis_index("dp")
    core = lax.axis_index("mp")
    micro, _, slot, width = tokens.shape
    count = micro * slot
    own, local_heads = heads_in.shape[0], bias_table.shape[1]
    head_width = heads_in.shape[2]
    inner = hidden_in.shape[1]
    pairs = local_heads // 2
    spans = 2 * (slot // LANES) - 1
    turn_matrix = lambda array: jnp.transpose(array, (1, 0, 2))
    heads_in, first_heads_in, second_heads_in = (
        turn_matrix(array) for array in (heads_in, first_heads_in, second_heads_in)
    )
    gains, tied_rows, bias_table = gains.T, tied_rows.T, bias_table.T
    first_gains, first_tied, first_table = first_gains.T, first_tied.T, first_table.T
    second_gains, second_tied, second_table = second_gains.T, second_tied.T, second_table.T

    packed_heads = call(
        pack_heads_kernel, "pack_heads", shape_of((own, 4 * head_width + LANES), low_type), vmem=56
    )(heads_in, heads_out, gains, tied_rows)
    packed_up, packed_down = call(
        pack_hidden_kernel, "pack_hidden", [shape_of((own, inner), low_type)] * 2
    )(hidden_in, hidden_out)
    weights = (heads_in, heads_out, hidden_in, hidden_out, gains, tied_rows, bias_table)
    firsts = (
        first_heads_in,
        first_heads_out,
        first_hidden_in,
        first_hidden_out,
        first_gains,
        first_tied,
        first_table,
    )
    seconds = (
        second_heads_in,
        second_heads_out,
        second_hidden_in,
        second_hidden_out,
        second_gains,
        second_tied,
        second_table,
    )
    states = [*weights, *firsts, *seconds]
    large = [index for index, state in enumerate(states) if index % 7 < 4]
    staged = call(
        stage_kernel, "stage", [shape_of(states[i].shape, full_type) for i in large], vmem=56
    )(*(states[i] for i in large))
    for i, array in zip(large, staged):
        states[i] = array

    lengths = pair_lengths.reshape(micro)
    device = me.reshape(1)
    order, lines, hot_spans, same_tile, positive_tile = call(
        functools.partial(prepare_kernel, size),
        "prepare",
        [
            shape_of((width, width), low_type),
            shape_of((pairs, 2, 2 * slot), full_type),
            shape_of((spans * 2 * LANES, LANES), low_type),
            shape_of((micro, size, LANES), full_type),
            shape_of((micro, size, LANES), full_type),
        ],
        grid=(1,),
        in_specs=[
            on_scalars(),
            whole((1, 2 * slot)),
            whole(bias_table.shape),
            whole(query_ids.shape),
        ],
    )(
        device,
        jnp.pad(distance_bucket, (0, 1), constant_values=-1).reshape(1, 2 * slot),
        bias_table,
        query_ids,
    )
    step_float = step_count.astype(full_type)
    corrections = jnp.stack(
        [1.0 / (1.0 - beta_first**step_float), 1.0 / (1.0 - beta_second**step_float)]
    )

    rows_low = call(
        order_kernel,
        "order_tokens",
        shape_of((count, width), low_type),
        cost=(600, 5000),
        grid=(count // ROWS,),
        in_specs=[row_blocks((ROWS, width)), whole((width, width))],
        out_specs=row_blocks((ROWS, width)),
    )(tokens.reshape(count, width), order)
    if size != 16:
        weight_heads, weight_up, weight_down = (
            [gather_doubling(part, size)] for part in (packed_heads, packed_up, packed_down)
        )
        qkv, normed_first, vectors = project(rows_low, weight_heads, pairs, ())
    else:
        heads_line, packed_up, packed_down = join(
            line_parts(packed_heads, size, "heads"),
            deps=(staged[0], order, corrections),
            passing=(packed_up, packed_down),
        )
        heads_sides = side_parts(heads_line, size, "heads")
        up_pair = join(
            [packed_up, swap(packed_up, 8, size, "up")],
            deps=(rows_low,),
        )
        up_near = swap(up_pair, 4, size, "up")
        low, high, packed_down = gather_step(*heads_sides, deps=(up_pair,), passing=(packed_down,))
        down_far = swap(packed_down, 8, size, "down")
        heads_corner = corner_parts(low, high, size, "heads_corner")
        up_line = join([up_pair, up_near], deps=(low,))
        down_pair = join([packed_down, down_far], deps=(up_line,))
        down_near = swap(down_pair, 4, size, "down")
        up_sides = side_parts(up_line, size, "up")
        weight_heads = [heads_line, *heads_sides, *heads_corner]
        qkv, normed_first, vectors = project(rows_low, weight_heads, pairs, (down_pair,))
    filled = attention(lengths, lines, qkv, 0, 1, slot)
    if size == 16:
        down_line = join([down_pair, down_near], deps=(filled[0],))
        down_sides = side_parts(down_line, size, "down")
    if pairs > 1:
        filled = attention(lengths, lines, qkv, 1, pairs - 1, slot, before=filled)
    if size == 16:
        low, high = gather_step(*up_sides, deps=(filled[0],))
        up_corner = corner_parts(low, high, size, "up_corner")
        weight_up = [up_line, *up_sides, *up_corner]
    turned_first = call(turn_kernel, "turn", shape_of((width, count), low_type))(normed_first)
    attended, probs, inverse = filled
    branch = branch_rows(
        attended, weight_heads, (low, *down_sides, turned_first) if size == 16 else ()
    )
    if size == 16:
        low, high = gather_step(*down_sides, deps=(branch,))
        down_corner = corner_parts(low, high, size, "down_corner")
        weight_down = [down_line, *down_sides, *down_corner]
    branch_came = other_core(branch, "branch_other_core")
    normed_second, slope, act_sum, middle_sum, full_up = hidden(
        lengths, rows_low, branch, branch_came, vectors, weight_up, slot
    )
    down, full_down = call(
        pool_kernel,
        "pool",
        [shape_of((8, width), full_type), shape_of((width, inner), low_type)],
        cost=(20, 5000),
    )(act_sum, *weight_down)
    small = call(
        margin_kernel,
        "margin",
        shape_of((8, width), full_type),
        grid=(1,),
        in_specs=[
            on_scalars(),
            *(whole(array.shape) for array in (down, down, middle_sum, act_sum, vectors)),
        ],
        out_specs=whole((8, width)),
    )(lengths, down, other_core(down, "pooled_part_other_core"), middle_sum, act_sum, vectors)
    small_all = gather_small(small, size, "small_sums")

    d_line, _, ranks, d_hidden, d_normed_second = rank_back(
        lengths, same_tile, positive_tile, vectors, slope, small_all, full_down, full_up, slot,
        (turned_first,),
    )
    d_normed_second_came = other_core(d_normed_second, "second_gradient_other_core")
    up_sum = Scatter(
        up_grad(normed_second, d_hidden, piece_rows(size, width)), size, "up_gradient"
    )
    d_middle, d_attended, g_out = middle_back(
        lengths, rows_low, branch, branch_came, d_normed_second, d_normed_second_came, vectors,
        d_line, attended, inverse, weight_heads, slot,
    )
    scatter_sides([up_sum], deps=(d_attended,))
    d_project, tables, *g_early = attention_back(
        probs, qkv, d_attended, attended, turned_first, hot_spans, piece_rows(size, width),
        0, pairs - 1, slot, own, grad_out=g_out,
    )
    early_sum = Scatter(g_early, size, "early_gradient")
    d_project, table, *g_late = attention_back(
        probs, qkv, d_attended, attended, turned_first, hot_spans, piece_rows(size, width),
        pairs - 1, 1, slot, own, tables=(tables,), before=(d_project,),
    )
    late_sum = Scatter(g_late, size, "late_gradient")
    up_sum.near(deps=(table,))
    sides = scatter_sides([early_sum, late_sum], deps=tuple(up_sum.came))
    d_normed_first = normed_back(d_project, weight_heads, sides)
    up_parts = up_sum.far(deps=sides)
    (d_normed_first,) = early_sum.near(deps=tuple(up_parts), passing=(d_normed_first,))
    token_gradient, token_done = token_back(
        d_middle, d_normed_first, other_core(d_normed_first, "first_gradient_other_core"), rows_low,
        vectors, order, early_sum.sources,
    )
    early_parts = early_sum.far(deps=(token_done,))
    late_parts, _ = late_sum.line(deps=(early_parts[0],))

    g_down, line, grad_sums = totals(
        small_all, ranks, vectors, [early_parts, late_parts, up_parts], heads_in, hidden_in, gains, tied_rows,
        (head_width * 3, 3 * LANES, inner), micro, (),
    )
    square_tile, extra = call(
        functools.partial(square_kernel, local_heads),
        "squares",
        [shape_of((24, LANES), full_type), shape_of((8, LANES), full_type)],
    )(line, other_core(line, "totals_other_core"))
    squares_all = gather_small(square_tile, size, "squares")
    grads = [*grad_sums, g_down]
    norm, *results = update(size, device, corrections, extra, squares_all, grads, states)
    for index in (0, 7, 14):
        results[index] = turn_matrix(results[index])
        for other in (4, 5, 6):
            results[index + other] = results[index + other].T
    return (norm.reshape(()), token_gradient.reshape(tokens.shape), *results)


def solution(mesh):
    in_specs = (
        P(None, "dp", None, None),
        P(None, "dp"),
        P(),
        P(),
        P(),
        P("dp", None, "mp"),
        P("dp", "mp"),
        P("dp", "mp"),
        P("dp", "mp"),
        P("dp", None),
        P("dp", None),
        P(None, "mp"),
        P("dp", None, "mp"),
        P("dp", "mp"),
        P("dp", "mp"),
        P("dp", "mp"),
        P("dp", None),
        P("dp", None),
        P(None, "mp"),
        P("dp", None, "mp"),
        P("dp", "mp"),
        P("dp", "mp"),
        P("dp", "mp"),
        P("dp", None),
        P("dp", None),
        P(None, "mp"),
    )
    out_specs = (
        P(),
        P(None, "dp", None, None),
        P("dp", None, "mp"),
        P("dp", "mp"),
        P("dp", "mp"),
        P("dp", "mp"),
        P("dp", None),
        P("dp", None),
        P(None, "mp"),
        P("dp", None, "mp"),
        P("dp", "mp"),
        P("dp", "mp"),
        P("dp", "mp"),
        P("dp", None),
        P("dp", None),
        P(None, "mp"),
        P("dp", None, "mp"),
        P("dp", "mp"),
        P("dp", "mp"),
        P("dp", "mp"),
        P("dp", None),
        P("dp", None),
        P(None, "mp"),
    )
    return jax.shard_map(body, mesh=mesh, in_specs=in_specs, out_specs=out_specs, check_vma=False)
```

```python
import functools

import jax
import jax.numpy as jnp
from jax import lax
from jax.experimental import pallas as pl
from jax.experimental.pallas import tpu as pltpu
from jax.sharding import PartitionSpec as P

BUCKETS = 32
LOSS_SCALE = 1024
LANES = 128
ROWS = 256
SPAN = 512

norm_eps = 1e-06
clip_limit = 0.01
beta_first = 0.9
beta_second = 0.999
adam_eps = 1e-08
rate_matrix = 0.03
rate_vector = 0.25
decay_matrix = 0.1
masked_score = -1e30
gelu_slope = 0.7978845608028654
gelu_cubic = 0.044715
low_type = jnp.bfloat16
full_type = jnp.float32
core_swap = [(0, 1), (1, 0)]


def rms_scale(rows_in):
    return lax.rsqrt(jnp.mean(rows_in * rows_in, axis=-1, keepdims=True) + norm_eps)


def norm_input_grad(d_normed, gain_row, rows_in, norm_scale):
    weighted = d_normed * gain_row
    return norm_scale * weighted - rows_in * norm_scale**3 * jnp.mean(
        weighted * rows_in, axis=-1, keepdims=True
    )


def dot_nt(left, right):
    return lax.dot_general(left, right, (((1,), (1,)), ((), ())), preferred_element_type=full_type)


def dot_tn(left, right):
    return lax.dot_general(left, right, (((0,), (0,)), ((), ())), preferred_element_type=full_type)


def dot_nn(left, right):
    return lax.dot_general(left, right, (((1,), (0,)), ((), ())), preferred_element_type=full_type)


def call(
    kernel, name, out_shape, cost=(0, 0), vmem=16, deps=(), passing=(), in_specs=None,
    out_specs=None, input_output_aliases=None, **options
):
    single = not isinstance(out_shape, (list, tuple))
    out_shapes = [out_shape] if single else list(out_shape)
    outputs, extra = len(out_shapes), len(deps) + len(passing)

    def apply(*operands):
        inputs = len(operands)
        if in_specs is None:
            options["grid"] = (1,)
        specs = [whole(operand.shape) for operand in operands] if in_specs is None else in_specs
        targets = out_specs or [whole(shape.shape) for shape in out_shapes]
        targets = targets if isinstance(targets, (list, tuple)) else [targets]
        aliases = dict(input_output_aliases or {})
        for i in range(len(passing)):
            aliases[inputs + len(deps) + i] = outputs + i

        def run(*refs):
            own = inputs + extra
            kernel(*refs[:inputs], *refs[own : own + outputs], *refs[own + outputs + len(passing) :])

        results = pl.pallas_call(
            run,
            out_shape=[*out_shapes, *(shape_of(a.shape, a.dtype) for a in passing)],
            in_specs=[*specs, *[in_place()] * extra],
            out_specs=[*targets, *[in_place()] * len(passing)],
            input_output_aliases=aliases,
            compiler_params=pltpu.CompilerParams(vmem_limit_bytes=vmem * 1024 * 1024),
            cost_estimate=pl.CostEstimate(
                flops=int(cost[0] * 2e6), bytes_accessed=int(cost[1] * 1e3), transcendentals=0
            ),
            name=name,
            **options,
        )(*operands, *deps, *passing)
        return results[0] if single and not passing else results

    return apply


def in_place():
    return pl.BlockSpec(memory_space=pl.ANY)


def shape_of(shape, dtype):
    return jax.ShapeDtypeStruct(tuple(shape), dtype)


def whole(shape):
    return pl.BlockSpec(tuple(shape), lambda *_: (0,) * len(shape))


def on_scalars():
    return pl.BlockSpec(memory_space=pltpu.SMEM)


def row_blocks(shape, step=0):
    return pl.BlockSpec(tuple(shape), lambda i: (i,) + (0,) * (len(shape) - 1))


def column_blocks(shape, offset=0):
    return pl.BlockSpec(tuple(shape), lambda i: (0,) * (len(shape) - 1) + (i + offset,))


def fill_rows(target, pieces, columns=slice(None)):
    start = 0
    for piece in pieces:
        rows = piece.shape[0]
        target[start : start + rows, :] = piece[:, columns]
        start += rows


def spill_rows(value, pieces, first=0):
    start = 0
    for piece in pieces:
        rows = piece.shape[0]
        low, high = max(start, first), min(start + rows, first + value.shape[0])
        if low < high:
            piece[low - start : high - start] = value[low - first : high - first].astype(piece.dtype)
        start += rows


def swap(array, mask, size, label="exchange"):
    with jax.named_scope(f"{label}_across_{mask}"):
        return lax.ppermute(array, "dp", [(i, i ^ mask) for i in range(size)])


def tie(arrays, deps):
    return call(lambda: None, "tie", [], deps=deps, passing=arrays, in_specs=[], grid=(1,))()


def other_core(array, label="other_core"):
    with jax.named_scope(label):
        return lax.ppermute(array, "mp", core_swap)


def stage_bits(size):
    if size == 16:
        return (8, 4, 2, 1)
    return tuple(1 << i for i in range(size.bit_length() - 1))


def device_of(place, me, size):
    mask = jnp.zeros_like(place)
    for i, bit in enumerate(stage_bits(size)):
        mask = mask + jnp.bitwise_and(place >> i, 1) * bit
    return jnp.bitwise_xor(mask, me)


def piece_rows(size, width):
    if size != 16:
        return [width]
    return [width // 4] * 3 + [width // 8] * 2


def join_kernel(*refs):
    *part_refs, out_ref = refs
    start = 0
    for part in part_refs:
        rows = part.shape[0]
        out_ref[start : start + rows] = part[...]
        start += rows


def join(parts, **options):
    rows = sum(part.shape[0] for part in parts)
    return call(
        join_kernel, "join", shape_of((rows, *parts[0].shape[1:]), parts[0].dtype), **options
    )(*parts)


def step_kernel(groups, y_ref, x_ref, *refs):
    part_refs, (low_ref, high_ref, *joined_refs) = refs[: sum(groups)], refs[sum(groups) :]
    low_ref[...] = y_ref[...]
    high_ref[...] = x_ref[...]
    for group, joined_ref in zip(groups, joined_refs):
        join_kernel(*part_refs[:group], joined_ref)
        part_refs = part_refs[group:]


def gather_step(across_y, across_x, *groups, **options):
    half = (across_y.shape[0] // 2, across_y.shape[1])
    shapes = [shape_of(half, across_y.dtype)] * 2
    for parts in groups:
        shapes.append(shape_of((sum(p.shape[0] for p in parts), parts[0].shape[1]), parts[0].dtype))
    flat = [part for parts in groups for part in parts]
    return call(
        functools.partial(step_kernel, tuple(len(parts) for parts in groups)),
        "gather_step",
        shapes,
        grid=(1,),
        in_specs=[
            pl.BlockSpec(half, lambda i: (0, 0)),
            pl.BlockSpec(half, lambda i: (1, 0)),
            *(whole(part.shape) for part in flat),
        ],
        out_specs=[whole(shape.shape) for shape in shapes],
        **options,
    )(across_y, across_x, *flat)


def line_parts(part, size, label):
    return [part] + [swap(part, mask, size, label) for mask in (8, 4, 12)]


def side_parts(quarter, size, label):
    return [swap(quarter, mask, size, label) for mask in (2, 1)]


def corner_parts(low, high, size, label):
    return [swap(low, 1, size, label), swap(high, 2, size, label)]


def gather_doubling(part, size):
    for bit in stage_bits(size):
        part = jnp.concatenate([part, swap(part, bit, size)], axis=0)
    return part


def small_line(part, size, label):
    if size != 16:
        return part[None]
    return join(line_parts(part[None], size, label))


def small_plane(quarter, size, label):
    if size != 16:
        return [gather_doubling(quarter, size)]
    return [quarter] + [swap(quarter, mask, size, label) for mask in (2, 1, 3)]


def stacked(refs):
    return jnp.concatenate([ref[...] for ref in refs], axis=0)


def stacked_row(refs, row):
    return jnp.concatenate([ref[:, row, :] for ref in refs], axis=0)


def gather_small(part, size, label):
    return small_plane(small_line(part, size, label), size, label)


def plane_sum_kernel(*refs):
    count = len(refs) // 6
    for i in range(count):
        y_ref, x_ref, low_ref, high_ref = refs[4 * i : 4 * i + 4]
        y_out, x_out = refs[4 * count + 2 * i : 4 * count + 2 * i + 2]
        half = low_ref.shape[0]
        y_out[:half] = (y_ref[:half].astype(full_type) + low_ref[...].astype(full_type)).astype(
            low_type
        )
        y_out[half:] = y_ref[half:]
        x_out[:half] = x_ref[:half]
        x_out[half:] = (x_ref[half:].astype(full_type) + high_ref[...].astype(full_type)).astype(
            low_type
        )


def line_sum_kernel(*refs):
    count = sum(ref.shape[0] == refs[0].shape[0] for ref in refs)
    add_refs, out_refs = refs[:count], refs[count:]
    rows = out_refs[0].shape[0]
    for i, out_ref in enumerate(out_refs):
        span = slice(i * rows, (i + 1) * rows)
        total = add_refs[0][span].astype(full_type)
        for ref in add_refs[1:]:
            total = total + ref[span].astype(full_type)
        out_ref[...] = total.astype(out_ref.dtype)


class Scatter:
    def __init__(self, pieces, size, label):
        self.pieces, self.size, self.label = pieces, size, label
        self.sources, self.came = (), ()
        if size == 16:
            *self.pieces, low, high = pieces
            self.came = [swap(low, 1, size, label), swap(high, 2, size, label)]

    def near(self, deps=(), passing=()):
        if self.size != 16:
            return passing
        keep = self.pieces[0]
        half = (keep.shape[0] // 2, keep.shape[1])
        kept, sent, *passed = call(
            line_sum_kernel,
            "line_sum",
            [shape_of(half, full_type), shape_of(half, low_type)],
            deps=deps,
            passing=passing,
        )(keep, *self.came)
        self.sources, self.came, self.pieces = (sent,), [swap(sent, 4, self.size, self.label)], [kept]
        return passed

    def far(self, deps=()):
        if self.size != 16:
            return self.line(deps)[0]
        kept = self.pieces[0]
        half = (kept.shape[0] // 2, kept.shape[1])
        own, sent = call(
            line_sum_kernel,
            "line_sum",
            [shape_of(half, full_type), shape_of(half, low_type)],
            deps=deps,
        )(kept, *self.came)
        self.sources = (sent,)
        return [own, swap(sent, 8, self.size, self.label)]

    def line(self, deps=(), passing=()):
        size, label = self.size, self.label
        if size != 16:
            grad = self.pieces[0]
            for bit in reversed(stage_bits(size)):
                half = grad.shape[0] // 2
                came = swap(grad[half:], bit, size, label)
                grad = (grad[:half].astype(full_type) + came.astype(full_type)).astype(low_type)
            return [grad.astype(full_type)], passing
        keep = self.pieces[0]
        part = (keep.shape[0] // 4, keep.shape[1])
        own, *others = call(
            line_sum_kernel,
            "line_sum",
            [shape_of(part, full_type)] + [shape_of(part, low_type)] * 3,
            deps=deps,
            passing=passing,
        )(keep, *self.came)
        came = [swap(other, mask, size, label) for other, mask in zip(others, (8, 4, 12))]
        self.sources = (own,)
        return [own] + came, others[3:]


def scatter_sides(scatters, deps=()):
    if scatters[0].size != 16:
        return ()
    sides = [part for scatter in scatters for part in scatter.pieces[1:]]
    operands = [part for s in scatters for part in (*s.pieces[1:], *s.came)]
    sums = call(
        plane_sum_kernel, "plane_sum", [shape_of(part.shape, low_type) for part in sides], deps=deps
    )(*operands)
    for i, scatter in enumerate(scatters):
        to_y, to_x = sums[2 * i : 2 * i + 2]
        scatter.came = [
            swap(to_y, 2, scatter.size, scatter.label), swap(to_x, 1, scatter.size, scatter.label)
        ]
    return tuple(sums)


def pack_heads_kernel(in_ref, out_ref, gain_ref, tied_ref, a_ref):
    parts, rows, width = in_ref.shape
    for c in range(parts):
        a_ref[:, c * width : (c + 1) * width] = in_ref[c].astype(low_type)
    a_ref[:, parts * width : (parts + 1) * width] = out_ref[...].astype(low_type)
    gains, tied = gain_ref[...], tied_ref[...]
    vectors = few_rows([gains[i : i + 1] for i in range(3)] + [tied[i : i + 1] for i in range(2)], 16)
    pick = lax.broadcasted_iota(jnp.int32, (16, LANES), 0) == lax.broadcasted_iota(
        jnp.int32, (16, LANES), 1
    )
    extra = dot_tn(vectors.astype(low_type), jnp.where(pick, 1.0, 0.0).astype(low_type))
    a_ref[:, (parts + 1) * width :] = extra.astype(low_type)


def pack_hidden_kernel(up_ref, down_ref, packed_ref, *part_refs):
    packed_ref[...] = up_ref[...].astype(low_type)
    start = 0
    for ref in part_refs:
        width = ref.shape[1]
        ref[...] = down_ref[:, start : start + width].astype(low_type)
        start += width


def fill_down(target, line_pieces, plane_pieces):
    width = line_pieces[0].shape[1]
    fill_rows(target.at[:, :width], line_pieces)
    own = target.shape[0] // 16
    for i, piece in enumerate(plane_pieces):
        for f in range(2):
            for q in range(4):
                rows = piece[(f * 4 + q) * own : (f * 4 + q + 1) * own, :]
                place = (4 * q + 2 * i + f) * own
                target[place : place + own, width:] = rows


def prepare_kernel(
    size, me_ref, line_ref, table_ref, query_ref, order_ref, bias_ref, hot_ref, same_ref, positive_ref
):
    me = me_ref[0]
    lane = lambda shape: lax.broadcasted_iota(jnp.int32, shape, 1)
    row = lambda shape: lax.broadcasted_iota(jnp.int32, shape, 0)
    low = lambda hit: jnp.where(hit, 1.0, 0.0).astype(low_type)
    width = order_ref.shape[0]
    own = width // size
    feature = lane((1, width))
    place = device_of(feature // own, me, size) * own + feature % own
    for start in range(0, width, LANES):
        order_ref[start : start + LANES] = low(row((LANES, width)) + start == place)
    length = line_ref.shape[1]
    hot = low(row((LANES, length)) == line_ref[...])
    lines = dot_nn(table_ref[...].astype(low_type), hot[:BUCKETS])
    for head in range(table_ref.shape[0]):
        bias_ref[head // 2, head % 2 : head % 2 + 1] = lines[head : head + 1]
    step = 2 * LANES
    for start in range(0, hot_ref.shape[0], step):
        wanted = start // 2 + step - 2 - row((step, length))
        hot_ref[start : start + step] = dot_nt(low(wanted == lane((step, length))), hot).astype(
            low_type
        )
    shape = (size, LANES)
    pair = device_of(row(shape), me, size)
    other = device_of(lane(shape), me, size)
    for m in range(query_ref.shape[0]):
        queries = query_ref[m : m + 1]
        if size < LANES:
            blank = jnp.zeros((1, LANES - size), jnp.int32)
            queries = jnp.concatenate([queries, blank], axis=1)
        picked = jnp.where(lane(shape) == pair, queries, 0).astype(full_type)
        mine = jnp.sum(picked, axis=1, keepdims=True)
        theirs = jnp.sum(jnp.where(lane(shape) == row(shape), mine, 0.0), axis=0, keepdims=True)
        same = jnp.where((mine == theirs) & (lane(shape) < size), 1.0, 0.0)
        same_ref[m] = same
        earlier = jnp.max(jnp.where(other < pair, same, 0.0), axis=1, keepdims=True)
        positive_ref[m] = jnp.broadcast_to(1.0 - earlier, shape)


def order_kernel(x_ref, order_ref, out_ref):
    out_ref[...] = dot_nn(x_ref[...], order_ref[...]).astype(low_type)


def turn_kernel(x_ref, out_ref):
    out_ref[...] = x_ref[...].T


def head_lanes():
    lane = lax.broadcasted_iota(jnp.int32, (1, LANES), 1)
    return [lane < LANES // 2, lane >= LANES // 2]


def project_kernel(pieces, pairs, x_ref, *refs):
    weight_refs, (qkv_ref, normed_ref, vector_ref, w_ref) = refs[:pieces], refs[pieces:]
    parts = qkv_ref.shape[1]
    in_width = pairs * parts * LANES

    @pl.when(pl.program_id(0) == 0)
    def assemble():
        fill_rows(w_ref, weight_refs)
        pick = lax.broadcasted_iota(jnp.int32, (16, LANES), 0) == lax.broadcasted_iota(
            jnp.int32, (16, LANES), 1
        )
        vectors = dot_nt(jnp.where(pick, 1.0, 0.0).astype(low_type), w_ref[:, -LANES:])
        vector_ref[...] = vectors[:8]

    x = x_ref[...].astype(full_type)
    normed = (x * rms_scale(x) * vector_ref[0:1]).astype(low_type)
    normed_ref[...] = normed
    projected = dot_nn(normed, w_ref[:, :in_width]).astype(low_type)
    for c in range(parts):
        for p in range(pairs):
            start = (c * pairs + p) * LANES
            qkv_ref[p, c] = projected[:, start : start + LANES]


def project(rows_low, weights, pairs, deps):
    count, width = rows_low.shape
    parts = 3
    return call(
        functools.partial(project_kernel, len(weights), pairs),
        "projection",
        [
            shape_of((pairs, parts, count, LANES), low_type),
            shape_of((count, width), low_type),
            shape_of((8, width), full_type),
        ],
        deps=deps,
        grid=(count // ROWS,),
        in_specs=[row_blocks((ROWS, width)), *(whole(piece.shape) for piece in weights)],
        out_specs=[
            pl.BlockSpec((pairs, parts, ROWS, LANES), lambda i: (0, 0, i, 0)),
            row_blocks((ROWS, width)),
            whole((8, width)),
        ],
        scratch_shapes=[pltpu.VMEM((width, weights[0].shape[1]), low_type)],
    )(rows_low, *weights)


def attention_kernel(len_ref, line_ref, qkv_ref, *refs):
    att_ref, prob_ref, inv_ref, tile_ref = refs[-4:]
    micro, slot = prob_ref.shape[1], prob_ref.shape[3]
    blocks = slot // LANES
    lanes = head_lanes()
    for h in range(2):
        for d in range(2 * blocks - 1):
            piece = jnp.broadcast_to(
                line_ref[0, h : h + 1, d * LANES : (d + 2) * LANES], (LANES, 2 * LANES)
            )
            turned = pltpu.roll(piece, LANES + 1, 1, stride=1, stride_axis=0)
            tile_ref[h, d] = turned[:, :LANES]

    def micro_step(m, carry):
        start = pl.multiple_of(m * slot, slot)
        key_valid = lax.broadcasted_iota(jnp.int32, (1, slot), 1) < len_ref[m]
        keys = qkv_ref[0, 1, pl.ds(start, slot), :]
        values = qkv_ref[0, 2, pl.ds(start, slot), :]
        values = jnp.concatenate([values, jnp.ones_like(values)], axis=1)
        for r in range(slot // ROWS):
            rows = pl.ds(start + r * ROWS, ROWS)
            queries = qkv_ref[0, 0, rows, :]
            queries = jnp.concatenate(
                [queries * lanes[h].astype(low_type) for h in range(2)], axis=0
            )
            first = r * (ROWS // LANES)
            bias = jnp.concatenate(
                [
                    jnp.concatenate(
                        [tile_ref[h, j - first - i + blocks - 1] for j in range(blocks)], axis=1
                    )
                    for h in range(2)
                    for i in range(ROWS // LANES)
                ],
                axis=0,
            )
            scores = dot_nt(queries, keys)
            scores = jnp.where(key_valid, scores + bias, masked_score)
            terms = jnp.exp(scores - jnp.max(scores, axis=1, keepdims=True)).astype(low_type)
            for h in range(2):
                prob_ref[0, m, h, r * ROWS : (r + 1) * ROWS, :] = terms[h * ROWS : (h + 1) * ROWS]
            mixed = dot_nn(terms, values)
            inverse = 1.0 / mixed[:, LANES:]
            mixed = mixed[:, :LANES] * inverse
            att_ref[rows, :] = jnp.where(lanes[0], mixed[:ROWS], mixed[ROWS:]).astype(low_type)
            inv_ref[rows, :] = jnp.where(lanes[0], inverse[:ROWS], inverse[ROWS:])
        return carry

    lax.fori_loop(0, micro, micro_step, 0)


def attention(lengths, lines, qkv, first, number, slot, before=(), deps=()):
    pairs, parts, count, _ = qkv.shape
    micro = count // slot
    spans = 2 * (slot // LANES) - 1
    column = pl.BlockSpec((count, LANES), lambda i: (0, i + first))
    return call(
        attention_kernel,
        "attention_forward",
        [
            shape_of((count, pairs * LANES), low_type),
            shape_of((pairs, micro, 2, slot, slot), low_type),
            shape_of((count, pairs * LANES), full_type),
        ],
        deps=deps,
        grid=(number,),
        in_specs=[
            on_scalars(),
            pl.BlockSpec((1, 2, lines.shape[2]), lambda i: (i + first, 0, 0)),
            pl.BlockSpec((1, parts, count, LANES), lambda i: (i + first, 0, 0, 0)),
            *[in_place()] * len(before),
        ],
        out_specs=[
            column,
            pl.BlockSpec((1, micro, 2, slot, slot), lambda i: (i + first, 0, 0, 0, 0)),
            column,
        ],
        input_output_aliases={3 + i: i for i in range(len(before))},
        scratch_shapes=[pltpu.VMEM((2, spans, LANES, LANES), full_type)],
    )(lengths, lines, qkv, *before)


def branch_kernel(att_ref, *refs):
    *weight_refs, out_ref, w_ref = refs

    @pl.when(pl.program_id(0) == 0)
    def assemble():
        fill_rows(w_ref, weight_refs)

    out_ref[...] = dot_nt(att_ref[...], w_ref[...]).astype(low_type)


def branch_rows(attended, weights, deps=()):
    count, head_width = attended.shape
    width = sum(piece.shape[0] for piece in weights)
    return call(
        branch_kernel,
        "branch",
        shape_of((count, width), low_type),
        deps=deps,
        grid=(count // (2 * ROWS),),
        in_specs=[
            row_blocks((2 * ROWS, head_width)),
            *(pl.BlockSpec((piece.shape[0], head_width), lambda i: (0, 3)) for piece in weights),
        ],
        out_specs=row_blocks((2 * ROWS, width)),
        scratch_shapes=[pltpu.VMEM((width, head_width), low_type)],
    )(attended, *weights)


def hidden_kernel(pieces, len_ref, x_ref, own_ref, came_ref, vector_ref, *refs):
    weight_refs, refs = refs[:pieces], refs[pieces:]
    normed_ref, slope_ref, act_ref, sum_ref, w_ref = refs
    m = pl.program_id(0)
    slot = x_ref.shape[0]

    @pl.when(m == 0)
    def assemble():
        fill_rows(w_ref, weight_refs)

    middle = middle_rows(x_ref, own_ref, came_ref)
    normed = (middle * rms_scale(middle) * vector_ref[1:2]).astype(low_type)
    valid = lax.broadcasted_iota(jnp.int32, (slot, 1), 0) < len_ref[m]
    normed_ref[...] = jnp.where(valid, normed, jnp.zeros_like(normed))
    sum_ref[0] = jnp.sum(jnp.where(valid, middle, 0.0), axis=0, keepdims=True)
    v = dot_nn(normed, w_ref[...])
    square = v * v
    gate = jnp.tanh(v * (gelu_slope + (gelu_slope * gelu_cubic) * square))
    half = 0.5 + 0.5 * gate
    active = (v * half).astype(low_type)
    counted = lax.broadcasted_iota(jnp.int32, (16, slot), 1) < len_ref[m]
    act_ref[0] = dot_nn(jnp.where(counted, 1.0, 0.0).astype(low_type), active)[0:1]
    inner = 0.5 * gelu_slope + (1.5 * gelu_slope * gelu_cubic) * square
    slope_ref[...] = (half + v * (1.0 - gate * gate) * inner).astype(low_type)


def middle_rows(x_ref, own_ref, came_ref):
    branch = own_ref[...].astype(full_type) + came_ref[...].astype(full_type)
    return x_ref[...].astype(full_type) + branch


def hidden(lengths, rows_low, own, came, vectors, weights, slot):
    count, width = rows_low.shape
    micro = count // slot
    inner = weights[0].shape[1]
    return call(
        functools.partial(hidden_kernel, len(weights)),
        "hidden_forward",
        [
            shape_of((count, width), low_type),
            shape_of((count, inner), low_type),
            shape_of((micro, 1, inner), full_type),
            shape_of((micro, 1, width), full_type),
            shape_of((width, inner), low_type),
        ],
        cost=(1200, 20000),
        grid=(micro,),
        in_specs=[
            on_scalars(),
            *[row_blocks((slot, width))] * 3,
            whole(vectors.shape),
            *(whole(piece.shape) for piece in weights),
        ],
        out_specs=[
            row_blocks((slot, width)),
            row_blocks((slot, inner)),
            row_blocks((1, 1, inner)),
            row_blocks((1, 1, width)),
            whole((width, inner)),
        ],
    )(lengths, rows_low, own, came, vectors, *weights)


def few_rows(rows, count):
    place = lax.broadcasted_iota(jnp.int32, (count, rows[0].shape[1]), 0)
    total = jnp.zeros(place.shape, full_type)
    for i, row in enumerate(rows):
        total = jnp.where(place == i, row, total)
    return total


def pool_kernel(lines, act_ref, *refs):
    *weight_refs, out_ref, w_ref = refs
    fill_down(w_ref, weight_refs[:lines], weight_refs[lines:])
    sums = [act_ref[m] for m in range(act_ref.shape[0])]
    highs = [row.astype(low_type).astype(full_type) for row in sums]
    rests = [row - high for row, high in zip(sums, highs)]
    down = dot_nt(few_rows(highs + rests, 16).astype(low_type), w_ref[...])
    micro = len(sums)
    out_ref[...] = few_rows([down[m : m + 1] + down[micro + m : micro + m + 1] for m in range(micro)], 8)


def margin_kernel(len_ref, own_ref, other_ref, sum_ref, act_ref, vector_ref, send_ref):
    margins, rows = [], []
    for m in range(sum_ref.shape[0]):
        length = len_ref[m].astype(full_type)
        total = own_ref[m : m + 1] + other_ref[m : m + 1] + sum_ref[m]
        pooled = (total / length).astype(low_type).astype(full_type)
        final = pooled * rms_scale(pooled) * vector_ref[2:3]
        logits = [
            jnp.sum(final * vector_ref[i : i + 1], axis=1, keepdims=True) * pooled.shape[1] ** (-0.5)
            for i in (3, 4)
        ]
        lane = lax.broadcasted_iota(jnp.int32, pooled.shape, 1)
        margins.append(jnp.where(lane < LANES, logits[0] - logits[1], length))
        rows.append(pooled)
    width = rows[0].shape[1]
    for m in range(sum_ref.shape[0]):
        sums = act_ref[m]
        rows += [sums[:, i * width : (i + 1) * width] for i in range(sums.shape[1] // width)]
    send_ref[...] = few_rows(rows + margins, 8)


def ranking(margins, same, positive):
    place = lax.broadcasted_iota(jnp.int32, margins.shape, 0)
    lane = lax.broadcasted_iota(jnp.int32, margins.shape, 1)
    others = jnp.sum(jnp.where(place == lane, margins, 0.0), axis=0, keepdims=True)
    row_max = jnp.max(jnp.where(same, others, masked_score), axis=1, keepdims=True)
    terms = jnp.where(same, jnp.exp(jnp.where(same, others - row_max, 0.0)), 0.0)
    chance = jnp.exp(margins - row_max) / jnp.sum(terms, axis=1, keepdims=True)
    return LOSS_SCALE * (chance - positive)


def pooled_grad(pooled, d_margin, vector_ref):
    scale = rms_scale(pooled)
    d_logit = d_margin * pooled.shape[1] ** (-0.5)
    d_final = d_logit * (vector_ref[3:4] - vector_ref[4:5])
    return norm_input_grad(d_final, vector_ref[2:3], pooled, scale)


def rank_kernel(
    small_pieces, len_ref, same_ref, positive_ref, vector_ref, slope_ref, down_ref, up_ref, *refs
):
    small_refs, refs = refs[:small_pieces], refs[small_pieces:]
    line_ref, act_ref, rank_ref, hidden_ref, d_ref = refs
    m = pl.program_id(0)

    @pl.when(m == 0)
    def rank():
        lines = []
        for i in range(2):
            margins = stacked_row(small_refs, 6 + i)[:, :LANES]
            d_margins = ranking(margins, same_ref[i] > 0.5, positive_ref[i])
            rank_ref[i] = d_margins
            pooled = small_refs[0][0, i : i + 1, :]
            d_pooled = pooled_grad(pooled, d_margins[0:1, 0:1], vector_ref)
            lines.append(d_pooled / len_ref[i].astype(full_type))
        line_ref[...] = few_rows(lines, 8)
        d_act = dot_nn(few_rows(lines, 16).astype(low_type), down_ref[...])
        act_ref[...] = d_act[:8]

    d_row = jnp.where(m == 0, act_ref[0:1], act_ref[1:2])
    d_hidden = (slope_ref[...].astype(full_type) * d_row).astype(low_type)
    hidden_ref[...] = d_hidden
    d_normed = dot_nt(d_hidden, up_ref[...])
    valid = lax.broadcasted_iota(jnp.int32, (d_normed.shape[0], 1), 0) < len_ref[m]
    d_ref[...] = jnp.where(valid, d_normed, 0.0).astype(low_type)


def rank_back(lengths, same, positive, vectors, slope, small_all, down, up, slot, deps):
    count, inner = slope.shape
    width = vectors.shape[1]
    return call(
        functools.partial(rank_kernel, len(small_all)),
        "rank_backward",
        [
            shape_of((8, width), full_type),
            shape_of((8, inner), full_type),
            shape_of(positive.shape, full_type),
            shape_of((count, inner), low_type),
            shape_of((count, width), low_type),
        ],
        cost=(1200, 20000),
        deps=deps,
        grid=(count // slot,),
        in_specs=[
            on_scalars(),
            *(whole(array.shape) for array in (same, positive, vectors)),
            row_blocks((slot, inner)),
            *(whole(array.shape) for array in (down, up, *small_all)),
        ],
        out_specs=[
            whole((8, width)),
            whole((8, inner)),
            whole(positive.shape),
            row_blocks((slot, inner)),
            row_blocks((slot, width)),
        ],
    )(lengths, same, positive, vectors, slope, down, up, *small_all)


def up_grad_kernel(normed_ref, d_ref, *out_refs):
    for n in range(normed_ref.shape[1] // ROWS):
        columns = slice(n * ROWS, (n + 1) * ROWS)
        spill_rows(dot_tn(normed_ref[:, columns], d_ref[...]), out_refs, n * ROWS)


def up_grad(normed, d_hidden, rows):
    return call(
        up_grad_kernel,
        "hidden_in_gradient",
        [shape_of((r, d_hidden.shape[1]), low_type) for r in rows],
        cost=(1200, 15000),
    )(normed, d_hidden)


def middle_kernel(
    pieces, len_ref, x_ref, branch_ref, other_ref, own_ref, came_ref, vector_ref, line_ref,
    att_ref, inv_ref, *refs
):
    weight_refs, refs = refs[:pieces], refs[pieces:]
    d_ref, d_att_ref, total_ref, w_ref = refs
    m = pl.program_id(0)

    @pl.when(m == 0)
    def assemble():
        fill_rows(w_ref, weight_refs)
        total_ref[...] = jnp.zeros_like(total_ref)

    middle = middle_rows(x_ref, branch_ref, other_ref)
    own = own_ref[...].astype(full_type)
    scale = rms_scale(middle)
    valid = lax.broadcasted_iota(jnp.int32, (middle.shape[0], 1), 0) < len_ref[m]
    line = jnp.where(m == 0, line_ref[0:1], line_ref[1:2])
    d_middle = jnp.where(valid, line, 0.0) + norm_input_grad(
        own + came_ref[...].astype(full_type), vector_ref[1:2], middle, scale
    )
    d_ref[...] = d_middle
    d_low = d_middle.astype(low_type)
    d_att_ref[...] = (dot_nn(d_low, w_ref[...]) * inv_ref[...]).astype(low_type)
    total_ref[...] += dot_tn(d_low, att_ref[...])


def middle_back(
    lengths, rows_low, branch, other, own, came, vectors, lines, attended, inverse, weights, slot
):
    count, width = rows_low.shape
    head_width = attended.shape[1]
    return call(
        functools.partial(middle_kernel, len(weights)),
        "middle_backward",
        [
            shape_of((count, width), full_type),
            shape_of((count, head_width), low_type),
            shape_of((width, head_width), full_type),
        ],
        cost=(600, 15000),
        grid=(count // slot,),
        in_specs=[
            on_scalars(),
            *[row_blocks((slot, width))] * 5,
            whole(vectors.shape),
            whole(lines.shape),
            row_blocks((slot, head_width)),
            row_blocks((slot, head_width)),
            *(
                pl.BlockSpec((piece.shape[0], head_width), lambda i: (0, 3)) for piece in weights
            ),
        ],
        out_specs=[
            row_blocks((slot, width)),
            row_blocks((slot, head_width)),
            whole((width, head_width)),
        ],
        scratch_shapes=[pltpu.VMEM((width, head_width), low_type)],
    )(
        lengths, rows_low, branch, other, own, came, vectors, lines, attended, inverse, *weights
    )


def attention_back_kernel(
    befores, grads, tables, own, prob_ref, qkv_ref, d_ref, att_ref, turned_ref, hot_ref, *refs
):
    table_refs, refs = refs[:tables], refs[tables:]
    grad_refs, refs = refs[:grads], refs[grads:]
    d_out_ref, table_ref, *out_refs, tile_ref, dk_ref, dv_ref = refs[befores:]
    step, last = pl.program_id(0), pl.num_programs(0) - 1
    steps = last - 1 if grads else last

    if grads:

        @pl.when(step == last)
        def projection():
            spill_rows(grad_refs[0][...], out_refs)

    @pl.when(step <= steps)
    def heads():
        pair_back(
            prob_ref, qkv_ref, d_ref, att_ref, turned_ref, hot_ref, d_out_ref, table_ref, out_refs,
            tile_ref, dk_ref, dv_ref
        )
        if tables:
            lines = [
                ref[p, h : h + 1]
                for ref in (*table_refs, table_ref)
                for p in range(ref.shape[0])
                for h in range(2)
            ]
            width = turned_ref.shape[0]
            place = lax.broadcasted_iota(jnp.int32, (width, 16), 0) % own
            pick = place == lax.broadcasted_iota(jnp.int32, (width, 16), 1)
            pick = jnp.where(pick, 1.0, 0.0).astype(low_type)
            spread = dot_nn(pick, few_rows(lines, 16).astype(low_type))
            spill_rows(spread, [ref.at[:, 3 * LANES :] for ref in out_refs])


def pair_back(
    prob_ref, qkv_ref, d_ref, att_ref, turned_ref, hot_ref, d_out_ref, table_ref, out_refs,
    tile_ref, dk_ref, dv_ref
):
    micro, slot = prob_ref.shape[1], prob_ref.shape[3]
    blocks = slot // LANES
    spans = 2 * blocks - 1
    lanes = head_lanes()

    tile_ref[...] = jnp.zeros_like(tile_ref)

    def micro_step(m, carry):
        start = pl.multiple_of(m * slot, slot)
        everything = pl.ds(start, slot)
        keys, values = qkv_ref[0, 1, everything, :], qkv_ref[0, 2, everything, :]
        for r in range(slot // SPAN):
            rows = pl.ds(start + r * SPAN, SPAN)
            queries = qkv_ref[0, 0, rows, :]
            queries = jnp.concatenate(
                [queries * lanes[h].astype(low_type) for h in range(2)], axis=0
            )
            d_att = d_ref[rows, :]
            product = d_att.astype(full_type) * att_ref[rows, :].astype(full_type)
            row_dot = jnp.concatenate(
                [
                    jnp.sum(jnp.where(lanes[h], product, 0.0), axis=1, keepdims=True)
                    for h in range(2)
                ],
                axis=0,
            )
            d_att = jnp.concatenate([d_att * lanes[h].astype(low_type) for h in range(2)], axis=0)
            span = slice(r * SPAN, (r + 1) * SPAN)
            probs = jnp.concatenate([prob_ref[0, m, h, span, :] for h in range(2)], axis=0)
            d_scores = probs.astype(full_type) * (dot_nt(d_att, values) - row_dot)
            d_low = d_scores.astype(low_type)
            for h in range(2):
                for i in range(SPAN // LANES):
                    for j in range(blocks):
                        top = h * SPAN + i * LANES
                        tile_ref[h, j - r * (SPAN // LANES) - i + blocks - 1] += d_scores[
                            top : top + LANES, j * LANES : (j + 1) * LANES
                        ]
            d_queries = dot_nn(d_low, keys)
            d_out_ref[0, 0, rows, :] = jnp.where(
                lanes[0], d_queries[:SPAN], d_queries[SPAN:]
            ).astype(low_type)
            d_keys, d_values = dot_tn(d_low, queries), dot_tn(probs, d_att)
            dk_ref[...] = d_keys if r == 0 else dk_ref[...] + d_keys
            dv_ref[...] = d_values if r == 0 else dv_ref[...] + d_values
        d_out_ref[0, 1, everything, :] = dk_ref[...].astype(low_type)
        d_out_ref[0, 2, everything, :] = dv_ref[...].astype(low_type)
        return carry

    lax.fori_loop(0, micro, micro_step, 0, unroll=True)
    d_project = jnp.concatenate([d_out_ref[0, c] for c in range(3)], axis=1)
    spill_rows(dot_nn(turned_ref[...], d_project), [ref.at[:, : 3 * LANES] for ref in out_refs])
    flip = (
        lax.broadcasted_iota(jnp.int32, (LANES, LANES), 0)
        + lax.broadcasted_iota(jnp.int32, (LANES, LANES), 1)
        == LANES - 1
    )
    flip = jnp.where(flip, 1.0, 0.0).astype(low_type)
    tiles = tile_ref[...].reshape(2 * spans * LANES, LANES)
    high = tiles.astype(low_type)
    rest = (tiles - high.astype(full_type)).astype(low_type)
    flipped = dot_nn(high, flip) + dot_nn(rest, flip)
    zeros = jnp.zeros((LANES, LANES), full_type)
    lines = []
    for h in range(2):
        sums = []
        for d in range(spans):
            top = (h * spans + d) * LANES
            wide = jnp.concatenate([flipped[top : top + LANES], zeros], axis=1)
            turned = pltpu.roll(wide, 0, 1, stride=1, stride_axis=0)
            sums.append(jnp.sum(turned, axis=0, keepdims=True))
        lines.append(jnp.concatenate(sums, axis=1))
    highs = [line.astype(low_type).astype(full_type) for line in lines]
    rests = [line - high for line, high in zip(lines, highs)]
    table = dot_nn(few_rows(highs + rests, 16).astype(low_type), hot_ref[...])
    table_ref[0] = few_rows([table[h : h + 1] + table[2 + h : 3 + h] for h in range(2)], 8)


def attention_back(
    probs, qkv, d_attended, attended, turned, hot, rows, first, number, slot, own,
    grad_out=None, tables=(), before=(), deps=()
):
    width, count = turned.shape
    micro = count // slot
    pairs = qkv.shape[0]
    spans = 2 * (slot // LANES) - 1
    at = lambda i: jnp.minimum(i, number - 1)
    lead = lambda shape: pl.BlockSpec(shape, lambda i: (at(i) + first,) + (0,) * (len(shape) - 1))
    column = pl.BlockSpec((count, LANES), lambda i: (0, at(i) + first))
    if tables:
        steps, extra, extra_specs = number, tables, [whole(table.shape) for table in tables]
        gradients = [shape_of((r, 4 * LANES), low_type) for r in rows]
        gradient_specs = [whole((r, 4 * LANES)) for r in rows]
    else:
        steps = number + (grad_out is not None)
        extra = () if grad_out is None else (grad_out,)
        extra_specs = [whole(array.shape) for array in extra]
        gradients = [shape_of((r, pairs * 3 * LANES), low_type) for r in rows]
        gradient_specs = [pl.BlockSpec((r, 3 * LANES), lambda i: (0, i + first)) for r in rows]
    position = 6 + len(extra)
    return call(
        functools.partial(
            attention_back_kernel, len(before), 0 if grad_out is None else 1, len(tables), own
        ),
        "attention_backward",
        [
            shape_of((pairs, 3, count, LANES), low_type),
            shape_of((number, 8, LANES), full_type),
            *gradients,
        ],
        deps=deps,
        grid=(steps,),
        in_specs=[
            lead((1, micro, 2, slot, slot)),
            lead((1, 3, count, LANES)),
            column,
            column,
            whole(turned.shape),
            whole(hot.shape),
            *extra_specs,
            *[in_place()] * len(before),
        ],
        out_specs=[lead((1, 3, count, LANES)), pl.BlockSpec((1, 8, LANES), lambda i: (at(i), 0, 0)), *gradient_specs],
        input_output_aliases={position + i: i if i == 0 else i + 1 for i in range(len(before))},
        scratch_shapes=[
            pltpu.VMEM((2, spans, LANES, LANES), full_type),
            pltpu.VMEM((slot, LANES), full_type),
            pltpu.VMEM((slot, LANES), full_type),
        ],
    )(probs, qkv, d_attended, attended, turned, hot, *extra, *before)


def normed_back_kernel(d_ref, *refs):
    *weight_refs, out_ref, w_ref = refs
    pairs, parts = d_ref.shape[0], d_ref.shape[1]

    @pl.when(pl.program_id(0) == 0)
    def assemble():
        fill_rows(w_ref, weight_refs, slice(0, w_ref.shape[1]))

    blocks = [d_ref[p, c] for c in range(parts) for p in range(pairs)]
    d_normed = dot_nt(jnp.concatenate(blocks, axis=1), w_ref[...])
    out_ref[...] = d_normed.astype(low_type)


def normed_back(d_project, weights, deps):
    pairs, parts, count, _ = d_project.shape
    width = sum(piece.shape[0] for piece in weights)
    return call(
        normed_back_kernel,
        "normed_backward",
        shape_of((count, width), low_type),
        cost=(900, 15000),
        deps=deps,
        grid=(count // ROWS,),
        in_specs=[
            pl.BlockSpec((pairs, parts, ROWS, LANES), lambda i: (0, 0, i, 0)),
            *(whole(piece.shape) for piece in weights),
        ],
        out_specs=row_blocks((ROWS, width)),
        scratch_shapes=[pltpu.VMEM((width, pairs * parts * LANES), low_type)],
    )(d_project, *weights)


def token_kernel(d_ref, own_ref, came_ref, x_ref, vector_ref, order_ref, out_ref, done_ref):
    x = x_ref[...].astype(full_type)
    d_normed = own_ref[...].astype(full_type) + came_ref[...].astype(full_type)
    grad = d_ref[...] + norm_input_grad(d_normed, vector_ref[0:1], x, rms_scale(x))
    high = grad.astype(low_type)
    rest = (grad - high.astype(full_type)).astype(low_type)
    order = order_ref[...]
    out_ref[...] = dot_nt(high, order) + dot_nt(rest, order)
    done_ref[...] = jnp.zeros_like(done_ref)


def token_back(d_middle, own, came, rows_low, vectors, order, deps):
    count, width = rows_low.shape
    return call(
        token_kernel,
        "token_gradient",
        [shape_of((count, width), full_type), shape_of((8, LANES), full_type)],
        cost=(1200, 15000),
        deps=deps,
        grid=(count // ROWS,),
        in_specs=[row_blocks((ROWS, width))] * 4 + [whole(vectors.shape), whole(order.shape)],
        out_specs=[row_blocks((ROWS, width)), whole((8, LANES))],
    )(d_middle, own, came, rows_low, vectors, order)


def total_kernel(smalls, counts, micro, pairs, *refs):
    small_refs, refs = refs[:smalls], refs[smalls:]
    groups = []
    for count in counts:
        groups.append(refs[:count])
        refs = refs[count:]
    rank_ref, vector_ref, in_ref, up_ref, gain_ref, tied_ref, down_ref, line_ref, *out_refs = refs
    size, width = sum(ref.shape[0] for ref in small_refs), small_refs[0].shape[2]
    row_of = lambda row: stacked_row(small_refs, row)
    own = down_ref.shape[0]
    inverse = 1.0 / LOSS_SCALE
    add_up = lambda values: jnp.sum(values, axis=0, keepdims=True).sum(axis=1, keepdims=True)
    squares, sums = 0.0, []
    for group, out_ref in zip(groups, out_refs):
        total = sum(ref[...].astype(full_type) for ref in group) * inverse
        total, rest = total[:, : out_ref.shape[1]], total[:, out_ref.shape[1] :]
        out_ref[...] = total
        sums.append((total, rest))
        squares = squares + add_up(total * total)
    table = sums[1][1]

    block = lax.broadcasted_iota(jnp.int32, (size, width), 1) // own
    mine = block == lax.broadcasted_iota(jnp.int32, (size, width), 0)
    fold = lax.broadcasted_iota(jnp.int32, (width, LANES), 0) % own == lax.broadcasted_iota(
        jnp.int32, (width, LANES), 1
    )
    fold = jnp.where(fold, 1.0, 0.0).astype(low_type)
    down, ranked = 0.0, 0.0
    lane = lax.broadcasted_iota(jnp.int32, (1, LANES), 1)
    own_factor = (vector_ref[3:4, :LANES] - vector_ref[4:5, :LANES]) * vector_ref[2:3, :LANES]
    own_factor = jnp.where(lane < own, own_factor, 0.0)
    parts = down_ref.shape[1] // width
    for m in range(micro):
        pooled = row_of(m)
        scale = rms_scale(pooled)
        lengths = row_of(micro + micro * parts + m)
        margins, lengths = lengths[:, 0:1], lengths[:, LANES : LANES + 1]
        d_logit = rank_ref[m][:, 0:1] * width ** (-0.5)
        mean = d_logit * margins * (width**0.5 / width) / scale
        mine_low = dot_nn(jnp.where(mine, pooled, 0.0).astype(low_type), fold)
        ranked = ranked + jnp.sum(mine_low * scale * d_logit, axis=0, keepdims=True)
        d_pooled = scale * d_logit * own_factor - mine_low * scale**3 * mean
        lines = (d_pooled / lengths).astype(low_type)
        acts = [row_of(micro + m * parts + i) for i in range(parts)]
        acts = jnp.concatenate(acts, axis=1)
        high = acts.astype(low_type)
        rest = (acts - high.astype(full_type)).astype(low_type)
        down = down + dot_tn(lines, high) + dot_tn(lines, rest)
    down = down[:own] * inverse
    down_ref[...] = down
    squares = squares + add_up(down * down)

    ranked = ranked[:, :own] * inverse
    rounded = lambda ref, i: ref[i : i + 1].astype(low_type).astype(full_type)
    tied_gap = rounded(tied_ref, 0) - rounded(tied_ref, 1)

    def through(products):
        ones = jnp.ones((16, products.shape[1]), low_type)
        high = products.astype(low_type)
        rest = (products - high.astype(full_type)).astype(low_type)
        return (dot_nt(ones, high) + dot_nt(ones, rest))[0:1]

    weighed = lambda ref, total: ref.astype(low_type).astype(full_type) * total
    first = 0.0
    for p in range(pairs):
        source = sums[0][0] if p < pairs - 1 else sums[1][0]
        offset = p * 3 * LANES if p < pairs - 1 else 0
        for c in range(3):
            columns = slice(offset + c * LANES, offset + (c + 1) * LANES)
            first = first + weighed(in_ref[c, :, p * LANES : (p + 1) * LANES], source[:, columns])
    rows = [
        through(first) / rounded(gain_ref, 0),
        through(weighed(up_ref[...], sums[2][0])) / rounded(gain_ref, 1),
        tied_gap * ranked,
        rounded(gain_ref, 2) * ranked,
    ]
    place = lax.broadcasted_iota(jnp.int32, (8, own), 0)
    extra = jnp.zeros((8, own), full_type)
    for i, row in enumerate(rows):
        extra = jnp.where(place == i, row, extra)
    line_ref[...] = jnp.zeros_like(line_ref)
    line_ref[:8, :own] = extra
    line_ref[8:16] = jnp.broadcast_to(squares, (8, LANES))
    line_ref[16 : 16 + 2 * pairs] = table[: 2 * pairs]


def totals(
    small_all, ranks, vectors, grads, heads_in, hidden_in, gains, tied_rows, widths, micro, deps
):
    counts = tuple(len(group) for group in grads)
    flat = [array for group in grads for array in group]
    own, inner = hidden_in.shape
    down, line, *sums = call(
        functools.partial(
            total_kernel, len(small_all), counts, micro, heads_in.shape[2] // LANES
        ),
        "gradient_totals",
        [
            shape_of((own, inner), full_type),
            shape_of((24, LANES), full_type),
            *(shape_of((own, width), full_type) for width in widths),
        ],
        cost=(100, 10000),
        deps=deps,
    )(*small_all, *flat, ranks, vectors, heads_in, hidden_in, gains, tied_rows)
    return down, line, sums


def stage_kernel(*refs):
    count = len(refs) // 2
    for ref, target in zip(refs[:count], refs[count:]):
        target[...] = ref[...]


def adam(weight, first_old, second, grad, factor, rate, decay, step_ref):
    clipped = grad * factor
    next_first = beta_first * first_old + (1.0 - beta_first) * clipped
    next_second = beta_second * second + (1.0 - beta_second) * clipped * clipped
    first_hat = next_first * step_ref[0]
    second_hat = next_second * step_ref[1]
    next_weight = weight - rate * (first_hat / (jnp.sqrt(second_hat) + adam_eps) + decay * weight)
    return next_weight, next_first, next_second


def square_kernel(heads, own_ref, other_ref, out_ref, extra_ref):
    place = lax.broadcasted_iota(jnp.int32, (8, LANES), 0)
    extra = own_ref[:8] + jnp.where(place < 2, other_ref[:8], 0.0)
    extra_ref[...] = extra
    counted = jnp.where(place == 3, 2.0, 1.0) * extra * extra
    add_up = lambda values: jnp.sum(values, axis=0, keepdims=True).sum(axis=1, keepdims=True)
    squares = own_ref[8:16] + other_ref[8:16] + add_up(counted)
    out_ref[:8] = squares
    tables = own_ref[16:24] * own_ref[16:24] + other_ref[16:24] * other_ref[16:24]
    out_ref[8:16] = own_ref[16:24]
    out_ref[16:24] = jnp.broadcast_to(add_up(tables), (8, LANES))


def update_kernel(size, squares, groups, me_ref, step_ref, extra_ref, *refs):
    square_refs, refs = refs[:squares], refs[squares:]
    grad_refs, refs = refs[:groups], refs[groups:]
    state_refs, refs = refs[:21], refs[21:]
    norm_ref, *out_refs = refs
    tiles = stacked(square_refs)
    place = lax.broadcasted_iota(jnp.int32, (tiles.shape[0], 1, 1), 0)
    first = device_of(place, me_ref[0], size) == 0
    tables = jnp.sum(jnp.where(first, tiles[:, 8:24], 0.0), axis=0)
    norm = jnp.sqrt(jnp.sum(tiles[:, 0:8], axis=0)[0:1, 0:1] + tables[8:9, 0:1])
    norm_ref[...] = norm
    factor = jnp.minimum(1.0, clip_limit / (norm + 1e-06))
    weights, firsts, seconds = state_refs[:7], state_refs[7:14], state_refs[14:]
    next_weights, next_firsts, next_seconds = out_refs[:7], out_refs[7:14], out_refs[14:]

    def step(index, where, grad, rate, decay):
        results = adam(
            weights[index][where], firsts[index][where], seconds[index][where], grad, factor,
            rate, decay, step_ref,
        )
        for target, result in zip((next_weights, next_firsts, next_seconds), results):
            target[index][where] = result

    everything = (slice(None), slice(None))
    early_ref, late_ref, up_ref, down_ref = grad_refs
    pairs = weights[0].shape[2] // LANES
    for p in range(pairs):
        source, offset = (early_ref, p * 3) if p < pairs - 1 else (late_ref, 0)
        for c in range(3):
            columns = slice((offset + c) * LANES, (offset + c + 1) * LANES)
            where = (c, slice(None), slice(p * LANES, (p + 1) * LANES))
            step(0, where, source[:, columns], rate_matrix, decay_matrix)
    step(1, everything, early_ref[:, (pairs - 1) * 3 * LANES :], rate_matrix, decay_matrix)
    step(2, everything, up_ref[...], rate_matrix, decay_matrix)
    step(3, everything, down_ref[...], rate_matrix, decay_matrix)
    rows = weights[4].shape[1]
    extra = extra_ref[...]
    step(4, everything, extra[0:3, :rows], rate_vector, 0.0)
    tied = extra[3:4, :rows]
    step(5, everything, jnp.concatenate([tied, -tied], axis=0), rate_vector, 0.0)
    step(6, everything, tables[: 2 * pairs, :BUCKETS], rate_vector, 0.0)


def update(size, pick, corrections, extra, squares, grads, states):
    return call(
        functools.partial(update_kernel, size, len(squares), len(grads)),
        "update",
        [shape_of((1, 1), full_type)] + [shape_of(s.shape, full_type) for s in states],
        cost=(0, 6000),
        grid=(1,),
        in_specs=[
            on_scalars(),
            on_scalars(),
            *(whole(array.shape) for array in (extra, *squares, *grads, *states)),
        ],
    )(pick, corrections, extra, *squares, *grads, *states)


def body(
    tokens,
    pair_lengths,
    query_ids,
    distance_bucket,
    step_count,
    heads_in,
    heads_out,
    hidden_in,
    hidden_out,
    gains,
    tied_rows,
    bias_table,
    first_heads_in,
    first_heads_out,
    first_hidden_in,
    first_hidden_out,
    first_gains,
    first_tied,
    first_table,
    second_heads_in,
    second_heads_out,
    second_hidden_in,
    second_hidden_out,
    second_gains,
    second_tied,
    second_table,
):
    size = lax.axis_size("dp")
    me = lax.axis_index("dp")
    core = lax.axis_index("mp")
    micro, _, slot, width = tokens.shape
    count = micro * slot
    own, local_heads = heads_in.shape[0], bias_table.shape[1]
    head_width = heads_in.shape[2]
    inner = hidden_in.shape[1]
    pairs = local_heads // 2
    spans = 2 * (slot // LANES) - 1
    turn_matrix = lambda array: jnp.transpose(array, (1, 0, 2))
    heads_in, first_heads_in, second_heads_in = (
        turn_matrix(array) for array in (heads_in, first_heads_in, second_heads_in)
    )
    gains, tied_rows, bias_table = gains.T, tied_rows.T, bias_table.T
    first_gains, first_tied, first_table = first_gains.T, first_tied.T, first_table.T
    second_gains, second_tied, second_table = second_gains.T, second_tied.T, second_table.T

    packed_heads = call(
        pack_heads_kernel, "pack_heads", shape_of((own, 4 * head_width + LANES), low_type), vmem=56
    )(heads_in, heads_out, gains, tied_rows)
    down_widths = [inner] if size != 16 else [inner - inner // 3, inner // 3]
    packed_up, packed_down, *packed_plane = call(
        pack_hidden_kernel,
        "pack_hidden",
        [shape_of((own, width_here), low_type) for width_here in (inner, *down_widths)],
    )(hidden_in, hidden_out)
    weights = (heads_in, heads_out, hidden_in, hidden_out, gains, tied_rows, bias_table)
    firsts = (
        first_heads_in,
        first_heads_out,
        first_hidden_in,
        first_hidden_out,
        first_gains,
        first_tied,
        first_table,
    )
    seconds = (
        second_heads_in,
        second_heads_out,
        second_hidden_in,
        second_hidden_out,
        second_gains,
        second_tied,
        second_table,
    )
    states = [*weights, *firsts, *seconds]
    large = [index for index, state in enumerate(states) if index % 7 < 4]
    staged = call(
        stage_kernel, "stage", [shape_of(states[i].shape, full_type) for i in large], vmem=56
    )(*(states[i] for i in large))
    for i, array in zip(large, staged):
        states[i] = array

    lengths = pair_lengths.reshape(micro)
    device = me.reshape(1)
    order, lines, hot_spans, same_tile, positive_tile = call(
        functools.partial(prepare_kernel, size),
        "prepare",
        [
            shape_of((width, width), low_type),
            shape_of((pairs, 2, 2 * slot), full_type),
            shape_of((spans * 2 * LANES, LANES), low_type),
            shape_of((micro, size, LANES), full_type),
            shape_of((micro, size, LANES), full_type),
        ],
        grid=(1,),
        in_specs=[
            on_scalars(),
            whole((1, 2 * slot)),
            whole(bias_table.shape),
            whole(query_ids.shape),
        ],
    )(
        device,
        jnp.pad(distance_bucket, (0, 1), constant_values=-1).reshape(1, 2 * slot),
        bias_table,
        query_ids,
    )
    step_float = step_count.astype(full_type)
    corrections = jnp.stack(
        [1.0 / (1.0 - beta_first**step_float), 1.0 / (1.0 - beta_second**step_float)]
    )

    rows_low = call(
        order_kernel,
        "order_tokens",
        shape_of((count, width), low_type),
        cost=(600, 5000),
        grid=(count // ROWS,),
        in_specs=[row_blocks((ROWS, width)), whole((width, width))],
        out_specs=row_blocks((ROWS, width)),
    )(tokens.reshape(count, width), order)
    if size != 16:
        weight_heads, weight_up, weight_down = (
            [gather_doubling(part, size)] for part in (packed_heads, packed_up, packed_down)
        )
        planes = []
        qkv, normed_first, vectors = project(rows_low, weight_heads, pairs, ())
    else:
        plane_sides = side_parts(*packed_plane, size, "down_plane")
        heads_line, packed_up, packed_down = join(
            line_parts(packed_heads, size, "heads"),
            deps=(staged[0], order, corrections, *plane_sides),
            passing=(packed_up, packed_down),
        )
        heads_sides = side_parts(heads_line, size, "heads")
        up_pair = join([packed_up, swap(packed_up, 8, size, "up")], deps=(rows_low,))
        up_near = swap(up_pair, 4, size, "up")
        plane_corner = swap(plane_sides[0], 1, size, "down_plane_corner")
        low, high, packed_down = gather_step(
            *heads_sides, deps=(up_pair, plane_corner), passing=(packed_down,)
        )
        down_far = swap(packed_down, 8, size, "down")
        heads_corner = corner_parts(low, high, size, "heads_corner")
        up_line = join([up_pair, up_near], deps=(low,))
        down_pair = join([packed_down, down_far], deps=(up_line,))
        down_near = swap(down_pair, 4, size, "down")
        up_sides = side_parts(up_line, size, "up")
        weight_heads = [heads_line, *heads_sides, *heads_corner]
        qkv, normed_first, vectors = project(rows_low, weight_heads, pairs, ())
    filled = attention(
        lengths, lines, qkv, 0, 1, slot, deps=(down_pair,) if size == 16 else ()
    )
    if size == 16:
        down_line = join([down_pair, down_near], deps=(filled[0],))
        down_sides = side_parts(down_line, size, "down")
        plane = join([*packed_plane, *plane_sides, plane_corner], deps=(down_line,))
        plane_far = swap(plane, 8, size, "down_plane")
    if pairs > 1:
        filled = attention(lengths, lines, qkv, 1, pairs - 1, slot, before=filled)
    if size == 16:
        low, high = gather_step(*up_sides, deps=(filled[0],))
        up_corner = corner_parts(low, high, size, "up_corner")
        plane_pair = join([plane, plane_far], deps=(filled[0],))
        planes = [plane_pair, swap(plane_pair, 4, size, "down_plane")]
        weight_up = [up_line, *up_sides, *up_corner]
    turned_first = call(turn_kernel, "turn", shape_of((width, count), low_type))(normed_first)
    attended, probs, inverse = filled
    branch = branch_rows(
        attended, weight_heads, (*up_corner, *down_sides, *planes, turned_first) if size == 16 else ()
    )
    if size == 16:
        low, high = gather_step(*down_sides, deps=(branch,))
        down_corner = corner_parts(low, high, size, "down_corner")
        weight_down = [down_line, *down_sides, *down_corner]
    branch_came = other_core(branch, "branch_other_core")
    normed_second, slope, act_sum, middle_sum, full_up = hidden(
        lengths, rows_low, branch, branch_came, vectors, weight_up, slot
    )
    down, full_down = call(
        functools.partial(pool_kernel, len(weight_down)),
        "pool",
        [shape_of((8, width), full_type), shape_of((width, inner), low_type)],
        cost=(20, 5000),
    )(act_sum, *weight_down, *planes)
    small = call(
        margin_kernel,
        "margin",
        shape_of((8, width), full_type),
        grid=(1,),
        in_specs=[
            on_scalars(),
            *(whole(array.shape) for array in (down, down, middle_sum, act_sum, vectors)),
        ],
        out_specs=whole((8, width)),
    )(lengths, down, other_core(down, "pooled_part_other_core"), middle_sum, act_sum, vectors)
    small_all = gather_small(small, size, "small_sums")

    d_line, _, ranks, d_hidden, d_normed_second = rank_back(
        lengths, same_tile, positive_tile, vectors, slope, small_all, full_down, full_up, slot,
        (turned_first,),
    )
    d_normed_second_came = other_core(d_normed_second, "second_gradient_other_core")
    up_sum = Scatter(
        up_grad(normed_second, d_hidden, piece_rows(size, width)), size, "up_gradient"
    )
    d_middle, d_attended, g_out = middle_back(
        lengths, rows_low, branch, branch_came, d_normed_second, d_normed_second_came, vectors,
        d_line, attended, inverse, weight_heads, slot,
    )
    scatter_sides([up_sum], deps=(d_attended,))
    d_project, tables, *g_early = attention_back(
        probs, qkv, d_attended, attended, turned_first, hot_spans, piece_rows(size, width),
        0, pairs - 1, slot, own, grad_out=g_out,
    )
    early_sum = Scatter(g_early, size, "early_gradient")
    d_project, table, *g_late = attention_back(
        probs, qkv, d_attended, attended, turned_first, hot_spans, piece_rows(size, width),
        pairs - 1, 1, slot, own, tables=(tables,), before=(d_project,),
    )
    late_sum = Scatter(g_late, size, "late_gradient")
    up_sum.near(deps=(table,))
    sides = scatter_sides([early_sum, late_sum], deps=tuple(up_sum.came))
    d_normed_first = normed_back(d_project, weight_heads, sides)
    up_parts = up_sum.far(deps=sides)
    (d_normed_first,) = early_sum.near(deps=tuple(up_parts), passing=(d_normed_first,))
    early_parts = early_sum.far()
    late_parts, _ = late_sum.line(deps=(early_parts[0],))

    token_gradient, token_done = token_back(
        d_middle, d_normed_first, other_core(d_normed_first, "first_gradient_other_core"), rows_low,
        vectors, order, late_sum.sources,
    )

    g_down, line, grad_sums = totals(
        small_all, ranks, vectors, [early_parts, late_parts, up_parts], heads_in, hidden_in, gains, tied_rows,
        (head_width * 3, 3 * LANES, inner), micro, (token_done,),
    )
    square_tile, extra = call(
        functools.partial(square_kernel, local_heads),
        "squares",
        [shape_of((24, LANES), full_type), shape_of((8, LANES), full_type)],
    )(line, other_core(line, "totals_other_core"))
    squares_all = gather_small(square_tile, size, "squares")
    grads = [*grad_sums, g_down]
    norm, *results = update(size, device, corrections, extra, squares_all, grads, states)
    for index in (0, 7, 14):
        results[index] = turn_matrix(results[index])
        for other in (4, 5, 6):
            results[index + other] = results[index + other].T
    return (norm.reshape(()), token_gradient.reshape(tokens.shape), *results)


def solution(mesh):
    in_specs = (
        P(None, "dp", None, None),
        P(None, "dp"),
        P(),
        P(),
        P(),
        P("dp", None, "mp"),
        P("dp", "mp"),
        P("dp", "mp"),
        P("dp", "mp"),
        P("dp", None),
        P("dp", None),
        P(None, "mp"),
        P("dp", None, "mp"),
        P("dp", "mp"),
        P("dp", "mp"),
        P("dp", "mp"),
        P("dp", None),
        P("dp", None),
        P(None, "mp"),
        P("dp", None, "mp"),
        P("dp", "mp"),
        P("dp", "mp"),
        P("dp", "mp"),
        P("dp", None),
        P("dp", None),
        P(None, "mp"),
    )
    out_specs = (
        P(),
        P(None, "dp", None, None),
        P("dp", None, "mp"),
        P("dp", "mp"),
        P("dp", "mp"),
        P("dp", "mp"),
        P("dp", None),
        P("dp", None),
        P(None, "mp"),
        P("dp", None, "mp"),
        P("dp", "mp"),
        P("dp", "mp"),
        P("dp", "mp"),
        P("dp", None),
        P("dp", None),
        P(None, "mp"),
        P("dp", None, "mp"),
        P("dp", "mp"),
        P("dp", "mp"),
        P("dp", "mp"),
        P("dp", None),
        P("dp", None),
        P(None, "mp"),
    )
    return jax.shard_map(body, mesh=mesh, in_specs=in_specs, out_specs=out_specs, check_vma=False)
```

```python
import functools

import jax
import jax.numpy as jnp
from jax import lax
from jax.experimental import pallas as pl
from jax.experimental.pallas import tpu as pltpu
from jax.sharding import PartitionSpec as P

BUCKETS = 32
LOSS_SCALE = 1024
LANES = 128
ROWS = 256
SPAN = 512

norm_eps = 1e-06
clip_limit = 0.01
beta_first = 0.9
beta_second = 0.999
adam_eps = 1e-08
rate_matrix = 0.03
rate_vector = 0.25
decay_matrix = 0.1
masked_score = -1e30
gelu_slope = 0.7978845608028654
gelu_cubic = 0.044715
low_type = jnp.bfloat16
full_type = jnp.float32
core_swap = [(0, 1), (1, 0)]


def rms_scale(rows_in):
    return lax.rsqrt(jnp.mean(rows_in * rows_in, axis=-1, keepdims=True) + norm_eps)


def norm_input_grad(d_normed, gain_row, rows_in, norm_scale):
    weighted = d_normed * gain_row
    return norm_scale * weighted - rows_in * norm_scale**3 * jnp.mean(
        weighted * rows_in, axis=-1, keepdims=True
    )


def dot_nt(left, right):
    return lax.dot_general(left, right, (((1,), (1,)), ((), ())), preferred_element_type=full_type)


def dot_tn(left, right):
    return lax.dot_general(left, right, (((0,), (0,)), ((), ())), preferred_element_type=full_type)


def dot_nn(left, right):
    return lax.dot_general(left, right, (((1,), (0,)), ((), ())), preferred_element_type=full_type)


def call(
    kernel, name, out_shape, cost=(0, 0), vmem=16, deps=(), passing=(), in_specs=None,
    out_specs=None, input_output_aliases=None, **options
):
    single = not isinstance(out_shape, (list, tuple))
    out_shapes = [out_shape] if single else list(out_shape)
    outputs, extra = len(out_shapes), len(deps) + len(passing)

    def apply(*operands):
        inputs = len(operands)
        if in_specs is None:
            options["grid"] = (1,)
        specs = [whole(operand.shape) for operand in operands] if in_specs is None else in_specs
        targets = out_specs or [whole(shape.shape) for shape in out_shapes]
        targets = targets if isinstance(targets, (list, tuple)) else [targets]
        aliases = dict(input_output_aliases or {})
        for i in range(len(passing)):
            aliases[inputs + len(deps) + i] = outputs + i

        def run(*refs):
            own = inputs + extra
            kernel(*refs[:inputs], *refs[own : own + outputs], *refs[own + outputs + len(passing) :])

        results = pl.pallas_call(
            run,
            out_shape=[*out_shapes, *(shape_of(a.shape, a.dtype) for a in passing)],
            in_specs=[*specs, *[in_place()] * extra],
            out_specs=[*targets, *[in_place()] * len(passing)],
            input_output_aliases=aliases,
            compiler_params=pltpu.CompilerParams(vmem_limit_bytes=vmem * 1024 * 1024),
            cost_estimate=pl.CostEstimate(
                flops=int(cost[0] * 2e6), bytes_accessed=int(cost[1] * 1e3), transcendentals=0
            ),
            name=name,
            **options,
        )(*operands, *deps, *passing)
        return results[0] if single and not passing else results

    return apply


def in_place():
    return pl.BlockSpec(memory_space=pl.ANY)


def shape_of(shape, dtype):
    return jax.ShapeDtypeStruct(tuple(shape), dtype)


def whole(shape):
    return pl.BlockSpec(tuple(shape), lambda *_: (0,) * len(shape))


def on_scalars():
    return pl.BlockSpec(memory_space=pltpu.SMEM)


def row_blocks(shape, step=0):
    return pl.BlockSpec(tuple(shape), lambda i: (i,) + (0,) * (len(shape) - 1))


def column_blocks(shape, offset=0):
    return pl.BlockSpec(tuple(shape), lambda i: (0,) * (len(shape) - 1) + (i + offset,))


def fill_rows(target, pieces, columns=slice(None)):
    start = 0
    for piece in pieces:
        rows = piece.shape[0]
        target[start : start + rows, :] = piece[:, columns]
        start += rows


def spill_rows(value, pieces, first=0):
    start = 0
    for piece in pieces:
        rows = piece.shape[0]
        low, high = max(start, first), min(start + rows, first + value.shape[0])
        if low < high:
            piece[low - start : high - start] = value[low - first : high - first].astype(piece.dtype)
        start += rows


def swap(array, mask, size, label="exchange"):
    with jax.named_scope(f"{label}_across_{mask}"):
        return lax.ppermute(array, "dp", [(i, i ^ mask) for i in range(size)])


def tie(arrays, deps):
    return call(lambda: None, "tie", [], deps=deps, passing=arrays, in_specs=[], grid=(1,))()


def other_core(array, label="other_core"):
    with jax.named_scope(label):
        return lax.ppermute(array, "mp", core_swap)


def stage_bits(size):
    if size == 16:
        return (8, 4, 2, 1)
    return tuple(1 << i for i in range(size.bit_length() - 1))


def device_of(place, me, size):
    mask = jnp.zeros_like(place)
    for i, bit in enumerate(stage_bits(size)):
        mask = mask + jnp.bitwise_and(place >> i, 1) * bit
    return jnp.bitwise_xor(mask, me)


def piece_rows(size, width):
    if size != 16:
        return [width]
    return [width // 4] * 3 + [width // 8] * 2


def join_kernel(*refs):
    *part_refs, out_ref = refs
    start = 0
    for part in part_refs:
        rows = part.shape[0]
        out_ref[start : start + rows] = part[...]
        start += rows


def join(parts, **options):
    rows = sum(part.shape[0] for part in parts)
    return call(
        join_kernel, "join", shape_of((rows, *parts[0].shape[1:]), parts[0].dtype), **options
    )(*parts)


def step_kernel(groups, y_ref, x_ref, *refs):
    part_refs, (low_ref, high_ref, *joined_refs) = refs[: sum(groups)], refs[sum(groups) :]
    low_ref[...] = y_ref[...]
    high_ref[...] = x_ref[...]
    for group, joined_ref in zip(groups, joined_refs):
        join_kernel(*part_refs[:group], joined_ref)
        part_refs = part_refs[group:]


def gather_step(across_y, across_x, *groups, **options):
    half = (across_y.shape[0] // 2, across_y.shape[1])
    shapes = [shape_of(half, across_y.dtype)] * 2
    for parts in groups:
        shapes.append(shape_of((sum(p.shape[0] for p in parts), parts[0].shape[1]), parts[0].dtype))
    flat = [part for parts in groups for part in parts]
    return call(
        functools.partial(step_kernel, tuple(len(parts) for parts in groups)),
        "gather_step",
        shapes,
        grid=(1,),
        in_specs=[
            pl.BlockSpec(half, lambda i: (0, 0)),
            pl.BlockSpec(half, lambda i: (1, 0)),
            *(whole(part.shape) for part in flat),
        ],
        out_specs=[whole(shape.shape) for shape in shapes],
        **options,
    )(across_y, across_x, *flat)


def line_parts(part, size, label):
    return [part] + [swap(part, mask, size, label) for mask in (8, 4, 12)]


def side_parts(quarter, size, label):
    return [swap(quarter, mask, size, label) for mask in (2, 1)]


def corner_parts(low, high, size, label):
    return [swap(low, 1, size, label), swap(high, 2, size, label)]


def gather_doubling(part, size):
    for bit in stage_bits(size):
        part = jnp.concatenate([part, swap(part, bit, size)], axis=0)
    return part


def small_line(part, size, label):
    if size != 16:
        return part[None]
    return join(line_parts(part[None], size, label))


def small_plane(quarter, size, label):
    if size != 16:
        return [gather_doubling(quarter, size)]
    return [quarter] + [swap(quarter, mask, size, label) for mask in (2, 1, 3)]


def stacked(refs):
    return jnp.concatenate([ref[...] for ref in refs], axis=0)


def stacked_row(refs, row):
    return jnp.concatenate([ref[:, row, :] for ref in refs], axis=0)


def gather_small(part, size, label):
    return small_plane(small_line(part, size, label), size, label)


def plane_sum_kernel(*refs):
    count = len(refs) // 6
    for i in range(count):
        y_ref, x_ref, low_ref, high_ref = refs[4 * i : 4 * i + 4]
        y_out, x_out = refs[4 * count + 2 * i : 4 * count + 2 * i + 2]
        half = low_ref.shape[0]
        y_out[:half] = (y_ref[:half].astype(full_type) + low_ref[...].astype(full_type)).astype(
            low_type
        )
        y_out[half:] = y_ref[half:]
        x_out[:half] = x_ref[:half]
        x_out[half:] = (x_ref[half:].astype(full_type) + high_ref[...].astype(full_type)).astype(
            low_type
        )


def line_sum_kernel(*refs):
    count = sum(ref.shape[0] == refs[0].shape[0] for ref in refs)
    add_refs, out_refs = refs[:count], refs[count:]
    rows = out_refs[0].shape[0]
    for i, out_ref in enumerate(out_refs):
        span = slice(i * rows, (i + 1) * rows)
        total = add_refs[0][span].astype(full_type)
        for ref in add_refs[1:]:
            total = total + ref[span].astype(full_type)
        out_ref[...] = total.astype(out_ref.dtype)


class Scatter:
    def __init__(self, pieces, size, label):
        self.pieces, self.size, self.label = pieces, size, label
        self.sources, self.came = (), ()
        if size == 16:
            *self.pieces, low, high = pieces
            self.came = [swap(low, 1, size, label), swap(high, 2, size, label)]

    def near(self, deps=(), passing=()):
        if self.size != 16:
            return passing
        keep = self.pieces[0]
        half = (keep.shape[0] // 2, keep.shape[1])
        kept, sent, *passed = call(
            line_sum_kernel,
            "line_sum",
            [shape_of(half, full_type), shape_of(half, low_type)],
            deps=deps,
            passing=passing,
        )(keep, *self.came)
        self.sources, self.came, self.pieces = (sent,), [swap(sent, 4, self.size, self.label)], [kept]
        return passed

    def far(self, deps=()):
        if self.size != 16:
            return self.line(deps)[0]
        kept = self.pieces[0]
        half = (kept.shape[0] // 2, kept.shape[1])
        own, sent = call(
            line_sum_kernel,
            "line_sum",
            [shape_of(half, full_type), shape_of(half, low_type)],
            deps=deps,
        )(kept, *self.came)
        self.sources = (sent,)
        return [own, swap(sent, 8, self.size, self.label)]

    def line(self, deps=(), passing=()):
        size, label = self.size, self.label
        if size != 16:
            grad = self.pieces[0]
            for bit in reversed(stage_bits(size)):
                half = grad.shape[0] // 2
                came = swap(grad[half:], bit, size, label)
                grad = (grad[:half].astype(full_type) + came.astype(full_type)).astype(low_type)
            return [grad.astype(full_type)], passing
        keep = self.pieces[0]
        part = (keep.shape[0] // 4, keep.shape[1])
        own, *others = call(
            line_sum_kernel,
            "line_sum",
            [shape_of(part, full_type)] + [shape_of(part, low_type)] * 3,
            deps=deps,
            passing=passing,
        )(keep, *self.came)
        came = [swap(other, mask, size, label) for other, mask in zip(others, (8, 4, 12))]
        self.sources = (own,)
        return [own] + came, others[3:]


def scatter_sides(scatters, deps=()):
    if scatters[0].size != 16:
        return ()
    sides = [part for scatter in scatters for part in scatter.pieces[1:]]
    operands = [part for s in scatters for part in (*s.pieces[1:], *s.came)]
    sums = call(
        plane_sum_kernel, "plane_sum", [shape_of(part.shape, low_type) for part in sides], deps=deps
    )(*operands)
    for i, scatter in enumerate(scatters):
        to_y, to_x = sums[2 * i : 2 * i + 2]
        scatter.came = [
            swap(to_y, 2, scatter.size, scatter.label), swap(to_x, 1, scatter.size, scatter.label)
        ]
    return tuple(sums)


def pack_heads_kernel(in_ref, out_ref, gain_ref, tied_ref, a_ref):
    parts, rows, width = in_ref.shape
    for c in range(parts):
        a_ref[:, c * width : (c + 1) * width] = in_ref[c].astype(low_type)
    a_ref[:, parts * width : (parts + 1) * width] = out_ref[...].astype(low_type)
    gains, tied = gain_ref[...], tied_ref[...]
    vectors = few_rows([gains[i : i + 1] for i in range(3)] + [tied[i : i + 1] for i in range(2)], 16)
    pick = lax.broadcasted_iota(jnp.int32, (16, LANES), 0) == lax.broadcasted_iota(
        jnp.int32, (16, LANES), 1
    )
    extra = dot_tn(vectors.astype(low_type), jnp.where(pick, 1.0, 0.0).astype(low_type))
    a_ref[:, (parts + 1) * width :] = extra.astype(low_type)


def pack_hidden_kernel(up_ref, down_ref, packed_ref, *part_refs):
    packed_ref[...] = up_ref[...].astype(low_type)
    start = 0
    for ref in part_refs:
        width = ref.shape[1]
        ref[...] = down_ref[:, start : start + width].astype(low_type)
        start += width


def fill_down(target, line_pieces, plane_pieces):
    width = line_pieces[0].shape[1]
    fill_rows(target.at[:, :width], line_pieces)
    own = target.shape[0] // 16
    for i, piece in enumerate(plane_pieces):
        for f in range(2):
            for q in range(4):
                rows = piece[(f * 4 + q) * own : (f * 4 + q + 1) * own, :]
                place = (4 * q + 2 * i + f) * own
                target[place : place + own, width:] = rows


def prepare_kernel(
    size, me_ref, line_ref, table_ref, query_ref, order_ref, bias_ref, hot_ref, same_ref, positive_ref
):
    me = me_ref[0]
    lane = lambda shape: lax.broadcasted_iota(jnp.int32, shape, 1)
    row = lambda shape: lax.broadcasted_iota(jnp.int32, shape, 0)
    low = lambda hit: jnp.where(hit, 1.0, 0.0).astype(low_type)
    width = order_ref.shape[0]
    own = width // size
    feature = lane((1, width))
    place = device_of(feature // own, me, size) * own + feature % own
    for start in range(0, width, LANES):
        order_ref[start : start + LANES] = low(row((LANES, width)) + start == place)
    length = line_ref.shape[1]
    hot = low(row((LANES, length)) == line_ref[...])
    lines = dot_nn(table_ref[...].astype(low_type), hot[:BUCKETS])
    for head in range(table_ref.shape[0]):
        bias_ref[head // 2, head % 2 : head % 2 + 1] = lines[head : head + 1]
    step = 2 * LANES
    for start in range(0, hot_ref.shape[0], step):
        wanted = start // 2 + step - 2 - row((step, length))
        hot_ref[start : start + step] = dot_nt(low(wanted == lane((step, length))), hot).astype(
            low_type
        )
    shape = (size, LANES)
    pair = device_of(row(shape), me, size)
    other = device_of(lane(shape), me, size)
    for m in range(query_ref.shape[0]):
        queries = query_ref[m : m + 1]
        if size < LANES:
            blank = jnp.zeros((1, LANES - size), jnp.int32)
            queries = jnp.concatenate([queries, blank], axis=1)
        picked = jnp.where(lane(shape) == pair, queries, 0).astype(full_type)
        mine = jnp.sum(picked, axis=1, keepdims=True)
        theirs = jnp.sum(jnp.where(lane(shape) == row(shape), mine, 0.0), axis=0, keepdims=True)
        same = jnp.where((mine == theirs) & (lane(shape) < size), 1.0, 0.0)
        same_ref[m] = same
        earlier = jnp.max(jnp.where(other < pair, same, 0.0), axis=1, keepdims=True)
        positive_ref[m] = jnp.broadcast_to(1.0 - earlier, shape)


def order_kernel(x_ref, order_ref, out_ref):
    out_ref[...] = dot_nn(x_ref[...], order_ref[...]).astype(low_type)


def turn_kernel(x_ref, out_ref):
    out_ref[...] = x_ref[...].T


def head_lanes():
    lane = lax.broadcasted_iota(jnp.int32, (1, LANES), 1)
    return [lane < LANES // 2, lane >= LANES // 2]


def project_kernel(pieces, pairs, x_ref, *refs):
    weight_refs, (qkv_ref, normed_ref, vector_ref, w_ref) = refs[:pieces], refs[pieces:]
    parts = qkv_ref.shape[1]
    in_width = pairs * parts * LANES

    @pl.when(pl.program_id(0) == 0)
    def assemble():
        fill_rows(w_ref, weight_refs)
        pick = lax.broadcasted_iota(jnp.int32, (16, LANES), 0) == lax.broadcasted_iota(
            jnp.int32, (16, LANES), 1
        )
        vectors = dot_nt(jnp.where(pick, 1.0, 0.0).astype(low_type), w_ref[:, -LANES:])
        vector_ref[...] = vectors[:8]

    x = x_ref[...].astype(full_type)
    normed = (x * rms_scale(x) * vector_ref[0:1]).astype(low_type)
    normed_ref[...] = normed
    projected = dot_nn(normed, w_ref[:, :in_width]).astype(low_type)
    for c in range(parts):
        for p in range(pairs):
            start = (c * pairs + p) * LANES
            qkv_ref[p, c] = projected[:, start : start + LANES]


def project(rows_low, weights, pairs, deps):
    count, width = rows_low.shape
    parts = 3
    return call(
        functools.partial(project_kernel, len(weights), pairs),
        "projection",
        [
            shape_of((pairs, parts, count, LANES), low_type),
            shape_of((count, width), low_type),
            shape_of((8, width), full_type),
        ],
        deps=deps,
        grid=(count // ROWS,),
        in_specs=[row_blocks((ROWS, width)), *(whole(piece.shape) for piece in weights)],
        out_specs=[
            pl.BlockSpec((pairs, parts, ROWS, LANES), lambda i: (0, 0, i, 0)),
            row_blocks((ROWS, width)),
            whole((8, width)),
        ],
        scratch_shapes=[pltpu.VMEM((width, weights[0].shape[1]), low_type)],
    )(rows_low, *weights)


def attention_kernel(len_ref, line_ref, qkv_ref, *refs):
    att_ref, prob_ref, inv_ref, tile_ref = refs[-4:]
    micro, slot = prob_ref.shape[1], prob_ref.shape[3]
    blocks = slot // LANES
    lanes = head_lanes()
    for h in range(2):
        for d in range(2 * blocks - 1):
            piece = jnp.broadcast_to(
                line_ref[0, h : h + 1, d * LANES : (d + 2) * LANES], (LANES, 2 * LANES)
            )
            turned = pltpu.roll(piece, LANES + 1, 1, stride=1, stride_axis=0)
            tile_ref[h, d] = turned[:, :LANES]

    def micro_step(m, carry):
        start = pl.multiple_of(m * slot, slot)
        key_valid = lax.broadcasted_iota(jnp.int32, (1, slot), 1) < len_ref[m]
        keys = qkv_ref[0, 1, pl.ds(start, slot), :]
        values = qkv_ref[0, 2, pl.ds(start, slot), :]
        values = jnp.concatenate([values, jnp.ones_like(values)], axis=1)
        for r in range(slot // ROWS):
            rows = pl.ds(start + r * ROWS, ROWS)
            queries = qkv_ref[0, 0, rows, :]
            queries = jnp.concatenate(
                [queries * lanes[h].astype(low_type) for h in range(2)], axis=0
            )
            first = r * (ROWS // LANES)
            bias = jnp.concatenate(
                [
                    jnp.concatenate(
                        [tile_ref[h, j - first - i + blocks - 1] for j in range(blocks)], axis=1
                    )
                    for h in range(2)
                    for i in range(ROWS // LANES)
                ],
                axis=0,
            )
            scores = dot_nt(queries, keys)
            scores = jnp.where(key_valid, scores + bias, masked_score)
            terms = jnp.exp(scores - jnp.max(scores, axis=1, keepdims=True)).astype(low_type)
            for h in range(2):
                prob_ref[0, m, h, r * ROWS : (r + 1) * ROWS, :] = terms[h * ROWS : (h + 1) * ROWS]
            mixed = dot_nn(terms, values)
            inverse = 1.0 / mixed[:, LANES:]
            mixed = mixed[:, :LANES] * inverse
            att_ref[rows, :] = jnp.where(lanes[0], mixed[:ROWS], mixed[ROWS:]).astype(low_type)
            inv_ref[rows, :] = jnp.where(lanes[0], inverse[:ROWS], inverse[ROWS:])
        return carry

    lax.fori_loop(0, micro, micro_step, 0)


def attention(lengths, lines, qkv, first, number, slot, before=(), deps=()):
    pairs, parts, count, _ = qkv.shape
    micro = count // slot
    spans = 2 * (slot // LANES) - 1
    column = pl.BlockSpec((count, LANES), lambda i: (0, i + first))
    return call(
        attention_kernel,
        "attention_forward",
        [
            shape_of((count, pairs * LANES), low_type),
            shape_of((pairs, micro, 2, slot, slot), low_type),
            shape_of((count, pairs * LANES), full_type),
        ],
        deps=deps,
        grid=(number,),
        in_specs=[
            on_scalars(),
            pl.BlockSpec((1, 2, lines.shape[2]), lambda i: (i + first, 0, 0)),
            pl.BlockSpec((1, parts, count, LANES), lambda i: (i + first, 0, 0, 0)),
            *[in_place()] * len(before),
        ],
        out_specs=[
            column,
            pl.BlockSpec((1, micro, 2, slot, slot), lambda i: (i + first, 0, 0, 0, 0)),
            column,
        ],
        input_output_aliases={3 + i: i for i in range(len(before))},
        scratch_shapes=[pltpu.VMEM((2, spans, LANES, LANES), full_type)],
    )(lengths, lines, qkv, *before)


def branch_kernel(att_ref, *refs):
    *weight_refs, out_ref, w_ref = refs

    @pl.when(pl.program_id(0) == 0)
    def assemble():
        fill_rows(w_ref, weight_refs)

    out_ref[...] = dot_nt(att_ref[...], w_ref[...]).astype(low_type)


def branch_rows(attended, weights, deps=()):
    count, head_width = attended.shape
    width = sum(piece.shape[0] for piece in weights)
    return call(
        branch_kernel,
        "branch",
        shape_of((count, width), low_type),
        deps=deps,
        grid=(count // (2 * ROWS),),
        in_specs=[
            row_blocks((2 * ROWS, head_width)),
            *(pl.BlockSpec((piece.shape[0], head_width), lambda i: (0, 3)) for piece in weights),
        ],
        out_specs=row_blocks((2 * ROWS, width)),
        scratch_shapes=[pltpu.VMEM((width, head_width), low_type)],
    )(attended, *weights)


def hidden_kernel(pieces, len_ref, x_ref, own_ref, came_ref, vector_ref, *refs):
    weight_refs, refs = refs[:pieces], refs[pieces:]
    normed_ref, slope_ref, act_ref, sum_ref, w_ref = refs
    m = pl.program_id(0)
    slot = x_ref.shape[0]

    @pl.when(m == 0)
    def assemble():
        fill_rows(w_ref, weight_refs)

    middle = middle_rows(x_ref, own_ref, came_ref)
    normed = (middle * rms_scale(middle) * vector_ref[1:2]).astype(low_type)
    valid = lax.broadcasted_iota(jnp.int32, (slot, 1), 0) < len_ref[m]
    normed_ref[...] = jnp.where(valid, normed, jnp.zeros_like(normed))
    sum_ref[0] = jnp.sum(jnp.where(valid, middle, 0.0), axis=0, keepdims=True)
    v = dot_nn(normed, w_ref[...])
    square = v * v
    gate = jnp.tanh(v * (gelu_slope + (gelu_slope * gelu_cubic) * square))
    half = 0.5 + 0.5 * gate
    active = (v * half).astype(low_type)
    counted = lax.broadcasted_iota(jnp.int32, (16, slot), 1) < len_ref[m]
    act_ref[0] = dot_nn(jnp.where(counted, 1.0, 0.0).astype(low_type), active)[0:1]
    inner = 0.5 * gelu_slope + (1.5 * gelu_slope * gelu_cubic) * square
    slope_ref[...] = (half + v * (1.0 - gate * gate) * inner).astype(low_type)


def middle_rows(x_ref, own_ref, came_ref):
    branch = own_ref[...].astype(full_type) + came_ref[...].astype(full_type)
    return x_ref[...].astype(full_type) + branch


def hidden(lengths, rows_low, own, came, vectors, weights, slot):
    count, width = rows_low.shape
    micro = count // slot
    inner = weights[0].shape[1]
    return call(
        functools.partial(hidden_kernel, len(weights)),
        "hidden_forward",
        [
            shape_of((count, width), low_type),
            shape_of((count, inner), low_type),
            shape_of((micro, 1, inner), full_type),
            shape_of((micro, 1, width), full_type),
            shape_of((width, inner), low_type),
        ],
        cost=(1200, 20000),
        grid=(micro,),
        in_specs=[
            on_scalars(),
            *[row_blocks((slot, width))] * 3,
            whole(vectors.shape),
            *(whole(piece.shape) for piece in weights),
        ],
        out_specs=[
            row_blocks((slot, width)),
            row_blocks((slot, inner)),
            row_blocks((1, 1, inner)),
            row_blocks((1, 1, width)),
            whole((width, inner)),
        ],
    )(lengths, rows_low, own, came, vectors, *weights)


def few_rows(rows, count):
    place = lax.broadcasted_iota(jnp.int32, (count, rows[0].shape[1]), 0)
    total = jnp.zeros(place.shape, full_type)
    for i, row in enumerate(rows):
        total = jnp.where(place == i, row, total)
    return total


def pool_kernel(lines, act_ref, *refs):
    *weight_refs, out_ref, w_ref = refs
    fill_down(w_ref, weight_refs[:lines], weight_refs[lines:])
    sums = [act_ref[m] for m in range(act_ref.shape[0])]
    highs = [row.astype(low_type).astype(full_type) for row in sums]
    rests = [row - high for row, high in zip(sums, highs)]
    down = dot_nt(few_rows(highs + rests, 16).astype(low_type), w_ref[...])
    micro = len(sums)
    out_ref[...] = few_rows([down[m : m + 1] + down[micro + m : micro + m + 1] for m in range(micro)], 8)


def margin_kernel(len_ref, own_ref, other_ref, sum_ref, act_ref, vector_ref, send_ref):
    margins, rows = [], []
    for m in range(sum_ref.shape[0]):
        length = len_ref[m].astype(full_type)
        total = own_ref[m : m + 1] + other_ref[m : m + 1] + sum_ref[m]
        pooled = (total / length).astype(low_type).astype(full_type)
        final = pooled * rms_scale(pooled) * vector_ref[2:3]
        logits = [
            jnp.sum(final * vector_ref[i : i + 1], axis=1, keepdims=True) * pooled.shape[1] ** (-0.5)
            for i in (3, 4)
        ]
        lane = lax.broadcasted_iota(jnp.int32, pooled.shape, 1)
        margins.append(jnp.where(lane < LANES, logits[0] - logits[1], length))
        rows.append(pooled)
    width = rows[0].shape[1]
    for m in range(sum_ref.shape[0]):
        sums = act_ref[m]
        rows += [sums[:, i * width : (i + 1) * width] for i in range(sums.shape[1] // width)]
    send_ref[...] = few_rows(rows + margins, 8)


def ranking(margins, same, positive):
    place = lax.broadcasted_iota(jnp.int32, margins.shape, 0)
    lane = lax.broadcasted_iota(jnp.int32, margins.shape, 1)
    others = jnp.sum(jnp.where(place == lane, margins, 0.0), axis=0, keepdims=True)
    row_max = jnp.max(jnp.where(same, others, masked_score), axis=1, keepdims=True)
    terms = jnp.where(same, jnp.exp(jnp.where(same, others - row_max, 0.0)), 0.0)
    chance = jnp.exp(margins - row_max) / jnp.sum(terms, axis=1, keepdims=True)
    return LOSS_SCALE * (chance - positive)


def pooled_grad(pooled, d_margin, vector_ref):
    scale = rms_scale(pooled)
    d_logit = d_margin * pooled.shape[1] ** (-0.5)
    d_final = d_logit * (vector_ref[3:4] - vector_ref[4:5])
    return norm_input_grad(d_final, vector_ref[2:3], pooled, scale)


def rank_kernel(
    small_pieces, len_ref, same_ref, positive_ref, vector_ref, slope_ref, down_ref, up_ref, *refs
):
    small_refs, refs = refs[:small_pieces], refs[small_pieces:]
    line_ref, act_ref, rank_ref, hidden_ref, d_ref = refs
    m = pl.program_id(0)

    @pl.when(m == 0)
    def rank():
        lines = []
        for i in range(2):
            margins = stacked_row(small_refs, 6 + i)[:, :LANES]
            d_margins = ranking(margins, same_ref[i] > 0.5, positive_ref[i])
            rank_ref[i] = d_margins
            pooled = small_refs[0][0, i : i + 1, :]
            d_pooled = pooled_grad(pooled, d_margins[0:1, 0:1], vector_ref)
            lines.append(d_pooled / len_ref[i].astype(full_type))
        line_ref[...] = few_rows(lines, 8)
        d_act = dot_nn(few_rows(lines, 16).astype(low_type), down_ref[...])
        act_ref[...] = d_act[:8]

    d_row = jnp.where(m == 0, act_ref[0:1], act_ref[1:2])
    d_hidden = (slope_ref[...].astype(full_type) * d_row).astype(low_type)
    hidden_ref[...] = d_hidden
    d_normed = dot_nt(d_hidden, up_ref[...])
    valid = lax.broadcasted_iota(jnp.int32, (d_normed.shape[0], 1), 0) < len_ref[m]
    d_ref[...] = jnp.where(valid, d_normed, 0.0).astype(low_type)


def rank_back(lengths, same, positive, vectors, slope, small_all, down, up, slot, deps):
    count, inner = slope.shape
    width = vectors.shape[1]
    return call(
        functools.partial(rank_kernel, len(small_all)),
        "rank_backward",
        [
            shape_of((8, width), full_type),
            shape_of((8, inner), full_type),
            shape_of(positive.shape, full_type),
            shape_of((count, inner), low_type),
            shape_of((count, width), low_type),
        ],
        cost=(1200, 20000),
        deps=deps,
        grid=(count // slot,),
        in_specs=[
            on_scalars(),
            *(whole(array.shape) for array in (same, positive, vectors)),
            row_blocks((slot, inner)),
            *(whole(array.shape) for array in (down, up, *small_all)),
        ],
        out_specs=[
            whole((8, width)),
            whole((8, inner)),
            whole(positive.shape),
            row_blocks((slot, inner)),
            row_blocks((slot, width)),
        ],
    )(lengths, same, positive, vectors, slope, down, up, *small_all)


def up_grad_kernel(normed_ref, d_ref, *out_refs):
    for n in range(normed_ref.shape[1] // ROWS):
        columns = slice(n * ROWS, (n + 1) * ROWS)
        spill_rows(dot_tn(normed_ref[:, columns], d_ref[...]), out_refs, n * ROWS)


def up_grad(normed, d_hidden, rows):
    return call(
        up_grad_kernel,
        "hidden_in_gradient",
        [shape_of((r, d_hidden.shape[1]), low_type) for r in rows],
        cost=(1200, 15000),
    )(normed, d_hidden)


def middle_kernel(
    pieces, len_ref, x_ref, branch_ref, other_ref, own_ref, came_ref, vector_ref, line_ref,
    att_ref, inv_ref, *refs
):
    weight_refs, refs = refs[:pieces], refs[pieces:]
    d_ref, d_att_ref, total_ref, w_ref = refs
    m = pl.program_id(0)

    @pl.when(m == 0)
    def assemble():
        fill_rows(w_ref, weight_refs)
        total_ref[...] = jnp.zeros_like(total_ref)

    middle = middle_rows(x_ref, branch_ref, other_ref)
    own = own_ref[...].astype(full_type)
    scale = rms_scale(middle)
    valid = lax.broadcasted_iota(jnp.int32, (middle.shape[0], 1), 0) < len_ref[m]
    line = jnp.where(m == 0, line_ref[0:1], line_ref[1:2])
    d_middle = jnp.where(valid, line, 0.0) + norm_input_grad(
        own + came_ref[...].astype(full_type), vector_ref[1:2], middle, scale
    )
    d_ref[...] = d_middle
    d_low = d_middle.astype(low_type)
    d_att_ref[...] = (dot_nn(d_low, w_ref[...]) * inv_ref[...]).astype(low_type)
    total_ref[...] += dot_tn(d_low, att_ref[...])


def middle_back(
    lengths, rows_low, branch, other, own, came, vectors, lines, attended, inverse, weights, slot
):
    count, width = rows_low.shape
    head_width = attended.shape[1]
    return call(
        functools.partial(middle_kernel, len(weights)),
        "middle_backward",
        [
            shape_of((count, width), full_type),
            shape_of((count, head_width), low_type),
            shape_of((width, head_width), full_type),
        ],
        cost=(600, 15000),
        grid=(count // slot,),
        in_specs=[
            on_scalars(),
            *[row_blocks((slot, width))] * 5,
            whole(vectors.shape),
            whole(lines.shape),
            row_blocks((slot, head_width)),
            row_blocks((slot, head_width)),
            *(
                pl.BlockSpec((piece.shape[0], head_width), lambda i: (0, 3)) for piece in weights
            ),
        ],
        out_specs=[
            row_blocks((slot, width)),
            row_blocks((slot, head_width)),
            whole((width, head_width)),
        ],
        scratch_shapes=[pltpu.VMEM((width, head_width), low_type)],
    )(
        lengths, rows_low, branch, other, own, came, vectors, lines, attended, inverse, *weights
    )


def attention_back_kernel(
    befores, grads, tables, own, prob_ref, qkv_ref, d_ref, att_ref, turned_ref, hot_ref, *refs
):
    table_refs, refs = refs[:tables], refs[tables:]
    grad_refs, refs = refs[:grads], refs[grads:]
    d_out_ref, table_ref, *out_refs, tile_ref, dk_ref, dv_ref = refs[befores:]
    step, last = pl.program_id(0), pl.num_programs(0) - 1
    steps = last - 1 if grads else last

    if grads:

        @pl.when(step == last)
        def projection():
            spill_rows(grad_refs[0][...], out_refs)

    @pl.when(step <= steps)
    def heads():
        pair_back(
            prob_ref, qkv_ref, d_ref, att_ref, turned_ref, hot_ref, d_out_ref, table_ref, out_refs,
            tile_ref, dk_ref, dv_ref
        )
        if tables:
            lines = [
                ref[p, h : h + 1]
                for ref in (*table_refs, table_ref)
                for p in range(ref.shape[0])
                for h in range(2)
            ]
            width = turned_ref.shape[0]
            place = lax.broadcasted_iota(jnp.int32, (width, 16), 0) % own
            pick = place == lax.broadcasted_iota(jnp.int32, (width, 16), 1)
            pick = jnp.where(pick, 1.0, 0.0).astype(low_type)
            spread = dot_nn(pick, few_rows(lines, 16).astype(low_type))
            spill_rows(spread, [ref.at[:, 3 * LANES :] for ref in out_refs])


def pair_back(
    prob_ref, qkv_ref, d_ref, att_ref, turned_ref, hot_ref, d_out_ref, table_ref, out_refs,
    tile_ref, dk_ref, dv_ref
):
    micro, slot = prob_ref.shape[1], prob_ref.shape[3]
    blocks = slot // LANES
    spans = 2 * blocks - 1
    lanes = head_lanes()

    tile_ref[...] = jnp.zeros_like(tile_ref)

    def micro_step(m, carry):
        start = pl.multiple_of(m * slot, slot)
        everything = pl.ds(start, slot)
        keys, values = qkv_ref[0, 1, everything, :], qkv_ref[0, 2, everything, :]
        for r in range(slot // SPAN):
            rows = pl.ds(start + r * SPAN, SPAN)
            queries = qkv_ref[0, 0, rows, :]
            queries = jnp.concatenate(
                [queries * lanes[h].astype(low_type) for h in range(2)], axis=0
            )
            d_att = d_ref[rows, :]
            product = d_att.astype(full_type) * att_ref[rows, :].astype(full_type)
            row_dot = jnp.concatenate(
                [
                    jnp.sum(jnp.where(lanes[h], product, 0.0), axis=1, keepdims=True)
                    for h in range(2)
                ],
                axis=0,
            )
            d_att = jnp.concatenate([d_att * lanes[h].astype(low_type) for h in range(2)], axis=0)
            span = slice(r * SPAN, (r + 1) * SPAN)
            probs = jnp.concatenate([prob_ref[0, m, h, span, :] for h in range(2)], axis=0)
            d_scores = probs.astype(full_type) * (dot_nt(d_att, values) - row_dot)
            d_low = d_scores.astype(low_type)
            for h in range(2):
                for i in range(SPAN // LANES):
                    for j in range(blocks):
                        top = h * SPAN + i * LANES
                        tile_ref[h, j - r * (SPAN // LANES) - i + blocks - 1] += d_scores[
                            top : top + LANES, j * LANES : (j + 1) * LANES
                        ]
            d_queries = dot_nn(d_low, keys)
            d_out_ref[0, 0, rows, :] = jnp.where(
                lanes[0], d_queries[:SPAN], d_queries[SPAN:]
            ).astype(low_type)
            d_keys, d_values = dot_tn(d_low, queries), dot_tn(probs, d_att)
            dk_ref[...] = d_keys if r == 0 else dk_ref[...] + d_keys
            dv_ref[...] = d_values if r == 0 else dv_ref[...] + d_values
        d_out_ref[0, 1, everything, :] = dk_ref[...].astype(low_type)
        d_out_ref[0, 2, everything, :] = dv_ref[...].astype(low_type)
        return carry

    lax.fori_loop(0, micro, micro_step, 0, unroll=True)
    d_project = jnp.concatenate([d_out_ref[0, c] for c in range(3)], axis=1)
    spill_rows(dot_nn(turned_ref[...], d_project), [ref.at[:, : 3 * LANES] for ref in out_refs])
    flip = (
        lax.broadcasted_iota(jnp.int32, (LANES, LANES), 0)
        + lax.broadcasted_iota(jnp.int32, (LANES, LANES), 1)
        == LANES - 1
    )
    flip = jnp.where(flip, 1.0, 0.0).astype(low_type)
    tiles = tile_ref[...].reshape(2 * spans * LANES, LANES)
    high = tiles.astype(low_type)
    rest = (tiles - high.astype(full_type)).astype(low_type)
    flipped = dot_nn(high, flip) + dot_nn(rest, flip)
    zeros = jnp.zeros((LANES, LANES), full_type)
    lines = []
    for h in range(2):
        sums = []
        for d in range(spans):
            top = (h * spans + d) * LANES
            wide = jnp.concatenate([flipped[top : top + LANES], zeros], axis=1)
            turned = pltpu.roll(wide, 0, 1, stride=1, stride_axis=0)
            sums.append(jnp.sum(turned, axis=0, keepdims=True))
        lines.append(jnp.concatenate(sums, axis=1))
    highs = [line.astype(low_type).astype(full_type) for line in lines]
    rests = [line - high for line, high in zip(lines, highs)]
    table = dot_nn(few_rows(highs + rests, 16).astype(low_type), hot_ref[...])
    table_ref[0] = few_rows([table[h : h + 1] + table[2 + h : 3 + h] for h in range(2)], 8)


def attention_back(
    probs, qkv, d_attended, attended, turned, hot, rows, first, number, slot, own,
    grad_out=None, tables=(), before=(), deps=()
):
    width, count = turned.shape
    micro = count // slot
    pairs = qkv.shape[0]
    spans = 2 * (slot // LANES) - 1
    at = lambda i: jnp.minimum(i, number - 1)
    lead = lambda shape: pl.BlockSpec(shape, lambda i: (at(i) + first,) + (0,) * (len(shape) - 1))
    column = pl.BlockSpec((count, LANES), lambda i: (0, at(i) + first))
    if tables:
        steps, extra, extra_specs = number, tables, [whole(table.shape) for table in tables]
        gradients = [shape_of((r, 4 * LANES), low_type) for r in rows]
        gradient_specs = [whole((r, 4 * LANES)) for r in rows]
    else:
        steps = number + (grad_out is not None)
        extra = () if grad_out is None else (grad_out,)
        extra_specs = [whole(array.shape) for array in extra]
        gradients = [shape_of((r, pairs * 3 * LANES), low_type) for r in rows]
        gradient_specs = [pl.BlockSpec((r, 3 * LANES), lambda i: (0, i + first)) for r in rows]
    position = 6 + len(extra)
    return call(
        functools.partial(
            attention_back_kernel, len(before), 0 if grad_out is None else 1, len(tables), own
        ),
        "attention_backward",
        [
            shape_of((pairs, 3, count, LANES), low_type),
            shape_of((number, 8, LANES), full_type),
            *gradients,
        ],
        deps=deps,
        grid=(steps,),
        in_specs=[
            lead((1, micro, 2, slot, slot)),
            lead((1, 3, count, LANES)),
            column,
            column,
            whole(turned.shape),
            whole(hot.shape),
            *extra_specs,
            *[in_place()] * len(before),
        ],
        out_specs=[lead((1, 3, count, LANES)), pl.BlockSpec((1, 8, LANES), lambda i: (at(i), 0, 0)), *gradient_specs],
        input_output_aliases={position + i: i if i == 0 else i + 1 for i in range(len(before))},
        scratch_shapes=[
            pltpu.VMEM((2, spans, LANES, LANES), full_type),
            pltpu.VMEM((slot, LANES), full_type),
            pltpu.VMEM((slot, LANES), full_type),
        ],
    )(probs, qkv, d_attended, attended, turned, hot, *extra, *before)


def normed_back_kernel(d_ref, *refs):
    *weight_refs, out_ref, w_ref = refs
    pairs, parts = d_ref.shape[0], d_ref.shape[1]

    @pl.when(pl.program_id(0) == 0)
    def assemble():
        fill_rows(w_ref, weight_refs, slice(0, w_ref.shape[1]))

    blocks = [d_ref[p, c] for c in range(parts) for p in range(pairs)]
    d_normed = dot_nt(jnp.concatenate(blocks, axis=1), w_ref[...])
    out_ref[...] = d_normed.astype(low_type)


def normed_back(d_project, weights, deps):
    pairs, parts, count, _ = d_project.shape
    width = sum(piece.shape[0] for piece in weights)
    return call(
        normed_back_kernel,
        "normed_backward",
        shape_of((count, width), low_type),
        cost=(900, 15000),
        deps=deps,
        grid=(count // ROWS,),
        in_specs=[
            pl.BlockSpec((pairs, parts, ROWS, LANES), lambda i: (0, 0, i, 0)),
            *(whole(piece.shape) for piece in weights),
        ],
        out_specs=row_blocks((ROWS, width)),
        scratch_shapes=[pltpu.VMEM((width, pairs * parts * LANES), low_type)],
    )(d_project, *weights)


def token_kernel(d_ref, own_ref, came_ref, x_ref, vector_ref, order_ref, out_ref, done_ref):
    x = x_ref[...].astype(full_type)
    d_normed = own_ref[...].astype(full_type) + came_ref[...].astype(full_type)
    grad = d_ref[...] + norm_input_grad(d_normed, vector_ref[0:1], x, rms_scale(x))
    high = grad.astype(low_type)
    rest = (grad - high.astype(full_type)).astype(low_type)
    order = order_ref[...]
    out_ref[...] = dot_nt(high, order) + dot_nt(rest, order)
    done_ref[...] = jnp.zeros_like(done_ref)


def token_back(d_middle, own, came, rows_low, vectors, order, deps):
    count, width = rows_low.shape
    return call(
        token_kernel,
        "token_gradient",
        [shape_of((count, width), full_type), shape_of((8, LANES), full_type)],
        cost=(1200, 15000),
        deps=deps,
        grid=(count // ROWS,),
        in_specs=[row_blocks((ROWS, width))] * 4 + [whole(vectors.shape), whole(order.shape)],
        out_specs=[row_blocks((ROWS, width)), whole((8, LANES))],
    )(d_middle, own, came, rows_low, vectors, order)


def total_kernel(smalls, counts, micro, pairs, *refs):
    small_refs, refs = refs[:smalls], refs[smalls:]
    groups = []
    for count in counts:
        groups.append(refs[:count])
        refs = refs[count:]
    rank_ref, vector_ref, in_ref, up_ref, gain_ref, tied_ref, down_ref, line_ref, *out_refs = refs
    size, width = sum(ref.shape[0] for ref in small_refs), small_refs[0].shape[2]
    row_of = lambda row: stacked_row(small_refs, row)
    own = down_ref.shape[0]
    inverse = 1.0 / LOSS_SCALE
    add_up = lambda values: jnp.sum(values, axis=0, keepdims=True).sum(axis=1, keepdims=True)
    squares, sums = 0.0, []
    for group, out_ref in zip(groups, out_refs):
        total = sum(ref[...].astype(full_type) for ref in group) * inverse
        total, rest = total[:, : out_ref.shape[1]], total[:, out_ref.shape[1] :]
        out_ref[...] = total
        sums.append((total, rest))
        squares = squares + add_up(total * total)
    table = sums[1][1]

    block = lax.broadcasted_iota(jnp.int32, (size, width), 1) // own
    mine = block == lax.broadcasted_iota(jnp.int32, (size, width), 0)
    fold = lax.broadcasted_iota(jnp.int32, (width, LANES), 0) % own == lax.broadcasted_iota(
        jnp.int32, (width, LANES), 1
    )
    fold = jnp.where(fold, 1.0, 0.0).astype(low_type)
    down, ranked = 0.0, 0.0
    lane = lax.broadcasted_iota(jnp.int32, (1, LANES), 1)
    own_factor = (vector_ref[3:4, :LANES] - vector_ref[4:5, :LANES]) * vector_ref[2:3, :LANES]
    own_factor = jnp.where(lane < own, own_factor, 0.0)
    parts = down_ref.shape[1] // width
    for m in range(micro):
        pooled = row_of(m)
        scale = rms_scale(pooled)
        lengths = row_of(micro + micro * parts + m)
        margins, lengths = lengths[:, 0:1], lengths[:, LANES : LANES + 1]
        d_logit = rank_ref[m][:, 0:1] * width ** (-0.5)
        mean = d_logit * margins * (width**0.5 / width) / scale
        mine_low = dot_nn(jnp.where(mine, pooled, 0.0).astype(low_type), fold)
        ranked = ranked + jnp.sum(mine_low * scale * d_logit, axis=0, keepdims=True)
        d_pooled = scale * d_logit * own_factor - mine_low * scale**3 * mean
        lines = (d_pooled / lengths).astype(low_type)
        acts = [row_of(micro + m * parts + i) for i in range(parts)]
        acts = jnp.concatenate(acts, axis=1)
        high = acts.astype(low_type)
        rest = (acts - high.astype(full_type)).astype(low_type)
        down = down + dot_tn(lines, high) + dot_tn(lines, rest)
    down = down[:own] * inverse
    down_ref[...] = down
    squares = squares + add_up(down * down)

    ranked = ranked[:, :own] * inverse
    rounded = lambda ref, i: ref[i : i + 1].astype(low_type).astype(full_type)
    tied_gap = rounded(tied_ref, 0) - rounded(tied_ref, 1)

    def through(products):
        ones = jnp.ones((16, products.shape[1]), low_type)
        high = products.astype(low_type)
        rest = (products - high.astype(full_type)).astype(low_type)
        return (dot_nt(ones, high) + dot_nt(ones, rest))[0:1]

    weighed = lambda ref, total: ref.astype(low_type).astype(full_type) * total
    first = 0.0
    for p in range(pairs):
        source = sums[0][0] if p < pairs - 1 else sums[1][0]
        offset = p * 3 * LANES if p < pairs - 1 else 0
        for c in range(3):
            columns = slice(offset + c * LANES, offset + (c + 1) * LANES)
            first = first + weighed(in_ref[c, :, p * LANES : (p + 1) * LANES], source[:, columns])
    rows = [
        through(first) / rounded(gain_ref, 0),
        through(weighed(up_ref[...], sums[2][0])) / rounded(gain_ref, 1),
        tied_gap * ranked,
        rounded(gain_ref, 2) * ranked,
    ]
    place = lax.broadcasted_iota(jnp.int32, (8, own), 0)
    extra = jnp.zeros((8, own), full_type)
    for i, row in enumerate(rows):
        extra = jnp.where(place == i, row, extra)
    line_ref[...] = jnp.zeros_like(line_ref)
    line_ref[:8, :own] = extra
    line_ref[8:16] = jnp.broadcast_to(squares, (8, LANES))
    line_ref[16 : 16 + 2 * pairs] = table[: 2 * pairs]


def totals(
    small_all, ranks, vectors, grads, heads_in, hidden_in, gains, tied_rows, widths, micro, deps
):
    counts = tuple(len(group) for group in grads)
    flat = [array for group in grads for array in group]
    own, inner = hidden_in.shape
    down, line, *sums = call(
        functools.partial(
            total_kernel, len(small_all), counts, micro, heads_in.shape[2] // LANES
        ),
        "gradient_totals",
        [
            shape_of((own, inner), full_type),
            shape_of((24, LANES), full_type),
            *(shape_of((own, width), full_type) for width in widths),
        ],
        cost=(100, 10000),
        deps=deps,
    )(*small_all, *flat, ranks, vectors, heads_in, hidden_in, gains, tied_rows)
    return down, line, sums


def stage_kernel(*refs):
    count = len(refs) // 2
    for ref, target in zip(refs[:count], refs[count:]):
        target[...] = ref[...]


def adam(weight, first_old, second, grad, factor, rate, decay, step_ref):
    clipped = grad * factor
    next_first = beta_first * first_old + (1.0 - beta_first) * clipped
    next_second = beta_second * second + (1.0 - beta_second) * clipped * clipped
    first_hat = next_first * step_ref[0]
    second_hat = next_second * step_ref[1]
    next_weight = weight - rate * (first_hat / (jnp.sqrt(second_hat) + adam_eps) + decay * weight)
    return next_weight, next_first, next_second


def square_kernel(heads, own_ref, other_ref, out_ref, extra_ref):
    place = lax.broadcasted_iota(jnp.int32, (8, LANES), 0)
    extra = own_ref[:8] + jnp.where(place < 2, other_ref[:8], 0.0)
    extra_ref[...] = extra
    counted = jnp.where(place == 3, 2.0, 1.0) * extra * extra
    add_up = lambda values: jnp.sum(values, axis=0, keepdims=True).sum(axis=1, keepdims=True)
    squares = own_ref[8:16] + other_ref[8:16] + add_up(counted)
    out_ref[:8] = squares
    tables = own_ref[16:24] * own_ref[16:24] + other_ref[16:24] * other_ref[16:24]
    out_ref[8:16] = own_ref[16:24]
    out_ref[16:24] = jnp.broadcast_to(add_up(tables), (8, LANES))


def update_kernel(size, squares, groups, me_ref, step_ref, extra_ref, *refs):
    square_refs, refs = refs[:squares], refs[squares:]
    grad_refs, refs = refs[:groups], refs[groups:]
    state_refs, refs = refs[:21], refs[21:]
    norm_ref, *out_refs = refs
    tiles = stacked(square_refs)
    place = lax.broadcasted_iota(jnp.int32, (tiles.shape[0], 1, 1), 0)
    first = device_of(place, me_ref[0], size) == 0
    tables = jnp.sum(jnp.where(first, tiles[:, 8:24], 0.0), axis=0)
    norm = jnp.sqrt(jnp.sum(tiles[:, 0:8], axis=0)[0:1, 0:1] + tables[8:9, 0:1])
    norm_ref[...] = norm
    factor = jnp.minimum(1.0, clip_limit / (norm + 1e-06))
    weights, firsts, seconds = state_refs[:7], state_refs[7:14], state_refs[14:]
    next_weights, next_firsts, next_seconds = out_refs[:7], out_refs[7:14], out_refs[14:]

    def step(index, where, grad, rate, decay):
        results = adam(
            weights[index][where], firsts[index][where], seconds[index][where], grad, factor,
            rate, decay, step_ref,
        )
        for target, result in zip((next_weights, next_firsts, next_seconds), results):
            target[index][where] = result

    everything = (slice(None), slice(None))
    early_ref, late_ref, up_ref, down_ref = grad_refs
    pairs = weights[0].shape[2] // LANES
    for p in range(pairs):
        source, offset = (early_ref, p * 3) if p < pairs - 1 else (late_ref, 0)
        for c in range(3):
            columns = slice((offset + c) * LANES, (offset + c + 1) * LANES)
            where = (c, slice(None), slice(p * LANES, (p + 1) * LANES))
            step(0, where, source[:, columns], rate_matrix, decay_matrix)
    step(1, everything, early_ref[:, (pairs - 1) * 3 * LANES :], rate_matrix, decay_matrix)
    step(2, everything, up_ref[...], rate_matrix, decay_matrix)
    step(3, everything, down_ref[...], rate_matrix, decay_matrix)
    rows = weights[4].shape[1]
    extra = extra_ref[...]
    step(4, everything, extra[0:3, :rows], rate_vector, 0.0)
    tied = extra[3:4, :rows]
    step(5, everything, jnp.concatenate([tied, -tied], axis=0), rate_vector, 0.0)
    step(6, everything, tables[: 2 * pairs, :BUCKETS], rate_vector, 0.0)


def update(size, pick, corrections, extra, squares, grads, states):
    return call(
        functools.partial(update_kernel, size, len(squares), len(grads)),
        "update",
        [shape_of((1, 1), full_type)] + [shape_of(s.shape, full_type) for s in states],
        cost=(0, 6000),
        grid=(1,),
        in_specs=[
            on_scalars(),
            on_scalars(),
            *(whole(array.shape) for array in (extra, *squares, *grads, *states)),
        ],
    )(pick, corrections, extra, *squares, *grads, *states)


def body(
    tokens,
    pair_lengths,
    query_ids,
    distance_bucket,
    step_count,
    heads_in,
    heads_out,
    hidden_in,
    hidden_out,
    gains,
    tied_rows,
    bias_table,
    first_heads_in,
    first_heads_out,
    first_hidden_in,
    first_hidden_out,
    first_gains,
    first_tied,
    first_table,
    second_heads_in,
    second_heads_out,
    second_hidden_in,
    second_hidden_out,
    second_gains,
    second_tied,
    second_table,
):
    size = lax.axis_size("dp")
    me = lax.axis_index("dp")
    core = lax.axis_index("mp")
    micro, _, slot, width = tokens.shape
    count = micro * slot
    own, local_heads = heads_in.shape[0], bias_table.shape[1]
    head_width = heads_in.shape[2]
    inner = hidden_in.shape[1]
    pairs = local_heads // 2
    spans = 2 * (slot // LANES) - 1
    turn_matrix = lambda array: jnp.transpose(array, (1, 0, 2))
    heads_in, first_heads_in, second_heads_in = (
        turn_matrix(array) for array in (heads_in, first_heads_in, second_heads_in)
    )
    gains, tied_rows, bias_table = gains.T, tied_rows.T, bias_table.T
    first_gains, first_tied, first_table = first_gains.T, first_tied.T, first_table.T
    second_gains, second_tied, second_table = second_gains.T, second_tied.T, second_table.T

    packed_heads = call(
        pack_heads_kernel, "pack_heads", shape_of((own, 4 * head_width + LANES), low_type), vmem=56
    )(heads_in, heads_out, gains, tied_rows)
    down_widths = [inner] if size != 16 else [inner - inner // 3, inner // 3]
    packed_up, packed_down, *packed_plane = call(
        pack_hidden_kernel,
        "pack_hidden",
        [shape_of((own, width_here), low_type) for width_here in (inner, *down_widths)],
    )(hidden_in, hidden_out)
    weights = (heads_in, heads_out, hidden_in, hidden_out, gains, tied_rows, bias_table)
    firsts = (
        first_heads_in,
        first_heads_out,
        first_hidden_in,
        first_hidden_out,
        first_gains,
        first_tied,
        first_table,
    )
    seconds = (
        second_heads_in,
        second_heads_out,
        second_hidden_in,
        second_hidden_out,
        second_gains,
        second_tied,
        second_table,
    )
    states = [*weights, *firsts, *seconds]
    large = [index for index, state in enumerate(states) if index % 7 < 4]
    staged = call(
        stage_kernel, "stage", [shape_of(states[i].shape, full_type) for i in large], vmem=56
    )(*(states[i] for i in large))
    for i, array in zip(large, staged):
        states[i] = array

    lengths = pair_lengths.reshape(micro)
    device = me.reshape(1)
    order, lines, hot_spans, same_tile, positive_tile = call(
        functools.partial(prepare_kernel, size),
        "prepare",
        [
            shape_of((width, width), low_type),
            shape_of((pairs, 2, 2 * slot), full_type),
            shape_of((spans * 2 * LANES, LANES), low_type),
            shape_of((micro, size, LANES), full_type),
            shape_of((micro, size, LANES), full_type),
        ],
        grid=(1,),
        in_specs=[
            on_scalars(),
            whole((1, 2 * slot)),
            whole(bias_table.shape),
            whole(query_ids.shape),
        ],
    )(
        device,
        jnp.pad(distance_bucket, (0, 1), constant_values=-1).reshape(1, 2 * slot),
        bias_table,
        query_ids,
    )
    step_float = step_count.astype(full_type)
    corrections = jnp.stack(
        [1.0 / (1.0 - beta_first**step_float), 1.0 / (1.0 - beta_second**step_float)]
    )

    rows_low = call(
        order_kernel,
        "order_tokens",
        shape_of((count, width), low_type),
        cost=(600, 5000),
        grid=(count // ROWS,),
        in_specs=[row_blocks((ROWS, width)), whole((width, width))],
        out_specs=row_blocks((ROWS, width)),
    )(tokens.reshape(count, width), order)
    if size != 16:
        weight_heads, weight_up, weight_down = (
            [gather_doubling(part, size)] for part in (packed_heads, packed_up, packed_down)
        )
        planes = []
        qkv, normed_first, vectors = project(rows_low, weight_heads, pairs, ())
    else:
        plane_sides = side_parts(*packed_plane, size, "down_plane")
        heads_line, packed_up, packed_down = join(
            line_parts(packed_heads, size, "heads"),
            deps=(staged[0], order, corrections, *plane_sides),
            passing=(packed_up, packed_down),
        )
        heads_sides = side_parts(heads_line, size, "heads")
        up_pair = join([packed_up, swap(packed_up, 8, size, "up")], deps=(rows_low,))
        up_near = swap(up_pair, 4, size, "up")
        plane_corner = swap(plane_sides[0], 1, size, "down_plane_corner")
        low, high, packed_down = gather_step(
            *heads_sides, deps=(up_pair, plane_corner), passing=(packed_down,)
        )
        down_far = swap(packed_down, 8, size, "down")
        heads_corner = corner_parts(low, high, size, "heads_corner")
        up_line = join([up_pair, up_near], deps=(low,))
        down_pair = join([packed_down, down_far], deps=(up_line,))
        down_near = swap(down_pair, 4, size, "down")
        up_sides = side_parts(up_line, size, "up")
        weight_heads = [heads_line, *heads_sides, *heads_corner]
        qkv, normed_first, vectors = project(rows_low, weight_heads, pairs, ())
    filled = attention(
        lengths, lines, qkv, 0, 1, slot, deps=(down_pair,) if size == 16 else ()
    )
    if size == 16:
        down_line = join([down_pair, down_near], deps=(filled[0],))
        down_sides = side_parts(down_line, size, "down")
        plane = join([*packed_plane, *plane_sides, plane_corner], deps=(down_line,))
        plane_far = swap(plane, 8, size, "down_plane")
    if pairs > 1:
        filled = attention(lengths, lines, qkv, 1, pairs - 1, slot, before=filled)
    if size == 16:
        low, high = gather_step(*up_sides, deps=(filled[0],))
        up_corner = corner_parts(low, high, size, "up_corner")
        plane_pair = join([plane, plane_far], deps=(filled[0],))
        planes = [plane_pair, swap(plane_pair, 4, size, "down_plane")]
        weight_up = [up_line, *up_sides, *up_corner]
    turned_first = call(turn_kernel, "turn", shape_of((width, count), low_type))(normed_first)
    attended, probs, inverse = filled
    branch = branch_rows(
        attended, weight_heads, (low, plane_pair, *down_sides, turned_first) if size == 16 else ()
    )
    if size == 16:
        low, high = gather_step(*down_sides, deps=(branch,))
        down_corner = corner_parts(low, high, size, "down_corner")
        weight_down = [down_line, *down_sides, *down_corner]
    branch_came = other_core(branch, "branch_other_core")
    normed_second, slope, act_sum, middle_sum, full_up = hidden(
        lengths, rows_low, branch, branch_came, vectors, weight_up, slot
    )
    down, full_down = call(
        functools.partial(pool_kernel, len(weight_down)),
        "pool",
        [shape_of((8, width), full_type), shape_of((width, inner), low_type)],
        cost=(20, 5000),
    )(act_sum, *weight_down, *planes)
    small = call(
        margin_kernel,
        "margin",
        shape_of((8, width), full_type),
        grid=(1,),
        in_specs=[
            on_scalars(),
            *(whole(array.shape) for array in (down, down, middle_sum, act_sum, vectors)),
        ],
        out_specs=whole((8, width)),
    )(lengths, down, other_core(down, "pooled_part_other_core"), middle_sum, act_sum, vectors)
    small_all = gather_small(small, size, "small_sums")

    d_line, _, ranks, d_hidden, d_normed_second = rank_back(
        lengths, same_tile, positive_tile, vectors, slope, small_all, full_down, full_up, slot,
        (turned_first,),
    )
    d_normed_second_came = other_core(d_normed_second, "second_gradient_other_core")
    up_sum = Scatter(
        up_grad(normed_second, d_hidden, piece_rows(size, width)), size, "up_gradient"
    )
    d_middle, d_attended, g_out = middle_back(
        lengths, rows_low, branch, branch_came, d_normed_second, d_normed_second_came, vectors,
        d_line, attended, inverse, weight_heads, slot,
    )
    scatter_sides([up_sum], deps=(d_attended,))
    d_project, tables, *g_early = attention_back(
        probs, qkv, d_attended, attended, turned_first, hot_spans, piece_rows(size, width),
        0, pairs - 1, slot, own, grad_out=g_out,
    )
    early_sum = Scatter(g_early, size, "early_gradient")
    d_project, table, *g_late = attention_back(
        probs, qkv, d_attended, attended, turned_first, hot_spans, piece_rows(size, width),
        pairs - 1, 1, slot, own, tables=(tables,), before=(d_project,),
    )
    late_sum = Scatter(g_late, size, "late_gradient")
    up_sum.near(deps=(table,))
    sides = scatter_sides([early_sum, late_sum], deps=up_sum.sources)
    d_normed_first = normed_back(d_project, weight_heads, sides)
    up_parts = up_sum.far(deps=sides)
    (d_normed_first,) = early_sum.near(deps=tuple(up_parts), passing=(d_normed_first,))
    early_parts = early_sum.far()
    late_parts, _ = late_sum.line(deps=(early_parts[0],))

    token_gradient, token_done = token_back(
        d_middle, d_normed_first, other_core(d_normed_first, "first_gradient_other_core"), rows_low,
        vectors, order, late_sum.sources,
    )

    g_down, line, grad_sums = totals(
        small_all, ranks, vectors, [early_parts, late_parts, up_parts], heads_in, hidden_in, gains, tied_rows,
        (head_width * 3, 3 * LANES, inner), micro, (token_done,),
    )
    square_tile, extra = call(
        functools.partial(square_kernel, local_heads),
        "squares",
        [shape_of((24, LANES), full_type), shape_of((8, LANES), full_type)],
    )(line, other_core(line, "totals_other_core"))
    squares_all = gather_small(square_tile, size, "squares")
    grads = [*grad_sums, g_down]
    norm, *results = update(size, device, corrections, extra, squares_all, grads, states)
    for index in (0, 7, 14):
        results[index] = turn_matrix(results[index])
        for other in (4, 5, 6):
            results[index + other] = results[index + other].T
    return (norm.reshape(()), token_gradient.reshape(tokens.shape), *results)


def solution(mesh):
    in_specs = (
        P(None, "dp", None, None),
        P(None, "dp"),
        P(),
        P(),
        P(),
        P("dp", None, "mp"),
        P("dp", "mp"),
        P("dp", "mp"),
        P("dp", "mp"),
        P("dp", None),
        P("dp", None),
        P(None, "mp"),
        P("dp", None, "mp"),
        P("dp", "mp"),
        P("dp", "mp"),
        P("dp", "mp"),
        P("dp", None),
        P("dp", None),
        P(None, "mp"),
        P("dp", None, "mp"),
        P("dp", "mp"),
        P("dp", "mp"),
        P("dp", "mp"),
        P("dp", None),
        P("dp", None),
        P(None, "mp"),
    )
    out_specs = (
        P(),
        P(None, "dp", None, None),
        P("dp", None, "mp"),
        P("dp", "mp"),
        P("dp", "mp"),
        P("dp", "mp"),
        P("dp", None),
        P("dp", None),
        P(None, "mp"),
        P("dp", None, "mp"),
        P("dp", "mp"),
        P("dp", "mp"),
        P("dp", "mp"),
        P("dp", None),
        P("dp", None),
        P(None, "mp"),
        P("dp", None, "mp"),
        P("dp", "mp"),
        P("dp", "mp"),
        P("dp", "mp"),
        P("dp", None),
        P("dp", None),
        P(None, "mp"),
    )
    return jax.shard_map(body, mesh=mesh, in_specs=in_specs, out_specs=out_specs, check_vma=False)
```

```python
import functools

import jax
import jax.numpy as jnp
from jax import lax
from jax.experimental import pallas as pl
from jax.experimental.pallas import tpu as pltpu
from jax.sharding import PartitionSpec as P

BUCKETS = 32
LOSS_SCALE = 1024
LANES = 128
ROWS = 256
SPAN = 512

norm_eps = 1e-06
clip_limit = 0.01
beta_first = 0.9
beta_second = 0.999
adam_eps = 1e-08
rate_matrix = 0.03
rate_vector = 0.25
decay_matrix = 0.1
masked_score = -1e30
gelu_slope = 0.7978845608028654
gelu_cubic = 0.044715
low_type = jnp.bfloat16
full_type = jnp.float32
core_swap = [(0, 1), (1, 0)]


def rms_scale(rows_in):
    return lax.rsqrt(jnp.mean(rows_in * rows_in, axis=-1, keepdims=True) + norm_eps)


def norm_input_grad(d_normed, gain_row, rows_in, norm_scale):
    weighted = d_normed * gain_row
    return norm_scale * weighted - rows_in * norm_scale**3 * jnp.mean(
        weighted * rows_in, axis=-1, keepdims=True
    )


def dot_nt(left, right):
    return lax.dot_general(left, right, (((1,), (1,)), ((), ())), preferred_element_type=full_type)


def dot_tn(left, right):
    return lax.dot_general(left, right, (((0,), (0,)), ((), ())), preferred_element_type=full_type)


def dot_nn(left, right):
    return lax.dot_general(left, right, (((1,), (0,)), ((), ())), preferred_element_type=full_type)


def call(
    kernel, name, out_shape, cost=(0, 0), vmem=16, deps=(), passing=(), in_specs=None,
    out_specs=None, input_output_aliases=None, **options
):
    single = not isinstance(out_shape, (list, tuple))
    out_shapes = [out_shape] if single else list(out_shape)
    outputs, extra = len(out_shapes), len(deps) + len(passing)

    def apply(*operands):
        inputs = len(operands)
        if in_specs is None:
            options["grid"] = (1,)
        specs = [whole(operand.shape) for operand in operands] if in_specs is None else in_specs
        targets = out_specs or [whole(shape.shape) for shape in out_shapes]
        targets = targets if isinstance(targets, (list, tuple)) else [targets]
        aliases = dict(input_output_aliases or {})
        for i in range(len(passing)):
            aliases[inputs + len(deps) + i] = outputs + i

        def run(*refs):
            own = inputs + extra
            kernel(*refs[:inputs], *refs[own : own + outputs], *refs[own + outputs + len(passing) :])

        results = pl.pallas_call(
            run,
            out_shape=[*out_shapes, *(shape_of(a.shape, a.dtype) for a in passing)],
            in_specs=[*specs, *[in_place()] * extra],
            out_specs=[*targets, *[in_place()] * len(passing)],
            input_output_aliases=aliases,
            compiler_params=pltpu.CompilerParams(vmem_limit_bytes=vmem * 1024 * 1024),
            cost_estimate=pl.CostEstimate(
                flops=int(cost[0] * 2e6), bytes_accessed=int(cost[1] * 1e3), transcendentals=0
            ),
            name=name,
            **options,
        )(*operands, *deps, *passing)
        return results[0] if single and not passing else results

    return apply


def in_place():
    return pl.BlockSpec(memory_space=pl.ANY)


def shape_of(shape, dtype):
    return jax.ShapeDtypeStruct(tuple(shape), dtype)


def whole(shape):
    return pl.BlockSpec(tuple(shape), lambda *_: (0,) * len(shape))


def on_scalars():
    return pl.BlockSpec(memory_space=pltpu.SMEM)


def row_blocks(shape, step=0):
    return pl.BlockSpec(tuple(shape), lambda i: (i,) + (0,) * (len(shape) - 1))


def column_blocks(shape, offset=0):
    return pl.BlockSpec(tuple(shape), lambda i: (0,) * (len(shape) - 1) + (i + offset,))


def fill_rows(target, pieces, columns=slice(None)):
    start = 0
    for piece in pieces:
        rows = piece.shape[0]
        target[start : start + rows, :] = piece[:, columns]
        start += rows


def spill_rows(value, pieces, first=0):
    start = 0
    for piece in pieces:
        rows = piece.shape[0]
        low, high = max(start, first), min(start + rows, first + value.shape[0])
        if low < high:
            piece[low - start : high - start] = value[low - first : high - first].astype(piece.dtype)
        start += rows


def swap(array, mask, size, label="exchange"):
    with jax.named_scope(f"{label}_across_{mask}"):
        return lax.ppermute(array, "dp", [(i, i ^ mask) for i in range(size)])


def tie(arrays, deps):
    return call(lambda: None, "tie", [], deps=deps, passing=arrays, in_specs=[], grid=(1,))()


def other_core(array, label="other_core"):
    with jax.named_scope(label):
        return lax.ppermute(array, "mp", core_swap)


def stage_bits(size):
    if size == 16:
        return (8, 4, 2, 1)
    return tuple(1 << i for i in range(size.bit_length() - 1))


def device_of(place, me, size):
    mask = jnp.zeros_like(place)
    for i, bit in enumerate(stage_bits(size)):
        mask = mask + jnp.bitwise_and(place >> i, 1) * bit
    return jnp.bitwise_xor(mask, me)


def piece_rows(size, width):
    if size != 16:
        return [width]
    return [width // 4] * 3 + [width // 8] * 2


def join_kernel(*refs):
    *part_refs, out_ref = refs
    start = 0
    for part in part_refs:
        rows = part.shape[0]
        out_ref[start : start + rows] = part[...]
        start += rows


def join(parts, **options):
    rows = sum(part.shape[0] for part in parts)
    return call(
        join_kernel, "join", shape_of((rows, *parts[0].shape[1:]), parts[0].dtype), **options
    )(*parts)


def step_kernel(groups, y_ref, x_ref, *refs):
    part_refs, (low_ref, high_ref, *joined_refs) = refs[: sum(groups)], refs[sum(groups) :]
    low_ref[...] = y_ref[...]
    high_ref[...] = x_ref[...]
    for group, joined_ref in zip(groups, joined_refs):
        join_kernel(*part_refs[:group], joined_ref)
        part_refs = part_refs[group:]


def gather_step(across_y, across_x, *groups, **options):
    half = (across_y.shape[0] // 2, across_y.shape[1])
    shapes = [shape_of(half, across_y.dtype)] * 2
    for parts in groups:
        shapes.append(shape_of((sum(p.shape[0] for p in parts), parts[0].shape[1]), parts[0].dtype))
    flat = [part for parts in groups for part in parts]
    return call(
        functools.partial(step_kernel, tuple(len(parts) for parts in groups)),
        "gather_step",
        shapes,
        grid=(1,),
        in_specs=[
            pl.BlockSpec(half, lambda i: (0, 0)),
            pl.BlockSpec(half, lambda i: (1, 0)),
            *(whole(part.shape) for part in flat),
        ],
        out_specs=[whole(shape.shape) for shape in shapes],
        **options,
    )(across_y, across_x, *flat)


def line_parts(part, size, label):
    return [part] + [swap(part, mask, size, label) for mask in (8, 4, 12)]


def side_parts(quarter, size, label):
    return [swap(quarter, mask, size, label) for mask in (2, 1)]


def corner_parts(low, high, size, label):
    return [swap(low, 1, size, label), swap(high, 2, size, label)]


def gather_doubling(part, size):
    for bit in stage_bits(size):
        part = jnp.concatenate([part, swap(part, bit, size)], axis=0)
    return part


def small_line(part, size, label):
    if size != 16:
        return part[None]
    return join(line_parts(part[None], size, label))


def small_plane(quarter, size, label):
    if size != 16:
        return [gather_doubling(quarter, size)]
    return [quarter] + [swap(quarter, mask, size, label) for mask in (2, 1, 3)]


def stacked(refs):
    return jnp.concatenate([ref[...] for ref in refs], axis=0)


def stacked_row(refs, row):
    return jnp.concatenate([ref[:, row, :] for ref in refs], axis=0)


def gather_small(part, size, label):
    return small_plane(small_line(part, size, label), size, label)


def plane_sum_kernel(*refs):
    count = len(refs) // 6
    for i in range(count):
        y_ref, x_ref, low_ref, high_ref = refs[4 * i : 4 * i + 4]
        y_out, x_out = refs[4 * count + 2 * i : 4 * count + 2 * i + 2]
        half = low_ref.shape[0]
        y_out[:half] = (y_ref[:half].astype(full_type) + low_ref[...].astype(full_type)).astype(
            low_type
        )
        y_out[half:] = y_ref[half:]
        x_out[:half] = x_ref[:half]
        x_out[half:] = (x_ref[half:].astype(full_type) + high_ref[...].astype(full_type)).astype(
            low_type
        )


def line_sum_kernel(*refs):
    count = sum(ref.shape[0] == refs[0].shape[0] for ref in refs)
    add_refs, out_refs = refs[:count], refs[count:]
    rows = out_refs[0].shape[0]
    for i, out_ref in enumerate(out_refs):
        span = slice(i * rows, (i + 1) * rows)
        total = add_refs[0][span].astype(full_type)
        for ref in add_refs[1:]:
            total = total + ref[span].astype(full_type)
        out_ref[...] = total.astype(out_ref.dtype)


class Scatter:
    def __init__(self, pieces, size, label):
        self.pieces, self.size, self.label = pieces, size, label
        self.sources, self.came = (), ()
        if size == 16:
            *self.pieces, low, high = pieces
            self.came = [swap(low, 1, size, label), swap(high, 2, size, label)]

    def near(self, deps=(), passing=()):
        if self.size != 16:
            return passing
        keep = self.pieces[0]
        half = (keep.shape[0] // 2, keep.shape[1])
        kept, sent, *passed = call(
            line_sum_kernel,
            "line_sum",
            [shape_of(half, full_type), shape_of(half, low_type)],
            deps=deps,
            passing=passing,
        )(keep, *self.came)
        self.sources, self.came, self.pieces = (sent,), [swap(sent, 4, self.size, self.label)], [kept]
        return passed

    def far(self, deps=()):
        if self.size != 16:
            return self.line(deps)[0]
        kept = self.pieces[0]
        half = (kept.shape[0] // 2, kept.shape[1])
        own, sent = call(
            line_sum_kernel,
            "line_sum",
            [shape_of(half, full_type), shape_of(half, low_type)],
            deps=deps,
        )(kept, *self.came)
        self.sources = (sent,)
        return [own, swap(sent, 8, self.size, self.label)]

    def line(self, deps=(), passing=()):
        size, label = self.size, self.label
        if size != 16:
            grad = self.pieces[0]
            for bit in reversed(stage_bits(size)):
                half = grad.shape[0] // 2
                came = swap(grad[half:], bit, size, label)
                grad = (grad[:half].astype(full_type) + came.astype(full_type)).astype(low_type)
            return [grad.astype(full_type)], passing
        keep = self.pieces[0]
        part = (keep.shape[0] // 4, keep.shape[1])
        own, *others = call(
            line_sum_kernel,
            "line_sum",
            [shape_of(part, full_type)] + [shape_of(part, low_type)] * 3,
            deps=deps,
            passing=passing,
        )(keep, *self.came)
        came = [swap(other, mask, size, label) for other, mask in zip(others, (8, 4, 12))]
        self.sources = (own,)
        return [own] + came, others[3:]


def scatter_sides(scatters, deps=()):
    if scatters[0].size != 16:
        return ()
    sides = [part for scatter in scatters for part in scatter.pieces[1:]]
    operands = [part for s in scatters for part in (*s.pieces[1:], *s.came)]
    sums = call(
        plane_sum_kernel, "plane_sum", [shape_of(part.shape, low_type) for part in sides], deps=deps
    )(*operands)
    for i, scatter in enumerate(scatters):
        to_y, to_x = sums[2 * i : 2 * i + 2]
        scatter.came = [
            swap(to_y, 2, scatter.size, scatter.label), swap(to_x, 1, scatter.size, scatter.label)
        ]
    return tuple(sums)


def pack_heads_kernel(in_ref, out_ref, gain_ref, tied_ref, a_ref):
    parts, rows, width = in_ref.shape
    for c in range(parts):
        a_ref[:, c * width : (c + 1) * width] = in_ref[c].astype(low_type)
    a_ref[:, parts * width : (parts + 1) * width] = out_ref[...].astype(low_type)
    gains, tied = gain_ref[...], tied_ref[...]
    vectors = few_rows([gains[i : i + 1] for i in range(3)] + [tied[i : i + 1] for i in range(2)], 16)
    pick = lax.broadcasted_iota(jnp.int32, (16, LANES), 0) == lax.broadcasted_iota(
        jnp.int32, (16, LANES), 1
    )
    extra = dot_tn(vectors.astype(low_type), jnp.where(pick, 1.0, 0.0).astype(low_type))
    a_ref[:, (parts + 1) * width :] = extra.astype(low_type)


def pack_hidden_kernel(up_ref, down_ref, packed_ref, *part_refs):
    packed_ref[...] = up_ref[...].astype(low_type)
    start = 0
    for ref in part_refs:
        width = ref.shape[1]
        ref[...] = down_ref[:, start : start + width].astype(low_type)
        start += width


def fill_down(target, line_pieces, plane_pieces):
    width = line_pieces[0].shape[1]
    fill_rows(target.at[:, :width], line_pieces)
    own = target.shape[0] // 16
    for i, piece in enumerate(plane_pieces):
        for f in range(2):
            for q in range(4):
                rows = piece[(f * 4 + q) * own : (f * 4 + q + 1) * own, :]
                place = (4 * q + 2 * i + f) * own
                target[place : place + own, width:] = rows


def prepare_kernel(
    size, me_ref, line_ref, table_ref, query_ref, order_ref, bias_ref, hot_ref, same_ref, positive_ref
):
    me = me_ref[0]
    lane = lambda shape: lax.broadcasted_iota(jnp.int32, shape, 1)
    row = lambda shape: lax.broadcasted_iota(jnp.int32, shape, 0)
    low = lambda hit: jnp.where(hit, 1.0, 0.0).astype(low_type)
    width = order_ref.shape[0]
    own = width // size
    feature = lane((1, width))
    place = device_of(feature // own, me, size) * own + feature % own
    for start in range(0, width, LANES):
        order_ref[start : start + LANES] = low(row((LANES, width)) + start == place)
    length = line_ref.shape[1]
    hot = low(row((LANES, length)) == line_ref[...])
    lines = dot_nn(table_ref[...].astype(low_type), hot[:BUCKETS])
    for head in range(table_ref.shape[0]):
        bias_ref[head // 2, head % 2 : head % 2 + 1] = lines[head : head + 1]
    step = 2 * LANES
    for start in range(0, hot_ref.shape[0], step):
        wanted = start // 2 + step - 2 - row((step, length))
        hot_ref[start : start + step] = dot_nt(low(wanted == lane((step, length))), hot).astype(
            low_type
        )
    shape = (size, LANES)
    pair = device_of(row(shape), me, size)
    other = device_of(lane(shape), me, size)
    for m in range(query_ref.shape[0]):
        queries = query_ref[m : m + 1]
        if size < LANES:
            blank = jnp.zeros((1, LANES - size), jnp.int32)
            queries = jnp.concatenate([queries, blank], axis=1)
        picked = jnp.where(lane(shape) == pair, queries, 0).astype(full_type)
        mine = jnp.sum(picked, axis=1, keepdims=True)
        theirs = jnp.sum(jnp.where(lane(shape) == row(shape), mine, 0.0), axis=0, keepdims=True)
        same = jnp.where((mine == theirs) & (lane(shape) < size), 1.0, 0.0)
        same_ref[m] = same
        earlier = jnp.max(jnp.where(other < pair, same, 0.0), axis=1, keepdims=True)
        positive_ref[m] = jnp.broadcast_to(1.0 - earlier, shape)


def order_kernel(x_ref, order_ref, out_ref):
    out_ref[...] = dot_nn(x_ref[...], order_ref[...]).astype(low_type)


def turn_kernel(x_ref, out_ref):
    out_ref[...] = x_ref[...].T


def head_lanes():
    lane = lax.broadcasted_iota(jnp.int32, (1, LANES), 1)
    return [lane < LANES // 2, lane >= LANES // 2]


def project_kernel(pieces, pairs, x_ref, *refs):
    weight_refs, (qkv_ref, normed_ref, vector_ref, w_ref) = refs[:pieces], refs[pieces:]
    parts = qkv_ref.shape[1]
    in_width = pairs * parts * LANES

    @pl.when(pl.program_id(0) == 0)
    def assemble():
        fill_rows(w_ref, weight_refs)
        pick = lax.broadcasted_iota(jnp.int32, (16, LANES), 0) == lax.broadcasted_iota(
            jnp.int32, (16, LANES), 1
        )
        vectors = dot_nt(jnp.where(pick, 1.0, 0.0).astype(low_type), w_ref[:, -LANES:])
        vector_ref[...] = vectors[:8]

    x = x_ref[...].astype(full_type)
    normed = (x * rms_scale(x) * vector_ref[0:1]).astype(low_type)
    normed_ref[...] = normed
    projected = dot_nn(normed, w_ref[:, :in_width]).astype(low_type)
    for c in range(parts):
        for p in range(pairs):
            start = (c * pairs + p) * LANES
            qkv_ref[p, c] = projected[:, start : start + LANES]


def project(rows_low, weights, pairs, deps):
    count, width = rows_low.shape
    parts = 3
    return call(
        functools.partial(project_kernel, len(weights), pairs),
        "projection",
        [
            shape_of((pairs, parts, count, LANES), low_type),
            shape_of((count, width), low_type),
            shape_of((8, width), full_type),
        ],
        deps=deps,
        grid=(count // ROWS,),
        in_specs=[row_blocks((ROWS, width)), *(whole(piece.shape) for piece in weights)],
        out_specs=[
            pl.BlockSpec((pairs, parts, ROWS, LANES), lambda i: (0, 0, i, 0)),
            row_blocks((ROWS, width)),
            whole((8, width)),
        ],
        scratch_shapes=[pltpu.VMEM((width, weights[0].shape[1]), low_type)],
    )(rows_low, *weights)


def attention_kernel(len_ref, line_ref, qkv_ref, *refs):
    att_ref, prob_ref, inv_ref, tile_ref = refs[-4:]
    micro, slot = prob_ref.shape[1], prob_ref.shape[3]
    blocks = slot // LANES
    lanes = head_lanes()
    for h in range(2):
        for d in range(2 * blocks - 1):
            piece = jnp.broadcast_to(
                line_ref[0, h : h + 1, d * LANES : (d + 2) * LANES], (LANES, 2 * LANES)
            )
            turned = pltpu.roll(piece, LANES + 1, 1, stride=1, stride_axis=0)
            tile_ref[h, d] = turned[:, :LANES]

    def micro_step(m, carry):
        start = pl.multiple_of(m * slot, slot)
        key_valid = lax.broadcasted_iota(jnp.int32, (1, slot), 1) < len_ref[m]
        keys = qkv_ref[0, 1, pl.ds(start, slot), :]
        values = qkv_ref[0, 2, pl.ds(start, slot), :]
        values = jnp.concatenate([values, jnp.ones_like(values)], axis=1)
        for r in range(slot // ROWS):
            rows = pl.ds(start + r * ROWS, ROWS)
            queries = qkv_ref[0, 0, rows, :]
            queries = jnp.concatenate(
                [queries * lanes[h].astype(low_type) for h in range(2)], axis=0
            )
            first = r * (ROWS // LANES)
            bias = jnp.concatenate(
                [
                    jnp.concatenate(
                        [tile_ref[h, j - first - i + blocks - 1] for j in range(blocks)], axis=1
                    )
                    for h in range(2)
                    for i in range(ROWS // LANES)
                ],
                axis=0,
            )
            scores = dot_nt(queries, keys)
            scores = jnp.where(key_valid, scores + bias, masked_score)
            terms = jnp.exp(scores - jnp.max(scores, axis=1, keepdims=True)).astype(low_type)
            for h in range(2):
                prob_ref[0, m, h, r * ROWS : (r + 1) * ROWS, :] = terms[h * ROWS : (h + 1) * ROWS]
            mixed = dot_nn(terms, values)
            inverse = 1.0 / mixed[:, LANES:]
            mixed = mixed[:, :LANES] * inverse
            att_ref[rows, :] = jnp.where(lanes[0], mixed[:ROWS], mixed[ROWS:]).astype(low_type)
            inv_ref[rows, :] = jnp.where(lanes[0], inverse[:ROWS], inverse[ROWS:])
        return carry

    lax.fori_loop(0, micro, micro_step, 0)


def attention(lengths, lines, qkv, first, number, slot, before=(), deps=()):
    pairs, parts, count, _ = qkv.shape
    micro = count // slot
    spans = 2 * (slot // LANES) - 1
    column = pl.BlockSpec((count, LANES), lambda i: (0, i + first))
    return call(
        attention_kernel,
        "attention_forward",
        [
            shape_of((count, pairs * LANES), low_type),
            shape_of((pairs, micro, 2, slot, slot), low_type),
            shape_of((count, pairs * LANES), full_type),
        ],
        deps=deps,
        grid=(number,),
        in_specs=[
            on_scalars(),
            pl.BlockSpec((1, 2, lines.shape[2]), lambda i: (i + first, 0, 0)),
            pl.BlockSpec((1, parts, count, LANES), lambda i: (i + first, 0, 0, 0)),
            *[in_place()] * len(before),
        ],
        out_specs=[
            column,
            pl.BlockSpec((1, micro, 2, slot, slot), lambda i: (i + first, 0, 0, 0, 0)),
            column,
        ],
        input_output_aliases={3 + i: i for i in range(len(before))},
        scratch_shapes=[pltpu.VMEM((2, spans, LANES, LANES), full_type)],
    )(lengths, lines, qkv, *before)


def branch_kernel(att_ref, *refs):
    *weight_refs, out_ref, w_ref = refs

    @pl.when(pl.program_id(0) == 0)
    def assemble():
        fill_rows(w_ref, weight_refs)

    out_ref[...] = dot_nt(att_ref[...], w_ref[...]).astype(low_type)


def branch_rows(attended, weights, deps=()):
    count, head_width = attended.shape
    width = sum(piece.shape[0] for piece in weights)
    return call(
        branch_kernel,
        "branch",
        shape_of((count, width), low_type),
        deps=deps,
        grid=(count // (2 * ROWS),),
        in_specs=[
            row_blocks((2 * ROWS, head_width)),
            *(pl.BlockSpec((piece.shape[0], head_width), lambda i: (0, 3)) for piece in weights),
        ],
        out_specs=row_blocks((2 * ROWS, width)),
        scratch_shapes=[pltpu.VMEM((width, head_width), low_type)],
    )(attended, *weights)


def hidden_kernel(pieces, len_ref, x_ref, own_ref, came_ref, vector_ref, *refs):
    weight_refs, refs = refs[:pieces], refs[pieces:]
    normed_ref, slope_ref, act_ref, sum_ref, w_ref = refs
    m = pl.program_id(0)
    slot = x_ref.shape[0]

    @pl.when(m == 0)
    def assemble():
        fill_rows(w_ref, weight_refs)

    middle = middle_rows(x_ref, own_ref, came_ref)
    normed = (middle * rms_scale(middle) * vector_ref[1:2]).astype(low_type)
    valid = lax.broadcasted_iota(jnp.int32, (slot, 1), 0) < len_ref[m]
    normed_ref[...] = jnp.where(valid, normed, jnp.zeros_like(normed))
    sum_ref[0] = jnp.sum(jnp.where(valid, middle, 0.0), axis=0, keepdims=True)
    v = dot_nn(normed, w_ref[...])
    square = v * v
    gate = jnp.tanh(v * (gelu_slope + (gelu_slope * gelu_cubic) * square))
    half = 0.5 + 0.5 * gate
    active = (v * half).astype(low_type)
    counted = lax.broadcasted_iota(jnp.int32, (16, slot), 1) < len_ref[m]
    act_ref[0] = dot_nn(jnp.where(counted, 1.0, 0.0).astype(low_type), active)[0:1]
    inner = 0.5 * gelu_slope + (1.5 * gelu_slope * gelu_cubic) * square
    slope_ref[...] = (half + v * (1.0 - gate * gate) * inner).astype(low_type)


def middle_rows(x_ref, own_ref, came_ref):
    branch = own_ref[...].astype(full_type) + came_ref[...].astype(full_type)
    return x_ref[...].astype(full_type) + branch


def hidden(lengths, rows_low, own, came, vectors, weights, slot):
    count, width = rows_low.shape
    micro = count // slot
    inner = weights[0].shape[1]
    return call(
        functools.partial(hidden_kernel, len(weights)),
        "hidden_forward",
        [
            shape_of((count, width), low_type),
            shape_of((count, inner), low_type),
            shape_of((micro, 1, inner), full_type),
            shape_of((micro, 1, width), full_type),
            shape_of((width, inner), low_type),
        ],
        cost=(1200, 20000),
        grid=(micro,),
        in_specs=[
            on_scalars(),
            *[row_blocks((slot, width))] * 3,
            whole(vectors.shape),
            *(whole(piece.shape) for piece in weights),
        ],
        out_specs=[
            row_blocks((slot, width)),
            row_blocks((slot, inner)),
            row_blocks((1, 1, inner)),
            row_blocks((1, 1, width)),
            whole((width, inner)),
        ],
    )(lengths, rows_low, own, came, vectors, *weights)


def few_rows(rows, count):
    place = lax.broadcasted_iota(jnp.int32, (count, rows[0].shape[1]), 0)
    total = jnp.zeros(place.shape, full_type)
    for i, row in enumerate(rows):
        total = jnp.where(place == i, row, total)
    return total


def pool_kernel(lines, act_ref, *refs):
    *weight_refs, out_ref, w_ref = refs
    fill_down(w_ref, weight_refs[:lines], weight_refs[lines:])
    sums = [act_ref[m] for m in range(act_ref.shape[0])]
    highs = [row.astype(low_type).astype(full_type) for row in sums]
    rests = [row - high for row, high in zip(sums, highs)]
    down = dot_nt(few_rows(highs + rests, 16).astype(low_type), w_ref[...])
    micro = len(sums)
    out_ref[...] = few_rows([down[m : m + 1] + down[micro + m : micro + m + 1] for m in range(micro)], 8)


def margin_kernel(len_ref, own_ref, other_ref, sum_ref, act_ref, vector_ref, send_ref):
    margins, rows = [], []
    for m in range(sum_ref.shape[0]):
        length = len_ref[m].astype(full_type)
        total = own_ref[m : m + 1] + other_ref[m : m + 1] + sum_ref[m]
        pooled = (total / length).astype(low_type).astype(full_type)
        final = pooled * rms_scale(pooled) * vector_ref[2:3]
        logits = [
            jnp.sum(final * vector_ref[i : i + 1], axis=1, keepdims=True) * pooled.shape[1] ** (-0.5)
            for i in (3, 4)
        ]
        lane = lax.broadcasted_iota(jnp.int32, pooled.shape, 1)
        margins.append(jnp.where(lane < LANES, logits[0] - logits[1], length))
        rows.append(pooled)
    width = rows[0].shape[1]
    for m in range(sum_ref.shape[0]):
        sums = act_ref[m]
        rows += [sums[:, i * width : (i + 1) * width] for i in range(sums.shape[1] // width)]
    send_ref[...] = few_rows(rows + margins, 8)


def ranking(margins, same, positive):
    place = lax.broadcasted_iota(jnp.int32, margins.shape, 0)
    lane = lax.broadcasted_iota(jnp.int32, margins.shape, 1)
    others = jnp.sum(jnp.where(place == lane, margins, 0.0), axis=0, keepdims=True)
    row_max = jnp.max(jnp.where(same, others, masked_score), axis=1, keepdims=True)
    terms = jnp.where(same, jnp.exp(jnp.where(same, others - row_max, 0.0)), 0.0)
    chance = jnp.exp(margins - row_max) / jnp.sum(terms, axis=1, keepdims=True)
    return LOSS_SCALE * (chance - positive)


def pooled_grad(pooled, d_margin, vector_ref):
    scale = rms_scale(pooled)
    d_logit = d_margin * pooled.shape[1] ** (-0.5)
    d_final = d_logit * (vector_ref[3:4] - vector_ref[4:5])
    return norm_input_grad(d_final, vector_ref[2:3], pooled, scale)


def rank_kernel(
    small_pieces, len_ref, same_ref, positive_ref, vector_ref, slope_ref, down_ref, up_ref, *refs
):
    small_refs, refs = refs[:small_pieces], refs[small_pieces:]
    line_ref, act_ref, rank_ref, hidden_ref, d_ref = refs
    m = pl.program_id(0)

    @pl.when(m == 0)
    def rank():
        lines = []
        for i in range(2):
            margins = stacked_row(small_refs, 6 + i)[:, :LANES]
            d_margins = ranking(margins, same_ref[i] > 0.5, positive_ref[i])
            rank_ref[i] = d_margins
            pooled = small_refs[0][0, i : i + 1, :]
            d_pooled = pooled_grad(pooled, d_margins[0:1, 0:1], vector_ref)
            lines.append(d_pooled / len_ref[i].astype(full_type))
        line_ref[...] = few_rows(lines, 8)
        d_act = dot_nn(few_rows(lines, 16).astype(low_type), down_ref[...])
        act_ref[...] = d_act[:8]

    d_row = jnp.where(m == 0, act_ref[0:1], act_ref[1:2])
    d_hidden = (slope_ref[...].astype(full_type) * d_row).astype(low_type)
    hidden_ref[...] = d_hidden
    d_normed = dot_nt(d_hidden, up_ref[...])
    valid = lax.broadcasted_iota(jnp.int32, (d_normed.shape[0], 1), 0) < len_ref[m]
    d_ref[...] = jnp.where(valid, d_normed, 0.0).astype(low_type)


def rank_back(lengths, same, positive, vectors, slope, small_all, down, up, slot, deps):
    count, inner = slope.shape
    width = vectors.shape[1]
    return call(
        functools.partial(rank_kernel, len(small_all)),
        "rank_backward",
        [
            shape_of((8, width), full_type),
            shape_of((8, inner), full_type),
            shape_of(positive.shape, full_type),
            shape_of((count, inner), low_type),
            shape_of((count, width), low_type),
        ],
        cost=(1200, 20000),
        deps=deps,
        grid=(count // slot,),
        in_specs=[
            on_scalars(),
            *(whole(array.shape) for array in (same, positive, vectors)),
            row_blocks((slot, inner)),
            *(whole(array.shape) for array in (down, up, *small_all)),
        ],
        out_specs=[
            whole((8, width)),
            whole((8, inner)),
            whole(positive.shape),
            row_blocks((slot, inner)),
            row_blocks((slot, width)),
        ],
    )(lengths, same, positive, vectors, slope, down, up, *small_all)


def up_grad_kernel(first, skip, normed_ref, d_ref, *out_refs):
    end = first + skip + sum(ref.shape[0] for ref in out_refs)
    for start in range(first, end, ROWS):
        stop = min(start + ROWS, -(-end // LANES) * LANES)
        grad = dot_tn(normed_ref[:, start:stop], d_ref[...])
        if start == first:
            spill_rows(grad[skip:], out_refs)
        else:
            spill_rows(grad, out_refs, start - first - skip)


def up_grad(normed, d_hidden, rows, first=0, skip=0, deps=()):
    return call(
        functools.partial(up_grad_kernel, first, skip),
        "hidden_in_gradient",
        [shape_of((r, d_hidden.shape[1]), low_type) for r in rows],
        cost=(1200, 15000),
        deps=deps,
    )(normed, d_hidden)


def middle_kernel(
    pieces, len_ref, x_ref, branch_ref, other_ref, own_ref, came_ref, vector_ref, line_ref,
    att_ref, inv_ref, *refs
):
    weight_refs, refs = refs[:pieces], refs[pieces:]
    d_ref, d_att_ref, total_ref, w_ref = refs
    m = pl.program_id(0)

    @pl.when(m == 0)
    def assemble():
        fill_rows(w_ref, weight_refs)
        total_ref[...] = jnp.zeros_like(total_ref)

    middle = middle_rows(x_ref, branch_ref, other_ref)
    own = own_ref[...].astype(full_type)
    scale = rms_scale(middle)
    valid = lax.broadcasted_iota(jnp.int32, (middle.shape[0], 1), 0) < len_ref[m]
    line = jnp.where(m == 0, line_ref[0:1], line_ref[1:2])
    d_middle = jnp.where(valid, line, 0.0) + norm_input_grad(
        own + came_ref[...].astype(full_type), vector_ref[1:2], middle, scale
    )
    d_ref[...] = d_middle
    d_low = d_middle.astype(low_type)
    d_att_ref[...] = (dot_nn(d_low, w_ref[...]) * inv_ref[...]).astype(low_type)
    total_ref[...] += dot_tn(d_low, att_ref[...])


def middle_back(
    lengths, rows_low, branch, other, own, came, vectors, lines, attended, inverse, weights, slot
):
    count, width = rows_low.shape
    head_width = attended.shape[1]
    return call(
        functools.partial(middle_kernel, len(weights)),
        "middle_backward",
        [
            shape_of((count, width), full_type),
            shape_of((count, head_width), low_type),
            shape_of((width, head_width), full_type),
        ],
        cost=(600, 15000),
        grid=(count // slot,),
        in_specs=[
            on_scalars(),
            *[row_blocks((slot, width))] * 5,
            whole(vectors.shape),
            whole(lines.shape),
            row_blocks((slot, head_width)),
            row_blocks((slot, head_width)),
            *(
                pl.BlockSpec((piece.shape[0], head_width), lambda i: (0, 3)) for piece in weights
            ),
        ],
        out_specs=[
            row_blocks((slot, width)),
            row_blocks((slot, head_width)),
            whole((width, head_width)),
        ],
        scratch_shapes=[pltpu.VMEM((width, head_width), low_type)],
    )(
        lengths, rows_low, branch, other, own, came, vectors, lines, attended, inverse, *weights
    )


def attention_back_kernel(
    befores, grads, tables, own, prob_ref, qkv_ref, d_ref, att_ref, turned_ref, hot_ref, *refs
):
    table_refs, refs = refs[:tables], refs[tables:]
    grad_refs, refs = refs[:grads], refs[grads:]
    d_out_ref, table_ref, *out_refs, tile_ref, dk_ref, dv_ref = refs[befores:]
    step, last = pl.program_id(0), pl.num_programs(0) - 1
    steps = last - 1 if grads else last

    if grads:

        @pl.when(step == last)
        def projection():
            spill_rows(grad_refs[0][...], out_refs)

    @pl.when(step <= steps)
    def heads():
        pair_back(
            prob_ref, qkv_ref, d_ref, att_ref, turned_ref, hot_ref, d_out_ref, table_ref, out_refs,
            tile_ref, dk_ref, dv_ref
        )
        if tables:
            lines = [
                ref[p, h : h + 1]
                for ref in (*table_refs, table_ref)
                for p in range(ref.shape[0])
                for h in range(2)
            ]
            width = turned_ref.shape[0]
            place = lax.broadcasted_iota(jnp.int32, (width, 16), 0) % own
            pick = place == lax.broadcasted_iota(jnp.int32, (width, 16), 1)
            pick = jnp.where(pick, 1.0, 0.0).astype(low_type)
            spread = dot_nn(pick, few_rows(lines, 16).astype(low_type))
            spill_rows(spread, [ref.at[:, 3 * LANES :] for ref in out_refs])


def pair_back(
    prob_ref, qkv_ref, d_ref, att_ref, turned_ref, hot_ref, d_out_ref, table_ref, out_refs,
    tile_ref, dk_ref, dv_ref
):
    micro, slot = prob_ref.shape[1], prob_ref.shape[3]
    blocks = slot // LANES
    spans = 2 * blocks - 1
    lanes = head_lanes()

    tile_ref[...] = jnp.zeros_like(tile_ref)

    def micro_step(m, carry):
        start = pl.multiple_of(m * slot, slot)
        everything = pl.ds(start, slot)
        keys, values = qkv_ref[0, 1, everything, :], qkv_ref[0, 2, everything, :]
        for r in range(slot // SPAN):
            rows = pl.ds(start + r * SPAN, SPAN)
            queries = qkv_ref[0, 0, rows, :]
            queries = jnp.concatenate(
                [queries * lanes[h].astype(low_type) for h in range(2)], axis=0
            )
            d_att = d_ref[rows, :]
            product = d_att.astype(full_type) * att_ref[rows, :].astype(full_type)
            row_dot = jnp.concatenate(
                [
                    jnp.sum(jnp.where(lanes[h], product, 0.0), axis=1, keepdims=True)
                    for h in range(2)
                ],
                axis=0,
            )
            d_att = jnp.concatenate([d_att * lanes[h].astype(low_type) for h in range(2)], axis=0)
            span = slice(r * SPAN, (r + 1) * SPAN)
            probs = jnp.concatenate([prob_ref[0, m, h, span, :] for h in range(2)], axis=0)
            d_scores = probs.astype(full_type) * (dot_nt(d_att, values) - row_dot)
            d_low = d_scores.astype(low_type)
            for h in range(2):
                for i in range(SPAN // LANES):
                    for j in range(blocks):
                        top = h * SPAN + i * LANES
                        tile_ref[h, j - r * (SPAN // LANES) - i + blocks - 1] += d_scores[
                            top : top + LANES, j * LANES : (j + 1) * LANES
                        ]
            d_queries = dot_nn(d_low, keys)
            d_out_ref[0, 0, rows, :] = jnp.where(
                lanes[0], d_queries[:SPAN], d_queries[SPAN:]
            ).astype(low_type)
            d_keys, d_values = dot_tn(d_low, queries), dot_tn(probs, d_att)
            dk_ref[...] = d_keys if r == 0 else dk_ref[...] + d_keys
            dv_ref[...] = d_values if r == 0 else dv_ref[...] + d_values
        d_out_ref[0, 1, everything, :] = dk_ref[...].astype(low_type)
        d_out_ref[0, 2, everything, :] = dv_ref[...].astype(low_type)
        return carry

    lax.fori_loop(0, micro, micro_step, 0, unroll=True)
    d_project = jnp.concatenate([d_out_ref[0, c] for c in range(3)], axis=1)
    spill_rows(dot_nn(turned_ref[...], d_project), [ref.at[:, : 3 * LANES] for ref in out_refs])
    flip = (
        lax.broadcasted_iota(jnp.int32, (LANES, LANES), 0)
        + lax.broadcasted_iota(jnp.int32, (LANES, LANES), 1)
        == LANES - 1
    )
    flip = jnp.where(flip, 1.0, 0.0).astype(low_type)
    tiles = tile_ref[...].reshape(2 * spans * LANES, LANES)
    high = tiles.astype(low_type)
    rest = (tiles - high.astype(full_type)).astype(low_type)
    flipped = dot_nn(high, flip) + dot_nn(rest, flip)
    zeros = jnp.zeros((LANES, LANES), full_type)
    lines = []
    for h in range(2):
        sums = []
        for d in range(spans):
            top = (h * spans + d) * LANES
            wide = jnp.concatenate([flipped[top : top + LANES], zeros], axis=1)
            turned = pltpu.roll(wide, 0, 1, stride=1, stride_axis=0)
            sums.append(jnp.sum(turned, axis=0, keepdims=True))
        lines.append(jnp.concatenate(sums, axis=1))
    highs = [line.astype(low_type).astype(full_type) for line in lines]
    rests = [line - high for line, high in zip(lines, highs)]
    table = dot_nn(few_rows(highs + rests, 16).astype(low_type), hot_ref[...])
    table_ref[0] = few_rows([table[h : h + 1] + table[2 + h : 3 + h] for h in range(2)], 8)


def attention_back(
    probs, qkv, d_attended, attended, turned, hot, rows, first, number, slot, own,
    grad_out=None, tables=(), before=(), deps=()
):
    width, count = turned.shape
    micro = count // slot
    pairs = qkv.shape[0]
    spans = 2 * (slot // LANES) - 1
    at = lambda i: jnp.minimum(i, number - 1)
    lead = lambda shape: pl.BlockSpec(shape, lambda i: (at(i) + first,) + (0,) * (len(shape) - 1))
    column = pl.BlockSpec((count, LANES), lambda i: (0, at(i) + first))
    if tables:
        steps, extra, extra_specs = number, tables, [whole(table.shape) for table in tables]
        gradients = [shape_of((r, 4 * LANES), low_type) for r in rows]
        gradient_specs = [whole((r, 4 * LANES)) for r in rows]
    else:
        steps = number + (grad_out is not None)
        extra = () if grad_out is None else (grad_out,)
        extra_specs = [whole(array.shape) for array in extra]
        gradients = [shape_of((r, pairs * 3 * LANES), low_type) for r in rows]
        gradient_specs = [pl.BlockSpec((r, 3 * LANES), lambda i: (0, i + first)) for r in rows]
    position = 6 + len(extra)
    return call(
        functools.partial(
            attention_back_kernel, len(before), 0 if grad_out is None else 1, len(tables), own
        ),
        "attention_backward",
        [
            shape_of((pairs, 3, count, LANES), low_type),
            shape_of((number, 8, LANES), full_type),
            *gradients,
        ],
        deps=deps,
        grid=(steps,),
        in_specs=[
            lead((1, micro, 2, slot, slot)),
            lead((1, 3, count, LANES)),
            column,
            column,
            whole(turned.shape),
            whole(hot.shape),
            *extra_specs,
            *[in_place()] * len(before),
        ],
        out_specs=[lead((1, 3, count, LANES)), pl.BlockSpec((1, 8, LANES), lambda i: (at(i), 0, 0)), *gradient_specs],
        input_output_aliases={position + i: i if i == 0 else i + 1 for i in range(len(before))},
        scratch_shapes=[
            pltpu.VMEM((2, spans, LANES, LANES), full_type),
            pltpu.VMEM((slot, LANES), full_type),
            pltpu.VMEM((slot, LANES), full_type),
        ],
    )(probs, qkv, d_attended, attended, turned, hot, *extra, *before)


def normed_back_kernel(d_ref, *refs):
    *weight_refs, out_ref, w_ref = refs
    pairs, parts = d_ref.shape[0], d_ref.shape[1]

    @pl.when(pl.program_id(0) == 0)
    def assemble():
        fill_rows(w_ref, weight_refs, slice(0, w_ref.shape[1]))

    blocks = [d_ref[p, c] for c in range(parts) for p in range(pairs)]
    d_normed = dot_nt(jnp.concatenate(blocks, axis=1), w_ref[...])
    out_ref[...] = d_normed.astype(low_type)


def normed_back(d_project, weights, deps):
    pairs, parts, count, _ = d_project.shape
    width = sum(piece.shape[0] for piece in weights)
    return call(
        normed_back_kernel,
        "normed_backward",
        shape_of((count, width), low_type),
        cost=(900, 15000),
        deps=deps,
        grid=(count // ROWS,),
        in_specs=[
            pl.BlockSpec((pairs, parts, ROWS, LANES), lambda i: (0, 0, i, 0)),
            *(whole(piece.shape) for piece in weights),
        ],
        out_specs=row_blocks((ROWS, width)),
        scratch_shapes=[pltpu.VMEM((width, pairs * parts * LANES), low_type)],
    )(d_project, *weights)


def token_kernel(d_ref, own_ref, came_ref, x_ref, vector_ref, order_ref, out_ref, done_ref):
    x = x_ref[...].astype(full_type)
    d_normed = own_ref[...].astype(full_type) + came_ref[...].astype(full_type)
    grad = d_ref[...] + norm_input_grad(d_normed, vector_ref[0:1], x, rms_scale(x))
    high = grad.astype(low_type)
    rest = (grad - high.astype(full_type)).astype(low_type)
    order = order_ref[...]
    out_ref[...] = dot_nt(high, order) + dot_nt(rest, order)
    done_ref[...] = jnp.zeros_like(done_ref)


def token_back(d_middle, own, came, rows_low, vectors, order, deps):
    count, width = rows_low.shape
    return call(
        token_kernel,
        "token_gradient",
        [shape_of((count, width), full_type), shape_of((8, LANES), full_type)],
        cost=(1200, 15000),
        deps=deps,
        grid=(count // ROWS,),
        in_specs=[row_blocks((ROWS, width))] * 4 + [whole(vectors.shape), whole(order.shape)],
        out_specs=[row_blocks((ROWS, width)), whole((8, LANES))],
    )(d_middle, own, came, rows_low, vectors, order)


def total_kernel(smalls, counts, micro, pairs, *refs):
    small_refs, refs = refs[:smalls], refs[smalls:]
    groups = []
    for count in counts:
        groups.append(refs[:count])
        refs = refs[count:]
    rank_ref, vector_ref, in_ref, up_ref, gain_ref, tied_ref, down_ref, line_ref, *out_refs = refs
    size, width = sum(ref.shape[0] for ref in small_refs), small_refs[0].shape[2]
    row_of = lambda row: stacked_row(small_refs, row)
    own = down_ref.shape[0]
    inverse = 1.0 / LOSS_SCALE
    add_up = lambda values: jnp.sum(values, axis=0, keepdims=True).sum(axis=1, keepdims=True)
    squares, sums = 0.0, []
    for group, out_ref in zip(groups, out_refs):
        total = sum(ref[...].astype(full_type) for ref in group) * inverse
        total, rest = total[:, : out_ref.shape[1]], total[:, out_ref.shape[1] :]
        out_ref[...] = total
        sums.append((total, rest))
        squares = squares + add_up(total * total)
    table = sums[1][1]

    block = lax.broadcasted_iota(jnp.int32, (size, width), 1) // own
    mine = block == lax.broadcasted_iota(jnp.int32, (size, width), 0)
    fold = lax.broadcasted_iota(jnp.int32, (width, LANES), 0) % own == lax.broadcasted_iota(
        jnp.int32, (width, LANES), 1
    )
    fold = jnp.where(fold, 1.0, 0.0).astype(low_type)
    down, ranked = 0.0, 0.0
    lane = lax.broadcasted_iota(jnp.int32, (1, LANES), 1)
    own_factor = (vector_ref[3:4, :LANES] - vector_ref[4:5, :LANES]) * vector_ref[2:3, :LANES]
    own_factor = jnp.where(lane < own, own_factor, 0.0)
    parts = down_ref.shape[1] // width
    for m in range(micro):
        pooled = row_of(m)
        scale = rms_scale(pooled)
        lengths = row_of(micro + micro * parts + m)
        margins, lengths = lengths[:, 0:1], lengths[:, LANES : LANES + 1]
        d_logit = rank_ref[m][:, 0:1] * width ** (-0.5)
        mean = d_logit * margins * (width**0.5 / width) / scale
        mine_low = dot_nn(jnp.where(mine, pooled, 0.0).astype(low_type), fold)
        ranked = ranked + jnp.sum(mine_low * scale * d_logit, axis=0, keepdims=True)
        d_pooled = scale * d_logit * own_factor - mine_low * scale**3 * mean
        lines = (d_pooled / lengths).astype(low_type)
        acts = [row_of(micro + m * parts + i) for i in range(parts)]
        acts = jnp.concatenate(acts, axis=1)
        high = acts.astype(low_type)
        rest = (acts - high.astype(full_type)).astype(low_type)
        down = down + dot_tn(lines, high) + dot_tn(lines, rest)
    down = down[:own] * inverse
    down_ref[...] = down
    squares = squares + add_up(down * down)

    ranked = ranked[:, :own] * inverse
    rounded = lambda ref, i: ref[i : i + 1].astype(low_type).astype(full_type)
    tied_gap = rounded(tied_ref, 0) - rounded(tied_ref, 1)

    def through(products):
        ones = jnp.ones((16, products.shape[1]), low_type)
        high = products.astype(low_type)
        rest = (products - high.astype(full_type)).astype(low_type)
        return (dot_nt(ones, high) + dot_nt(ones, rest))[0:1]

    weighed = lambda ref, total: ref.astype(low_type).astype(full_type) * total
    first = 0.0
    for p in range(pairs):
        source = sums[0][0] if p < pairs - 1 else sums[1][0]
        offset = p * 3 * LANES if p < pairs - 1 else 0
        for c in range(3):
            columns = slice(offset + c * LANES, offset + (c + 1) * LANES)
            first = first + weighed(in_ref[c, :, p * LANES : (p + 1) * LANES], source[:, columns])
    rows = [
        through(first) / rounded(gain_ref, 0),
        through(weighed(up_ref[...], sums[2][0])) / rounded(gain_ref, 1),
        tied_gap * ranked,
        rounded(gain_ref, 2) * ranked,
    ]
    place = lax.broadcasted_iota(jnp.int32, (8, own), 0)
    extra = jnp.zeros((8, own), full_type)
    for i, row in enumerate(rows):
        extra = jnp.where(place == i, row, extra)
    line_ref[...] = jnp.zeros_like(line_ref)
    line_ref[:8, :own] = extra
    line_ref[8:16] = jnp.broadcast_to(squares, (8, LANES))
    line_ref[16 : 16 + 2 * pairs] = table[: 2 * pairs]


def totals(
    small_all, ranks, vectors, grads, heads_in, hidden_in, gains, tied_rows, widths, micro, deps
):
    counts = tuple(len(group) for group in grads)
    flat = [array for group in grads for array in group]
    own, inner = hidden_in.shape
    down, line, *sums = call(
        functools.partial(
            total_kernel, len(small_all), counts, micro, heads_in.shape[2] // LANES
        ),
        "gradient_totals",
        [
            shape_of((own, inner), full_type),
            shape_of((24, LANES), full_type),
            *(shape_of((own, width), full_type) for width in widths),
        ],
        cost=(100, 10000),
        deps=deps,
    )(*small_all, *flat, ranks, vectors, heads_in, hidden_in, gains, tied_rows)
    return down, line, sums


def stage_kernel(*refs):
    count = len(refs) // 2
    for ref, target in zip(refs[:count], refs[count:]):
        target[...] = ref[...]


def adam(weight, first_old, second, grad, factor, rate, decay, step_ref):
    clipped = grad * factor
    next_first = beta_first * first_old + (1.0 - beta_first) * clipped
    next_second = beta_second * second + (1.0 - beta_second) * clipped * clipped
    first_hat = next_first * step_ref[0]
    second_hat = next_second * step_ref[1]
    next_weight = weight - rate * (first_hat / (jnp.sqrt(second_hat) + adam_eps) + decay * weight)
    return next_weight, next_first, next_second


def square_kernel(heads, own_ref, other_ref, out_ref, extra_ref):
    place = lax.broadcasted_iota(jnp.int32, (8, LANES), 0)
    extra = own_ref[:8] + jnp.where(place < 2, other_ref[:8], 0.0)
    extra_ref[...] = extra
    counted = jnp.where(place == 3, 2.0, 1.0) * extra * extra
    add_up = lambda values: jnp.sum(values, axis=0, keepdims=True).sum(axis=1, keepdims=True)
    squares = own_ref[8:16] + other_ref[8:16] + add_up(counted)
    out_ref[:8] = squares
    tables = own_ref[16:24] * own_ref[16:24] + other_ref[16:24] * other_ref[16:24]
    out_ref[8:16] = own_ref[16:24]
    out_ref[16:24] = jnp.broadcast_to(add_up(tables), (8, LANES))


def update_kernel(size, squares, groups, me_ref, step_ref, extra_ref, *refs):
    square_refs, refs = refs[:squares], refs[squares:]
    grad_refs, refs = refs[:groups], refs[groups:]
    state_refs, refs = refs[:21], refs[21:]
    norm_ref, *out_refs = refs
    tiles = stacked(square_refs)
    place = lax.broadcasted_iota(jnp.int32, (tiles.shape[0], 1, 1), 0)
    first = device_of(place, me_ref[0], size) == 0
    tables = jnp.sum(jnp.where(first, tiles[:, 8:24], 0.0), axis=0)
    norm = jnp.sqrt(jnp.sum(tiles[:, 0:8], axis=0)[0:1, 0:1] + tables[8:9, 0:1])
    norm_ref[...] = norm
    factor = jnp.minimum(1.0, clip_limit / (norm + 1e-06))
    weights, firsts, seconds = state_refs[:7], state_refs[7:14], state_refs[14:]
    next_weights, next_firsts, next_seconds = out_refs[:7], out_refs[7:14], out_refs[14:]

    def step(index, where, grad, rate, decay):
        results = adam(
            weights[index][where], firsts[index][where], seconds[index][where], grad, factor,
            rate, decay, step_ref,
        )
        for target, result in zip((next_weights, next_firsts, next_seconds), results):
            target[index][where] = result

    everything = (slice(None), slice(None))
    early_ref, late_ref, up_ref, down_ref = grad_refs
    pairs = weights[0].shape[2] // LANES
    for p in range(pairs):
        source, offset = (early_ref, p * 3) if p < pairs - 1 else (late_ref, 0)
        for c in range(3):
            columns = slice((offset + c) * LANES, (offset + c + 1) * LANES)
            where = (c, slice(None), slice(p * LANES, (p + 1) * LANES))
            step(0, where, source[:, columns], rate_matrix, decay_matrix)
    step(1, everything, early_ref[:, (pairs - 1) * 3 * LANES :], rate_matrix, decay_matrix)
    step(2, everything, up_ref[...], rate_matrix, decay_matrix)
    step(3, everything, down_ref[...], rate_matrix, decay_matrix)
    rows = weights[4].shape[1]
    extra = extra_ref[...]
    step(4, everything, extra[0:3, :rows], rate_vector, 0.0)
    tied = extra[3:4, :rows]
    step(5, everything, jnp.concatenate([tied, -tied], axis=0), rate_vector, 0.0)
    step(6, everything, tables[: 2 * pairs, :BUCKETS], rate_vector, 0.0)


def update(size, pick, corrections, extra, squares, grads, states):
    return call(
        functools.partial(update_kernel, size, len(squares), len(grads)),
        "update",
        [shape_of((1, 1), full_type)] + [shape_of(s.shape, full_type) for s in states],
        cost=(0, 6000),
        grid=(1,),
        in_specs=[
            on_scalars(),
            on_scalars(),
            *(whole(array.shape) for array in (extra, *squares, *grads, *states)),
        ],
    )(pick, corrections, extra, *squares, *grads, *states)


def body(
    tokens,
    pair_lengths,
    query_ids,
    distance_bucket,
    step_count,
    heads_in,
    heads_out,
    hidden_in,
    hidden_out,
    gains,
    tied_rows,
    bias_table,
    first_heads_in,
    first_heads_out,
    first_hidden_in,
    first_hidden_out,
    first_gains,
    first_tied,
    first_table,
    second_heads_in,
    second_heads_out,
    second_hidden_in,
    second_hidden_out,
    second_gains,
    second_tied,
    second_table,
):
    size = lax.axis_size("dp")
    me = lax.axis_index("dp")
    core = lax.axis_index("mp")
    micro, _, slot, width = tokens.shape
    count = micro * slot
    own, local_heads = heads_in.shape[0], bias_table.shape[1]
    head_width = heads_in.shape[2]
    inner = hidden_in.shape[1]
    pairs = local_heads // 2
    spans = 2 * (slot // LANES) - 1
    turn_matrix = lambda array: jnp.transpose(array, (1, 0, 2))
    heads_in, first_heads_in, second_heads_in = (
        turn_matrix(array) for array in (heads_in, first_heads_in, second_heads_in)
    )
    gains, tied_rows, bias_table = gains.T, tied_rows.T, bias_table.T
    first_gains, first_tied, first_table = first_gains.T, first_tied.T, first_table.T
    second_gains, second_tied, second_table = second_gains.T, second_tied.T, second_table.T

    packed_heads = call(
        pack_heads_kernel, "pack_heads", shape_of((own, 4 * head_width + LANES), low_type), vmem=56
    )(heads_in, heads_out, gains, tied_rows)
    down_widths = [inner] if size != 16 else [inner - inner // 3, inner // 3]
    packed_up, packed_down, *packed_plane = call(
        pack_hidden_kernel,
        "pack_hidden",
        [shape_of((own, width_here), low_type) for width_here in (inner, *down_widths)],
    )(hidden_in, hidden_out)
    weights = (heads_in, heads_out, hidden_in, hidden_out, gains, tied_rows, bias_table)
    firsts = (
        first_heads_in,
        first_heads_out,
        first_hidden_in,
        first_hidden_out,
        first_gains,
        first_tied,
        first_table,
    )
    seconds = (
        second_heads_in,
        second_heads_out,
        second_hidden_in,
        second_hidden_out,
        second_gains,
        second_tied,
        second_table,
    )
    states = [*weights, *firsts, *seconds]
    large = [index for index, state in enumerate(states) if index % 7 < 4]
    staged = call(
        stage_kernel, "stage", [shape_of(states[i].shape, full_type) for i in large], vmem=56
    )(*(states[i] for i in large))
    for i, array in zip(large, staged):
        states[i] = array

    lengths = pair_lengths.reshape(micro)
    device = me.reshape(1)
    order, lines, hot_spans, same_tile, positive_tile = call(
        functools.partial(prepare_kernel, size),
        "prepare",
        [
            shape_of((width, width), low_type),
            shape_of((pairs, 2, 2 * slot), full_type),
            shape_of((spans * 2 * LANES, LANES), low_type),
            shape_of((micro, size, LANES), full_type),
            shape_of((micro, size, LANES), full_type),
        ],
        grid=(1,),
        in_specs=[
            on_scalars(),
            whole((1, 2 * slot)),
            whole(bias_table.shape),
            whole(query_ids.shape),
        ],
    )(
        device,
        jnp.pad(distance_bucket, (0, 1), constant_values=-1).reshape(1, 2 * slot),
        bias_table,
        query_ids,
    )
    step_float = step_count.astype(full_type)
    corrections = jnp.stack(
        [1.0 / (1.0 - beta_first**step_float), 1.0 / (1.0 - beta_second**step_float)]
    )

    rows_low = call(
        order_kernel,
        "order_tokens",
        shape_of((count, width), low_type),
        cost=(600, 5000),
        grid=(count // ROWS,),
        in_specs=[row_blocks((ROWS, width)), whole((width, width))],
        out_specs=row_blocks((ROWS, width)),
    )(tokens.reshape(count, width), order)
    if size != 16:
        weight_heads, weight_up, weight_down = (
            [gather_doubling(part, size)] for part in (packed_heads, packed_up, packed_down)
        )
        planes = []
        qkv, normed_first, vectors = project(rows_low, weight_heads, pairs, ())
    else:
        plane_sides = side_parts(*packed_plane, size, "down_plane")
        heads_line, packed_up, packed_down = join(
            line_parts(packed_heads, size, "heads"),
            deps=(staged[0], order, corrections, *plane_sides),
            passing=(packed_up, packed_down),
        )
        heads_sides = side_parts(heads_line, size, "heads")
        up_pair = join([packed_up, swap(packed_up, 8, size, "up")], deps=(rows_low,))
        up_near = swap(up_pair, 4, size, "up")
        plane_corner = swap(plane_sides[0], 1, size, "down_plane_corner")
        low, high, packed_down = gather_step(
            *heads_sides, deps=(up_pair, plane_corner), passing=(packed_down,)
        )
        down_far = swap(packed_down, 8, size, "down")
        heads_corner = corner_parts(low, high, size, "heads_corner")
        up_line = join([up_pair, up_near], deps=(low,))
        down_pair = join([packed_down, down_far], deps=(up_line,))
        down_near = swap(down_pair, 4, size, "down")
        up_sides = side_parts(up_line, size, "up")
        weight_heads = [heads_line, *heads_sides, *heads_corner]
        qkv, normed_first, vectors = project(rows_low, weight_heads, pairs, ())
    filled = attention(
        lengths, lines, qkv, 0, 1, slot, deps=(down_pair,) if size == 16 else ()
    )
    if size == 16:
        down_line = join([down_pair, down_near], deps=(filled[0],))
        down_sides = side_parts(down_line, size, "down")
        plane = join([*packed_plane, *plane_sides, plane_corner], deps=(down_line,))
        plane_far = swap(plane, 8, size, "down_plane")
    if pairs > 1:
        filled = attention(lengths, lines, qkv, 1, pairs - 1, slot, before=filled)
    if size == 16:
        low, high = gather_step(*up_sides, deps=(filled[0],))
        up_corner = corner_parts(low, high, size, "up_corner")
        plane_pair = join([plane, plane_far], deps=(filled[0],))
        planes = [plane_pair, swap(plane_pair, 4, size, "down_plane")]
        weight_up = [up_line, *up_sides, *up_corner]
    turned_first = call(turn_kernel, "turn", shape_of((width, count), low_type))(normed_first)
    attended, probs, inverse = filled
    branch = branch_rows(
        attended, weight_heads, (low, plane_pair, *down_sides, turned_first) if size == 16 else ()
    )
    if size == 16:
        low, high = gather_step(*down_sides, deps=(branch,))
        down_corner = corner_parts(low, high, size, "down_corner")
        weight_down = [down_line, *down_sides, *down_corner]
    branch_came = other_core(branch, "branch_other_core")
    normed_second, slope, act_sum, middle_sum, full_up = hidden(
        lengths, rows_low, branch, branch_came, vectors, weight_up, slot
    )
    down, full_down = call(
        functools.partial(pool_kernel, len(weight_down)),
        "pool",
        [shape_of((8, width), full_type), shape_of((width, inner), low_type)],
        cost=(20, 5000),
    )(act_sum, *weight_down, *planes)
    small = call(
        margin_kernel,
        "margin",
        shape_of((8, width), full_type),
        grid=(1,),
        in_specs=[
            on_scalars(),
            *(whole(array.shape) for array in (down, down, middle_sum, act_sum, vectors)),
        ],
        out_specs=whole((8, width)),
    )(lengths, down, other_core(down, "pooled_part_other_core"), middle_sum, act_sum, vectors)
    small_all = gather_small(small, size, "small_sums")

    d_line, _, ranks, d_hidden, d_normed_second = rank_back(
        lengths, same_tile, positive_tile, vectors, slope, small_all, full_down, full_up, slot,
        (turned_first,),
    )
    d_normed_second_came = other_core(d_normed_second, "second_gradient_other_core")
    rows = piece_rows(size, width)
    if size == 16:
        start = sum(rows[:3])
        aligned = start // ROWS * ROWS
        corner = up_grad(normed_second, d_hidden, rows[3:], aligned, start - aligned)
        up_rows = [*up_grad(normed_second, d_hidden, rows[:3], deps=(corner[0],)), *corner]
    else:
        up_rows = up_grad(normed_second, d_hidden, rows)
    up_sum = Scatter(up_rows, size, "up_gradient")
    d_middle, d_attended, g_out = middle_back(
        lengths, rows_low, branch, branch_came, d_normed_second, d_normed_second_came, vectors,
        d_line, attended, inverse, weight_heads, slot,
    )
    scatter_sides([up_sum], deps=(d_attended,))
    d_project, tables, *g_early = attention_back(
        probs, qkv, d_attended, attended, turned_first, hot_spans, piece_rows(size, width),
        0, pairs - 1, slot, own, grad_out=g_out,
    )
    early_sum = Scatter(g_early, size, "early_gradient")
    d_project, table, *g_late = attention_back(
        probs, qkv, d_attended, attended, turned_first, hot_spans, piece_rows(size, width),
        pairs - 1, 1, slot, own, tables=(tables,), before=(d_project,),
    )
    late_sum = Scatter(g_late, size, "late_gradient")
    up_sum.near(deps=(table,))
    sides = scatter_sides([early_sum, late_sum], deps=up_sum.sources)
    d_normed_first = normed_back(d_project, weight_heads, sides)
    up_parts = up_sum.far(deps=sides)
    (d_normed_first,) = early_sum.near(deps=tuple(up_parts), passing=(d_normed_first,))
    early_parts = early_sum.far()
    late_parts, _ = late_sum.line(deps=(early_parts[0],))

    token_gradient, token_done = token_back(
        d_middle, d_normed_first, other_core(d_normed_first, "first_gradient_other_core"), rows_low,
        vectors, order, late_sum.sources,
    )

    g_down, line, grad_sums = totals(
        small_all, ranks, vectors, [early_parts, late_parts, up_parts], heads_in, hidden_in, gains, tied_rows,
        (head_width * 3, 3 * LANES, inner), micro, (token_done,),
    )
    square_tile, extra = call(
        functools.partial(square_kernel, local_heads),
        "squares",
        [shape_of((24, LANES), full_type), shape_of((8, LANES), full_type)],
    )(line, other_core(line, "totals_other_core"))
    squares_all = gather_small(square_tile, size, "squares")
    grads = [*grad_sums, g_down]
    norm, *results = update(size, device, corrections, extra, squares_all, grads, states)
    for index in (0, 7, 14):
        results[index] = turn_matrix(results[index])
        for other in (4, 5, 6):
            results[index + other] = results[index + other].T
    return (norm.reshape(()), token_gradient.reshape(tokens.shape), *results)


def solution(mesh):
    in_specs = (
        P(None, "dp", None, None),
        P(None, "dp"),
        P(),
        P(),
        P(),
        P("dp", None, "mp"),
        P("dp", "mp"),
        P("dp", "mp"),
        P("dp", "mp"),
        P("dp", None),
        P("dp", None),
        P(None, "mp"),
        P("dp", None, "mp"),
        P("dp", "mp"),
        P("dp", "mp"),
        P("dp", "mp"),
        P("dp", None),
        P("dp", None),
        P(None, "mp"),
        P("dp", None, "mp"),
        P("dp", "mp"),
        P("dp", "mp"),
        P("dp", "mp"),
        P("dp", None),
        P("dp", None),
        P(None, "mp"),
    )
    out_specs = (
        P(),
        P(None, "dp", None, None),
        P("dp", None, "mp"),
        P("dp", "mp"),
        P("dp", "mp"),
        P("dp", "mp"),
        P("dp", None),
        P("dp", None),
        P(None, "mp"),
        P("dp", None, "mp"),
        P("dp", "mp"),
        P("dp", "mp"),
        P("dp", "mp"),
        P("dp", None),
        P("dp", None),
        P(None, "mp"),
        P("dp", None, "mp"),
        P("dp", "mp"),
        P("dp", "mp"),
        P("dp", "mp"),
        P("dp", None),
        P("dp", None),
        P(None, "mp"),
    )
    return jax.shard_map(body, mesh=mesh, in_specs=in_specs, out_specs=out_specs, check_vma=False)
```
